32 devices in a mesh: seq: 8 (over z, y), head: 4 (over x, core).
Axes of the slice: x: 2, y: 2, z: 4, core: 2. Of those that a mesh axis runs over, the one named last changes fastest.
Arguments:
- queries: bfloat16 [4096, 4096], P(('seq', 'head')), may hold values from -52 to 52
- keys: bfloat16 [4096, 4096], P(('seq', 'head')), may hold values from -4 to 4
- values: bfloat16 [4096, 4096], P(('seq', 'head')), may hold values from -32 to 32
- grad_out: bfloat16 [4096, 4096], P(('seq', 'head')), may hold values from -64 to 64
- rand_blocks: int32 [32, 64, 3], P('head', 'seq'), may hold values from 0 to 63, as said below
- global_ids: int32 [2], replicated, may hold values from 0 to 63
- drop_mask: int32 [32, 64, 8], P('head', 'seq'), may hold values 0 or 1
Outputs:
- attended: bfloat16 [4096, 4096], P('seq', 'head')
- grad_queries: bfloat16 [4096, 4096], P('seq', 'head')
- grad_keys: bfloat16 [4096, 4096], P('seq', 'head')
- grad_values: bfloat16 [4096, 4096], P('seq', 'head')
The draws below stay inside these ranges and needn't reach their ends.
Inputs may be any that keep to these rules, and one draw needn't show every extreme that they name: `rand_blocks`: for every sequence shard s (query blocks s * 8 onward) and head group g (heads g * 8 onward), the 192 listed random blocks come from a g-dependent hot shard exactly 30 times, and from no shard more than 30 times; the rest spread evenly over the other shards; the hot shard is the same for all s of one head group.
All inputs are finite; a program needn't handle non-finite values. No bound on the sum of `drop_mask` on one device may be relied on, other than what follows from the above.
Results may differ from the reference program's by a relative error of at most 0.015.
Values may be sent and summed in bfloat16 or wider, within the bound.
No kernel may reach another device: no remote copies, remote signals or barrier semaphores. Data moves between devices by JAX's collectives and lax.ppermute only.
A program may use at most 128 MiB of HBM per device.

```python
import jax
import jax.numpy as jnp
from jax import lax

D = 4096
H = 32
HEAD_WIDTH = 128
BLOCK_TOKENS = 64
R = 3
G = 2
SEQ_LEN = 4096
SEQUENCE_BLOCKS = 64
NBD = 8
HD = 8
KEY_BLOCKS = 8
REQ = 192
CAP = 30


def query_key_pair(key):
    key_seed = jax.random.fold_in(key, 11)
    query_seed = jax.random.fold_in(key, 12)
    shape = (SEQ_LEN, D)
    key_rows = jax.random.truncated_normal(key_seed, -4.0, 4.0, shape, jnp.float32)
    query_lines = jax.random.truncated_normal(query_seed, -4.0, 4.0, shape, jnp.float32)
    return (key_rows, query_lines)


def draw_queries(key, part):
    return query_key_pair(key)[1].astype(jnp.bfloat16)


def draw_keys(key, part):
    return query_key_pair(key)[0].astype(jnp.bfloat16)


def draw_rand_blocks(key, part):
    shard_count = SEQUENCE_BLOCKS // NBD
    group_count = H // HD
    hottest = jax.random.randint(jax.random.fold_in(key, 21), (group_count,), 0, shard_count)
    position = jnp.arange(REQ)
    others = (hottest[None, :, None] + 1 + (position[None, None, :] - CAP) % (shard_count - 1)) % shard_count
    labels = jnp.where(position[None, None, :] < CAP, hottest[None, :, None], others)
    labels = jnp.broadcast_to(labels, (shard_count, group_count, REQ))
    noise = jax.random.randint(jax.random.fold_in(key, 22), (shard_count, group_count, REQ), 0, 2 ** 20)
    order = jnp.argsort(noise * REQ + position[None, None, :], axis=-1, stable=True)
    labels = jnp.take_along_axis(labels, order, axis=-1)
    inside = jax.random.randint(jax.random.fold_in(key, 23), (shard_count, group_count, REQ), 0, NBD)
    chosen = labels * NBD + inside
    chosen = chosen.reshape(shard_count, group_count, HD, NBD, R).transpose(1, 2, 0, 3, 4)
    return chosen.reshape(H, SEQUENCE_BLOCKS, R).astype(jnp.int32)


def with_ends(entries, stream_key, smallest, top_value):
    place = [jax.random.randint(jax.random.fold_in(stream_key, axis), (), 0, length) for axis, length in enumerate(entries.shape)]
    widest = entries.shape.index(max(entries.shape))
    neighbour = place[:widest] + [(place[widest] + 1) % entries.shape[widest]] + place[widest + 1:]
    return entries.at[tuple(place)].set(smallest).at[tuple(neighbour)].set(top_value)


def level_of(own_key, shape, cuts, least, top_value):
    loudness, own = 1.0, jax.random.fold_in(own_key, 6)
    for axis_at, parts in cuts:
        steps = jnp.exp(jax.random.uniform(jax.random.fold_in(own, axis_at), (parts,), jnp.float32, least / len(cuts), top_value / len(cuts)))
        loudness = loudness * jnp.repeat(steps, shape[axis_at] // parts).reshape([-1 if axis == axis_at else 1 for axis in range(len(shape))])
    return loudness


def bell_draw(key, extent, scale, reach, shards=(), held_as=jnp.bfloat16):
    array = scale * jax.random.normal(key, extent, jnp.float32)
    if shards:
        array = array * level_of(key, extent, shards, -0.22, 0.18)
    return jnp.clip(array, -reach, reach).astype(held_as)


def setup_inputs(seed: int = 0) -> dict:
    splits = jax.random.split(jax.random.key(seed), 8)
    queries = draw_queries(jax.random.fold_in(splits[7], 71), 0)
    keys = draw_keys(jax.random.fold_in(splits[7], 71), 0)
    values = bell_draw(splits[2], (SEQ_LEN, D), 6.0, 32.0, ((0, 32),))
    grad_out = bell_draw(splits[3], (SEQ_LEN, D), 12.0, 64.0, ((0, 32),))
    rand_blocks = draw_rand_blocks(jax.random.fold_in(splits[7], 71), 0)
    global_ids = jax.random.randint(splits[5], (G,), 0, SEQUENCE_BLOCKS).astype(jnp.int32)
    drop_mask = with_ends((jax.random.randint(splits[6], (H, SEQUENCE_BLOCKS, KEY_BLOCKS), 0, 10) < 9).astype(jnp.int32), jax.random.fold_in(splits[6], 1), 0, 1)
    return {"queries": queries, "keys": keys, "values": values, "grad_out": grad_out, "rand_blocks": rand_blocks, "global_ids": global_ids, "drop_mask": drop_mask}


keep_prob = 0.9


def head_major(tensor):
    return tensor.reshape(SEQUENCE_BLOCKS, BLOCK_TOKENS, H, HEAD_WIDTH).transpose(2, 0, 1, 3)


def token_major(tensor):
    return tensor.transpose(1, 2, 0, 3).reshape(SEQ_LEN, D)


def reference(queries, keys, values, grad_out, rand_blocks, global_ids, drop_mask):
    logit_scale = HEAD_WIDTH ** -0.5
    blocks = jnp.arange(SEQUENCE_BLOCKS, dtype=jnp.int32)
    window = jnp.stack([blocks - 1, blocks, blocks + 1], axis=1)
    globals_listed = jnp.broadcast_to(global_ids.astype(jnp.int32)[None, :], (SEQUENCE_BLOCKS, G))
    present = jnp.concatenate([(blocks >= 1)[:, None], jnp.ones((SEQUENCE_BLOCKS, 1), bool), (blocks <= SEQUENCE_BLOCKS - 2)[:, None], jnp.ones((SEQUENCE_BLOCKS, G + R), bool)], axis=1)
    wide_present = jnp.repeat(present, BLOCK_TOKENS, axis=1)[:, None, :]

    def one_head(inputs):
        query_lines, key_rows, value_rows, gradient_rows, random_ids, drop_bits = inputs
        key_lists = jnp.concatenate([window, globals_listed, random_ids.astype(jnp.int32)], axis=1)
        safe_ids = jnp.clip(key_lists, 0, SEQUENCE_BLOCKS - 1).astype(jnp.int32)
        every_key = key_rows[safe_ids].reshape(SEQUENCE_BLOCKS, KEY_BLOCKS * BLOCK_TOKENS, HEAD_WIDTH).astype(jnp.float32)
        every_value = value_rows[safe_ids].reshape(SEQUENCE_BLOCKS, KEY_BLOCKS * BLOCK_TOKENS, HEAD_WIDTH).astype(jnp.float32)
        query_float = query_lines.astype(jnp.float32)
        float_gradient = gradient_rows.astype(jnp.float32)
        attention_logits = jnp.einsum('ran,rln->ral', query_float, every_key) * logit_scale
        attention_logits = jnp.where(wide_present, attention_logits, -jnp.inf)
        top = jnp.max(attention_logits, axis=-1, keepdims=True)
        expd = jnp.exp(attention_logits - top)
        probs = expd / jnp.sum(expd, axis=-1, keepdims=True)
        retain_scale = jnp.repeat(drop_bits.astype(jnp.float32) / keep_prob, BLOCK_TOKENS, axis=1)[:, None, :]
        after_dropout = (probs * retain_scale).astype(jnp.bfloat16).astype(jnp.float32)
        attended = jnp.einsum('ymn,ynh->ymh', after_dropout, every_value).astype(jnp.bfloat16)
        probability_grad = jnp.einsum('ran,rln->ral', float_gradient, every_value) * retain_scale
        delta = jnp.sum(probs * probability_grad, axis=-1, keepdims=True)
        score_grad = (probs * (probability_grad - delta)).astype(jnp.bfloat16).astype(jnp.float32)
        query_gradient = (jnp.einsum('ymn,ynh->ymh', score_grad, every_key) * logit_scale).astype(jnp.bfloat16)
        key_pieces = (jnp.einsum('efu,efy->euy', score_grad, query_float) * logit_scale).reshape(SEQUENCE_BLOCKS, KEY_BLOCKS, BLOCK_TOKENS, HEAD_WIDTH)
        value_pieces = jnp.einsum('efu,efy->euy', after_dropout, float_gradient).reshape(SEQUENCE_BLOCKS, KEY_BLOCKS, BLOCK_TOKENS, HEAD_WIDTH)
        split_position = 3 + G
        rounded_k = lax.optimization_barrier(key_pieces[:, split_position:].astype(jnp.bfloat16)).astype(jnp.float32)
        rounded_v = lax.optimization_barrier(value_pieces[:, split_position:].astype(jnp.bfloat16)).astype(jnp.float32)
        key_pieces = jnp.concatenate([key_pieces[:, :split_position], rounded_k], axis=1)
        value_pieces = jnp.concatenate([value_pieces[:, :split_position], rounded_v], axis=1)
        grad_k = jnp.zeros((SEQUENCE_BLOCKS, BLOCK_TOKENS, HEAD_WIDTH), jnp.float32).at[safe_ids].add(key_pieces)
        grad_v = jnp.zeros((SEQUENCE_BLOCKS, BLOCK_TOKENS, HEAD_WIDTH), jnp.float32).at[safe_ids].add(value_pieces)
        return attended, query_gradient, grad_k.astype(jnp.bfloat16), grad_v.astype(jnp.bfloat16)

    results = lax.map(one_head, (head_major(queries), head_major(keys), head_major(values), head_major(grad_out), rand_blocks, drop_mask))
    return (token_major(results[0]), token_major(results[1]), token_major(results[2]), token_major(results[3]))
```

```python
import functools

import jax
import jax.numpy as jnp
from jax import lax
from jax.experimental import pallas as pl
from jax.experimental.pallas import tpu as pltpu
from jax.sharding import PartitionSpec as P

HEAD_WIDTH = 128
BLOCK_TOKENS = 64
R = 3
G = 2
SLOTS = 3 + G + R

keep_prob = 0.9


def attention_kernel(
    last_block,
    ids_ref,
    first_ref,
    drop_ref,
    q_ref,
    do_ref,
    k_ref,
    v_ref,
    att_ref,
    dq_ref,
    dk_ref,
    dv_ref,
    dk_acc,
    dv_acc,
    retain,
):
    scale = HEAD_WIDTH ** (-0.5)
    wide = SLOTS * BLOCK_TOKENS
    steps = drop_ref.shape[0]
    slot_of_lane = lax.broadcasted_iota(jnp.int32, (SLOTS, wide), 1) // BLOCK_TOKENS
    slot_row = lax.broadcasted_iota(jnp.int32, (SLOTS, wide), 0)
    expand = (slot_of_lane == slot_row).astype(jnp.float32)
    retain[...] = jnp.dot(
        drop_ref[...].astype(jnp.float32), expand, preferred_element_type=jnp.float32
    ) * (1.0 / keep_prob)
    dk_acc[...] = jnp.zeros_like(dk_acc)
    dv_acc[...] = jnp.zeros_like(dv_acc)
    lane = lax.broadcasted_iota(jnp.int32, (1, wide), 1)
    nt = (((1,), (1,)), ((), ()))
    tn = (((0,), (0,)), ((), ()))

    def one_block(j):
        rows = pl.ds(pl.multiple_of(j * BLOCK_TOKENS, BLOCK_TOKENS), BLOCK_TOKENS)
        places = [
            pl.ds(pl.multiple_of(ids_ref[j * SLOTS + s] * BLOCK_TOKENS, BLOCK_TOKENS), BLOCK_TOKENS)
            for s in range(SLOTS)
        ]
        block_id = first_ref[0] + j
        absent = ((block_id == 0) & (lane < BLOCK_TOKENS)) | (
            (block_id == last_block) & (lane >= 2 * BLOCK_TOKENS) & (lane < 3 * BLOCK_TOKENS)
        )
        q = q_ref[rows, :]
        do = do_ref[rows, :]
        keys = jnp.concatenate([k_ref[p, :] for p in places], axis=0)
        vals = jnp.concatenate([v_ref[p, :] for p in places], axis=0)
        logits = lax.dot_general(q, keys, nt, preferred_element_type=jnp.float32) * scale
        logits = jnp.where(absent, -jnp.inf, logits)
        top = jnp.max(logits, axis=-1, keepdims=True)
        expd = jnp.exp(logits - top)
        probs = expd * (1.0 / jnp.sum(expd, axis=-1, keepdims=True))
        keep = retain[pl.ds(j, 1), :]
        dropped = (probs * keep).astype(jnp.bfloat16)
        dprobs = lax.dot_general(do, vals, nt, preferred_element_type=jnp.float32) * keep
        delta = jnp.sum(probs * dprobs, axis=-1, keepdims=True)
        dscores = (probs * (dprobs - delta)).astype(jnp.bfloat16)
        att_ref[rows, :] = jnp.dot(dropped, vals, preferred_element_type=jnp.float32).astype(
            jnp.bfloat16
        )
        dq_ref[rows, :] = (
            jnp.dot(dscores, keys, preferred_element_type=jnp.float32) * scale
        ).astype(jnp.bfloat16)
        key_terms = lax.dot_general(dscores, q, tn, preferred_element_type=jnp.float32) * scale
        value_terms = lax.dot_general(dropped, do, tn, preferred_element_type=jnp.float32)
        for s, p in enumerate(places):
            part = slice(s * BLOCK_TOKENS, (s + 1) * BLOCK_TOKENS)
            dk_acc[p, :] += key_terms[part]
            dv_acc[p, :] += value_terms[part]

    def step(j, carry):
        one_block(j)
        return carry

    lax.fori_loop(0, steps, step, 0)
    dk_ref[...] = dk_acc[...].astype(dk_ref.dtype)
    dv_ref[...] = dv_acc[...].astype(dv_ref.dtype)


def attend(ids, first_block, drop, q, do, k, v, last_block, grad_type):
    steps = drop.shape[0]
    length = k.shape[0]
    vmem = pl.BlockSpec(memory_space=pltpu.VMEM)
    smem = pl.BlockSpec(memory_space=pltpu.SMEM)
    rows = q.shape
    pairs = steps * BLOCK_TOKENS * SLOTS * BLOCK_TOKENS
    return pl.pallas_call(
        functools.partial(attention_kernel, last_block),
        out_shape=(
            jax.ShapeDtypeStruct(rows, jnp.bfloat16),
            jax.ShapeDtypeStruct(rows, jnp.bfloat16),
            jax.ShapeDtypeStruct(k.shape, grad_type),
            jax.ShapeDtypeStruct(k.shape, grad_type),
        ),
        in_specs=[smem, smem, vmem, vmem, vmem, vmem, vmem],
        out_specs=(vmem, vmem, vmem, vmem),
        scratch_shapes=[
            pltpu.VMEM((length, HEAD_WIDTH), jnp.float32),
            pltpu.VMEM((length, HEAD_WIDTH), jnp.float32),
            pltpu.VMEM((steps, SLOTS * BLOCK_TOKENS), jnp.float32),
        ],
        compiler_params=pltpu.CompilerParams(vmem_limit_bytes=56 * 1024 * 1024),
        cost_estimate=pl.CostEstimate(
            flops=12 * pairs * HEAD_WIDTH,
            bytes_accessed=2 * (4 * q.size + 4 * k.size),
            transcendentals=pairs,
        ),
    )(ids, first_block, drop, q, do, k, v)


def per_device(queries, keys, values, grad_out, rand_blocks, global_ids, drop_mask):
    shards = lax.axis_size("seq")
    groups = lax.axis_size("head")
    shard = lax.axis_index("seq")
    heads, shard_blocks, _ = rand_blocks.shape
    tokens = queries.shape[0]
    teams = shards // heads
    team, member = shard // heads, shard % heads
    team_blocks = heads * shard_blocks
    total_blocks = shards * shard_blocks
    first_block = team * team_blocks
    whole = teams == 1
    same_team = None if whole else [[t * heads + m for m in range(heads)] for t in range(teams)]
    same_team_all = (
        None
        if whole
        else [
            [(t * heads + m) * groups + g for m in range(heads) for g in range(groups)]
            for t in range(teams)
        ]
    )
    same_head = [[t * heads + m for t in range(teams)] for m in range(heads)]

    tables = lax.all_gather(
        jnp.concatenate([rand_blocks, drop_mask], axis=2), "seq", axis=1, tiled=True
    )
    tables = lax.dynamic_slice(
        tables, (member, first_block, 0), (1, team_blocks, R + SLOTS)
    )[0]

    def by_head(tensor):
        return tensor.reshape(tokens, groups, heads, HEAD_WIDTH).transpose(2, 1, 0, 3)

    sent = jnp.stack([by_head(t) for t in (queries, keys, values, grad_out)], axis=2)
    sent = sent.reshape(heads * groups, 4, tokens, HEAD_WIDTH)
    got = lax.all_to_all(
        sent, ("seq", "head"), split_axis=0, concat_axis=0, tiled=True, axis_index_groups=same_team_all
    )
    q, k, v, do = [got[:, i].reshape(-1, HEAD_WIDTH) for i in range(4)]
    if not whole:
        k, v = [
            lax.all_gather(t, "seq", axis=0, tiled=True, axis_index_groups=same_head)
            for t in (k, v)
        ]
    blocks = first_block + jnp.arange(team_blocks, dtype=jnp.int32)
    window = jnp.stack([blocks - 1, blocks, blocks + 1], axis=1)
    listed = jnp.concatenate(
        [window, jnp.broadcast_to(global_ids[None], (team_blocks, G)), tables[:, :R]], axis=1
    )
    listed = jnp.clip(listed, 0, total_blocks - 1).reshape(-1)
    att, dq, dk, dv = attend(
        listed,
        first_block.reshape(1),
        tables[:, R:],
        q,
        do,
        k,
        v,
        total_blocks - 1,
        jnp.bfloat16 if whole else jnp.float32,
    )
    if not whole:
        dk, dv = [
            lax.psum_scatter(
                t, "seq", scatter_dimension=0, tiled=True, axis_index_groups=same_head
            ).astype(jnp.bfloat16)
            for t in (dk, dv)
        ]
    back = jnp.stack(
        [t.reshape(heads, groups * tokens, HEAD_WIDTH) for t in (att, dq, dk, dv)], axis=1
    )
    back = lax.all_to_all(
        back, "seq", split_axis=0, concat_axis=0, tiled=True, axis_index_groups=same_team
    )
    return tuple(
        back[:, i].transpose(1, 0, 2).reshape(groups * tokens, heads * HEAD_WIDTH)
        for i in range(4)
    )


def solution(mesh):
    return jax.shard_map(
        per_device,
        mesh=mesh,
        in_specs=(
            P(("seq", "head"), None),
            P(("seq", "head"), None),
            P(("seq", "head"), None),
            P(("seq", "head"), None),
            P("head", "seq", None),
            P(),
            P("head", "seq", None),
        ),
        out_specs=(P("seq", "head"), P("seq", "head"), P("seq", "head"), P("seq", "head")),
        check_vma=False,
    )
```

```python
import functools

import jax
import jax.numpy as jnp
from jax import lax
from jax.experimental import pallas as pl
from jax.experimental.pallas import tpu as pltpu
from jax.sharding import PartitionSpec as P

HEAD_WIDTH = 128
BLOCK_TOKENS = 64
R = 3
G = 2
SLOTS = 3 + G + R
VMEM_LIMIT = 56 * 1024 * 1024

keep_prob = 0.9

vmem = pl.BlockSpec(memory_space=pltpu.VMEM)
smem = pl.BlockSpec(memory_space=pltpu.SMEM)


def copy_cost(size):
    return pl.CostEstimate(flops=0, bytes_accessed=4 * size, transcendentals=0)


def pack_kernel(groups, heads, begin, *refs):
    sources, tables, out_ref = refs[:2], refs[2:-1], refs[-1]
    rows = (out_ref.shape[1] - (tables[0].shape[1] if tables else 0)) // 2
    for m in range(heads):
        for g in range(groups):
            columns = pl.ds((g * heads + m) * HEAD_WIDTH, HEAD_WIDTH)
            for n, ref in enumerate(sources):
                out_ref[m * groups + g, pl.ds(n * rows, rows), :] = ref[pl.ds(begin, rows), columns]
            for ref in tables:
                out_ref[m * groups + g, pl.ds(2 * rows, ref.shape[1]), :] = ref[m]


def pack(first, second, begin, rows, groups, heads, tables=()):
    extra = sum(t.shape[1] for t in tables)
    shape = (groups * heads, 2 * rows + extra, HEAD_WIDTH)
    return pl.pallas_call(
        functools.partial(pack_kernel, groups, heads, begin),
        out_shape=jax.ShapeDtypeStruct(shape, jnp.bfloat16),
        in_specs=[vmem] * (2 + len(tables)),
        out_specs=vmem,
        compiler_params=pltpu.CompilerParams(vmem_limit_bytes=VMEM_LIMIT),
        cost_estimate=copy_cost(shape[0] * shape[1] * shape[2]),
    )(first, second, *tables)


def unpack_kernel(device_blocks, *refs):
    pieces, outs = refs[:-2], refs[-2:]
    per = device_blocks // len(pieces)
    for c, piece in enumerate(pieces):
        heads, _, rows, _ = piece.shape
        run = per * BLOCK_TOKENS
        for n, out in enumerate(outs):
            for m in range(heads):
                for i in range(rows // run):
                    target = (i * device_blocks + c * per) * BLOCK_TOKENS
                    out[pl.ds(target, run), pl.ds(m * HEAD_WIDTH, HEAD_WIDTH)] = piece[
                        m, n, pl.ds(i * run, run), :
                    ]


def unpack(device_blocks, *pieces):
    heads = pieces[0].shape[0]
    rows = sum(p.shape[2] for p in pieces)
    shape = jax.ShapeDtypeStruct((rows, heads * HEAD_WIDTH), jnp.bfloat16)
    return pl.pallas_call(
        functools.partial(unpack_kernel, device_blocks),
        out_shape=(shape, shape),
        in_specs=[vmem] * len(pieces),
        out_specs=(vmem, vmem),
        compiler_params=pltpu.CompilerParams(vmem_limit_bytes=VMEM_LIMIT),
        cost_estimate=copy_cost(2 * rows * heads * HEAD_WIDTH),
    )(*pieces)


def attention_kernel(
    last_block, device_blocks, piece, has_start, is_last, ids_ref, first_ref, drop_ref, qd_ref, kv_ref, *refs
):
    refs = list(refs)
    starts = [refs.pop(0), refs.pop(0)] if has_start else None
    out_ref = refs.pop(0)
    if is_last:
        dkv_ref, dk_acc, dv_acc, retain = refs
    else:
        dk_acc, dv_acc, retain = refs
    scale = HEAD_WIDTH ** (-0.5)
    wide = SLOTS * BLOCK_TOKENS
    per = qd_ref.shape[1] // (2 * BLOCK_TOKENS)
    steps = qd_ref.shape[0] * per
    tokens = device_blocks * BLOCK_TOKENS
    slot_of_lane = lax.broadcasted_iota(jnp.int32, (SLOTS, wide), 1) // BLOCK_TOKENS
    slot_row = lax.broadcasted_iota(jnp.int32, (SLOTS, wide), 0)
    expand = (slot_of_lane == slot_row).astype(jnp.float32)
    retain[...] = jnp.dot(
        drop_ref[...].astype(jnp.float32), expand, preferred_element_type=jnp.float32
    ) * (1.0 / keep_prob)
    dk_acc[...] = starts[0][...] if has_start else jnp.zeros_like(dk_acc)
    dv_acc[...] = starts[1][...] if has_start else jnp.zeros_like(dv_acc)
    lane = lax.broadcasted_iota(jnp.int32, (1, wide), 1)
    nt = (((1,), (1,)), ((), ()))
    tn = (((0,), (0,)), ((), ()))
    out_steps = steps // out_ref.shape[0]

    def block_rows(number):
        return pl.ds(pl.multiple_of(number * BLOCK_TOKENS, BLOCK_TOKENS), BLOCK_TOKENS)

    def one_block(i):
        source, sub = i // per, i % per
        j = source * device_blocks + piece * per + sub
        ids = [ids_ref[j * SLOTS + s] for s in range(SLOTS)]
        places = [block_rows(b) for b in ids]
        block_id = first_ref[0] + j
        absent = ((block_id == 0) & (lane < BLOCK_TOKENS)) | (
            (block_id == last_block) & (lane >= 2 * BLOCK_TOKENS) & (lane < 3 * BLOCK_TOKENS)
        )
        q = qd_ref[source, block_rows(sub), :]
        do = qd_ref[source, block_rows(per + sub), :]
        keys = jnp.concatenate(
            [kv_ref[b // device_blocks, block_rows(b % device_blocks), :] for b in ids], axis=0
        )
        vals = jnp.concatenate(
            [
                kv_ref[b // device_blocks, block_rows(device_blocks + b % device_blocks), :]
                for b in ids
            ],
            axis=0,
        )
        logits = lax.dot_general(q, keys, nt, preferred_element_type=jnp.float32) * scale
        logits = jnp.where(absent, -jnp.inf, logits)
        top = jnp.max(logits, axis=-1, keepdims=True)
        expd = jnp.exp(logits - top)
        probs = expd * (1.0 / jnp.sum(expd, axis=-1, keepdims=True))
        keep = retain[pl.ds(j, 1), :]
        dropped = (probs * keep).astype(jnp.bfloat16)
        dprobs = lax.dot_general(do, vals, nt, preferred_element_type=jnp.float32) * keep
        delta = jnp.sum(probs * dprobs, axis=-1, keepdims=True)
        dscores = (probs * (dprobs - delta)).astype(jnp.bfloat16)
        target, pos = i // out_steps, i % out_steps
        out_ref[target, 0, block_rows(pos), :] = jnp.dot(
            dropped, vals, preferred_element_type=jnp.float32
        ).astype(jnp.bfloat16)
        out_ref[target, 1, block_rows(pos), :] = (
            jnp.dot(dscores, keys, preferred_element_type=jnp.float32) * scale
        ).astype(jnp.bfloat16)
        key_terms = lax.dot_general(dscores, q, tn, preferred_element_type=jnp.float32) * scale
        value_terms = lax.dot_general(dropped, do, tn, preferred_element_type=jnp.float32)
        return places, key_terms, value_terms

    def step(i, carry):
        done = [one_block(2 * i), one_block(2 * i + 1)]
        for places, key_terms, value_terms in done:
            for s, p in enumerate(places):
                part = slice(s * BLOCK_TOKENS, (s + 1) * BLOCK_TOKENS)
                dk_acc[p, :] += key_terms[part]
                dv_acc[p, :] += value_terms[part]
        return carry

    lax.fori_loop(0, steps // 2, step, 0)
    if is_last:
        shards, _, rows, _ = dkv_ref.shape
        for s in range(shards):
            dkv_ref[s, 0] = dk_acc[pl.ds(s * rows, rows), :].astype(dkv_ref.dtype)
            dkv_ref[s, 1] = dv_acc[pl.ds(s * rows, rows), :].astype(dkv_ref.dtype)


def attend(ids, first_block, drop, qd, kv, starts, piece, is_last, device_blocks, total_blocks, shards, targets, grad_type):
    team_blocks = drop.shape[0]
    steps = qd.shape[0] * qd.shape[1] // (2 * BLOCK_TOKENS)
    length = total_blocks * BLOCK_TOKENS
    pairs = steps * BLOCK_TOKENS * SLOTS * BLOCK_TOKENS
    accumulator = (length, HEAD_WIDTH)
    out_shape = [
        jax.ShapeDtypeStruct((targets, 2, steps * BLOCK_TOKENS // targets, HEAD_WIDTH), jnp.bfloat16)
    ]
    scratch = [pltpu.VMEM((team_blocks, SLOTS * BLOCK_TOKENS), jnp.float32)]
    if is_last:
        out_shape.append(
            jax.ShapeDtypeStruct((shards, 2, length // shards, HEAD_WIDTH), grad_type)
        )
        scratch = [pltpu.VMEM(accumulator, jnp.float32)] * 2 + scratch
    else:
        out_shape += [jax.ShapeDtypeStruct(accumulator, jnp.float32)] * 2
    return pl.pallas_call(
        functools.partial(
            attention_kernel, total_blocks - 1, device_blocks, piece, bool(starts), is_last
        ),
        out_shape=out_shape,
        in_specs=[smem, smem] + [vmem] * (3 + len(starts)),
        out_specs=[vmem] * len(out_shape),
        scratch_shapes=scratch,
        compiler_params=pltpu.CompilerParams(vmem_limit_bytes=VMEM_LIMIT),
        cost_estimate=pl.CostEstimate(
            flops=12 * pairs * HEAD_WIDTH,
            bytes_accessed=2 * (2 * qd.size + kv.size) + 8 * length * HEAD_WIDTH,
            transcendentals=pairs,
        ),
    )(ids, first_block, drop, qd, kv, *starts)


def per_device(queries, keys, values, grad_out, rand_blocks, global_ids, drop_mask):
    shards = lax.axis_size("seq")
    groups = lax.axis_size("head")
    shard = lax.axis_index("seq")
    heads, shard_blocks, _ = rand_blocks.shape
    tokens = queries.shape[0]
    device_blocks = tokens // BLOCK_TOKENS
    teams = shards // heads
    team = shard // heads
    team_blocks = heads * shard_blocks
    total_blocks = shards * shard_blocks
    first_block = team * team_blocks
    whole = teams == 1
    pieces = device_blocks if whole else 1
    rows = tokens // pieces
    same_team = None if whole else [[t * heads + m for m in range(heads)] for t in range(teams)]
    same_team_all = (
        None
        if whole
        else [
            [(t * heads + m) * groups + g for m in range(heads) for g in range(groups)]
            for t in range(teams)
        ]
    )
    same_head = [[t * heads + m for t in range(teams)] for m in range(heads)]

    def to_heads(packed):
        return lax.all_to_all(
            packed,
            ("seq", "head"),
            split_axis=0,
            concat_axis=0,
            tiled=True,
            axis_index_groups=same_team_all,
        )

    def to_shards(results):
        return lax.all_to_all(
            results, "seq", split_axis=0, concat_axis=0, tiled=True, axis_index_groups=same_team
        )

    table_rows = -(-shard_blocks // 16) * 16
    tables = jnp.concatenate([rand_blocks, drop_mask], axis=2).astype(jnp.bfloat16)
    tables = jnp.pad(
        tables, ((0, 0), (0, table_rows - shard_blocks), (0, HEAD_WIDTH - R - SLOTS))
    )
    kv = to_heads(pack(keys, values, 0, tokens, groups, heads, (tables,)))
    qd = [
        to_heads(pack(queries, grad_out, c * rows, rows, groups, heads)) for c in range(pieces)
    ]
    tables = lax.dynamic_index_in_dim(
        kv.reshape(heads, groups, -1, HEAD_WIDTH)[
            :, :, 2 * tokens : 2 * tokens + shard_blocks, : R + SLOTS
        ],
        lax.axis_index("head"),
        axis=1,
        keepdims=False,
    )
    tables = tables.reshape(team_blocks, R + SLOTS).astype(jnp.int32)
    if not whole:
        kv = lax.all_gather(kv, "seq", axis=0, tiled=True, axis_index_groups=same_head)
    blocks = first_block + jnp.arange(team_blocks, dtype=jnp.int32)
    window = jnp.stack([blocks - 1, blocks, blocks + 1], axis=1)
    listed = jnp.concatenate(
        [window, jnp.broadcast_to(global_ids[None], (team_blocks, G)), tables[:, :R]], axis=1
    )
    listed = jnp.clip(listed, 0, total_blocks - 1).reshape(-1)
    near, sums = [], ()
    for c in range(pieces):
        result, *sums = attend(
            listed,
            first_block.reshape(1),
            tables[:, R:],
            qd[c],
            kv,
            sums,
            c,
            c == pieces - 1,
            device_blocks,
            total_blocks,
            shards,
            heads,
            jnp.bfloat16 if whole else jnp.float32,
        )
        near.append(to_shards(result))
    grads = sums[0]
    if not whole:
        grads = lax.psum_scatter(
            grads, "seq", scatter_dimension=0, tiled=True, axis_index_groups=same_head
        ).astype(jnp.bfloat16)
    grads = to_shards(grads)
    return (*unpack(device_blocks, *near), *unpack(device_blocks, grads))


def solution(mesh):
    return jax.shard_map(
        per_device,
        mesh=mesh,
        in_specs=(
            P(("seq", "head"), None),
            P(("seq", "head"), None),
            P(("seq", "head"), None),
            P(("seq", "head"), None),
            P("head", "seq", None),
            P(),
            P("head", "seq", None),
        ),
        out_specs=(P("seq", "head"), P("seq", "head"), P("seq", "head"), P("seq", "head")),
        check_vma=False,
    )
```

```python
import functools
import math

import jax
import jax.numpy as jnp
from jax import lax
from jax.experimental import pallas as pl
from jax.experimental.pallas import tpu as pltpu
from jax.sharding import PartitionSpec as P

HEAD_WIDTH = 128
BLOCK_TOKENS = 64
R = 3
G = 2
SLOTS = 3 + G + R
WIDE = SLOTS * BLOCK_TOKENS
UNROLL = 4
VMEM_LIMIT = 56 * 1024 * 1024

keep_prob = 0.9

vmem = pl.BlockSpec(memory_space=pltpu.VMEM)
smem = pl.BlockSpec(memory_space=pltpu.SMEM)


def copy_cost(size):
    return pl.CostEstimate(flops=0, bytes_accessed=4 * size, transcendentals=0)


def block_rows(number):
    start = number * BLOCK_TOKENS
    if not isinstance(number, int):
        start = pl.multiple_of(start, BLOCK_TOKENS)
    return pl.ds(start, BLOCK_TOKENS)


def pack_kernel(heads, *refs):
    out_ref = refs[-1]
    begin = 0
    for ref in refs[:-1]:
        if len(ref.shape) == 3:
            rows = ref.shape[1]
            for m in range(heads):
                out_ref[m, 0, pl.ds(begin, rows), :] = ref[m]
        else:
            rows = ref.shape[0]
            for m in range(heads):
                out_ref[m, 0, pl.ds(begin, rows), :] = ref[:, pl.ds(m * HEAD_WIDTH, HEAD_WIDTH)]
        begin += rows


def pack(groups, heads, *sources):
    specs, arrays, total = [], [], 0
    for source in sources:
        if isinstance(source, tuple):
            array, at, rows = source
            specs.append(
                pl.BlockSpec((rows, heads * HEAD_WIDTH), functools.partial(lambda at, g: (at, g), at))
            )
        else:
            array, rows = source, source.shape[1]
            specs.append(pl.BlockSpec(source.shape, lambda g: (0, 0, 0)))
        arrays.append(array)
        total += rows
    shape = (heads, groups, total, HEAD_WIDTH)
    packed = pl.pallas_call(
        functools.partial(pack_kernel, heads),
        grid=(groups,),
        out_shape=jax.ShapeDtypeStruct(shape, jnp.bfloat16),
        in_specs=specs,
        out_specs=pl.BlockSpec((heads, 1, total, HEAD_WIDTH), lambda g: (0, g, 0, 0)),
        compiler_params=pltpu.CompilerParams(vmem_limit_bytes=VMEM_LIMIT),
        cost_estimate=copy_cost(math.prod(shape)),
    )(*arrays)
    return packed.reshape(heads * groups, total, HEAD_WIDTH)


def unpack_kernel(begins, step_heads, piece_ref, *refs):
    outs = refs[len(refs) - len(begins) :]
    for begin, out in zip(begins, outs):
        runs, _, rows, _ = out.shape
        for m in range(step_heads):
            for i in range(runs):
                out[i, 0, :, pl.ds(m * HEAD_WIDTH, HEAD_WIDTH)] = piece_ref[
                    m, pl.ds(begin + i * rows, rows), :
                ]


def unpack(received, parts):
    heads, total, _ = received.shape
    step_heads = 2 if heads % 2 == 0 else 1
    width = step_heads * HEAD_WIDTH
    shapes, out_specs, begins, olds, aliases = [], [], [], [], {}
    size = 0
    for n, (begin, rows, runs, pieces, piece, old) in enumerate(parts):
        begins.append(begin)
        shapes.append(
            jax.ShapeDtypeStruct((runs, pieces, rows, heads * HEAD_WIDTH), jnp.bfloat16)
        )
        out_specs.append(
            pl.BlockSpec(
                (runs, 1, rows, width), functools.partial(lambda piece, h: (0, piece, 0, h), piece)
            )
        )
        size += rows * runs * heads * HEAD_WIDTH
        if old is not None:
            aliases[1 + len(olds)] = n
            olds.append(old)
    return pl.pallas_call(
        functools.partial(unpack_kernel, begins, step_heads),
        grid=(heads // step_heads,),
        out_shape=shapes,
        in_specs=[pl.BlockSpec((step_heads, total, HEAD_WIDTH), lambda h: (h, 0, 0))]
        + [pl.BlockSpec(memory_space=pl.ANY)] * len(olds),
        out_specs=out_specs,
        input_output_aliases=aliases,
        compiler_params=pltpu.CompilerParams(vmem_limit_bytes=VMEM_LIMIT),
        cost_estimate=copy_cost(size),
    )(received, *olds)


def attention_kernel(
    last_block,
    device_blocks,
    per,
    piece,
    qd_begin,
    has_qd,
    has_start,
    is_last,
    joined,
    ids_ref,
    first_ref,
    drop_ref,
    kv_ref,
    *refs,
):
    refs = list(refs)
    qd_ref = refs.pop(0) if has_qd else kv_ref
    start_ref = refs.pop(0) if has_start else None
    out_ref = refs.pop(0)
    dkv_ref = None
    if is_last and not joined:
        dkv_ref = refs.pop(0)
    acc, retain = refs
    scale = HEAD_WIDTH ** (-0.5)
    steps = qd_ref.shape[0] * per
    slot_of_lane = lax.broadcasted_iota(jnp.int32, (SLOTS, WIDE), 1) // BLOCK_TOKENS
    slot_row = lax.broadcasted_iota(jnp.int32, (SLOTS, WIDE), 0)
    expand = (slot_of_lane == slot_row).astype(jnp.float32)
    retain[...] = jnp.dot(
        drop_ref[...].astype(jnp.float32), expand, preferred_element_type=jnp.float32
    ) * (1.0 / keep_prob)
    acc[...] = start_ref[...] if has_start else jnp.zeros_like(acc)
    lane = lax.broadcasted_iota(jnp.int32, (1, WIDE), 1)
    nt = (((1,), (1,)), ((), ()))
    tn = (((0,), (0,)), ((), ()))
    targets = out_ref.shape[0]
    out_steps = steps // targets
    out_rows = out_steps * BLOCK_TOKENS
    q_block = qd_begin // BLOCK_TOKENS

    def load(i):
        source, sub = i // per, i % per
        j = source * device_blocks + piece * per + sub
        ids = [ids_ref[j * SLOTS + s] for s in range(SLOTS)]
        qd_rows = [pl.ds(qd_begin, BLOCK_TOKENS), pl.ds(qd_begin + BLOCK_TOKENS, BLOCK_TOKENS)]
        if per > 1:
            qd_rows = [
                pl.ds(pl.multiple_of(qd_begin + (n * per + sub) * BLOCK_TOKENS, 16), BLOCK_TOKENS)
                for n in range(2)
            ]
        q = qd_ref[source, qd_rows[0], :]
        do = qd_ref[source, qd_rows[1], :]
        keys, vals = [
            jnp.concatenate(
                [
                    kv_ref[b // device_blocks, block_rows(n * device_blocks + b % device_blocks), :]
                    for b in ids
                ],
                axis=0,
            )
            for n in range(2)
        ]
        keep = retain[pl.ds(j, 1), :]
        return i, first_ref[0] + j, ids, q, do, keys, vals, keep

    def work(i, block_id, ids, q, do, keys, vals, keep):
        absent = ((block_id == 0) & (lane < BLOCK_TOKENS)) | (
            (block_id == last_block) & (lane >= 2 * BLOCK_TOKENS) & (lane < 3 * BLOCK_TOKENS)
        )
        logits = lax.dot_general(q, keys, nt, preferred_element_type=jnp.float32)
        raw = lax.dot_general(do, vals, nt, preferred_element_type=jnp.float32)
        logits = jnp.where(absent, -jnp.inf, logits)
        top = jnp.max(logits, axis=-1, keepdims=True)
        expd = jnp.exp2((logits - top) * (scale / math.log(2.0)))
        probs = expd * (1.0 / jnp.sum(expd, axis=-1, keepdims=True))
        kept = probs * keep
        weighted = kept * raw
        delta = jnp.sum(weighted, axis=-1, keepdims=True)
        dropped = kept.astype(jnp.bfloat16)
        dscores = (weighted - probs * delta).astype(jnp.bfloat16)
        att = jnp.dot(dropped, vals, preferred_element_type=jnp.float32)
        dq = jnp.dot(dscores, keys, preferred_element_type=jnp.float32) * scale
        none = jnp.zeros_like(q)
        terms = lax.dot_general(
            jnp.concatenate([dscores, dropped], axis=0),
            jnp.concatenate(
                [jnp.concatenate([q, none], axis=1), jnp.concatenate([none, do], axis=1)], axis=0
            ),
            tn,
            preferred_element_type=jnp.float32,
        )
        for s, b in enumerate(ids):
            acc[block_rows(b), :] += terms[s * BLOCK_TOKENS : (s + 1) * BLOCK_TOKENS]
        target, pos = i // out_steps, i % out_steps
        out_ref[target, block_rows(pos), :] = att.astype(jnp.bfloat16)
        out_ref[target, block_rows(out_steps + pos), :] = dq.astype(jnp.bfloat16)

    def step(t, carry):
        loaded = [load(t * UNROLL + u) for u in range(UNROLL)]
        for block in loaded:
            work(*block)
        return carry

    lax.fori_loop(0, steps // UNROLL, step, 0)
    if is_last:
        target_ref, begin = (out_ref, 2 * out_rows) if joined else (dkv_ref, 0)
        shards = target_ref.shape[0]
        rows = acc.shape[0] // shards
        for s in range(shards):
            part = pl.ds(s * rows, rows)
            target_ref[s, pl.ds(begin, rows), :] = (acc[part, :HEAD_WIDTH] * scale).astype(
                target_ref.dtype
            )
            target_ref[s, pl.ds(begin + rows, rows), :] = acc[part, HEAD_WIDTH:].astype(
                target_ref.dtype
            )


def attend(
    ids, first_block, drop, kv, qd, qd_begin, start, piece, per, is_last, device_blocks, total_blocks, shards, targets
):
    team_blocks = drop.shape[0]
    source = kv if qd is None else qd
    steps = source.shape[0] * per
    length = total_blocks * BLOCK_TOKENS
    pairs = steps * BLOCK_TOKENS * WIDE
    joined = shards == targets
    accumulator = (length, 2 * HEAD_WIDTH)
    out_rows = 2 * steps * BLOCK_TOKENS // targets
    grad_rows = 2 * length // shards
    out_shape = []
    scratch = [pltpu.VMEM((team_blocks, WIDE), jnp.float32)]
    if is_last:
        scratch = [pltpu.VMEM(accumulator, jnp.float32)] + scratch
        if joined:
            out_rows += grad_rows
        else:
            out_shape.append(jax.ShapeDtypeStruct((shards, grad_rows, HEAD_WIDTH), jnp.float32))
    else:
        out_shape.append(jax.ShapeDtypeStruct(accumulator, jnp.float32))
    out_shape.insert(0, jax.ShapeDtypeStruct((targets, out_rows, HEAD_WIDTH), jnp.bfloat16))
    operands = [kv] + [t for t in (qd, start) if t is not None]
    return pl.pallas_call(
        functools.partial(
            attention_kernel,
            total_blocks - 1,
            device_blocks,
            per,
            piece,
            qd_begin,
            qd is not None,
            start is not None,
            is_last,
            joined,
        ),
        out_shape=out_shape,
        in_specs=[smem, smem, vmem] + [vmem] * len(operands),
        out_specs=[vmem] * len(out_shape),
        scratch_shapes=scratch,
        compiler_params=pltpu.CompilerParams(vmem_limit_bytes=VMEM_LIMIT),
        cost_estimate=pl.CostEstimate(
            flops=12 * pairs * HEAD_WIDTH,
            bytes_accessed=2 * (source.size + kv.size) + 8 * length * HEAD_WIDTH,
            transcendentals=pairs,
        ),
    )(ids, first_block, drop, *operands)


def per_device(queries, keys, values, grad_out, rand_blocks, global_ids, drop_mask):
    shards = lax.axis_size("seq")
    groups = lax.axis_size("head")
    shard = lax.axis_index("seq")
    heads, shard_blocks, _ = rand_blocks.shape
    tokens = queries.shape[0]
    device_blocks = tokens // BLOCK_TOKENS
    shard_tokens = shard_blocks * BLOCK_TOKENS
    teams = shards // heads
    team = shard // heads
    team_blocks = heads * shard_blocks
    total_blocks = shards * shard_blocks
    first_block = team * team_blocks
    whole = teams == 1
    pieces = device_blocks if whole else 1
    per = device_blocks // pieces
    rows = tokens // pieces
    same_team = None if whole else [[t * heads + m for m in range(heads)] for t in range(teams)]
    same_team_all = (
        None
        if whole
        else [
            [(t * heads + m) * groups + g for m in range(heads) for g in range(groups)]
            for t in range(teams)
        ]
    )
    same_head = [[t * heads + m for t in range(teams)] for m in range(heads)]

    def to_heads(packed):
        return lax.all_to_all(
            packed,
            ("seq", "head"),
            split_axis=0,
            concat_axis=0,
            tiled=True,
            axis_index_groups=same_team_all,
        )

    def to_shards(results):
        return lax.all_to_all(
            results, "seq", split_axis=0, concat_axis=0, tiled=True, axis_index_groups=same_team
        )

    table_rows = -(-shard_blocks // 16) * 16
    tables = jnp.concatenate([rand_blocks, drop_mask], axis=2).astype(jnp.bfloat16)
    tables = jnp.pad(
        tables, ((0, 0), (0, table_rows - shard_blocks), (0, HEAD_WIDTH - R - SLOTS))
    )
    kv_sources = [(keys, 0, tokens), (values, 0, tokens), tables]
    qd_sources = [[(queries, c, rows), (grad_out, c, rows)] for c in range(pieces)]
    qd_begin = 2 * tokens + table_rows
    kv = to_heads(pack(groups, heads, *kv_sources, *qd_sources[0]))
    later = [to_heads(pack(groups, heads, *sources)) for sources in qd_sources[1:]]
    tables = lax.dynamic_index_in_dim(
        kv.reshape(heads, groups, -1, HEAD_WIDTH)[
            :, :, 2 * tokens : 2 * tokens + shard_blocks, : R + SLOTS
        ],
        lax.axis_index("head"),
        axis=1,
        keepdims=False,
    )
    tables = tables.reshape(team_blocks, R + SLOTS).astype(jnp.int32)
    qd = [None] + later
    if not whole:
        qd[0] = kv[:, qd_begin:]
        kv = lax.all_gather(kv[:, : 2 * tokens], "seq", axis=0, tiled=True, axis_index_groups=same_head)
    blocks = first_block + jnp.arange(team_blocks, dtype=jnp.int32)
    window = jnp.stack([blocks - 1, blocks, blocks + 1], axis=1)
    listed = jnp.concatenate(
        [window, jnp.broadcast_to(global_ids[None], (team_blocks, G)), tables[:, :R]], axis=1
    )
    listed = jnp.clip(listed, 0, total_blocks - 1).reshape(-1)
    near = []
    sums = None
    for c in range(pieces):
        result, *sums = attend(
            listed,
            first_block.reshape(1),
            tables[:, R:],
            kv,
            qd[c],
            qd_begin if qd[c] is None else 0,
            sums[0] if sums else None,
            c,
            per,
            c == pieces - 1,
            device_blocks,
            total_blocks,
            shards,
            heads,
        )
        near.append(to_shards(result))
    runs = shard_blocks // device_blocks
    att, dq = None, None
    for c in range(pieces):
        begin = shard_tokens // pieces
        parts = [(0, rows, runs, pieces, c, att), (begin, rows, runs, pieces, c, dq)]
        if c < pieces - 1:
            att, dq = unpack(near[c], parts)
        elif whole:
            grads = [(2 * begin + n * shard_tokens, shard_tokens, 1, 1, 0, None) for n in range(2)]
            att, dq, dk, dv = unpack(near[c], parts + grads)
        else:
            att, dq = unpack(near[c], parts)
            grads = lax.psum_scatter(
                sums[0], "seq", scatter_dimension=0, tiled=True, axis_index_groups=same_head
            ).astype(jnp.bfloat16)
            grads = to_shards(grads)
            dk, dv = unpack(
                grads, [(n * shard_tokens, shard_tokens, 1, 1, 0, None) for n in range(2)]
            )
    return tuple(t.reshape(shard_tokens, heads * HEAD_WIDTH) for t in (att, dq, dk, dv))


def solution(mesh):
    return jax.shard_map(
        per_device,
        mesh=mesh,
        in_specs=(
            P(("seq", "head"), None),
            P(("seq", "head"), None),
            P(("seq", "head"), None),
            P(("seq", "head"), None),
            P("head", "seq", None),
            P(),
            P("head", "seq", None),
        ),
        out_specs=(P("seq", "head"), P("seq", "head"), P("seq", "head"), P("seq", "head")),
        check_vma=False,
    )
```

```python
import functools
import math

import jax
import jax.numpy as jnp
from jax import lax
from jax.experimental import pallas as pl
from jax.experimental.pallas import tpu as pltpu
from jax.sharding import PartitionSpec as P

HEAD_WIDTH = 128
BLOCK_TOKENS = 64
R = 3
G = 2
SLOTS = 3 + G + R
WIDE = SLOTS * BLOCK_TOKENS
UNROLL = 4
VMEM_LIMIT = 56 * 1024 * 1024

keep_prob = 0.9

vmem = pl.BlockSpec(memory_space=pltpu.VMEM)
smem = pl.BlockSpec(memory_space=pltpu.SMEM)


def copy_cost(size):
    return pl.CostEstimate(flops=0, bytes_accessed=4 * size, transcendentals=0)


def block_rows(number):
    start = number * BLOCK_TOKENS
    if not isinstance(number, int):
        start = pl.multiple_of(start, BLOCK_TOKENS)
    return pl.ds(start, BLOCK_TOKENS)


def pack_kernel(heads, *refs):
    out_ref = refs[-1]
    begin = 0
    for ref in refs[:-1]:
        if len(ref.shape) == 3:
            rows = ref.shape[1]
            for m in range(heads):
                out_ref[m, 0, pl.ds(begin, rows), :] = ref[m]
        else:
            rows = ref.shape[0]
            for m in range(heads):
                out_ref[m, 0, pl.ds(begin, rows), :] = ref[:, pl.ds(m * HEAD_WIDTH, HEAD_WIDTH)]
        begin += rows


def pack(groups, heads, *sources):
    specs, arrays, total = [], [], 0
    for source in sources:
        if isinstance(source, tuple):
            array, at, rows = source
            specs.append(
                pl.BlockSpec((rows, heads * HEAD_WIDTH), functools.partial(lambda at, g: (at, g), at))
            )
        else:
            array, rows = source, source.shape[1]
            specs.append(pl.BlockSpec(source.shape, lambda g: (0, 0, 0)))
        arrays.append(array)
        total += rows
    shape = (heads, groups, total, HEAD_WIDTH)
    packed = pl.pallas_call(
        functools.partial(pack_kernel, heads),
        grid=(groups,),
        out_shape=jax.ShapeDtypeStruct(shape, jnp.bfloat16),
        in_specs=specs,
        out_specs=pl.BlockSpec((heads, 1, total, HEAD_WIDTH), lambda g: (0, g, 0, 0)),
        compiler_params=pltpu.CompilerParams(vmem_limit_bytes=VMEM_LIMIT),
        cost_estimate=copy_cost(math.prod(shape)),
    )(*arrays)
    return packed.reshape(heads * groups, total, HEAD_WIDTH)


def unpack_kernel(begins, step_heads, piece_ref, *refs):
    outs = refs[len(refs) - len(begins) :]
    for begin, out in zip(begins, outs):
        runs, _, rows, _ = out.shape
        for m in range(step_heads):
            for i in range(runs):
                out[i, 0, :, pl.ds(m * HEAD_WIDTH, HEAD_WIDTH)] = piece_ref[
                    m, pl.ds(begin + i * rows, rows), :
                ]


def unpack(received, parts):
    heads, total, _ = received.shape
    step_heads = 2 if heads % 2 == 0 else 1
    width = step_heads * HEAD_WIDTH
    shapes, out_specs, begins, olds, aliases = [], [], [], [], {}
    size = 0
    for n, (begin, rows, runs, pieces, piece, old) in enumerate(parts):
        begins.append(begin)
        shapes.append(
            jax.ShapeDtypeStruct((runs, pieces, rows, heads * HEAD_WIDTH), jnp.bfloat16)
        )
        out_specs.append(
            pl.BlockSpec(
                (runs, 1, rows, width), functools.partial(lambda piece, h: (0, piece, 0, h), piece)
            )
        )
        size += rows * runs * heads * HEAD_WIDTH
        if old is not None:
            aliases[1 + len(olds)] = n
            olds.append(old)
    return pl.pallas_call(
        functools.partial(unpack_kernel, begins, step_heads),
        grid=(heads // step_heads,),
        out_shape=shapes,
        in_specs=[pl.BlockSpec((step_heads, total, HEAD_WIDTH), lambda h: (h, 0, 0))]
        + [pl.BlockSpec(memory_space=pl.ANY)] * len(olds),
        out_specs=out_specs,
        input_output_aliases=aliases,
        compiler_params=pltpu.CompilerParams(vmem_limit_bytes=VMEM_LIMIT),
        cost_estimate=copy_cost(size),
    )(received, *olds)


def attention_kernel(
    last_block,
    device_blocks,
    per,
    piece,
    qd_begin,
    has_qd,
    has_start,
    is_last,
    joined,
    ids_ref,
    first_ref,
    drop_ref,
    kv_ref,
    *refs,
):
    refs = list(refs)
    qd_ref = refs.pop(0) if has_qd else kv_ref
    start_ref = refs.pop(0) if has_start else None
    out_ref = refs.pop(0)
    dkv_ref = None
    if is_last and not joined:
        dkv_ref = refs.pop(0)
    acc, retain = refs
    scale = HEAD_WIDTH ** (-0.5)
    steps = qd_ref.shape[0] * per
    slot_of_lane = lax.broadcasted_iota(jnp.int32, (SLOTS, WIDE), 1) // BLOCK_TOKENS
    slot_row = lax.broadcasted_iota(jnp.int32, (SLOTS, WIDE), 0)
    expand = (slot_of_lane == slot_row).astype(jnp.float32)
    retain[...] = jnp.dot(
        drop_ref[...].astype(jnp.float32), expand, preferred_element_type=jnp.float32
    ) * (1.0 / keep_prob)
    acc[...] = start_ref[...] if has_start else jnp.zeros_like(acc)
    lane = lax.broadcasted_iota(jnp.int32, (1, WIDE), 1)
    nt = (((1,), (1,)), ((), ()))
    tn = (((0,), (0,)), ((), ()))
    targets = out_ref.shape[0]
    out_steps = steps // targets
    out_rows = out_steps * BLOCK_TOKENS
    q_block = qd_begin // BLOCK_TOKENS

    def load(i):
        source, sub = i // per, i % per
        j = source * device_blocks + piece * per + sub
        ids = [ids_ref[j * SLOTS + s] for s in range(SLOTS)]
        qd_rows = [pl.ds(qd_begin, BLOCK_TOKENS), pl.ds(qd_begin + BLOCK_TOKENS, BLOCK_TOKENS)]
        if per > 1:
            qd_rows = [
                pl.ds(pl.multiple_of(qd_begin + (n * per + sub) * BLOCK_TOKENS, 16), BLOCK_TOKENS)
                for n in range(2)
            ]
        q = qd_ref[source, qd_rows[0], :]
        do = qd_ref[source, qd_rows[1], :]
        listed = jnp.concatenate(
            [
                jnp.concatenate(
                    [
                        kv_ref[b // device_blocks, block_rows(n * device_blocks + b % device_blocks), :]
                        for n in range(2)
                    ],
                    axis=1,
                )
                for b in ids
            ],
            axis=0,
        )
        keep = retain[pl.ds(j, 1), :]
        return i, first_ref[0] + j, ids, q, do, listed, keep

    def work(i, block_id, ids, q, do, listed, keep):
        absent = ((block_id == 0) & (lane < BLOCK_TOKENS)) | (
            (block_id == last_block) & (lane >= 2 * BLOCK_TOKENS) & (lane < 3 * BLOCK_TOKENS)
        )
        none = jnp.zeros_like(q)
        pair = jnp.concatenate(
            [jnp.concatenate([q, none], axis=1), jnp.concatenate([none, do], axis=1)], axis=0
        )
        both = lax.dot_general(pair, listed, nt, preferred_element_type=jnp.float32)
        logits, raw = both[:BLOCK_TOKENS], both[BLOCK_TOKENS:]
        logits = jnp.where(absent, -jnp.inf, logits)
        top = jnp.max(logits, axis=-1, keepdims=True)
        expd = jnp.exp2((logits - top) * (scale / math.log(2.0)))
        probs = expd * (1.0 / jnp.sum(expd, axis=-1, keepdims=True))
        kept = probs * keep
        weighted = kept * raw
        delta = jnp.sum(weighted, axis=-1, keepdims=True)
        factors = jnp.concatenate(
            [(weighted - probs * delta).astype(jnp.bfloat16), kept.astype(jnp.bfloat16)], axis=0
        )
        near = jnp.dot(factors, listed, preferred_element_type=jnp.float32)
        dq = near[:BLOCK_TOKENS, :HEAD_WIDTH] * scale
        att = near[BLOCK_TOKENS:, HEAD_WIDTH:]
        terms = lax.dot_general(factors, pair, tn, preferred_element_type=jnp.float32)
        for s, b in enumerate(ids):
            acc[block_rows(b), :] += terms[s * BLOCK_TOKENS : (s + 1) * BLOCK_TOKENS]
        target, pos = i // out_steps, i % out_steps
        out_ref[target, block_rows(pos), :] = att.astype(jnp.bfloat16)
        out_ref[target, block_rows(out_steps + pos), :] = dq.astype(jnp.bfloat16)

    def step(t, carry):
        loaded = [load(t * UNROLL + u) for u in range(UNROLL)]
        for block in loaded:
            work(*block)
        return carry

    lax.fori_loop(0, steps // UNROLL, step, 0)
    if is_last:
        target_ref, begin = (out_ref, 2 * out_rows) if joined else (dkv_ref, 0)
        shards = target_ref.shape[0]
        rows = acc.shape[0] // shards
        for s in range(shards):
            part = pl.ds(s * rows, rows)
            target_ref[s, pl.ds(begin, rows), :] = (acc[part, :HEAD_WIDTH] * scale).astype(
                target_ref.dtype
            )
            target_ref[s, pl.ds(begin + rows, rows), :] = acc[part, HEAD_WIDTH:].astype(
                target_ref.dtype
            )


def attend(
    ids, first_block, drop, kv, qd, qd_begin, start, piece, per, is_last, device_blocks, total_blocks, shards, targets
):
    team_blocks = drop.shape[0]
    source = kv if qd is None else qd
    steps = source.shape[0] * per
    length = total_blocks * BLOCK_TOKENS
    pairs = steps * BLOCK_TOKENS * WIDE
    joined = shards == targets
    accumulator = (length, 2 * HEAD_WIDTH)
    out_rows = 2 * steps * BLOCK_TOKENS // targets
    grad_rows = 2 * length // shards
    out_shape = []
    scratch = [pltpu.VMEM((team_blocks, WIDE), jnp.float32)]
    if is_last:
        scratch = [pltpu.VMEM(accumulator, jnp.float32)] + scratch
        if joined:
            out_rows += grad_rows
        else:
            out_shape.append(jax.ShapeDtypeStruct((shards, grad_rows, HEAD_WIDTH), jnp.float32))
    else:
        out_shape.append(jax.ShapeDtypeStruct(accumulator, jnp.float32))
    out_shape.insert(0, jax.ShapeDtypeStruct((targets, out_rows, HEAD_WIDTH), jnp.bfloat16))
    operands = [kv] + [t for t in (qd, start) if t is not None]
    return pl.pallas_call(
        functools.partial(
            attention_kernel,
            total_blocks - 1,
            device_blocks,
            per,
            piece,
            qd_begin,
            qd is not None,
            start is not None,
            is_last,
            joined,
        ),
        out_shape=out_shape,
        in_specs=[smem, smem, vmem] + [vmem] * len(operands),
        out_specs=[vmem] * len(out_shape),
        scratch_shapes=scratch,
        compiler_params=pltpu.CompilerParams(vmem_limit_bytes=VMEM_LIMIT),
        cost_estimate=pl.CostEstimate(
            flops=12 * pairs * HEAD_WIDTH,
            bytes_accessed=2 * (source.size + kv.size) + 8 * length * HEAD_WIDTH,
            transcendentals=pairs,
        ),
    )(ids, first_block, drop, *operands)


def per_device(queries, keys, values, grad_out, rand_blocks, global_ids, drop_mask):
    shards = lax.axis_size("seq")
    groups = lax.axis_size("head")
    shard = lax.axis_index("seq")
    heads, shard_blocks, _ = rand_blocks.shape
    tokens = queries.shape[0]
    device_blocks = tokens // BLOCK_TOKENS
    shard_tokens = shard_blocks * BLOCK_TOKENS
    teams = shards // heads
    team = shard // heads
    team_blocks = heads * shard_blocks
    total_blocks = shards * shard_blocks
    first_block = team * team_blocks
    whole = teams == 1
    pieces = device_blocks if whole else 1
    per = device_blocks // pieces
    rows = tokens // pieces
    same_team = None if whole else [[t * heads + m for m in range(heads)] for t in range(teams)]
    same_team_all = (
        None
        if whole
        else [
            [(t * heads + m) * groups + g for m in range(heads) for g in range(groups)]
            for t in range(teams)
        ]
    )
    same_head = [[t * heads + m for t in range(teams)] for m in range(heads)]

    def to_heads(packed):
        return lax.all_to_all(
            packed,
            ("seq", "head"),
            split_axis=0,
            concat_axis=0,
            tiled=True,
            axis_index_groups=same_team_all,
        )

    def to_shards(results):
        return lax.all_to_all(
            results, "seq", split_axis=0, concat_axis=0, tiled=True, axis_index_groups=same_team
        )

    table_rows = -(-shard_blocks // 16) * 16
    tables = jnp.concatenate([rand_blocks, drop_mask], axis=2).astype(jnp.bfloat16)
    tables = jnp.pad(
        tables, ((0, 0), (0, table_rows - shard_blocks), (0, HEAD_WIDTH - R - SLOTS))
    )
    kv_sources = [(keys, 0, tokens), (values, 0, tokens), tables]
    qd_sources = [[(queries, c, rows), (grad_out, c, rows)] for c in range(pieces)]
    qd_begin = 2 * tokens + table_rows
    kv = to_heads(pack(groups, heads, *kv_sources, *qd_sources[0]))
    later = [to_heads(pack(groups, heads, *sources)) for sources in qd_sources[1:]]
    tables = lax.dynamic_index_in_dim(
        kv.reshape(heads, groups, -1, HEAD_WIDTH)[
            :, :, 2 * tokens : 2 * tokens + shard_blocks, : R + SLOTS
        ],
        lax.axis_index("head"),
        axis=1,
        keepdims=False,
    )
    tables = tables.reshape(team_blocks, R + SLOTS).astype(jnp.int32)
    qd = [None] + later
    if not whole:
        qd[0] = kv[:, qd_begin:]
        kv = lax.all_gather(kv[:, : 2 * tokens], "seq", axis=0, tiled=True, axis_index_groups=same_head)
    blocks = first_block + jnp.arange(team_blocks, dtype=jnp.int32)
    window = jnp.stack([blocks - 1, blocks, blocks + 1], axis=1)
    listed = jnp.concatenate(
        [window, jnp.broadcast_to(global_ids[None], (team_blocks, G)), tables[:, :R]], axis=1
    )
    listed = jnp.clip(listed, 0, total_blocks - 1).reshape(-1)
    near = []
    sums = None
    for c in range(pieces):
        result, *sums = attend(
            listed,
            first_block.reshape(1),
            tables[:, R:],
            kv,
            qd[c],
            qd_begin if qd[c] is None else 0,
            sums[0] if sums else None,
            c,
            per,
            c == pieces - 1,
            device_blocks,
            total_blocks,
            shards,
            heads,
        )
        near.append(to_shards(result))
    runs = shard_blocks // device_blocks
    att, dq = None, None
    for c in range(pieces):
        begin = shard_tokens // pieces
        parts = [(0, rows, runs, pieces, c, att), (begin, rows, runs, pieces, c, dq)]
        if c < pieces - 1:
            att, dq = unpack(near[c], parts)
        elif whole:
            grads = [(2 * begin + n * shard_tokens, shard_tokens, 1, 1, 0, None) for n in range(2)]
            att, dq, dk, dv = unpack(near[c], parts + grads)
        else:
            att, dq = unpack(near[c], parts)
            grads = lax.psum_scatter(
                sums[0], "seq", scatter_dimension=0, tiled=True, axis_index_groups=same_head
            ).astype(jnp.bfloat16)
            grads = to_shards(grads)
            dk, dv = unpack(
                grads, [(n * shard_tokens, shard_tokens, 1, 1, 0, None) for n in range(2)]
            )
    return tuple(t.reshape(shard_tokens, heads * HEAD_WIDTH) for t in (att, dq, dk, dv))


def solution(mesh):
    return jax.shard_map(
        per_device,
        mesh=mesh,
        in_specs=(
            P(("seq", "head"), None),
            P(("seq", "head"), None),
            P(("seq", "head"), None),
            P(("seq", "head"), None),
            P("head", "seq", None),
            P(),
            P("head", "seq", None),
        ),
        out_specs=(P("seq", "head"), P("seq", "head"), P("seq", "head"), P("seq", "head")),
        check_vma=False,
    )
```

```python
import functools
import math

import jax
import jax.numpy as jnp
from jax import lax
from jax.experimental import pallas as pl
from jax.experimental.pallas import tpu as pltpu
from jax.sharding import PartitionSpec as P

HEAD_WIDTH = 128
BLOCK_TOKENS = 64
R = 3
G = 2
SLOTS = 3 + G + R
WIDE = SLOTS * BLOCK_TOKENS
UNROLL = 4
VMEM_LIMIT = 56 * 1024 * 1024

keep_prob = 0.9

vmem = pl.BlockSpec(memory_space=pltpu.VMEM)
smem = pl.BlockSpec(memory_space=pltpu.SMEM)


def copy_cost(size):
    return pl.CostEstimate(flops=0, bytes_accessed=4 * size, transcendentals=0)


def block_rows(number):
    start = number * BLOCK_TOKENS
    if not isinstance(number, int):
        start = pl.multiple_of(start, BLOCK_TOKENS)
    return pl.ds(start, BLOCK_TOKENS)


def pack_kernel(heads, *refs):
    out_ref = refs[-1]
    begin = 0
    for ref in refs[:-1]:
        if len(ref.shape) == 3:
            rows = ref.shape[1]
            for m in range(heads):
                out_ref[m, 0, pl.ds(begin, rows), :] = ref[m]
        else:
            rows = ref.shape[0]
            for m in range(heads):
                out_ref[m, 0, pl.ds(begin, rows), :] = ref[:, pl.ds(m * HEAD_WIDTH, HEAD_WIDTH)]
        begin += rows


def pack(groups, heads, *sources):
    specs, arrays, total = [], [], 0
    for source in sources:
        if isinstance(source, tuple):
            array, at, rows = source
            specs.append(
                pl.BlockSpec((rows, heads * HEAD_WIDTH), functools.partial(lambda at, g: (at, g), at))
            )
        else:
            array, rows = source, source.shape[1]
            specs.append(pl.BlockSpec(source.shape, lambda g: (0, 0, 0)))
        arrays.append(array)
        total += rows
    shape = (heads, groups, total, HEAD_WIDTH)
    packed = pl.pallas_call(
        functools.partial(pack_kernel, heads),
        grid=(groups,),
        out_shape=jax.ShapeDtypeStruct(shape, jnp.bfloat16),
        in_specs=specs,
        out_specs=pl.BlockSpec((heads, 1, total, HEAD_WIDTH), lambda g: (0, g, 0, 0)),
        compiler_params=pltpu.CompilerParams(vmem_limit_bytes=VMEM_LIMIT),
        cost_estimate=copy_cost(math.prod(shape)),
    )(*arrays)
    return packed.reshape(heads * groups, total, HEAD_WIDTH)


def unpack_kernel(begins, step_heads, piece_ref, *refs):
    outs = refs[len(refs) - len(begins) :]
    for begin, out in zip(begins, outs):
        runs, _, rows, _ = out.shape
        for m in range(step_heads):
            for i in range(runs):
                out[i, 0, :, pl.ds(m * HEAD_WIDTH, HEAD_WIDTH)] = piece_ref[
                    m, pl.ds(begin + i * rows, rows), :
                ]


def unpack(received, parts):
    heads, total, _ = received.shape
    step_heads = 2 if heads % 2 == 0 else 1
    width = step_heads * HEAD_WIDTH
    shapes, out_specs, begins, olds, aliases = [], [], [], [], {}
    size = 0
    for n, (begin, rows, runs, pieces, piece, old) in enumerate(parts):
        begins.append(begin)
        shapes.append(
            jax.ShapeDtypeStruct((runs, pieces, rows, heads * HEAD_WIDTH), jnp.bfloat16)
        )
        out_specs.append(
            pl.BlockSpec(
                (runs, 1, rows, width), functools.partial(lambda piece, h: (0, piece, 0, h), piece)
            )
        )
        size += rows * runs * heads * HEAD_WIDTH
        if old is not None:
            aliases[1 + len(olds)] = n
            olds.append(old)
    return pl.pallas_call(
        functools.partial(unpack_kernel, begins, step_heads),
        grid=(heads // step_heads,),
        out_shape=shapes,
        in_specs=[pl.BlockSpec((step_heads, total, HEAD_WIDTH), lambda h: (h, 0, 0))]
        + [pl.BlockSpec(memory_space=pl.ANY)] * len(olds),
        out_specs=out_specs,
        input_output_aliases=aliases,
        compiler_params=pltpu.CompilerParams(vmem_limit_bytes=VMEM_LIMIT),
        cost_estimate=copy_cost(size),
    )(received, *olds)


def attention_kernel(
    last_block,
    device_blocks,
    per,
    piece,
    out_rows,
    source_rows,
    qd_rows,
    qd_begin,
    has_qd,
    has_start,
    joined,
    tokens,
    ids_ref,
    starts_ref,
    first_ref,
    drop_ref,
    kv_ref,
    *refs,
):
    refs = list(refs)
    qd_ref = refs.pop(0) if has_qd else kv_ref
    start_ref = refs.pop(0) if has_start else None
    out_ref = refs.pop(0)
    acc, retain, flipped = refs
    scale = HEAD_WIDTH ** (-0.5)
    steps = out_ref.shape[0] * (out_rows // BLOCK_TOKENS)
    slot_of_lane = lax.broadcasted_iota(jnp.int32, (SLOTS, WIDE), 1) // BLOCK_TOKENS
    slot_row = lax.broadcasted_iota(jnp.int32, (SLOTS, WIDE), 0)
    expand = (slot_of_lane == slot_row).astype(jnp.float32)
    retain[...] = jnp.dot(
        drop_ref[...].astype(jnp.float32), expand, preferred_element_type=jnp.float32
    ) * (1.0 / keep_prob)
    acc[...] = start_ref[...] if has_start else jnp.zeros_like(acc)
    lane = lax.broadcasted_iota(jnp.int32, (1, WIDE), 1)
    low_half = lax.broadcasted_iota(jnp.int32, (HEAD_WIDTH, 2 * BLOCK_TOKENS), 1) < BLOCK_TOKENS
    tn = (((0,), (0,)), ((), ()))
    targets = out_ref.shape[0]
    out_steps = steps // targets

    def flip(i, carry):
        for n in range(2):
            pair = [
                kv_ref[
                    pl.ds(
                        pl.multiple_of(i * source_rows + n * tokens + h * BLOCK_TOKENS, 16),
                        BLOCK_TOKENS,
                    ),
                    :,
                ]
                for h in range(2)
            ]
            flipped[n, 2 * i] = jnp.concatenate(pair, axis=0).T
            flipped[n, 2 * i + 1] = jnp.concatenate(pair[::-1], axis=0).T
        return carry

    lax.fori_loop(0, flipped.shape[1] // 2, flip, 0)

    def load(i):
        if per == 1:
            source, sub = i, 0
        else:
            source, sub = lax.div(i, per), lax.rem(i, per)
        j = source * device_blocks + piece * per + sub
        ids = [ids_ref[j * SLOTS + s] for s in range(SLOTS)]
        starts = [starts_ref[j * SLOTS + s] for s in range(SLOTS)]
        q, do = [
            qd_ref[
                pl.ds(
                    pl.multiple_of(
                        source * qd_rows + (n * per + sub) * BLOCK_TOKENS + qd_begin, 16
                    ),
                    BLOCK_TOKENS,
                ),
                :,
            ]
            for n in range(2)
        ]
        keys, vals = [
            jnp.concatenate(
                [kv_ref[pl.ds(pl.multiple_of(r + n * tokens, 16), BLOCK_TOKENS), :] for r in starts],
                axis=0,
            )
            for n in range(2)
        ]
        keys_t, vals_t = [
            jnp.concatenate(
                [
                    jnp.where(low_half, flipped[n, ids[s]], flipped[n, ids[s + 1] ^ 1])
                    for s in range(0, SLOTS, 2)
                ],
                axis=1,
            )
            for n in range(2)
        ]
        keep = retain[pl.ds(j, 1), :]
        return i, first_ref[0] + j, ids, q, do, keys, vals, keys_t, vals_t, keep

    def work(i, block_id, ids, q, do, keys, vals, keys_t, vals_t, keep):
        absent = ((block_id == 0) & (lane < BLOCK_TOKENS)) | (
            (block_id == last_block) & (lane >= 2 * BLOCK_TOKENS) & (lane < 3 * BLOCK_TOKENS)
        )
        logits = jnp.dot(q, keys_t, preferred_element_type=jnp.float32)
        raw = jnp.dot(do, vals_t, preferred_element_type=jnp.float32)
        logits = jnp.where(absent, -jnp.inf, logits)
        top = jnp.max(logits, axis=-1, keepdims=True)
        expd = jnp.exp2((logits - top) * (scale / math.log(2.0)))
        probs = expd * (1.0 / jnp.sum(expd, axis=-1, keepdims=True))
        kept = probs * keep
        weighted = kept * raw
        delta = jnp.sum(weighted, axis=-1, keepdims=True)
        dropped = kept.astype(jnp.bfloat16)
        dscores = (weighted - probs * delta).astype(jnp.bfloat16)
        att = jnp.dot(dropped, vals, preferred_element_type=jnp.float32)
        dq = jnp.dot(dscores, keys, preferred_element_type=jnp.float32) * scale
        none = jnp.zeros_like(q)
        terms = lax.dot_general(
            jnp.concatenate([dscores, dropped], axis=0),
            jnp.concatenate(
                [jnp.concatenate([q, none], axis=1), jnp.concatenate([none, do], axis=1)], axis=0
            ),
            tn,
            preferred_element_type=jnp.float32,
        )
        for s, b in enumerate(ids):
            acc[block_rows(b), :] += terms[s * BLOCK_TOKENS : (s + 1) * BLOCK_TOKENS]
        target, pos = lax.div(i, out_steps), lax.rem(i, out_steps)
        out_ref[target, block_rows(pos), :] = att.astype(jnp.bfloat16)
        out_ref[target, block_rows(out_steps + pos), :] = dq.astype(jnp.bfloat16)

    def step(t, carry):
        loaded = [load(t * UNROLL + u) for u in range(UNROLL)]
        for block in loaded:
            work(*block)
        return carry

    lax.fori_loop(0, steps // UNROLL, step, 0)
    if joined:
        rows = acc.shape[0] // targets
        for s in range(targets):
            part = pl.ds(s * rows, rows)
            out_ref[s, pl.ds(2 * out_rows, rows), :] = (acc[part, :HEAD_WIDTH] * scale).astype(
                jnp.bfloat16
            )
            out_ref[s, pl.ds(2 * out_rows + rows, rows), :] = acc[part, HEAD_WIDTH:].astype(
                jnp.bfloat16
            )


def attend(
    ids, starts, first_block, drop, kv, qd, qd_begin, start, piece, per, joined, device_blocks, total_blocks, tokens, targets
):
    team_blocks = drop.shape[0]
    source = kv if qd is None else qd
    steps = team_blocks * per // device_blocks
    length = total_blocks * BLOCK_TOKENS
    pairs = steps * BLOCK_TOKENS * WIDE
    accumulator = (length, 2 * HEAD_WIDTH)
    out_rows = steps * BLOCK_TOKENS // targets
    total_rows = 2 * out_rows + (2 * length // targets if joined else 0)
    out_shape = [jax.ShapeDtypeStruct((targets, total_rows, HEAD_WIDTH), jnp.bfloat16)]
    scratch = [
        pltpu.VMEM((team_blocks, WIDE), jnp.float32),
        pltpu.VMEM((2, total_blocks, HEAD_WIDTH, 2 * BLOCK_TOKENS), jnp.bfloat16),
    ]
    if joined:
        scratch = [pltpu.VMEM(accumulator, jnp.float32)] + scratch
    else:
        out_shape.append(jax.ShapeDtypeStruct(accumulator, jnp.float32))
    flat = [t.reshape(-1, HEAD_WIDTH) for t in (kv, qd) if t is not None]
    operands = flat + ([] if start is None else [start])
    return pl.pallas_call(
        functools.partial(
            attention_kernel,
            total_blocks - 1,
            device_blocks,
            per,
            piece,
            out_rows,
            kv.shape[1],
            source.shape[1],
            qd_begin,
            qd is not None,
            start is not None,
            joined,
            tokens,
        ),
        out_shape=out_shape,
        in_specs=[smem, smem, smem, vmem] + [vmem] * len(operands),
        out_specs=[vmem] * len(out_shape),
        scratch_shapes=scratch,
        compiler_params=pltpu.CompilerParams(vmem_limit_bytes=VMEM_LIMIT),
        cost_estimate=pl.CostEstimate(
            flops=12 * pairs * HEAD_WIDTH,
            bytes_accessed=2 * (source.size + kv.size) + 8 * length * HEAD_WIDTH,
            transcendentals=pairs,
        ),
    )(ids, starts, first_block, drop, *operands)


def per_device(queries, keys, values, grad_out, rand_blocks, global_ids, drop_mask):
    shards = lax.axis_size("seq")
    groups = lax.axis_size("head")
    shard = lax.axis_index("seq")
    heads, shard_blocks, _ = rand_blocks.shape
    tokens = queries.shape[0]
    device_blocks = tokens // BLOCK_TOKENS
    shard_tokens = shard_blocks * BLOCK_TOKENS
    teams = shards // heads
    team = shard // heads
    team_blocks = heads * shard_blocks
    total_blocks = shards * shard_blocks
    first_block = team * team_blocks
    whole = teams == 1
    pieces = device_blocks if whole else 1
    per = device_blocks // pieces
    rows = tokens // pieces
    same_team = None if whole else [[t * heads + m for m in range(heads)] for t in range(teams)]
    same_team_all = (
        None
        if whole
        else [
            [(t * heads + m) * groups + g for m in range(heads) for g in range(groups)]
            for t in range(teams)
        ]
    )
    same_head = [[t * heads + m for t in range(teams)] for m in range(heads)]

    def to_heads(packed):
        return lax.all_to_all(
            packed,
            ("seq", "head"),
            split_axis=0,
            concat_axis=0,
            tiled=True,
            axis_index_groups=same_team_all,
        )

    def to_shards(results):
        return lax.all_to_all(
            results, "seq", split_axis=0, concat_axis=0, tiled=True, axis_index_groups=same_team
        )

    table_rows = -(-shard_blocks // 16) * 16
    tables = jnp.concatenate([rand_blocks, drop_mask], axis=2).astype(jnp.bfloat16)
    tables = jnp.pad(
        tables, ((0, 0), (0, table_rows - shard_blocks), (0, HEAD_WIDTH - R - SLOTS))
    )
    kv_sources = [(keys, 0, tokens), (values, 0, tokens), tables]
    qd_sources = [[(queries, c, rows), (grad_out, c, rows)] for c in range(pieces)]
    qd_begin = 2 * tokens + table_rows
    kv = to_heads(pack(groups, heads, *kv_sources, *qd_sources[0]))
    later = [to_heads(pack(groups, heads, *sources)) for sources in qd_sources[1:]]
    tables = lax.dynamic_index_in_dim(
        kv.reshape(heads, groups, -1, HEAD_WIDTH)[
            :, :, 2 * tokens : 2 * tokens + shard_blocks, : R + SLOTS
        ],
        lax.axis_index("head"),
        axis=1,
        keepdims=False,
    )
    tables = tables.reshape(team_blocks, R + SLOTS).astype(jnp.int32)
    qd = [None] + later
    if not whole:
        qd[0] = kv[:, qd_begin:]
        kv = lax.all_gather(kv[:, : 2 * tokens], "seq", axis=0, tiled=True, axis_index_groups=same_head)
    blocks = first_block + jnp.arange(team_blocks, dtype=jnp.int32)
    window = jnp.stack([blocks - 1, blocks, blocks + 1], axis=1)
    listed = jnp.concatenate(
        [window, jnp.broadcast_to(global_ids[None], (team_blocks, G)), tables[:, :R]], axis=1
    )
    listed = jnp.clip(listed, 0, total_blocks - 1).reshape(-1)
    starts = listed // device_blocks * kv.shape[1] + listed % device_blocks * BLOCK_TOKENS
    near = []
    sums = None
    for c in range(pieces):
        result, *sums = attend(
            listed,
            starts,
            first_block.reshape(1),
            tables[:, R:],
            kv,
            qd[c],
            qd_begin if qd[c] is None else 0,
            sums[0] if sums else None,
            c,
            per,
            whole and c == pieces - 1,
            device_blocks,
            total_blocks,
            tokens,
            heads,
        )
        near.append(to_shards(result))
    runs = shard_blocks // device_blocks
    att, dq = None, None
    for c in range(pieces):
        begin = shard_tokens // pieces
        parts = [(0, rows, runs, pieces, c, att), (begin, rows, runs, pieces, c, dq)]
        if c < pieces - 1:
            att, dq = unpack(near[c], parts)
        elif whole:
            grads = [(2 * begin + n * shard_tokens, shard_tokens, 1, 1, 0, None) for n in range(2)]
            att, dq, dk, dv = unpack(near[c], parts + grads)
        else:
            att, dq = unpack(near[c], parts)
            grads = lax.psum_scatter(
                sums[0], "seq", scatter_dimension=0, tiled=True, axis_index_groups=same_head
            ).reshape(heads, shard_tokens, 2, HEAD_WIDTH)
            grads = jnp.concatenate(
                [grads[:, :, 0] * HEAD_WIDTH ** (-0.5), grads[:, :, 1]], axis=1
            ).astype(jnp.bfloat16)
            grads = to_shards(grads)
            dk, dv = unpack(
                grads, [(n * shard_tokens, shard_tokens, 1, 1, 0, None) for n in range(2)]
            )
    return tuple(t.reshape(shard_tokens, heads * HEAD_WIDTH) for t in (att, dq, dk, dv))


def solution(mesh):
    return jax.shard_map(
        per_device,
        mesh=mesh,
        in_specs=(
            P(("seq", "head"), None),
            P(("seq", "head"), None),
            P(("seq", "head"), None),
            P(("seq", "head"), None),
            P("head", "seq", None),
            P(),
            P("head", "seq", None),
        ),
        out_specs=(P("seq", "head"), P("seq", "head"), P("seq", "head"), P("seq", "head")),
        check_vma=False,
    )
```

```python
import functools
import math

import jax
import jax.numpy as jnp
from jax import lax
from jax.experimental import pallas as pl
from jax.experimental.pallas import tpu as pltpu
from jax.sharding import PartitionSpec as P

HEAD_WIDTH = 128
BLOCK_TOKENS = 64
R = 3
G = 2
SLOTS = 3 + G + R
WIDE = SLOTS * BLOCK_TOKENS
UNROLL = 2
STRIP = 16
VMEM_LIMIT = 56 * 1024 * 1024

keep_prob = 0.9

vmem = pl.BlockSpec(memory_space=pltpu.VMEM)
smem = pl.BlockSpec(memory_space=pltpu.SMEM)


def copy_cost(size):
    return pl.CostEstimate(flops=0, bytes_accessed=4 * size, transcendentals=0)


def block_rows(number):
    start = number * BLOCK_TOKENS
    if not isinstance(number, int):
        start = pl.multiple_of(start, BLOCK_TOKENS)
    return pl.ds(start, BLOCK_TOKENS)


def pack_kernel(heads, table_rows, *refs):
    refs = list(refs)
    if table_rows:
        drop_ref, rand_ref, table = refs.pop(0), refs.pop(0), refs.pop()
    out_ref = refs.pop()
    begin = 0
    for ref in refs:
        rows = ref.shape[0]
        for m in range(heads):
            out_ref[m, 0, pl.ds(begin, rows), :] = ref[:, pl.ds(m * HEAD_WIDTH, HEAD_WIDTH)]
        begin += rows
    if table_rows:
        blocks = drop_ref.shape[1]
        table[...] = jnp.zeros_like(table)
        for m in range(heads):
            table[pl.ds(0, blocks), pl.ds(0, SLOTS)] = drop_ref[m].astype(jnp.float32)
            for r in range(R):
                table[pl.ds(blocks + r, 1), pl.ds(0, blocks)] = rand_ref[
                    r, pl.ds(m, 1), :
                ].astype(jnp.float32)
            out_ref[m, 0, pl.ds(begin, table_rows), :] = table[...].astype(jnp.bfloat16)


def pack(groups, heads, sources, tables=(), table_rows=0):
    specs = [pl.BlockSpec(t.shape, lambda g: (0, 0, 0)) for t in tables]
    for _, at, rows in sources:
        specs.append(
            pl.BlockSpec((rows, heads * HEAD_WIDTH), functools.partial(lambda at, g: (at, g), at))
        )
    total = sum(rows for _, _, rows in sources) + table_rows
    shape = (heads, groups, total, HEAD_WIDTH)
    packed = pl.pallas_call(
        functools.partial(pack_kernel, heads, table_rows),
        grid=(groups,),
        out_shape=jax.ShapeDtypeStruct(shape, jnp.bfloat16),
        in_specs=specs,
        out_specs=pl.BlockSpec((heads, 1, total, HEAD_WIDTH), lambda g: (0, g, 0, 0)),
        scratch_shapes=[pltpu.VMEM((table_rows, HEAD_WIDTH), jnp.float32)] if table_rows else [],
        compiler_params=pltpu.CompilerParams(vmem_limit_bytes=VMEM_LIMIT),
        cost_estimate=copy_cost(math.prod(shape)),
    )(*tables, *[array for array, _, _ in sources])
    return packed.reshape(heads * groups, total, HEAD_WIDTH)


def unpack_kernel(parts, piece_ref, *refs):
    outs, sems = refs[len(refs) - 1 - len(parts) : -1], refs[-1]
    copies = []
    for (begin, rows, runs, _, piece, _), out in zip(parts, outs):
        for m in range(piece_ref.shape[0]):
            for i in range(runs):
                copies.append(
                    pltpu.make_async_copy(
                        piece_ref.at[m, pl.ds(begin + i * rows, rows), :],
                        out.at[i, piece, :, pl.ds(m * HEAD_WIDTH, HEAD_WIDTH)],
                        sems.at[len(copies)],
                    )
                )
    for copy in copies:
        copy.start()
    for copy in copies:
        copy.wait()


def unpack(received, parts):
    heads = received.shape[0]
    shapes, olds, aliases, size, count = [], [], {}, 0, 0
    for n, (begin, rows, runs, pieces, piece, old) in enumerate(parts):
        shapes.append(
            jax.ShapeDtypeStruct((runs, pieces, rows, heads * HEAD_WIDTH), jnp.bfloat16)
        )
        size += rows * runs * heads * HEAD_WIDTH
        count += heads * runs
        if old is not None:
            aliases[1 + len(olds)] = n
            olds.append(old)
    anywhere = pl.BlockSpec(memory_space=pl.ANY)
    return pl.pallas_call(
        functools.partial(unpack_kernel, parts),
        out_shape=shapes,
        in_specs=[anywhere] * (1 + len(olds)),
        out_specs=[anywhere] * len(shapes),
        input_output_aliases=aliases,
        scratch_shapes=[pltpu.SemaphoreType.DMA((count,))],
        cost_estimate=copy_cost(size),
    )(received, *olds)


def attention_kernel(
    last_block,
    device_blocks,
    per,
    piece,
    out_rows,
    source_rows,
    qd_rows,
    qd_begin,
    has_qd,
    has_start,
    joined,
    tokens,
    ids_ref,
    starts_ref,
    first_ref,
    drop_ref,
    kv_ref,
    *refs,
):
    refs = list(refs)
    qd_ref = refs.pop(0) if has_qd else kv_ref
    start_ref = refs.pop(0) if has_start else None
    out_ref = refs.pop(0)
    acc, retain, waiting = refs
    scale = HEAD_WIDTH ** (-0.5)
    steps = out_ref.shape[0] * (out_rows // BLOCK_TOKENS)
    slot_of_lane = lax.broadcasted_iota(jnp.int32, (SLOTS, WIDE), 1) // BLOCK_TOKENS
    slot_row = lax.broadcasted_iota(jnp.int32, (SLOTS, WIDE), 0)
    expand = (slot_of_lane == slot_row).astype(jnp.float32)
    retain[...] = jnp.dot(
        drop_ref[...].astype(jnp.float32), expand, preferred_element_type=jnp.float32
    ) * (1.0 / keep_prob)
    acc[...] = start_ref[...] if has_start else jnp.zeros_like(acc)
    lane = lax.broadcasted_iota(jnp.int32, (1, WIDE), 1)
    nt = (((1,), (1,)), ((), ()))
    tn = (((0,), (0,)), ((), ()))
    targets = out_ref.shape[0]
    out_steps = steps // targets

    def place(i):
        if per == 1:
            source, sub = i, 0
        else:
            source, sub = lax.div(i, per), lax.rem(i, per)
        return source, sub, source * device_blocks + piece * per + sub

    def load(i):
        source, sub, j = place(i)
        starts = [starts_ref[j * SLOTS + s] for s in range(SLOTS)]
        q, do = [
            qd_ref[
                pl.ds(
                    pl.multiple_of(
                        source * qd_rows + (n * per + sub) * BLOCK_TOKENS + qd_begin, 16
                    ),
                    BLOCK_TOKENS,
                ),
                :,
            ]
            for n in range(2)
        ]
        keys, vals = [
            jnp.concatenate(
                [kv_ref[pl.ds(pl.multiple_of(r + n * tokens, 16), BLOCK_TOKENS), :] for r in starts],
                axis=0,
            )
            for n in range(2)
        ]
        return q, do, keys, vals

    def score(i):
        q, do, keys, vals = load(i)
        logits = lax.dot_general(q, keys, nt, preferred_element_type=jnp.float32)
        raw = lax.dot_general(do, vals, nt, preferred_element_type=jnp.float32)
        return logits, raw

    def factor(i, u, logits, raw):
        j = place(i)[2]
        block_id = first_ref[0] + j
        absent = ((block_id == 0) & (lane < BLOCK_TOKENS)) | (
            (block_id == last_block) & (lane >= 2 * BLOCK_TOKENS) & (lane < 3 * BLOCK_TOKENS)
        )
        keep = retain[pl.ds(j, 1), :]
        for r in range(0, BLOCK_TOKENS, STRIP):
            part = jnp.where(absent, -jnp.inf, logits[r : r + STRIP])
            top = jnp.max(part, axis=-1, keepdims=True)
            expd = jnp.exp2((part - top) * (scale / math.log(2.0)))
            probs = expd * (1.0 / jnp.sum(expd, axis=-1, keepdims=True))
            kept = probs * keep
            weighted = kept * raw[r : r + STRIP]
            delta = jnp.sum(weighted, axis=-1, keepdims=True)
            waiting[u, pl.ds(r, STRIP), :] = (weighted - probs * delta).astype(jnp.bfloat16)
            waiting[u, pl.ds(BLOCK_TOKENS + r, STRIP), :] = kept.astype(jnp.bfloat16)

    def finish(i, u):
        j = place(i)[2]
        q, do, keys, vals = load(i)
        factors = waiting[u]
        dq = jnp.dot(factors[:BLOCK_TOKENS], keys, preferred_element_type=jnp.float32) * scale
        att = jnp.dot(factors[BLOCK_TOKENS:], vals, preferred_element_type=jnp.float32)
        none = jnp.zeros_like(q)
        pair = jnp.concatenate(
            [jnp.concatenate([q, none], axis=1), jnp.concatenate([none, do], axis=1)], axis=0
        )
        terms = lax.dot_general(factors, pair, tn, preferred_element_type=jnp.float32)
        for s in range(SLOTS):
            acc[block_rows(ids_ref[j * SLOTS + s]), :] += terms[
                s * BLOCK_TOKENS : (s + 1) * BLOCK_TOKENS
            ]
        target, pos = lax.div(i, out_steps), lax.rem(i, out_steps)
        out_ref[target, block_rows(pos), :] = att.astype(jnp.bfloat16)
        out_ref[target, block_rows(out_steps + pos), :] = dq.astype(jnp.bfloat16)

    def step(t, carry):
        scores = [score(t * UNROLL + u) for u in range(UNROLL)]
        for u in range(UNROLL):
            finish((t - 1) * UNROLL + u, u)
        for u in range(UNROLL):
            factor(t * UNROLL + u, u, *scores[u])
        return carry

    for u in range(UNROLL):
        factor(u, u, *score(u))
    lax.fori_loop(1, steps // UNROLL, step, 0)
    for u in range(UNROLL):
        finish(steps - UNROLL + u, u)
    if joined:
        rows = acc.shape[0] // targets
        for s in range(targets):
            part = pl.ds(s * rows, rows)
            out_ref[s, pl.ds(2 * out_rows, rows), :] = (acc[part, :HEAD_WIDTH] * scale).astype(
                jnp.bfloat16
            )
            out_ref[s, pl.ds(2 * out_rows + rows, rows), :] = acc[part, HEAD_WIDTH:].astype(
                jnp.bfloat16
            )


def attend(
    ids, starts, first_block, drop, kv, qd, qd_begin, start, piece, per, joined, device_blocks, total_blocks, tokens, targets
):
    team_blocks = drop.shape[0]
    source = kv if qd is None else qd
    steps = team_blocks * per // device_blocks
    length = total_blocks * BLOCK_TOKENS
    pairs = steps * BLOCK_TOKENS * WIDE
    accumulator = (length, 2 * HEAD_WIDTH)
    out_rows = steps * BLOCK_TOKENS // targets
    total_rows = 2 * out_rows + (2 * length // targets if joined else 0)
    out_shape = [jax.ShapeDtypeStruct((targets, total_rows, HEAD_WIDTH), jnp.bfloat16)]
    scratch = [
        pltpu.VMEM((team_blocks, WIDE), jnp.float32),
        pltpu.VMEM((UNROLL, 2 * BLOCK_TOKENS, WIDE), jnp.bfloat16),
    ]
    if joined:
        scratch = [pltpu.VMEM(accumulator, jnp.float32)] + scratch
    else:
        out_shape.append(jax.ShapeDtypeStruct(accumulator, jnp.float32))
    flat = [t.reshape(-1, HEAD_WIDTH) for t in (kv, qd) if t is not None]
    operands = flat + ([] if start is None else [start])
    return pl.pallas_call(
        functools.partial(
            attention_kernel,
            total_blocks - 1,
            device_blocks,
            per,
            piece,
            out_rows,
            kv.shape[1],
            source.shape[1],
            qd_begin,
            qd is not None,
            start is not None,
            joined,
            tokens,
        ),
        out_shape=out_shape,
        in_specs=[smem, smem, smem, vmem] + [vmem] * len(operands),
        out_specs=[vmem] * len(out_shape),
        scratch_shapes=scratch,
        compiler_params=pltpu.CompilerParams(vmem_limit_bytes=VMEM_LIMIT),
        cost_estimate=pl.CostEstimate(
            flops=12 * pairs * HEAD_WIDTH,
            bytes_accessed=2 * (source.size + kv.size) + 8 * length * HEAD_WIDTH,
            transcendentals=pairs,
        ),
    )(ids, starts, first_block, drop, *operands)


def per_device(queries, keys, values, grad_out, rand_blocks, global_ids, drop_mask):
    shards = lax.axis_size("seq")
    groups = lax.axis_size("head")
    shard = lax.axis_index("seq")
    heads, shard_blocks, _ = rand_blocks.shape
    tokens = queries.shape[0]
    device_blocks = tokens // BLOCK_TOKENS
    shard_tokens = shard_blocks * BLOCK_TOKENS
    teams = shards // heads
    team = shard // heads
    team_blocks = heads * shard_blocks
    total_blocks = shards * shard_blocks
    first_block = team * team_blocks
    whole = teams == 1
    pieces = device_blocks if whole else 1
    per = device_blocks // pieces
    rows = tokens // pieces
    same_team = None if whole else [[t * heads + m for m in range(heads)] for t in range(teams)]
    same_team_all = (
        None
        if whole
        else [
            [(t * heads + m) * groups + g for m in range(heads) for g in range(groups)]
            for t in range(teams)
        ]
    )
    same_head = [[t * heads + m for t in range(teams)] for m in range(heads)]

    def to_heads(packed):
        return lax.all_to_all(
            packed,
            ("seq", "head"),
            split_axis=0,
            concat_axis=0,
            tiled=True,
            axis_index_groups=same_team_all,
        )

    def to_shards(results):
        return lax.all_to_all(
            results, "seq", split_axis=0, concat_axis=0, tiled=True, axis_index_groups=same_team
        )

    table_rows = -(-(shard_blocks + R) // 16) * 16
    sources = [[(queries, c, rows), (grad_out, c, rows)] for c in range(pieces)]
    qd_begin = 2 * tokens
    table_begin = qd_begin + 2 * rows
    kv = to_heads(
        pack(
            groups,
            heads,
            [(keys, 0, tokens), (values, 0, tokens)] + sources[0],
            (drop_mask, rand_blocks.transpose(2, 0, 1)),
            table_rows,
        )
    )
    later = [to_heads(pack(groups, heads, each)) for each in sources[1:]]
    tables = lax.dynamic_index_in_dim(
        kv.reshape(heads, groups, -1, HEAD_WIDTH)[:, :, table_begin:],
        lax.axis_index("head"),
        axis=1,
        keepdims=False,
    ).astype(jnp.int32)
    drops = tables[:, :shard_blocks, :SLOTS].reshape(team_blocks, SLOTS)
    randoms = tables[:, shard_blocks : shard_blocks + R, :shard_blocks].transpose(0, 2, 1)
    randoms = randoms.reshape(team_blocks, R)
    qd = [None] + later
    if not whole:
        qd[0] = kv[:, qd_begin:table_begin]
        kv = lax.all_gather(kv[:, : 2 * tokens], "seq", axis=0, tiled=True, axis_index_groups=same_head)
    blocks = first_block + jnp.arange(team_blocks, dtype=jnp.int32)
    window = jnp.stack([blocks - 1, blocks, blocks + 1], axis=1)
    listed = jnp.concatenate(
        [window, jnp.broadcast_to(global_ids[None], (team_blocks, G)), randoms], axis=1
    )
    listed = jnp.clip(listed, 0, total_blocks - 1).reshape(-1)
    starts = listed // device_blocks * kv.shape[1] + listed % device_blocks * BLOCK_TOKENS
    near = []
    sums = None
    for c in range(pieces):
        result, *sums = attend(
            listed,
            starts,
            first_block.reshape(1),
            drops,
            kv,
            qd[c],
            qd_begin if qd[c] is None else 0,
            sums[0] if sums else None,
            c,
            per,
            whole and c == pieces - 1,
            device_blocks,
            total_blocks,
            tokens,
            heads,
        )
        near.append(to_shards(result))
    runs = shard_blocks // device_blocks
    att, dq = None, None
    for c in range(pieces):
        begin = shard_tokens // pieces
        parts = [(0, rows, runs, pieces, c, att), (begin, rows, runs, pieces, c, dq)]
        if c < pieces - 1:
            att, dq = unpack(near[c], parts)
        elif whole:
            grads = [(2 * begin + n * shard_tokens, shard_tokens, 1, 1, 0, None) for n in range(2)]
            att, dq, dk, dv = unpack(near[c], parts + grads)
        else:
            att, dq = unpack(near[c], parts)
            grads = lax.psum_scatter(
                sums[0], "seq", scatter_dimension=0, tiled=True, axis_index_groups=same_head
            ).reshape(heads, shard_tokens, 2, HEAD_WIDTH)
            grads = jnp.concatenate(
                [grads[:, :, 0] * HEAD_WIDTH ** (-0.5), grads[:, :, 1]], axis=1
            ).astype(jnp.bfloat16)
            grads = to_shards(grads)
            dk, dv = unpack(
                grads, [(n * shard_tokens, shard_tokens, 1, 1, 0, None) for n in range(2)]
            )
    return tuple(t.reshape(shard_tokens, heads * HEAD_WIDTH) for t in (att, dq, dk, dv))


def solution(mesh):
    return jax.shard_map(
        per_device,
        mesh=mesh,
        in_specs=(
            P(("seq", "head"), None),
            P(("seq", "head"), None),
            P(("seq", "head"), None),
            P(("seq", "head"), None),
            P("head", "seq", None),
            P(),
            P("head", "seq", None),
        ),
        out_specs=(P("seq", "head"), P("seq", "head"), P("seq", "head"), P("seq", "head")),
        check_vma=False,
    )
```

```python
import functools
import math

import jax
import jax.numpy as jnp
from jax import lax
from jax.experimental import pallas as pl
from jax.experimental.pallas import tpu as pltpu
from jax.sharding import PartitionSpec as P

HEAD_WIDTH = 128
BLOCK_TOKENS = 64
R = 3
G = 2
SLOTS = 3 + G + R
WIDE = SLOTS * BLOCK_TOKENS
UNROLL = 2
STRIP = 16
VMEM_LIMIT = 56 * 1024 * 1024

keep_prob = 0.9

vmem = pl.BlockSpec(memory_space=pltpu.VMEM)
smem = pl.BlockSpec(memory_space=pltpu.SMEM)


def copy_cost(size):
    return pl.CostEstimate(flops=0, bytes_accessed=4 * size, transcendentals=0)


def block_rows(number):
    start = number * BLOCK_TOKENS
    if not isinstance(number, int):
        start = pl.multiple_of(start, BLOCK_TOKENS)
    return pl.ds(start, BLOCK_TOKENS)


def pack_kernel(heads, table_rows, *refs):
    refs = list(refs)
    if table_rows:
        drop_ref, rand_ref, table = refs.pop(0), refs.pop(0), refs.pop()
    out_ref = refs.pop()
    begin = 0
    for ref in refs:
        rows = ref.shape[0]
        for m in range(heads):
            out_ref[m, 0, pl.ds(begin, rows), :] = ref[:, pl.ds(m * HEAD_WIDTH, HEAD_WIDTH)]
        begin += rows
    if table_rows:
        blocks = drop_ref.shape[1]
        table[...] = jnp.zeros_like(table)
        for m in range(heads):
            table[pl.ds(0, blocks), pl.ds(0, SLOTS)] = drop_ref[m].astype(jnp.float32)
            for r in range(R):
                table[pl.ds(blocks + r, 1), pl.ds(0, blocks)] = rand_ref[
                    r, pl.ds(m, 1), :
                ].astype(jnp.float32)
            out_ref[m, 0, pl.ds(begin, table_rows), :] = table[...].astype(jnp.bfloat16)


def pack(groups, heads, sources, tables=(), table_rows=0):
    specs = [pl.BlockSpec(t.shape, lambda g: (0, 0, 0)) for t in tables]
    for _, at, rows in sources:
        specs.append(
            pl.BlockSpec((rows, heads * HEAD_WIDTH), functools.partial(lambda at, g: (at, g), at))
        )
    total = sum(rows for _, _, rows in sources) + table_rows
    shape = (heads, groups, total, HEAD_WIDTH)
    packed = pl.pallas_call(
        functools.partial(pack_kernel, heads, table_rows),
        grid=(groups,),
        out_shape=jax.ShapeDtypeStruct(shape, jnp.bfloat16),
        in_specs=specs,
        out_specs=pl.BlockSpec((heads, 1, total, HEAD_WIDTH), lambda g: (0, g, 0, 0)),
        scratch_shapes=[pltpu.VMEM((table_rows, HEAD_WIDTH), jnp.float32)] if table_rows else [],
        compiler_params=pltpu.CompilerParams(vmem_limit_bytes=VMEM_LIMIT),
        cost_estimate=copy_cost(math.prod(shape)),
    )(*tables, *[array for array, _, _ in sources])
    return packed.reshape(heads * groups, total, HEAD_WIDTH)


def unpack_kernel(parts, member_ref, *refs):
    outs = refs[len(refs) - len(parts) :]
    heads = outs[0].shape[-1] // HEAD_WIDTH
    for k in range(heads):
        column = pl.multiple_of((member_ref[0] ^ k) * HEAD_WIDTH, HEAD_WIDTH)
        for begin, out in zip(parts, outs):
            runs, _, rows, _ = out.shape
            for i in range(runs):
                out[i, 0, :, pl.ds(column, HEAD_WIDTH)] = refs[k][pl.ds(begin + i * rows, rows), :]


def unpack(member, received, parts):
    heads = len(received)
    shapes, specs, olds, aliases, size = [], [], [], {}, 0
    for n, (_, rows, runs, pieces, piece, old) in enumerate(parts):
        shapes.append(
            jax.ShapeDtypeStruct((runs, pieces, rows, heads * HEAD_WIDTH), jnp.bfloat16)
        )
        specs.append(
            pl.BlockSpec(
                (runs, 1, rows, heads * HEAD_WIDTH),
                functools.partial(lambda piece, h: (0, piece, 0, 0), piece),
            )
        )
        size += rows * runs * heads * HEAD_WIDTH
        if old is not None:
            aliases[1 + heads + len(olds)] = n
            olds.append(old)
    return pl.pallas_call(
        functools.partial(unpack_kernel, tuple(part[0] for part in parts)),
        grid=(1,),
        out_shape=shapes,
        in_specs=[smem]
        + [pl.BlockSpec(received[0].shape, lambda h: (0, 0))] * heads
        + [pl.BlockSpec(memory_space=pl.ANY)] * len(olds),
        out_specs=specs,
        input_output_aliases=aliases,
        compiler_params=pltpu.CompilerParams(vmem_limit_bytes=VMEM_LIMIT),
        cost_estimate=copy_cost(size),
    )(member, *received, *olds)


def attention_kernel(
    last_block,
    device_blocks,
    per,
    piece,
    out_rows,
    source_rows,
    qd_rows,
    qd_begin,
    has_qd,
    has_start,
    joined,
    tokens,
    targets,
    ids_ref,
    starts_ref,
    first_ref,
    member_ref,
    drop_ref,
    kv_ref,
    *refs,
):
    refs = list(refs)
    qd_ref = refs.pop(0) if has_qd else kv_ref
    start_ref = refs.pop(0) if has_start else None
    out_refs = [refs.pop(0) for _ in range(targets)]
    acc, retain, waiting, near = refs
    scale = HEAD_WIDTH ** (-0.5)
    steps = targets * (out_rows // BLOCK_TOKENS)
    slot_of_lane = lax.broadcasted_iota(jnp.int32, (SLOTS, WIDE), 1) // BLOCK_TOKENS
    slot_row = lax.broadcasted_iota(jnp.int32, (SLOTS, WIDE), 0)
    expand = (slot_of_lane == slot_row).astype(jnp.float32)
    retain[...] = jnp.dot(
        drop_ref[...].astype(jnp.float32), expand, preferred_element_type=jnp.float32
    ) * (1.0 / keep_prob)
    acc[...] = start_ref[...] if has_start else jnp.zeros_like(acc)
    lane = lax.broadcasted_iota(jnp.int32, (1, WIDE), 1)
    nt = (((1,), (1,)), ((), ()))
    tn = (((0,), (0,)), ((), ()))
    out_steps = steps // targets

    def place(i):
        if per == 1:
            source, sub = i, 0
        else:
            source, sub = lax.div(i, per), lax.rem(i, per)
        return source, sub, source * device_blocks + piece * per + sub

    def load(i):
        source, sub, j = place(i)
        starts = [starts_ref[j * SLOTS + s] for s in range(SLOTS)]
        q, do = [
            qd_ref[
                pl.ds(
                    pl.multiple_of(
                        source * qd_rows + (n * per + sub) * BLOCK_TOKENS + qd_begin, 16
                    ),
                    BLOCK_TOKENS,
                ),
                :,
            ]
            for n in range(2)
        ]
        keys, vals = [
            jnp.concatenate(
                [kv_ref[pl.ds(pl.multiple_of(r + n * tokens, 16), BLOCK_TOKENS), :] for r in starts],
                axis=0,
            )
            for n in range(2)
        ]
        return q, do, keys, vals

    def score(i):
        q, do, keys, vals = load(i)
        logits = lax.dot_general(q, keys, nt, preferred_element_type=jnp.float32)
        raw = lax.dot_general(do, vals, nt, preferred_element_type=jnp.float32)
        return logits, raw

    def factor(i, u, logits, raw):
        j = place(i)[2]
        block_id = first_ref[0] + j
        absent = ((block_id == 0) & (lane < BLOCK_TOKENS)) | (
            (block_id == last_block) & (lane >= 2 * BLOCK_TOKENS) & (lane < 3 * BLOCK_TOKENS)
        )
        keep = retain[pl.ds(j, 1), :]
        for r in range(0, BLOCK_TOKENS, STRIP):
            part = jnp.where(absent, -jnp.inf, logits[r : r + STRIP])
            top = jnp.max(part, axis=-1, keepdims=True)
            expd = jnp.exp2((part - top) * (scale / math.log(2.0)))
            probs = expd * (1.0 / jnp.sum(expd, axis=-1, keepdims=True))
            kept = probs * keep
            weighted = kept * raw[r : r + STRIP]
            delta = jnp.sum(weighted, axis=-1, keepdims=True)
            waiting[u, pl.ds(r, STRIP), :] = (weighted - probs * delta).astype(jnp.bfloat16)
            waiting[u, pl.ds(BLOCK_TOKENS + r, STRIP), :] = kept.astype(jnp.bfloat16)

    def finish(i, u):
        j = place(i)[2]
        q, do, keys, vals = load(i)
        factors = waiting[u]
        dq = jnp.dot(factors[:BLOCK_TOKENS], keys, preferred_element_type=jnp.float32) * scale
        att = jnp.dot(factors[BLOCK_TOKENS:], vals, preferred_element_type=jnp.float32)
        none = jnp.zeros_like(q)
        pair = jnp.concatenate(
            [jnp.concatenate([q, none], axis=1), jnp.concatenate([none, do], axis=1)], axis=0
        )
        terms = lax.dot_general(factors, pair, tn, preferred_element_type=jnp.float32)
        for s in range(SLOTS):
            acc[block_rows(ids_ref[j * SLOTS + s]), :] += terms[
                s * BLOCK_TOKENS : (s + 1) * BLOCK_TOKENS
            ]
        target, pos = lax.div(i, out_steps), lax.rem(i, out_steps)
        near[target, block_rows(pos), :] = att.astype(jnp.bfloat16)
        near[target, block_rows(out_steps + pos), :] = dq.astype(jnp.bfloat16)

    def step(t, carry):
        scores = [score(t * UNROLL + u) for u in range(UNROLL)]
        for u in range(UNROLL):
            finish((t - 1) * UNROLL + u, u)
        for u in range(UNROLL):
            factor(t * UNROLL + u, u, *scores[u])
        return carry

    for u in range(UNROLL):
        factor(u, u, *score(u))
    lax.fori_loop(1, steps // UNROLL, step, 0)
    for u in range(UNROLL):
        finish(steps - UNROLL + u, u)
    for k, out_ref in enumerate(out_refs):
        target = member_ref[0] ^ k
        out_ref[pl.ds(0, 2 * out_rows), :] = near[target]
        if joined:
            rows = acc.shape[0] // targets
            part = pl.ds(pl.multiple_of(target * rows, rows), rows)
            out_ref[pl.ds(2 * out_rows, rows), :] = (acc[part, :HEAD_WIDTH] * scale).astype(
                jnp.bfloat16
            )
            out_ref[pl.ds(2 * out_rows + rows, rows), :] = acc[part, HEAD_WIDTH:].astype(
                jnp.bfloat16
            )


def attend(
    ids, starts, first_block, member, drop, kv, qd, qd_begin, start, piece, per, joined, device_blocks, total_blocks, tokens, targets
):
    team_blocks = drop.shape[0]
    source = kv if qd is None else qd
    steps = team_blocks * per // device_blocks
    length = total_blocks * BLOCK_TOKENS
    pairs = steps * BLOCK_TOKENS * WIDE
    accumulator = (length, 2 * HEAD_WIDTH)
    out_rows = steps * BLOCK_TOKENS // targets
    total_rows = 2 * out_rows + (2 * length // targets if joined else 0)
    out_shape = [jax.ShapeDtypeStruct((total_rows, HEAD_WIDTH), jnp.bfloat16)] * targets
    scratch = [
        pltpu.VMEM((team_blocks, WIDE), jnp.float32),
        pltpu.VMEM((UNROLL, 2 * BLOCK_TOKENS, WIDE), jnp.bfloat16),
        pltpu.VMEM((targets, 2 * out_rows, HEAD_WIDTH), jnp.bfloat16),
    ]
    if joined:
        scratch = [pltpu.VMEM(accumulator, jnp.float32)] + scratch
    else:
        out_shape.append(jax.ShapeDtypeStruct(accumulator, jnp.float32))
    flat = [t.reshape(-1, HEAD_WIDTH) for t in (kv, qd) if t is not None]
    operands = flat + ([] if start is None else [start])
    return pl.pallas_call(
        functools.partial(
            attention_kernel,
            total_blocks - 1,
            device_blocks,
            per,
            piece,
            out_rows,
            kv.shape[1],
            source.shape[1],
            qd_begin,
            qd is not None,
            start is not None,
            joined,
            tokens,
            targets,
        ),
        out_shape=out_shape,
        in_specs=[smem, smem, smem, smem, vmem] + [vmem] * len(operands),
        out_specs=[vmem] * len(out_shape),
        scratch_shapes=scratch,
        compiler_params=pltpu.CompilerParams(vmem_limit_bytes=VMEM_LIMIT),
        cost_estimate=pl.CostEstimate(
            flops=12 * pairs * HEAD_WIDTH,
            bytes_accessed=2 * (source.size + kv.size) + 8 * length * HEAD_WIDTH,
            transcendentals=pairs,
        ),
    )(ids, starts, first_block, member, drop, *operands)


def per_device(queries, keys, values, grad_out, rand_blocks, global_ids, drop_mask):
    shards = lax.axis_size("seq")
    groups = lax.axis_size("head")
    shard = lax.axis_index("seq")
    heads, shard_blocks, _ = rand_blocks.shape
    tokens = queries.shape[0]
    device_blocks = tokens // BLOCK_TOKENS
    shard_tokens = shard_blocks * BLOCK_TOKENS
    teams = shards // heads
    team, member = lax.div(shard, heads), lax.rem(shard, heads)
    team_blocks = heads * shard_blocks
    total_blocks = shards * shard_blocks
    first_block = team * team_blocks
    whole = teams == 1
    pieces = device_blocks if whole else 1
    per = device_blocks // pieces
    rows = tokens // pieces
    same_team_all = (
        None
        if whole
        else [
            [(t * heads + m) * groups + g for m in range(heads) for g in range(groups)]
            for t in range(teams)
        ]
    )
    same_head = [[t * heads + m for t in range(teams)] for m in range(heads)]

    def to_heads(packed):
        return lax.all_to_all(
            packed,
            ("seq", "head"),
            split_axis=0,
            concat_axis=0,
            tiled=True,
            axis_index_groups=same_team_all,
        )

    def to_shards(results):
        received = list(results)
        for k in reversed(range(1, heads)):
            pairs = [(s, s ^ k) for s in range(shards)]
            received[k] = lax.ppermute(results[k], "seq", pairs)
        return received

    table_rows = -(-(shard_blocks + R) // 16) * 16
    sources = [[(queries, c, rows), (grad_out, c, rows)] for c in range(pieces)]
    qd_begin = 2 * tokens
    table_begin = qd_begin + 2 * rows
    kv = to_heads(
        pack(
            groups,
            heads,
            [(keys, 0, tokens), (values, 0, tokens)] + sources[0],
            (drop_mask, rand_blocks.transpose(2, 0, 1)),
            table_rows,
        )
    )
    later = [to_heads(pack(groups, heads, each)) for each in sources[1:]]
    tables = lax.dynamic_index_in_dim(
        kv.reshape(heads, groups, -1, HEAD_WIDTH)[:, :, table_begin:],
        lax.axis_index("head"),
        axis=1,
        keepdims=False,
    ).astype(jnp.int32)
    drops = tables[:, :shard_blocks, :SLOTS].reshape(team_blocks, SLOTS)
    randoms = tables[:, shard_blocks : shard_blocks + R, :shard_blocks].transpose(0, 2, 1)
    randoms = randoms.reshape(team_blocks, R)
    qd = [None] + later
    if not whole:
        qd[0] = kv[:, qd_begin:table_begin]
        kv = lax.all_gather(kv[:, : 2 * tokens], "seq", axis=0, tiled=True, axis_index_groups=same_head)
    blocks = first_block + jnp.arange(team_blocks, dtype=jnp.int32)
    window = jnp.stack([blocks - 1, blocks, blocks + 1], axis=1)
    listed = jnp.concatenate(
        [window, jnp.broadcast_to(global_ids[None], (team_blocks, G)), randoms], axis=1
    )
    listed = jnp.clip(listed, 0, total_blocks - 1).reshape(-1)
    starts = listed // device_blocks * kv.shape[1] + listed % device_blocks * BLOCK_TOKENS
    near = []
    sums = None
    for c in range(pieces):
        results = attend(
            listed,
            starts,
            first_block.reshape(1),
            member.reshape(1),
            drops,
            kv,
            qd[c],
            qd_begin if qd[c] is None else 0,
            sums[0] if sums else None,
            c,
            per,
            whole and c == pieces - 1,
            device_blocks,
            total_blocks,
            tokens,
            heads,
        )
        near.append(to_shards(results[:heads]))
        sums = results[heads:]
    runs = shard_blocks // device_blocks
    att, dq = None, None
    for c in range(pieces):
        begin = shard_tokens // pieces
        parts = [(0, rows, runs, pieces, c, att), (begin, rows, runs, pieces, c, dq)]
        if c < pieces - 1:
            att, dq = unpack(member.reshape(1), near[c], parts)
        elif whole:
            grads = [(2 * begin + n * shard_tokens, shard_tokens, 1, 1, 0, None) for n in range(2)]
            att, dq, dk, dv = unpack(member.reshape(1), near[c], parts + grads)
        else:
            att, dq = unpack(member.reshape(1), near[c], parts)
            grads = lax.psum_scatter(
                sums[0], "seq", scatter_dimension=0, tiled=True, axis_index_groups=same_head
            ).reshape(heads, shard_tokens, 2, HEAD_WIDTH)
            grads = jnp.concatenate(
                [grads[:, :, 0] * HEAD_WIDTH ** (-0.5), grads[:, :, 1]], axis=1
            ).astype(jnp.bfloat16)
            grads = to_shards(
                [lax.dynamic_index_in_dim(grads, member ^ k, 0, keepdims=False) for k in range(heads)]
            )
            dk, dv = unpack(
                member.reshape(1), grads, [(n * shard_tokens, shard_tokens, 1, 1, 0, None) for n in range(2)]
            )
    return tuple(t.reshape(shard_tokens, heads * HEAD_WIDTH) for t in (att, dq, dk, dv))


def solution(mesh):
    return jax.shard_map(
        per_device,
        mesh=mesh,
        in_specs=(
            P(("seq", "head"), None),
            P(("seq", "head"), None),
            P(("seq", "head"), None),
            P(("seq", "head"), None),
            P("head", "seq", None),
            P(),
            P("head", "seq", None),
        ),
        out_specs=(P("seq", "head"), P("seq", "head"), P("seq", "head"), P("seq", "head")),
        check_vma=False,
    )
```

```python
import functools
import math

import jax
import jax.numpy as jnp
from jax import lax
from jax.experimental import pallas as pl
from jax.experimental.pallas import tpu as pltpu
from jax.sharding import PartitionSpec as P

HEAD_WIDTH = 128
BLOCK_TOKENS = 64
R = 3
G = 2
SLOTS = 3 + G + R
WIDE = SLOTS * BLOCK_TOKENS
UNROLL = 2
STRIP = 16
VMEM_LIMIT = 56 * 1024 * 1024

keep_prob = 0.9

vmem = pl.BlockSpec(memory_space=pltpu.VMEM)
smem = pl.BlockSpec(memory_space=pltpu.SMEM)


def copy_cost(size):
    return pl.CostEstimate(flops=0, bytes_accessed=4 * size, transcendentals=0)


def block_rows(number):
    start = number * BLOCK_TOKENS
    if not isinstance(number, int):
        start = pl.multiple_of(start, BLOCK_TOKENS)
    return pl.ds(start, BLOCK_TOKENS)


def pack_kernel(heads, table_rows, *refs):
    refs = list(refs)
    if table_rows:
        drop_ref, rand_ref, table = refs.pop(0), refs.pop(0), refs.pop()
    out_ref = refs.pop()
    begin = 0
    for ref in refs:
        rows = ref.shape[0]
        for m in range(heads):
            out_ref[m, 0, pl.ds(begin, rows), :] = ref[:, pl.ds(m * HEAD_WIDTH, HEAD_WIDTH)]
        begin += rows
    if table_rows:
        blocks = drop_ref.shape[1]
        table[...] = jnp.zeros_like(table)
        for m in range(heads):
            table[pl.ds(0, blocks), pl.ds(0, SLOTS)] = drop_ref[m].astype(jnp.float32)
            for r in range(R):
                table[pl.ds(blocks + r, 1), pl.ds(0, blocks)] = rand_ref[
                    r, pl.ds(m, 1), :
                ].astype(jnp.float32)
            out_ref[m, 0, pl.ds(begin, table_rows), :] = table[...].astype(jnp.bfloat16)


def pack(groups, heads, sources, tables=(), table_rows=0):
    specs = [pl.BlockSpec(t.shape, lambda g: (0, 0, 0)) for t in tables]
    for _, at, rows in sources:
        specs.append(
            pl.BlockSpec((rows, heads * HEAD_WIDTH), functools.partial(lambda at, g: (at, g), at))
        )
    total = sum(rows for _, _, rows in sources) + table_rows
    shape = (heads, groups, total, HEAD_WIDTH)
    packed = pl.pallas_call(
        functools.partial(pack_kernel, heads, table_rows),
        grid=(groups,),
        out_shape=jax.ShapeDtypeStruct(shape, jnp.bfloat16),
        in_specs=specs,
        out_specs=pl.BlockSpec((heads, 1, total, HEAD_WIDTH), lambda g: (0, g, 0, 0)),
        scratch_shapes=[pltpu.VMEM((table_rows, HEAD_WIDTH), jnp.float32)] if table_rows else [],
        compiler_params=pltpu.CompilerParams(vmem_limit_bytes=VMEM_LIMIT),
        cost_estimate=copy_cost(math.prod(shape)),
    )(*tables, *[array for array, _, _ in sources])
    return packed.reshape(heads * groups, total, HEAD_WIDTH)


def unpack_kernel(parts, member_ref, *refs):
    outs = refs[len(refs) - len(parts) :]
    heads = outs[0].shape[-1] // HEAD_WIDTH
    for k in range(heads):
        column = pl.multiple_of((member_ref[0] ^ k) * HEAD_WIDTH, HEAD_WIDTH)
        for begin, out in zip(parts, outs):
            runs, _, rows, _ = out.shape
            for i in range(runs):
                out[i, 0, :, pl.ds(column, HEAD_WIDTH)] = refs[k][pl.ds(begin + i * rows, rows), :]


def unpack(member, received, parts):
    heads = len(received)
    shapes, specs, olds, aliases, size = [], [], [], {}, 0
    for n, (_, rows, runs, pieces, piece, old) in enumerate(parts):
        shapes.append(
            jax.ShapeDtypeStruct((runs, pieces, rows, heads * HEAD_WIDTH), jnp.bfloat16)
        )
        specs.append(
            pl.BlockSpec(
                (runs, 1, rows, heads * HEAD_WIDTH),
                functools.partial(lambda piece, h: (0, piece, 0, 0), piece),
            )
        )
        size += rows * runs * heads * HEAD_WIDTH
        if old is not None:
            aliases[1 + heads + len(olds)] = n
            olds.append(old)
    return pl.pallas_call(
        functools.partial(unpack_kernel, tuple(part[0] for part in parts)),
        grid=(1,),
        out_shape=shapes,
        in_specs=[smem]
        + [pl.BlockSpec(received[0].shape, lambda h: (0, 0))] * heads
        + [pl.BlockSpec(memory_space=pl.ANY)] * len(olds),
        out_specs=specs,
        input_output_aliases=aliases,
        compiler_params=pltpu.CompilerParams(vmem_limit_bytes=VMEM_LIMIT),
        cost_estimate=copy_cost(size),
    )(member, *received, *olds)


def unpack_all_kernel(begins, step_heads, piece_ref, *refs):
    outs = refs[len(refs) - len(begins) :]
    for begin, out in zip(begins, outs):
        runs, _, rows, _ = out.shape
        for m in range(step_heads):
            for i in range(runs):
                out[i, 0, :, pl.ds(m * HEAD_WIDTH, HEAD_WIDTH)] = piece_ref[
                    m, pl.ds(begin + i * rows, rows), :
                ]


def unpack_all(received, parts):
    heads, total, _ = received.shape
    step_heads = 2 if heads % 2 == 0 else 1
    width = step_heads * HEAD_WIDTH
    shapes, out_specs, begins, olds, aliases = [], [], [], [], {}
    size = 0
    for n, (begin, rows, runs, pieces, piece, old) in enumerate(parts):
        begins.append(begin)
        shapes.append(
            jax.ShapeDtypeStruct((runs, pieces, rows, heads * HEAD_WIDTH), jnp.bfloat16)
        )
        out_specs.append(
            pl.BlockSpec(
                (runs, 1, rows, width), functools.partial(lambda piece, h: (0, piece, 0, h), piece)
            )
        )
        size += rows * runs * heads * HEAD_WIDTH
        if old is not None:
            aliases[1 + len(olds)] = n
            olds.append(old)
    return pl.pallas_call(
        functools.partial(unpack_all_kernel, begins, step_heads),
        grid=(heads // step_heads,),
        out_shape=shapes,
        in_specs=[pl.BlockSpec((step_heads, total, HEAD_WIDTH), lambda h: (h, 0, 0))]
        + [pl.BlockSpec(memory_space=pl.ANY)] * len(olds),
        out_specs=out_specs,
        input_output_aliases=aliases,
        compiler_params=pltpu.CompilerParams(vmem_limit_bytes=VMEM_LIMIT),
        cost_estimate=copy_cost(size),
    )(received, *olds)


def attention_kernel(
    last_block,
    device_blocks,
    per,
    piece,
    out_rows,
    source_rows,
    qd_rows,
    qd_begin,
    has_qd,
    has_start,
    joined,
    tokens,
    targets,
    ids_ref,
    starts_ref,
    first_ref,
    member_ref,
    drop_ref,
    kv_ref,
    *refs,
):
    refs = list(refs)
    qd_ref = refs.pop(0) if has_qd else kv_ref
    start_ref = refs.pop(0) if has_start else None
    out_refs = [refs.pop(0) for _ in range(1 if joined else targets)]
    acc, retain, waiting, near = refs
    scale = HEAD_WIDTH ** (-0.5)
    steps = targets * (out_rows // BLOCK_TOKENS)
    slot_of_lane = lax.broadcasted_iota(jnp.int32, (SLOTS, WIDE), 1) // BLOCK_TOKENS
    slot_row = lax.broadcasted_iota(jnp.int32, (SLOTS, WIDE), 0)
    expand = (slot_of_lane == slot_row).astype(jnp.float32)
    retain[...] = jnp.dot(
        drop_ref[...].astype(jnp.float32), expand, preferred_element_type=jnp.float32
    ) * (1.0 / keep_prob)
    acc[...] = start_ref[...] if has_start else jnp.zeros_like(acc)
    lane = lax.broadcasted_iota(jnp.int32, (1, WIDE), 1)
    nt = (((1,), (1,)), ((), ()))
    tn = (((0,), (0,)), ((), ()))
    out_steps = steps // targets

    def place(i):
        if per == 1:
            source, sub = i, 0
        else:
            source, sub = lax.div(i, per), lax.rem(i, per)
        return source, sub, source * device_blocks + piece * per + sub

    def load(i):
        source, sub, j = place(i)
        starts = [starts_ref[j * SLOTS + s] for s in range(SLOTS)]
        q, do = [
            qd_ref[
                pl.ds(
                    pl.multiple_of(
                        source * qd_rows + (n * per + sub) * BLOCK_TOKENS + qd_begin, 16
                    ),
                    BLOCK_TOKENS,
                ),
                :,
            ]
            for n in range(2)
        ]
        keys, vals = [
            jnp.concatenate(
                [kv_ref[pl.ds(pl.multiple_of(r + n * tokens, 16), BLOCK_TOKENS), :] for r in starts],
                axis=0,
            )
            for n in range(2)
        ]
        return q, do, keys, vals

    def score(i):
        q, do, keys, vals = load(i)
        logits = lax.dot_general(q, keys, nt, preferred_element_type=jnp.float32)
        raw = lax.dot_general(do, vals, nt, preferred_element_type=jnp.float32)
        return logits, raw

    def factor(i, u, logits, raw):
        j = place(i)[2]
        block_id = first_ref[0] + j
        absent = ((block_id == 0) & (lane < BLOCK_TOKENS)) | (
            (block_id == last_block) & (lane >= 2 * BLOCK_TOKENS) & (lane < 3 * BLOCK_TOKENS)
        )
        keep = retain[pl.ds(j, 1), :]
        for r in range(0, BLOCK_TOKENS, STRIP):
            part = jnp.where(absent, -jnp.inf, logits[r : r + STRIP])
            top = jnp.max(part, axis=-1, keepdims=True)
            expd = jnp.exp2((part - top) * (scale / math.log(2.0)))
            probs = expd * (1.0 / jnp.sum(expd, axis=-1, keepdims=True))
            kept = probs * keep
            weighted = kept * raw[r : r + STRIP]
            delta = jnp.sum(weighted, axis=-1, keepdims=True)
            waiting[u, pl.ds(r, STRIP), :] = (weighted - probs * delta).astype(jnp.bfloat16)
            waiting[u, pl.ds(BLOCK_TOKENS + r, STRIP), :] = kept.astype(jnp.bfloat16)

    def finish(i, u):
        j = place(i)[2]
        q, do, keys, vals = load(i)
        factors = waiting[u]
        dq = jnp.dot(factors[:BLOCK_TOKENS], keys, preferred_element_type=jnp.float32) * scale
        att = jnp.dot(factors[BLOCK_TOKENS:], vals, preferred_element_type=jnp.float32)
        none = jnp.zeros_like(q)
        pair = jnp.concatenate(
            [jnp.concatenate([q, none], axis=1), jnp.concatenate([none, do], axis=1)], axis=0
        )
        terms = lax.dot_general(factors, pair, tn, preferred_element_type=jnp.float32)
        for s in range(SLOTS):
            acc[block_rows(ids_ref[j * SLOTS + s]), :] += terms[
                s * BLOCK_TOKENS : (s + 1) * BLOCK_TOKENS
            ]
        target, pos = lax.div(i, out_steps), lax.rem(i, out_steps)
        near[target, block_rows(pos), :] = att.astype(jnp.bfloat16)
        near[target, block_rows(out_steps + pos), :] = dq.astype(jnp.bfloat16)

    def step(t, carry):
        scores = [score(t * UNROLL + u) for u in range(UNROLL)]
        for u in range(UNROLL):
            finish((t - 1) * UNROLL + u, u)
        for u in range(UNROLL):
            factor(t * UNROLL + u, u, *scores[u])
        return carry

    for u in range(UNROLL):
        factor(u, u, *score(u))
    lax.fori_loop(1, steps // UNROLL, step, 0)
    for u in range(UNROLL):
        finish(steps - UNROLL + u, u)
    if joined:
        rows = acc.shape[0] // targets
        for target in range(targets):
            part = pl.ds(target * rows, rows)
            out_refs[0][target, pl.ds(0, 2 * out_rows), :] = near[target]
            out_refs[0][target, pl.ds(2 * out_rows, rows), :] = (
                acc[part, :HEAD_WIDTH] * scale
            ).astype(jnp.bfloat16)
            out_refs[0][target, pl.ds(2 * out_rows + rows, rows), :] = acc[
                part, HEAD_WIDTH:
            ].astype(jnp.bfloat16)
    else:
        for k, out_ref in enumerate(out_refs):
            out_ref[...] = near[member_ref[0] ^ k]


def attend(
    ids, starts, first_block, member, drop, kv, qd, qd_begin, start, piece, per, joined, device_blocks, total_blocks, tokens, targets
):
    team_blocks = drop.shape[0]
    source = kv if qd is None else qd
    steps = team_blocks * per // device_blocks
    length = total_blocks * BLOCK_TOKENS
    pairs = steps * BLOCK_TOKENS * WIDE
    accumulator = (length, 2 * HEAD_WIDTH)
    out_rows = steps * BLOCK_TOKENS // targets
    if joined:
        out_shape = [
            jax.ShapeDtypeStruct(
                (targets, 2 * out_rows + 2 * length // targets, HEAD_WIDTH), jnp.bfloat16
            )
        ]
    else:
        out_shape = [jax.ShapeDtypeStruct((2 * out_rows, HEAD_WIDTH), jnp.bfloat16)] * targets
    scratch = [
        pltpu.VMEM((team_blocks, WIDE), jnp.float32),
        pltpu.VMEM((UNROLL, 2 * BLOCK_TOKENS, WIDE), jnp.bfloat16),
        pltpu.VMEM((targets, 2 * out_rows, HEAD_WIDTH), jnp.bfloat16),
    ]
    if joined:
        scratch = [pltpu.VMEM(accumulator, jnp.float32)] + scratch
    else:
        out_shape.append(jax.ShapeDtypeStruct(accumulator, jnp.float32))
    flat = [t.reshape(-1, HEAD_WIDTH) for t in (kv, qd) if t is not None]
    operands = flat + ([] if start is None else [start])
    return pl.pallas_call(
        functools.partial(
            attention_kernel,
            total_blocks - 1,
            device_blocks,
            per,
            piece,
            out_rows,
            kv.shape[1],
            source.shape[1],
            qd_begin,
            qd is not None,
            start is not None,
            joined,
            tokens,
            targets,
        ),
        out_shape=out_shape,
        in_specs=[smem, smem, smem, smem, vmem] + [vmem] * len(operands),
        out_specs=[vmem] * len(out_shape),
        scratch_shapes=scratch,
        compiler_params=pltpu.CompilerParams(vmem_limit_bytes=VMEM_LIMIT),
        cost_estimate=pl.CostEstimate(
            flops=128 * pairs * HEAD_WIDTH,
            bytes_accessed=2 * (source.size + kv.size) + 8 * length * HEAD_WIDTH,
            transcendentals=pairs,
        ),
    )(ids, starts, first_block, member, drop, *operands)


def per_device(queries, keys, values, grad_out, rand_blocks, global_ids, drop_mask):
    shards = lax.axis_size("seq")
    groups = lax.axis_size("head")
    shard = lax.axis_index("seq")
    heads, shard_blocks, _ = rand_blocks.shape
    tokens = queries.shape[0]
    device_blocks = tokens // BLOCK_TOKENS
    shard_tokens = shard_blocks * BLOCK_TOKENS
    teams = shards // heads
    team, member = lax.div(shard, heads), lax.rem(shard, heads)
    team_blocks = heads * shard_blocks
    total_blocks = shards * shard_blocks
    first_block = team * team_blocks
    whole = teams == 1
    pieces = device_blocks if whole else 1
    per = device_blocks // pieces
    rows = tokens // pieces
    same_team_all = (
        None
        if whole
        else [
            [(t * heads + m) * groups + g for m in range(heads) for g in range(groups)]
            for t in range(teams)
        ]
    )
    same_head = [[t * heads + m for t in range(teams)] for m in range(heads)]

    def to_heads(packed):
        return lax.all_to_all(
            packed,
            ("seq", "head"),
            split_axis=0,
            concat_axis=0,
            tiled=True,
            axis_index_groups=same_team_all,
        )

    def to_shards(results):
        received = list(results)
        for k in reversed(range(1, heads)):
            pairs = [(s, s ^ k) for s in range(shards)]
            received[k] = lax.ppermute(results[k], "seq", pairs)
        return received

    table_rows = -(-(shard_blocks + R) // 16) * 16
    sources = [[(queries, c, rows), (grad_out, c, rows)] for c in range(pieces)]
    qd_begin = 2 * tokens
    table_begin = qd_begin + 2 * rows
    kv = to_heads(
        pack(
            groups,
            heads,
            [(keys, 0, tokens), (values, 0, tokens)] + sources[0],
            (drop_mask, rand_blocks.transpose(2, 0, 1)),
            table_rows,
        )
    )
    later = [to_heads(pack(groups, heads, each)) for each in sources[1:]]
    tables = lax.dynamic_index_in_dim(
        kv.reshape(heads, groups, -1, HEAD_WIDTH)[:, :, table_begin:],
        lax.axis_index("head"),
        axis=1,
        keepdims=False,
    ).astype(jnp.int32)
    drops = tables[:, :shard_blocks, :SLOTS].reshape(team_blocks, SLOTS)
    randoms = tables[:, shard_blocks : shard_blocks + R, :shard_blocks].transpose(0, 2, 1)
    randoms = randoms.reshape(team_blocks, R)
    qd = [None] + later
    if not whole:
        qd[0] = kv[:, qd_begin:table_begin]
        kv = lax.all_gather(kv[:, : 2 * tokens], "seq", axis=0, tiled=True, axis_index_groups=same_head)
    blocks = first_block + jnp.arange(team_blocks, dtype=jnp.int32)
    window = jnp.stack([blocks - 1, blocks, blocks + 1], axis=1)
    listed = jnp.concatenate(
        [window, jnp.broadcast_to(global_ids[None], (team_blocks, G)), randoms], axis=1
    )
    listed = jnp.clip(listed, 0, total_blocks - 1).reshape(-1)
    starts = listed // device_blocks * kv.shape[1] + listed % device_blocks * BLOCK_TOKENS
    pieces_out = []
    sums = []
    for c in range(pieces):
        pieces_out.append(
            attend(
                listed,
                starts,
                first_block.reshape(1),
                member.reshape(1),
                drops,
                kv,
                qd[c],
                qd_begin if qd[c] is None else 0,
                sums[0] if sums else None,
                c,
                per,
                whole and c == pieces - 1,
                device_blocks,
                total_blocks,
                tokens,
                heads,
            )
        )
        sums = pieces_out[c][heads:]
    runs = shard_blocks // device_blocks
    begin = shard_tokens // pieces
    near = [to_shards(out[:heads]) for out in pieces_out if len(out) > 1]
    att, dq = None, None
    if whole:
        rest = pieces_out[-1][0]
        if near:
            rest, *near[-1][heads // 2 :] = lax.optimization_barrier(
                (rest, *near[-1][heads // 2 :])
            )
        rest = lax.all_to_all(rest, "seq", split_axis=0, concat_axis=0, tiled=True)
    for c in range(len(near)):
        parts = [(0, rows, runs, pieces, c, att), (begin, rows, runs, pieces, c, dq)]
        att, dq = unpack(member.reshape(1), near[c], parts)
    if whole:
        c = pieces - 1
        parts = [(0, rows, runs, pieces, c, att), (begin, rows, runs, pieces, c, dq)]
        grads = [(2 * begin + n * shard_tokens, shard_tokens, 1, 1, 0, None) for n in range(2)]
        att, dq, dk, dv = unpack_all(rest, parts + grads)
    else:
        grads = lax.psum_scatter(
            sums[0], "seq", scatter_dimension=0, tiled=True, axis_index_groups=same_head
        ).reshape(heads, shard_tokens, 2, HEAD_WIDTH)
        grads = jnp.concatenate(
            [grads[:, :, 0] * HEAD_WIDTH ** (-0.5), grads[:, :, 1]], axis=1
        ).astype(jnp.bfloat16)
        grads = to_shards(
            [lax.dynamic_index_in_dim(grads, member ^ k, 0, keepdims=False) for k in range(heads)]
        )
        dk, dv = unpack(
            member.reshape(1),
            grads,
            [(n * shard_tokens, shard_tokens, 1, 1, 0, None) for n in range(2)],
        )
    return tuple(t.reshape(shard_tokens, heads * HEAD_WIDTH) for t in (att, dq, dk, dv))


def solution(mesh):
    return jax.shard_map(
        per_device,
        mesh=mesh,
        in_specs=(
            P(("seq", "head"), None),
            P(("seq", "head"), None),
            P(("seq", "head"), None),
            P(("seq", "head"), None),
            P("head", "seq", None),
            P(),
            P("head", "seq", None),
        ),
        out_specs=(P("seq", "head"), P("seq", "head"), P("seq", "head"), P("seq", "head")),
        check_vma=False,
    )
```

```python
import functools
import math

import jax
import jax.numpy as jnp
from jax import lax
from jax.experimental import pallas as pl
from jax.experimental.pallas import tpu as pltpu
from jax.sharding import PartitionSpec as P

HEAD_WIDTH = 128
BLOCK_TOKENS = 64
R = 3
G = 2
SLOTS = 3 + G + R
WIDE = SLOTS * BLOCK_TOKENS
UNROLL = 2
STRIP = 16
VMEM_LIMIT = 56 * 1024 * 1024

keep_prob = 0.9

vmem = pl.BlockSpec(memory_space=pltpu.VMEM)
smem = pl.BlockSpec(memory_space=pltpu.SMEM)


def copy_cost(size):
    return pl.CostEstimate(flops=0, bytes_accessed=4 * size, transcendentals=0)


def block_rows(number):
    start = number * BLOCK_TOKENS
    if not isinstance(number, int):
        start = pl.multiple_of(start, BLOCK_TOKENS)
    return pl.ds(start, BLOCK_TOKENS)


def pack_kernel(heads, table_rows, *refs):
    refs = list(refs)
    if table_rows:
        drop_ref, rand_ref, table = refs.pop(0), refs.pop(0), refs.pop()
    out_ref = refs.pop()
    begin = 0
    for ref in refs:
        rows = ref.shape[0]
        for m in range(heads):
            out_ref[m, 0, pl.ds(begin, rows), :] = ref[:, pl.ds(m * HEAD_WIDTH, HEAD_WIDTH)]
        begin += rows
    if table_rows:
        blocks = drop_ref.shape[1]
        table[...] = jnp.zeros_like(table)
        for m in range(heads):
            table[pl.ds(0, blocks), pl.ds(0, SLOTS)] = drop_ref[m].astype(jnp.float32)
            for r in range(R):
                table[pl.ds(blocks + r, 1), pl.ds(0, blocks)] = rand_ref[
                    r, pl.ds(m, 1), :
                ].astype(jnp.float32)
            out_ref[m, 0, pl.ds(begin, table_rows), :] = table[...].astype(jnp.bfloat16)


def pack(groups, heads, sources, tables=(), table_rows=0):
    specs = [pl.BlockSpec(t.shape, lambda g: (0, 0, 0)) for t in tables]
    for _, at, rows in sources:
        specs.append(
            pl.BlockSpec((rows, heads * HEAD_WIDTH), functools.partial(lambda at, g: (at, g), at))
        )
    total = sum(rows for _, _, rows in sources) + table_rows
    shape = (heads, groups, total, HEAD_WIDTH)
    packed = pl.pallas_call(
        functools.partial(pack_kernel, heads, table_rows),
        grid=(groups,),
        out_shape=jax.ShapeDtypeStruct(shape, jnp.bfloat16),
        in_specs=specs,
        out_specs=pl.BlockSpec((heads, 1, total, HEAD_WIDTH), lambda g: (0, g, 0, 0)),
        scratch_shapes=[pltpu.VMEM((table_rows, HEAD_WIDTH), jnp.float32)] if table_rows else [],
        compiler_params=pltpu.CompilerParams(vmem_limit_bytes=VMEM_LIMIT),
        cost_estimate=copy_cost(math.prod(shape)),
    )(*tables, *[array for array, _, _ in sources])
    return packed.reshape(heads * groups, total, HEAD_WIDTH)


def unpack_kernel(parts, member_ref, *refs):
    outs = refs[len(refs) - len(parts) :]
    heads = outs[0].shape[-1] // HEAD_WIDTH
    for k in range(heads):
        column = pl.multiple_of((member_ref[0] ^ k) * HEAD_WIDTH, HEAD_WIDTH)
        for begin, out in zip(parts, outs):
            runs, _, rows, _ = out.shape
            for i in range(runs):
                out[i, 0, :, pl.ds(column, HEAD_WIDTH)] = refs[k][pl.ds(begin + i * rows, rows), :]


def unpack(member, received, parts):
    heads = len(received)
    shapes, specs, olds, aliases, size = [], [], [], {}, 0
    for n, (_, rows, runs, pieces, piece, old) in enumerate(parts):
        shapes.append(
            jax.ShapeDtypeStruct((runs, pieces, rows, heads * HEAD_WIDTH), jnp.bfloat16)
        )
        specs.append(
            pl.BlockSpec(
                (runs, 1, rows, heads * HEAD_WIDTH),
                functools.partial(lambda piece, h: (0, piece, 0, 0), piece),
            )
        )
        size += rows * runs * heads * HEAD_WIDTH
        if old is not None:
            aliases[1 + heads + len(olds)] = n
            olds.append(old)
    return pl.pallas_call(
        functools.partial(unpack_kernel, tuple(part[0] for part in parts)),
        grid=(1,),
        out_shape=shapes,
        in_specs=[smem]
        + [pl.BlockSpec(received[0].shape, lambda h: (0, 0))] * heads
        + [pl.BlockSpec(memory_space=pl.ANY)] * len(olds),
        out_specs=specs,
        input_output_aliases=aliases,
        compiler_params=pltpu.CompilerParams(vmem_limit_bytes=VMEM_LIMIT),
        cost_estimate=copy_cost(size),
    )(member, *received, *olds)


def unpack_all_kernel(begins, step_heads, piece_ref, *refs):
    outs = refs[len(refs) - len(begins) :]
    for begin, out in zip(begins, outs):
        runs, _, rows, _ = out.shape
        for m in range(step_heads):
            for i in range(runs):
                out[i, 0, :, pl.ds(m * HEAD_WIDTH, HEAD_WIDTH)] = piece_ref[
                    m, pl.ds(begin + i * rows, rows), :
                ]


def unpack_all(received, parts):
    heads, total, _ = received.shape
    step_heads = 2 if heads % 2 == 0 else 1
    width = step_heads * HEAD_WIDTH
    shapes, out_specs, begins, olds, aliases = [], [], [], [], {}
    size = 0
    for n, (begin, rows, runs, pieces, piece, old) in enumerate(parts):
        begins.append(begin)
        shapes.append(
            jax.ShapeDtypeStruct((runs, pieces, rows, heads * HEAD_WIDTH), jnp.bfloat16)
        )
        out_specs.append(
            pl.BlockSpec(
                (runs, 1, rows, width), functools.partial(lambda piece, h: (0, piece, 0, h), piece)
            )
        )
        size += rows * runs * heads * HEAD_WIDTH
        if old is not None:
            aliases[1 + len(olds)] = n
            olds.append(old)
    return pl.pallas_call(
        functools.partial(unpack_all_kernel, begins, step_heads),
        grid=(heads // step_heads,),
        out_shape=shapes,
        in_specs=[pl.BlockSpec((step_heads, total, HEAD_WIDTH), lambda h: (h, 0, 0))]
        + [pl.BlockSpec(memory_space=pl.ANY)] * len(olds),
        out_specs=out_specs,
        input_output_aliases=aliases,
        compiler_params=pltpu.CompilerParams(vmem_limit_bytes=VMEM_LIMIT),
        cost_estimate=copy_cost(size),
    )(received, *olds)


def attention_kernel(
    last_block,
    device_blocks,
    per,
    piece,
    out_rows,
    source_rows,
    qd_rows,
    qd_begin,
    has_qd,
    has_start,
    joined,
    tokens,
    targets,
    ids_ref,
    starts_ref,
    first_ref,
    member_ref,
    drop_ref,
    kv_ref,
    *refs,
):
    refs = list(refs)
    qd_ref = refs.pop(0) if has_qd else kv_ref
    start_ref = refs.pop(0) if has_start else None
    out_refs = [refs.pop(0) for _ in range(1 if joined else targets)]
    acc, retain, waiting, near = refs[:4]
    earlier, sem = refs[4:] if has_start else (None, None)
    scale = HEAD_WIDTH ** (-0.5)
    steps = targets * (out_rows // BLOCK_TOKENS)
    slot_of_lane = lax.broadcasted_iota(jnp.int32, (SLOTS, WIDE), 1) // BLOCK_TOKENS
    slot_row = lax.broadcasted_iota(jnp.int32, (SLOTS, WIDE), 0)
    expand = (slot_of_lane == slot_row).astype(jnp.float32)
    retain[...] = jnp.dot(
        drop_ref[...].astype(jnp.float32), expand, preferred_element_type=jnp.float32
    ) * (1.0 / keep_prob)
    acc[...] = jnp.zeros_like(acc)
    if has_start:
        fetch = pltpu.make_async_copy(start_ref, earlier, sem)
        fetch.start()
    lane = lax.broadcasted_iota(jnp.int32, (1, WIDE), 1)
    nt = (((1,), (1,)), ((), ()))
    tn = (((0,), (0,)), ((), ()))
    out_steps = steps // targets

    def place(i):
        if per == 1:
            source, sub = i, 0
        else:
            source, sub = lax.div(i, per), lax.rem(i, per)
        return source, sub, source * device_blocks + piece * per + sub

    def load(i):
        source, sub, j = place(i)
        starts = [starts_ref[j * SLOTS + s] for s in range(SLOTS)]
        q, do = [
            qd_ref[
                pl.ds(
                    pl.multiple_of(
                        source * qd_rows + (n * per + sub) * BLOCK_TOKENS + qd_begin, 16
                    ),
                    BLOCK_TOKENS,
                ),
                :,
            ]
            for n in range(2)
        ]
        keys, vals = [
            jnp.concatenate(
                [kv_ref[pl.ds(pl.multiple_of(r + n * tokens, 16), BLOCK_TOKENS), :] for r in starts],
                axis=0,
            )
            for n in range(2)
        ]
        return q, do, keys, vals

    def score(i):
        q, do, keys, vals = load(i)
        logits = lax.dot_general(q, keys, nt, preferred_element_type=jnp.float32)
        raw = lax.dot_general(do, vals, nt, preferred_element_type=jnp.float32)
        return logits, raw

    def factor(i, u, logits, raw):
        j = place(i)[2]
        block_id = first_ref[0] + j
        absent = ((block_id == 0) & (lane < BLOCK_TOKENS)) | (
            (block_id == last_block) & (lane >= 2 * BLOCK_TOKENS) & (lane < 3 * BLOCK_TOKENS)
        )
        keep = retain[pl.ds(j, 1), :]
        for r in range(0, BLOCK_TOKENS, STRIP):
            part = jnp.where(absent, -jnp.inf, logits[r : r + STRIP])
            top = jnp.max(part, axis=-1, keepdims=True)
            expd = jnp.exp2((part - top) * (scale / math.log(2.0)))
            probs = expd * (1.0 / jnp.sum(expd, axis=-1, keepdims=True))
            kept = probs * keep
            weighted = kept * raw[r : r + STRIP]
            delta = jnp.sum(weighted, axis=-1, keepdims=True)
            waiting[u, pl.ds(r, STRIP), :] = (weighted - probs * delta).astype(jnp.bfloat16)
            waiting[u, pl.ds(BLOCK_TOKENS + r, STRIP), :] = kept.astype(jnp.bfloat16)

    def finish(i, u):
        j = place(i)[2]
        q, do, keys, vals = load(i)
        factors = waiting[u]
        dq = jnp.dot(factors[:BLOCK_TOKENS], keys, preferred_element_type=jnp.float32) * scale
        att = jnp.dot(factors[BLOCK_TOKENS:], vals, preferred_element_type=jnp.float32)
        none = jnp.zeros_like(q)
        pair = jnp.concatenate(
            [jnp.concatenate([q, none], axis=1), jnp.concatenate([none, do], axis=1)], axis=0
        )
        terms = lax.dot_general(factors, pair, tn, preferred_element_type=jnp.float32)
        for s in range(SLOTS):
            acc[block_rows(ids_ref[j * SLOTS + s]), :] += terms[
                s * BLOCK_TOKENS : (s + 1) * BLOCK_TOKENS
            ]
        target, pos = lax.div(i, out_steps), lax.rem(i, out_steps)
        near[target, block_rows(pos), :] = att.astype(jnp.bfloat16)
        near[target, block_rows(out_steps + pos), :] = dq.astype(jnp.bfloat16)

    def step(t, carry):
        scores = [score(t * UNROLL + u) for u in range(UNROLL)]
        for u in range(UNROLL):
            finish((t - 1) * UNROLL + u, u)
        for u in range(UNROLL):
            factor(t * UNROLL + u, u, *scores[u])
        return carry

    for u in range(UNROLL):
        factor(u, u, *score(u))
    lax.fori_loop(1, steps // UNROLL, step, 0)
    for u in range(UNROLL):
        finish(steps - UNROLL + u, u)
    if has_start:
        fetch.wait()
        acc[...] += earlier[...]
    if joined:
        rows = acc.shape[0] // targets
        for target in range(targets):
            part = pl.ds(target * rows, rows)
            out_refs[0][target, pl.ds(0, 2 * out_rows), :] = near[target]
            out_refs[0][target, pl.ds(2 * out_rows, rows), :] = (
                acc[part, :HEAD_WIDTH] * scale
            ).astype(jnp.bfloat16)
            out_refs[0][target, pl.ds(2 * out_rows + rows, rows), :] = acc[
                part, HEAD_WIDTH:
            ].astype(jnp.bfloat16)
    else:
        for k, out_ref in enumerate(out_refs):
            out_ref[...] = near[member_ref[0] ^ k]


def attend(
    ids, starts, first_block, member, drop, kv, qd, qd_begin, start, piece, per, joined, device_blocks, total_blocks, tokens, targets
):
    team_blocks = drop.shape[0]
    source = kv if qd is None else qd
    steps = team_blocks * per // device_blocks
    length = total_blocks * BLOCK_TOKENS
    pairs = steps * BLOCK_TOKENS * WIDE
    accumulator = (length, 2 * HEAD_WIDTH)
    out_rows = steps * BLOCK_TOKENS // targets
    if joined:
        out_shape = [
            jax.ShapeDtypeStruct(
                (targets, 2 * out_rows + 2 * length // targets, HEAD_WIDTH), jnp.bfloat16
            )
        ]
    else:
        out_shape = [jax.ShapeDtypeStruct((2 * out_rows, HEAD_WIDTH), jnp.bfloat16)] * targets
    scratch = [
        pltpu.VMEM((team_blocks, WIDE), jnp.float32),
        pltpu.VMEM((UNROLL, 2 * BLOCK_TOKENS, WIDE), jnp.bfloat16),
        pltpu.VMEM((targets, 2 * out_rows, HEAD_WIDTH), jnp.bfloat16),
    ]
    if joined:
        scratch = [pltpu.VMEM(accumulator, jnp.float32)] + scratch
    else:
        out_shape.append(jax.ShapeDtypeStruct(accumulator, jnp.float32))
    if start is not None:
        scratch += [pltpu.VMEM(accumulator, jnp.float32), pltpu.SemaphoreType.DMA]
    flat = [t.reshape(-1, HEAD_WIDTH) for t in (kv, qd) if t is not None]
    operands = flat + ([] if start is None else [start])
    operand_specs = [vmem] * len(flat) + [pl.BlockSpec(memory_space=pl.ANY)] * (start is not None)
    return pl.pallas_call(
        functools.partial(
            attention_kernel,
            total_blocks - 1,
            device_blocks,
            per,
            piece,
            out_rows,
            kv.shape[1],
            source.shape[1],
            qd_begin,
            qd is not None,
            start is not None,
            joined,
            tokens,
            targets,
        ),
        out_shape=out_shape,
        in_specs=[smem, smem, smem, smem, vmem] + operand_specs,
        out_specs=[vmem] * len(out_shape),
        scratch_shapes=scratch,
        compiler_params=pltpu.CompilerParams(vmem_limit_bytes=VMEM_LIMIT),
        cost_estimate=pl.CostEstimate(
            flops=128 * pairs * HEAD_WIDTH,
            bytes_accessed=2 * (source.size + kv.size) + 8 * length * HEAD_WIDTH,
            transcendentals=pairs,
        ),
    )(ids, starts, first_block, member, drop, *operands)


def per_device(queries, keys, values, grad_out, rand_blocks, global_ids, drop_mask):
    shards = lax.axis_size("seq")
    groups = lax.axis_size("head")
    shard = lax.axis_index("seq")
    heads, shard_blocks, _ = rand_blocks.shape
    tokens = queries.shape[0]
    device_blocks = tokens // BLOCK_TOKENS
    shard_tokens = shard_blocks * BLOCK_TOKENS
    teams = shards // heads
    team, member = lax.div(shard, heads), lax.rem(shard, heads)
    team_blocks = heads * shard_blocks
    total_blocks = shards * shard_blocks
    first_block = team * team_blocks
    whole = teams == 1
    pieces = device_blocks if whole else 1
    per = device_blocks // pieces
    rows = tokens // pieces
    same_team_all = (
        None
        if whole
        else [
            [(t * heads + m) * groups + g for m in range(heads) for g in range(groups)]
            for t in range(teams)
        ]
    )
    same_head = [[t * heads + m for t in range(teams)] for m in range(heads)]

    def to_heads(packed):
        return lax.all_to_all(
            packed,
            ("seq", "head"),
            split_axis=0,
            concat_axis=0,
            tiled=True,
            axis_index_groups=same_team_all,
        )

    def to_shards(results):
        received = list(results)
        for k in reversed(range(1, heads)):
            pairs = [(s, s ^ k) for s in range(shards)]
            received[k] = lax.ppermute(results[k], "seq", pairs)
        return received

    table_rows = -(-(shard_blocks + R) // 16) * 16
    sources = [[(queries, c, rows), (grad_out, c, rows)] for c in range(pieces)]
    qd_begin = 2 * tokens
    table_begin = qd_begin + 2 * rows
    kv = to_heads(
        pack(
            groups,
            heads,
            [(keys, 0, tokens), (values, 0, tokens)] + sources[0],
            (drop_mask, rand_blocks.transpose(2, 0, 1)),
            table_rows,
        )
    )
    later = [to_heads(pack(groups, heads, each)) for each in sources[1:]]
    tables = lax.dynamic_index_in_dim(
        kv.reshape(heads, groups, -1, HEAD_WIDTH)[:, :, table_begin:],
        lax.axis_index("head"),
        axis=1,
        keepdims=False,
    ).astype(jnp.int32)
    drops = tables[:, :shard_blocks, :SLOTS].reshape(team_blocks, SLOTS)
    randoms = tables[:, shard_blocks : shard_blocks + R, :shard_blocks].transpose(0, 2, 1)
    randoms = randoms.reshape(team_blocks, R)
    qd = [None] + later
    if not whole:
        qd[0] = kv[:, qd_begin:table_begin]
        kv = lax.all_gather(kv[:, : 2 * tokens], "seq", axis=0, tiled=True, axis_index_groups=same_head)
    blocks = first_block + jnp.arange(team_blocks, dtype=jnp.int32)
    window = jnp.stack([blocks - 1, blocks, blocks + 1], axis=1)
    listed = jnp.concatenate(
        [window, jnp.broadcast_to(global_ids[None], (team_blocks, G)), randoms], axis=1
    )
    listed = jnp.clip(listed, 0, total_blocks - 1).reshape(-1)
    starts = listed // device_blocks * kv.shape[1] + listed % device_blocks * BLOCK_TOKENS
    pieces_out = []
    held = []
    sums = []
    for c in range(pieces):
        pieces_out.append(
            attend(
                listed,
                starts,
                first_block.reshape(1),
                member.reshape(1),
                drops,
                kv,
                qd[c],
                qd_begin if qd[c] is None else 0,
                sums[0] if sums else None,
                c,
                per,
                whole and c == pieces - 1,
                device_blocks,
                total_blocks,
                tokens,
                heads,
            )
        )
        sums = pieces_out[c][heads:]
        if c + 1 < pieces:
            qd[c + 1], *results = lax.optimization_barrier((qd[c + 1], *pieces_out[c][1:heads]))
            held.append(results)
    runs = shard_blocks // device_blocks
    begin = shard_tokens // pieces
    near = []
    for c, out in enumerate(pieces_out):
        if len(out) > 1:
            results = out[:heads]
            if c + 1 < pieces:
                results = [results[0], *held[c]]
            near.append(to_shards(results))
    att, dq = None, None
    if whole:
        rest = pieces_out[-1][0]
        if near:
            rest, *near[-1][heads // 2 :] = lax.optimization_barrier(
                (rest, *near[-1][heads // 2 :])
            )
        rest = lax.all_to_all(rest, "seq", split_axis=0, concat_axis=0, tiled=True)
    for c in range(len(near)):
        parts = [(0, rows, runs, pieces, c, att), (begin, rows, runs, pieces, c, dq)]
        att, dq = unpack(member.reshape(1), near[c], parts)
    if whole:
        c = pieces - 1
        parts = [(0, rows, runs, pieces, c, att), (begin, rows, runs, pieces, c, dq)]
        grads = [(2 * begin + n * shard_tokens, shard_tokens, 1, 1, 0, None) for n in range(2)]
        att, dq, dk, dv = unpack_all(rest, parts + grads)
    else:
        grads = lax.psum_scatter(
            sums[0], "seq", scatter_dimension=0, tiled=True, axis_index_groups=same_head
        ).reshape(heads, shard_tokens, 2, HEAD_WIDTH)
        grads = jnp.concatenate(
            [grads[:, :, 0] * HEAD_WIDTH ** (-0.5), grads[:, :, 1]], axis=1
        ).astype(jnp.bfloat16)
        grads = to_shards(
            [lax.dynamic_index_in_dim(grads, member ^ k, 0, keepdims=False) for k in range(heads)]
        )
        dk, dv = unpack(
            member.reshape(1),
            grads,
            [(n * shard_tokens, shard_tokens, 1, 1, 0, None) for n in range(2)],
        )
    return tuple(t.reshape(shard_tokens, heads * HEAD_WIDTH) for t in (att, dq, dk, dv))


def solution(mesh):
    return jax.shard_map(
        per_device,
        mesh=mesh,
        in_specs=(
            P(("seq", "head"), None),
            P(("seq", "head"), None),
            P(("seq", "head"), None),
            P(("seq", "head"), None),
            P("head", "seq", None),
            P(),
            P("head", "seq", None),
        ),
        out_specs=(P("seq", "head"), P("seq", "head"), P("seq", "head"), P("seq", "head")),
        check_vma=False,
    )
```

```python
import functools
import math

import jax
import jax.numpy as jnp
from jax import lax
from jax.experimental import pallas as pl
from jax.experimental.pallas import tpu as pltpu
from jax.sharding import PartitionSpec as P

HEAD_WIDTH = 128
BLOCK_TOKENS = 64
R = 3
G = 2
SLOTS = 3 + G + R
WIDE = SLOTS * BLOCK_TOKENS
UNROLL = 2
STRIP = 16
VMEM_LIMIT = 16 * 1024 * 1024

keep_prob = 0.9

vmem = pl.BlockSpec(memory_space=pltpu.VMEM)
smem = pl.BlockSpec(memory_space=pltpu.SMEM)


def in_vmem(array):
    return pltpu.with_memory_space_constraint(array, pltpu.VMEM)


def copy_cost(size):
    return pl.CostEstimate(flops=0, bytes_accessed=4 * size, transcendentals=0)


def block_rows(number):
    start = number * BLOCK_TOKENS
    if not isinstance(number, int):
        start = pl.multiple_of(start, BLOCK_TOKENS)
    return pl.ds(start, BLOCK_TOKENS)


def pack_kernel(heads, table_rows, *refs):
    refs = list(refs)
    if table_rows:
        drop_ref, rand_ref, table = refs.pop(0), refs.pop(0), refs.pop()
    out_ref = refs.pop()
    begin = 0
    for ref in refs:
        rows = ref.shape[0]
        for m in range(heads):
            out_ref[m, 0, pl.ds(begin, rows), :] = ref[:, pl.ds(m * HEAD_WIDTH, HEAD_WIDTH)]
        begin += rows
    if table_rows:
        blocks = drop_ref.shape[1]
        table[...] = jnp.zeros_like(table)
        for m in range(heads):
            table[pl.ds(0, blocks), pl.ds(0, SLOTS)] = drop_ref[m].astype(jnp.float32)
            for r in range(R):
                table[pl.ds(blocks + r, 1), pl.ds(0, blocks)] = rand_ref[
                    r, pl.ds(m, 1), :
                ].astype(jnp.float32)
            out_ref[m, 0, pl.ds(begin, table_rows), :] = table[...].astype(jnp.bfloat16)


def pack(groups, heads, sources, tables=(), table_rows=0):
    specs = [pl.BlockSpec(t.shape, lambda g: (0, 0, 0)) for t in tables]
    for _, at, rows in sources:
        specs.append(
            pl.BlockSpec((rows, heads * HEAD_WIDTH), functools.partial(lambda at, g: (at, g), at))
        )
    total = sum(rows for _, _, rows in sources) + table_rows
    shape = (heads, groups, total, HEAD_WIDTH)
    packed = pl.pallas_call(
        functools.partial(pack_kernel, heads, table_rows),
        grid=(groups,),
        out_shape=pltpu.VMEM(shape, jnp.bfloat16),
        in_specs=specs,
        out_specs=pl.BlockSpec((heads, 1, total, HEAD_WIDTH), lambda g: (0, g, 0, 0)),
        scratch_shapes=[pltpu.VMEM((table_rows, HEAD_WIDTH), jnp.float32)] if table_rows else [],
        compiler_params=pltpu.CompilerParams(vmem_limit_bytes=VMEM_LIMIT),
        cost_estimate=copy_cost(math.prod(shape)),
    )(*tables, *[pltpu.with_memory_space_constraint(a, pltpu.HBM) for a, _, _ in sources])
    return packed.reshape(heads * groups, total, HEAD_WIDTH)


def unpack_kernel(parts, member_ref, *refs):
    outs = refs[len(refs) - len(parts) :]
    heads = outs[0].shape[-1] // HEAD_WIDTH
    for n in range(heads):
        k = (heads - n) % heads
        column = pl.multiple_of((member_ref[0] ^ k) * HEAD_WIDTH, HEAD_WIDTH)
        for begin, out in zip(parts, outs):
            runs, _, rows, _ = out.shape
            for i in range(runs):
                out[i, 0, :, pl.ds(column, HEAD_WIDTH)] = refs[n][pl.ds(begin + i * rows, rows), :]


def unpack(member, received, parts):
    heads = len(received)
    shapes, specs, olds, aliases, size = [], [], [], {}, 0
    for n, (_, rows, runs, pieces, piece, old) in enumerate(parts):
        shapes.append(
            jax.ShapeDtypeStruct((runs, pieces, rows, heads * HEAD_WIDTH), jnp.bfloat16)
        )
        specs.append(
            pl.BlockSpec(
                (runs, 1, rows, heads * HEAD_WIDTH),
                functools.partial(lambda piece, h: (0, piece, 0, 0), piece),
            )
        )
        size += rows * runs * heads * HEAD_WIDTH
        if old is not None:
            aliases[1 + heads + len(olds)] = n
            olds.append(old)
    return pl.pallas_call(
        functools.partial(unpack_kernel, tuple(part[0] for part in parts)),
        grid=(1,),
        out_shape=shapes,
        in_specs=[smem]
        + [pl.BlockSpec(received[0].shape, lambda h: (0, 0))] * heads
        + [pl.BlockSpec(memory_space=pl.ANY)] * len(olds),
        out_specs=specs,
        input_output_aliases=aliases,
        compiler_params=pltpu.CompilerParams(vmem_limit_bytes=VMEM_LIMIT),
        cost_estimate=copy_cost(size),
    )(member, received[0], *received[:0:-1], *olds)


def unpack_all_kernel(begins, step_heads, piece_ref, *refs):
    outs = refs[len(refs) - len(begins) :]
    for begin, out in zip(begins, outs):
        runs, _, rows, _ = out.shape
        for m in range(step_heads):
            for i in range(runs):
                out[i, 0, :, pl.ds(m * HEAD_WIDTH, HEAD_WIDTH)] = piece_ref[
                    m, pl.ds(begin + i * rows, rows), :
                ]


def unpack_all(received, parts):
    heads, total, _ = received.shape
    step_heads = 2 if heads % 2 == 0 else 1
    width = step_heads * HEAD_WIDTH
    shapes, out_specs, begins, olds, aliases = [], [], [], [], {}
    size = 0
    for n, (begin, rows, runs, pieces, piece, old) in enumerate(parts):
        begins.append(begin)
        shapes.append(
            jax.ShapeDtypeStruct((runs, pieces, rows, heads * HEAD_WIDTH), jnp.bfloat16)
        )
        out_specs.append(
            pl.BlockSpec(
                (runs, 1, rows, width), functools.partial(lambda piece, h: (0, piece, 0, h), piece)
            )
        )
        size += rows * runs * heads * HEAD_WIDTH
        if old is not None:
            aliases[1 + len(olds)] = n
            olds.append(old)
    return pl.pallas_call(
        functools.partial(unpack_all_kernel, begins, step_heads),
        grid=(heads // step_heads,),
        out_shape=shapes,
        in_specs=[pl.BlockSpec((step_heads, total, HEAD_WIDTH), lambda h: (h, 0, 0))]
        + [pl.BlockSpec(memory_space=pl.ANY)] * len(olds),
        out_specs=out_specs,
        input_output_aliases=aliases,
        compiler_params=pltpu.CompilerParams(vmem_limit_bytes=VMEM_LIMIT),
        cost_estimate=copy_cost(size),
    )(in_vmem(received), *olds)


def attention_kernel(
    last_block,
    device_blocks,
    per,
    piece,
    out_rows,
    source_rows,
    qd_rows,
    qd_begin,
    has_qd,
    has_start,
    joined,
    tokens,
    targets,
    ids_ref,
    starts_ref,
    first_ref,
    member_ref,
    drop_ref,
    kv_ref,
    *refs,
):
    refs = list(refs)
    qd_ref = refs.pop(0) if has_qd else kv_ref
    start_ref = refs.pop(0) if has_start else None
    out_refs = [refs.pop(0) for _ in range(1 if joined else targets)]
    acc, retain, waiting, near = refs[:4]
    earlier, sem = refs[4:] if has_start else (None, None)
    scale = HEAD_WIDTH ** (-0.5)
    steps = targets * (out_rows // BLOCK_TOKENS)
    slot_of_lane = lax.broadcasted_iota(jnp.int32, (SLOTS, WIDE), 1) // BLOCK_TOKENS
    slot_row = lax.broadcasted_iota(jnp.int32, (SLOTS, WIDE), 0)
    expand = (slot_of_lane == slot_row).astype(jnp.float32)
    retain[...] = jnp.dot(
        drop_ref[...].astype(jnp.float32), expand, preferred_element_type=jnp.float32
    ) * (1.0 / keep_prob)
    acc[...] = jnp.zeros_like(acc)
    if has_start:
        fetch = pltpu.make_async_copy(start_ref, earlier, sem)
        fetch.start()
    lane = lax.broadcasted_iota(jnp.int32, (1, WIDE), 1)
    nt = (((1,), (1,)), ((), ()))
    tn = (((0,), (0,)), ((), ()))
    out_steps = steps // targets

    def place(i):
        if per == 1:
            source, sub = i, 0
        else:
            source, sub = lax.div(i, per), lax.rem(i, per)
        return source, sub, source * device_blocks + piece * per + sub

    def load(i):
        source, sub, j = place(i)
        starts = [starts_ref[j * SLOTS + s] for s in range(SLOTS)]
        q, do = [
            qd_ref[
                pl.ds(
                    pl.multiple_of(
                        source * qd_rows + (n * per + sub) * BLOCK_TOKENS + qd_begin, 16
                    ),
                    BLOCK_TOKENS,
                ),
                :,
            ]
            for n in range(2)
        ]
        keys, vals = [
            jnp.concatenate(
                [kv_ref[pl.ds(pl.multiple_of(r + n * tokens, 16), BLOCK_TOKENS), :] for r in starts],
                axis=0,
            )
            for n in range(2)
        ]
        return q, do, keys, vals

    def score(i):
        q, do, keys, vals = load(i)
        logits = lax.dot_general(q, keys, nt, preferred_element_type=jnp.float32)
        raw = lax.dot_general(do, vals, nt, preferred_element_type=jnp.float32)
        return logits, raw

    def factor(i, u, logits, raw):
        j = place(i)[2]
        block_id = first_ref[0] + j
        absent = ((block_id == 0) & (lane < BLOCK_TOKENS)) | (
            (block_id == last_block) & (lane >= 2 * BLOCK_TOKENS) & (lane < 3 * BLOCK_TOKENS)
        )
        keep = retain[pl.ds(j, 1), :]
        for r in range(0, BLOCK_TOKENS, STRIP):
            part = jnp.where(absent, -jnp.inf, logits[r : r + STRIP])
            top = jnp.max(part, axis=-1, keepdims=True)
            expd = jnp.exp2((part - top) * (scale / math.log(2.0)))
            probs = expd * (1.0 / jnp.sum(expd, axis=-1, keepdims=True))
            kept = probs * keep
            weighted = kept * raw[r : r + STRIP]
            delta = jnp.sum(weighted, axis=-1, keepdims=True)
            waiting[u, pl.ds(r, STRIP), :] = (weighted - probs * delta).astype(jnp.bfloat16)
            waiting[u, pl.ds(BLOCK_TOKENS + r, STRIP), :] = kept.astype(jnp.bfloat16)

    def finish(i, u):
        j = place(i)[2]
        q, do, keys, vals = load(i)
        factors = waiting[u]
        dq = jnp.dot(factors[:BLOCK_TOKENS], keys, preferred_element_type=jnp.float32) * scale
        att = jnp.dot(factors[BLOCK_TOKENS:], vals, preferred_element_type=jnp.float32)
        none = jnp.zeros_like(q)
        pair = jnp.concatenate(
            [jnp.concatenate([q, none], axis=1), jnp.concatenate([none, do], axis=1)], axis=0
        )
        terms = lax.dot_general(factors, pair, tn, preferred_element_type=jnp.float32)
        for s in range(SLOTS):
            acc[block_rows(ids_ref[j * SLOTS + s]), :] += terms[
                s * BLOCK_TOKENS : (s + 1) * BLOCK_TOKENS
            ]
        target, pos = lax.div(i, out_steps), lax.rem(i, out_steps)
        near[target, block_rows(pos), :] = att.astype(jnp.bfloat16)
        near[target, block_rows(out_steps + pos), :] = dq.astype(jnp.bfloat16)

    def step(t, carry):
        scores = [score(t * UNROLL + u) for u in range(UNROLL)]
        for u in range(UNROLL):
            finish((t - 1) * UNROLL + u, u)
        for u in range(UNROLL):
            factor(t * UNROLL + u, u, *scores[u])
        return carry

    for u in range(UNROLL):
        factor(u, u, *score(u))
    lax.fori_loop(1, steps // UNROLL, step, 0)
    for u in range(UNROLL):
        finish(steps - UNROLL + u, u)
    if has_start:
        fetch.wait()
        acc[...] += earlier[...]
    if joined:
        rows = acc.shape[0] // targets
        for target in range(targets):
            part = pl.ds(target * rows, rows)
            out_refs[0][target, pl.ds(0, 2 * out_rows), :] = near[target]
            out_refs[0][target, pl.ds(2 * out_rows, rows), :] = (
                acc[part, :HEAD_WIDTH] * scale
            ).astype(jnp.bfloat16)
            out_refs[0][target, pl.ds(2 * out_rows + rows, rows), :] = acc[
                part, HEAD_WIDTH:
            ].astype(jnp.bfloat16)
    else:
        for k, out_ref in enumerate(out_refs):
            out_ref[...] = near[member_ref[0] ^ k]


def attend(
    ids, starts, first_block, member, drop, kv, qd, qd_begin, start, piece, per, joined, device_blocks, total_blocks, tokens, targets
):
    team_blocks = drop.shape[0]
    source = kv if qd is None else qd
    steps = team_blocks * per // device_blocks
    length = total_blocks * BLOCK_TOKENS
    pairs = steps * BLOCK_TOKENS * WIDE
    accumulator = (length, 2 * HEAD_WIDTH)
    out_rows = steps * BLOCK_TOKENS // targets
    if joined:
        out_shape = [
            pltpu.VMEM((targets, 2 * out_rows + 2 * length // targets, HEAD_WIDTH), jnp.bfloat16)
        ]
    else:
        out_shape = [jax.ShapeDtypeStruct((2 * out_rows, HEAD_WIDTH), jnp.bfloat16)] * targets
    scratch = [
        pltpu.VMEM((team_blocks, WIDE), jnp.float32),
        pltpu.VMEM((UNROLL, 2 * BLOCK_TOKENS, WIDE), jnp.bfloat16),
        pltpu.VMEM((targets, 2 * out_rows, HEAD_WIDTH), jnp.bfloat16),
    ]
    if joined:
        scratch = [pltpu.VMEM(accumulator, jnp.float32)] + scratch
    else:
        out_shape.append(jax.ShapeDtypeStruct(accumulator, jnp.float32))
    if start is not None:
        scratch += [pltpu.VMEM(accumulator, jnp.float32), pltpu.SemaphoreType.DMA]
    sums_bytes = 8 * length * HEAD_WIDTH
    limit = VMEM_LIMIT + 2 * (kv.size + source.size) + (2 if start is not None else 1) * sums_bytes
    flat = [in_vmem(t.reshape(-1, HEAD_WIDTH)) for t in (kv, qd) if t is not None]
    operands = flat + ([] if start is None else [start])
    operand_specs = [vmem] * len(flat) + [pl.BlockSpec(memory_space=pl.ANY)] * (start is not None)
    return pl.pallas_call(
        functools.partial(
            attention_kernel,
            total_blocks - 1,
            device_blocks,
            per,
            piece,
            out_rows,
            kv.shape[1],
            source.shape[1],
            qd_begin,
            qd is not None,
            start is not None,
            joined,
            tokens,
            targets,
        ),
        out_shape=out_shape,
        in_specs=[smem, smem, smem, smem, vmem] + operand_specs,
        out_specs=[vmem] * len(out_shape),
        scratch_shapes=scratch,
        compiler_params=pltpu.CompilerParams(vmem_limit_bytes=limit),
        cost_estimate=pl.CostEstimate(
            flops=128 * pairs * HEAD_WIDTH,
            bytes_accessed=2 * (source.size + kv.size) + 8 * length * HEAD_WIDTH,
            transcendentals=pairs,
        ),
    )(ids, starts, first_block, member, drop, *operands)


def per_device(queries, keys, values, grad_out, rand_blocks, global_ids, drop_mask):
    shards = lax.axis_size("seq")
    groups = lax.axis_size("head")
    shard = lax.axis_index("seq")
    heads, shard_blocks, _ = rand_blocks.shape
    tokens = queries.shape[0]
    device_blocks = tokens // BLOCK_TOKENS
    shard_tokens = shard_blocks * BLOCK_TOKENS
    teams = shards // heads
    team, member = lax.div(shard, heads), lax.rem(shard, heads)
    team_blocks = heads * shard_blocks
    total_blocks = shards * shard_blocks
    first_block = team * team_blocks
    whole = teams == 1
    pieces = device_blocks if whole else 1
    per = device_blocks // pieces
    rows = tokens // pieces
    same_team_all = (
        None
        if whole
        else [
            [(t * heads + m) * groups + g for m in range(heads) for g in range(groups)]
            for t in range(teams)
        ]
    )
    same_head = [[t * heads + m for t in range(teams)] for m in range(heads)]

    def to_heads(packed):
        return lax.all_to_all(
            packed,
            ("seq", "head"),
            split_axis=0,
            concat_axis=0,
            tiled=True,
            axis_index_groups=same_team_all,
        )

    def to_shards(results):
        received = list(results)
        for k in reversed(range(1, heads)):
            pairs = [(s, s ^ k) for s in range(shards)]
            received[k] = lax.ppermute(results[k], "seq", pairs)
        return received

    table_rows = -(-(shard_blocks + R) // 16) * 16
    sources = [[(queries, c, rows), (grad_out, c, rows)] for c in range(pieces)]
    qd_begin = 2 * tokens
    table_begin = qd_begin + 2 * rows
    kv = to_heads(
        pack(
            groups,
            heads,
            [(keys, 0, tokens), (values, 0, tokens)] + sources[0],
            (drop_mask, rand_blocks.transpose(2, 0, 1)),
            table_rows,
        )
    )
    later = [to_heads(pack(groups, heads, each)) for each in sources[1:]]
    tables = lax.dynamic_index_in_dim(
        kv.reshape(heads, groups, -1, HEAD_WIDTH)[:, :, table_begin:],
        lax.axis_index("head"),
        axis=1,
        keepdims=False,
    ).astype(jnp.int32)
    drops = tables[:, :shard_blocks, :SLOTS].reshape(team_blocks, SLOTS)
    randoms = tables[:, shard_blocks : shard_blocks + R, :shard_blocks].transpose(0, 2, 1)
    randoms = randoms.reshape(team_blocks, R)
    qd = [None] + later
    if not whole:
        qd[0] = kv[:, qd_begin:table_begin]
        kv = lax.all_gather(kv[:, : 2 * tokens], "seq", axis=0, tiled=True, axis_index_groups=same_head)
    blocks = first_block + jnp.arange(team_blocks, dtype=jnp.int32)
    window = jnp.stack([blocks - 1, blocks, blocks + 1], axis=1)
    listed = jnp.concatenate(
        [window, jnp.broadcast_to(global_ids[None], (team_blocks, G)), randoms], axis=1
    )
    listed = jnp.clip(listed, 0, total_blocks - 1).reshape(-1)
    starts = listed // device_blocks * kv.shape[1] + listed % device_blocks * BLOCK_TOKENS
    pieces_out = []
    held = []
    sums = []
    for c in range(pieces):
        pieces_out.append(
            attend(
                listed,
                starts,
                first_block.reshape(1),
                member.reshape(1),
                drops,
                kv,
                qd[c],
                qd_begin if qd[c] is None else 0,
                sums[0] if sums else None,
                c,
                per,
                whole and c == pieces - 1,
                device_blocks,
                total_blocks,
                tokens,
                heads,
            )
        )
        sums = pieces_out[c][heads:]
        if c + 1 < pieces:
            qd[c + 1], *results = lax.optimization_barrier((qd[c + 1], *pieces_out[c][1:heads]))
            held.append(results)
    runs = shard_blocks // device_blocks
    begin = shard_tokens // pieces
    near = []
    for c, out in enumerate(pieces_out):
        if len(out) > 1:
            results = out[:heads]
            if c + 1 < pieces:
                results = [results[0], *held[c]]
            near.append(to_shards(results))
    att, dq = None, None
    if whole:
        rest = pieces_out[-1][0]
        if near:
            rest, near[-1][heads // 2] = lax.optimization_barrier((rest, near[-1][heads // 2]))
        rest = lax.all_to_all(rest, "seq", split_axis=0, concat_axis=0, tiled=True)
    for c in range(len(near)):
        parts = [(0, rows, runs, pieces, c, att), (begin, rows, runs, pieces, c, dq)]
        att, dq = unpack(member.reshape(1), near[c], parts)
    if whole:
        c = pieces - 1
        parts = [(0, rows, runs, pieces, c, att), (begin, rows, runs, pieces, c, dq)]
        grads = [(2 * begin + n * shard_tokens, shard_tokens, 1, 1, 0, None) for n in range(2)]
        att, dq, dk, dv = unpack_all(rest, parts + grads)
    else:
        grads = lax.psum_scatter(
            sums[0], "seq", scatter_dimension=0, tiled=True, axis_index_groups=same_head
        ).reshape(heads, shard_tokens, 2, HEAD_WIDTH)
        grads = jnp.concatenate(
            [grads[:, :, 0] * HEAD_WIDTH ** (-0.5), grads[:, :, 1]], axis=1
        ).astype(jnp.bfloat16)
        grads = to_shards(
            [lax.dynamic_index_in_dim(grads, member ^ k, 0, keepdims=False) for k in range(heads)]
        )
        dk, dv = unpack(
            member.reshape(1),
            grads,
            [(n * shard_tokens, shard_tokens, 1, 1, 0, None) for n in range(2)],
        )
    return tuple(t.reshape(shard_tokens, heads * HEAD_WIDTH) for t in (att, dq, dk, dv))


def solution(mesh):
    return jax.shard_map(
        per_device,
        mesh=mesh,
        in_specs=(
            P(("seq", "head"), None),
            P(("seq", "head"), None),
            P(("seq", "head"), None),
            P(("seq", "head"), None),
            P("head", "seq", None),
            P(),
            P("head", "seq", None),
        ),
        out_specs=(P("seq", "head"), P("seq", "head"), P("seq", "head"), P("seq", "head")),
        check_vma=False,
    )
```

```python
import functools
import math

import jax
import jax.numpy as jnp
from jax import lax
from jax.experimental import pallas as pl
from jax.experimental.pallas import tpu as pltpu
from jax.sharding import PartitionSpec as P

HEAD_WIDTH = 128
BLOCK_TOKENS = 64
R = 3
G = 2
SLOTS = 3 + G + R
WIDE = SLOTS * BLOCK_TOKENS
UNROLL = 2
STRIP = 16
VMEM_LIMIT = 16 * 1024 * 1024

keep_prob = 0.9

vmem = pl.BlockSpec(memory_space=pltpu.VMEM)
smem = pl.BlockSpec(memory_space=pltpu.SMEM)


def in_vmem(array):
    return pltpu.with_memory_space_constraint(array, pltpu.VMEM)


def in_hbm(array):
    return pltpu.with_memory_space_constraint(array, pltpu.HBM)


def copy_cost(size):
    return pl.CostEstimate(flops=0, bytes_accessed=4 * size, transcendentals=0)


def block_rows(number):
    start = number * BLOCK_TOKENS
    if not isinstance(number, int):
        start = pl.multiple_of(start, BLOCK_TOKENS)
    return pl.ds(start, BLOCK_TOKENS)


def pack_kernel(heads, groups, sources, table_rows, *refs):
    refs = list(refs)
    if table_rows:
        drop_ref, rand_ref, table = refs.pop(0), refs.pop(0), refs.pop()
    count = len(sources)
    arrays, out_ref = refs[:count], refs[count]
    wholes, packed, in_sems, out_sems = refs[count + 1 : -3], refs[-3], refs[-2], refs[-1]
    width = heads * HEAD_WIDTH
    loads = []
    for g in range(groups):
        for n, (at, rows) in enumerate(sources):
            columns = pl.ds(g * width, width)
            loads.append(
                pltpu.make_async_copy(
                    arrays[n].at[pl.ds(at * rows, rows), columns],
                    wholes[n].at[:, columns],
                    in_sems.at[g, n],
                )
            )
    for load in loads:
        load.start()
    begin = sum(rows for _, rows in sources)
    if table_rows:
        blocks = drop_ref.shape[1]
        table[...] = jnp.zeros_like(table)
        for m in range(heads):
            table[pl.ds(0, blocks), pl.ds(0, SLOTS)] = drop_ref[m].astype(jnp.float32)
            for r in range(R):
                table[pl.ds(blocks + r, 1), pl.ds(0, blocks)] = rand_ref[
                    r, pl.ds(m, 1), :
                ].astype(jnp.float32)
            rounded = table[...].astype(jnp.bfloat16)
            for g in range(groups):
                packed[m, g, pl.ds(begin, table_rows), :] = rounded
    stores = []
    for g in range(groups):
        for n in range(count):
            loads[g * count + n].wait()
        for m in range(heads):
            begin = 0
            for n, (_, rows) in enumerate(sources):
                packed[m, g, pl.ds(begin, rows), :] = wholes[n][
                    :, pl.ds((g * heads + m) * HEAD_WIDTH, HEAD_WIDTH)
                ]
                begin += rows
            stores.append(
                pltpu.make_async_copy(packed.at[m, g], out_ref.at[m, g], out_sems.at[g, m])
            )
            stores[-1].start()
    for store in stores:
        store.wait()


def pack(groups, heads, sources, tables=(), table_rows=0):
    total = sum(rows for _, _, rows in sources) + table_rows
    shape = (heads, groups, total, HEAD_WIDTH)
    scratch = [
        pltpu.VMEM((rows, groups * heads * HEAD_WIDTH), jnp.bfloat16) for _, _, rows in sources
    ] + [
        pltpu.VMEM(shape, jnp.bfloat16),
        pltpu.SemaphoreType.DMA((groups, len(sources))),
        pltpu.SemaphoreType.DMA((groups, heads)),
    ]
    if table_rows:
        scratch.append(pltpu.VMEM((table_rows, HEAD_WIDTH), jnp.float32))
    anywhere = pl.BlockSpec(memory_space=pl.ANY)
    packed = pl.pallas_call(
        functools.partial(
            pack_kernel, heads, groups, tuple((at, rows) for _, at, rows in sources), table_rows
        ),
        out_shape=pltpu.HBM(shape, jnp.bfloat16),
        in_specs=[vmem] * len(tables) + [anywhere] * len(sources),
        out_specs=anywhere,
        scratch_shapes=scratch,
        compiler_params=pltpu.CompilerParams(vmem_limit_bytes=VMEM_LIMIT),
        cost_estimate=copy_cost(math.prod(shape)),
    )(*[in_hbm(t) for t in tables], *[in_hbm(a) for a, _, _ in sources])
    return packed.reshape(heads * groups, total, HEAD_WIDTH)


def unpack_kernel(parts, member_ref, *refs):
    outs = refs[len(refs) - len(parts) :]
    heads = outs[0].shape[-1] // HEAD_WIDTH
    for n in range(heads):
        k = (heads - n) % heads
        column = pl.multiple_of((member_ref[0] ^ k) * HEAD_WIDTH, HEAD_WIDTH)
        for begin, out in zip(parts, outs):
            runs, _, rows, _ = out.shape
            for i in range(runs):
                out[i, 0, :, pl.ds(column, HEAD_WIDTH)] = refs[n][pl.ds(begin + i * rows, rows), :]


def unpack(member, received, parts):
    heads = len(received)
    shapes, specs, olds, aliases, size = [], [], [], {}, 0
    for n, (_, rows, runs, pieces, piece, old) in enumerate(parts):
        shapes.append(
            jax.ShapeDtypeStruct((runs, pieces, rows, heads * HEAD_WIDTH), jnp.bfloat16)
        )
        specs.append(
            pl.BlockSpec(
                (runs, 1, rows, heads * HEAD_WIDTH),
                functools.partial(lambda piece, h: (0, piece, 0, 0), piece),
            )
        )
        size += rows * runs * heads * HEAD_WIDTH
        if old is not None:
            aliases[1 + heads + len(olds)] = n
            olds.append(old)
    return pl.pallas_call(
        functools.partial(unpack_kernel, tuple(part[0] for part in parts)),
        grid=(1,),
        out_shape=shapes,
        in_specs=[smem]
        + [pl.BlockSpec(received[0].shape, lambda h: (0, 0))] * heads
        + [pl.BlockSpec(memory_space=pl.ANY)] * len(olds),
        out_specs=specs,
        input_output_aliases=aliases,
        compiler_params=pltpu.CompilerParams(vmem_limit_bytes=VMEM_LIMIT),
        cost_estimate=copy_cost(size),
    )(member, received[0], *received[:0:-1], *olds)


def unpack_all_kernel(begins, step_heads, piece_ref, *refs):
    outs = refs[len(refs) - len(begins) :]
    for begin, out in zip(begins, outs):
        runs, _, rows, _ = out.shape
        for m in range(step_heads):
            for i in range(runs):
                out[i, 0, :, pl.ds(m * HEAD_WIDTH, HEAD_WIDTH)] = piece_ref[
                    m, pl.ds(begin + i * rows, rows), :
                ]


def unpack_all(received, parts):
    heads, total, _ = received.shape
    step_heads = 2 if heads % 2 == 0 else 1
    width = step_heads * HEAD_WIDTH
    shapes, out_specs, begins, olds, aliases = [], [], [], [], {}
    size = 0
    for n, (begin, rows, runs, pieces, piece, old) in enumerate(parts):
        begins.append(begin)
        shapes.append(
            jax.ShapeDtypeStruct((runs, pieces, rows, heads * HEAD_WIDTH), jnp.bfloat16)
        )
        out_specs.append(
            pl.BlockSpec(
                (runs, 1, rows, width), functools.partial(lambda piece, h: (0, piece, 0, h), piece)
            )
        )
        size += rows * runs * heads * HEAD_WIDTH
        if old is not None:
            aliases[1 + len(olds)] = n
            olds.append(old)
    return pl.pallas_call(
        functools.partial(unpack_all_kernel, begins, step_heads),
        grid=(heads // step_heads,),
        out_shape=shapes,
        in_specs=[pl.BlockSpec((step_heads, total, HEAD_WIDTH), lambda h: (h, 0, 0))]
        + [pl.BlockSpec(memory_space=pl.ANY)] * len(olds),
        out_specs=out_specs,
        input_output_aliases=aliases,
        compiler_params=pltpu.CompilerParams(vmem_limit_bytes=VMEM_LIMIT),
        cost_estimate=copy_cost(size),
    )(in_vmem(received), *olds)


def attention_kernel(
    last_block,
    device_blocks,
    per,
    piece,
    out_rows,
    source_rows,
    qd_rows,
    qd_begin,
    has_qd,
    has_start,
    joined,
    tokens,
    targets,
    ids_ref,
    starts_ref,
    first_ref,
    member_ref,
    drop_ref,
    kv_ref,
    *refs,
):
    refs = list(refs)
    qd_ref = refs.pop(0) if has_qd else kv_ref
    start_ref = refs.pop(0) if has_start else None
    out_refs = [refs.pop(0) for _ in range(1 if joined else targets)]
    acc, retain, waiting, near = refs[:4]
    done, sems = refs[4:] if joined else (None, None)
    scale = HEAD_WIDTH ** (-0.5)
    steps = targets * (out_rows // BLOCK_TOKENS)
    slot_of_lane = lax.broadcasted_iota(jnp.int32, (SLOTS, WIDE), 1) // BLOCK_TOKENS
    slot_row = lax.broadcasted_iota(jnp.int32, (SLOTS, WIDE), 0)
    expand = (slot_of_lane == slot_row).astype(jnp.float32)
    retain[...] = jnp.dot(
        drop_ref[...].astype(jnp.float32), expand, preferred_element_type=jnp.float32
    ) * (1.0 / keep_prob)
    acc[...] = jnp.zeros_like(acc)
    lane = lax.broadcasted_iota(jnp.int32, (1, WIDE), 1)
    nt = (((1,), (1,)), ((), ()))
    tn = (((0,), (0,)), ((), ()))
    out_steps = steps // targets

    def place(i):
        if per == 1:
            source, sub = i, 0
        else:
            source, sub = lax.div(i, per), lax.rem(i, per)
        return source, sub, source * device_blocks + piece * per + sub

    def load(i):
        source, sub, j = place(i)
        starts = [starts_ref[j * SLOTS + s] for s in range(SLOTS)]
        q, do = [
            qd_ref[
                pl.ds(
                    pl.multiple_of(
                        source * qd_rows + (n * per + sub) * BLOCK_TOKENS + qd_begin, 16
                    ),
                    BLOCK_TOKENS,
                ),
                :,
            ]
            for n in range(2)
        ]
        keys, vals = [
            jnp.concatenate(
                [kv_ref[pl.ds(pl.multiple_of(r + n * tokens, 16), BLOCK_TOKENS), :] for r in starts],
                axis=0,
            )
            for n in range(2)
        ]
        return q, do, keys, vals

    def score(i):
        q, do, keys, vals = load(i)
        logits = lax.dot_general(q, keys, nt, preferred_element_type=jnp.float32)
        raw = lax.dot_general(do, vals, nt, preferred_element_type=jnp.float32)
        return logits, raw

    def factor(i, u, logits, raw):
        j = place(i)[2]
        block_id = first_ref[0] + j
        absent = ((block_id == 0) & (lane < BLOCK_TOKENS)) | (
            (block_id == last_block) & (lane >= 2 * BLOCK_TOKENS) & (lane < 3 * BLOCK_TOKENS)
        )
        keep = retain[pl.ds(j, 1), :]
        for r in range(0, BLOCK_TOKENS, STRIP):
            part = jnp.where(absent, -jnp.inf, logits[r : r + STRIP])
            top = jnp.max(part, axis=-1, keepdims=True)
            expd = jnp.exp2((part - top) * (scale / math.log(2.0)))
            probs = expd * (1.0 / jnp.sum(expd, axis=-1, keepdims=True))
            kept = probs * keep
            weighted = kept * raw[r : r + STRIP]
            delta = jnp.sum(weighted, axis=-1, keepdims=True)
            waiting[u, pl.ds(r, STRIP), :] = (weighted - probs * delta).astype(jnp.bfloat16)
            waiting[u, pl.ds(BLOCK_TOKENS + r, STRIP), :] = kept.astype(jnp.bfloat16)

    def finish(i, u):
        j = place(i)[2]
        q, do, keys, vals = load(i)
        factors = waiting[u]
        dq = jnp.dot(factors[:BLOCK_TOKENS], keys, preferred_element_type=jnp.float32) * scale
        att = jnp.dot(factors[BLOCK_TOKENS:], vals, preferred_element_type=jnp.float32)
        none = jnp.zeros_like(q)
        pair = jnp.concatenate(
            [jnp.concatenate([q, none], axis=1), jnp.concatenate([none, do], axis=1)], axis=0
        )
        terms = lax.dot_general(factors, pair, tn, preferred_element_type=jnp.float32)
        for s in range(SLOTS):
            acc[block_rows(ids_ref[j * SLOTS + s]), :] += terms[
                s * BLOCK_TOKENS : (s + 1) * BLOCK_TOKENS
            ]
        target, pos = lax.div(i, out_steps), lax.rem(i, out_steps)
        near[target, block_rows(pos), :] = att.astype(jnp.bfloat16)
        near[target, block_rows(out_steps + pos), :] = dq.astype(jnp.bfloat16)

    def step(t, carry):
        scores = [score(t * UNROLL + u) for u in range(UNROLL)]
        for u in range(UNROLL):
            finish((t - 1) * UNROLL + u, u)
        for u in range(UNROLL):
            factor(t * UNROLL + u, u, *scores[u])
        return carry

    for u in range(UNROLL):
        factor(u, u, *score(u))
    lax.fori_loop(1, steps // UNROLL, step, 0)
    for u in range(UNROLL):
        finish(steps - UNROLL + u, u)
    if joined:
        rows = acc.shape[0] // targets
        stores = []
        for target in range(targets):
            part = pl.ds(target * rows, rows)
            sums = acc[part, :]
            if has_start:
                sums += start_ref[part, :]
            done[target, pl.ds(0, 2 * out_rows), :] = near[target]
            done[target, pl.ds(2 * out_rows, rows), :] = (sums[:, :HEAD_WIDTH] * scale).astype(
                jnp.bfloat16
            )
            done[target, pl.ds(2 * out_rows + rows, rows), :] = sums[:, HEAD_WIDTH:].astype(
                jnp.bfloat16
            )
            stores.append(
                pltpu.make_async_copy(done.at[target], out_refs[0].at[target], sems.at[target])
            )
            stores[-1].start()
        for store in stores:
            store.wait()
    else:
        for k, out_ref in enumerate(out_refs):
            out_ref[...] = near[member_ref[0] ^ k]


def attend(
    ids, starts, first_block, member, drop, kv, qd, qd_begin, start, piece, per, joined, device_blocks, total_blocks, tokens, targets, keep_sums
):
    team_blocks = drop.shape[0]
    source = kv if qd is None else qd
    steps = team_blocks * per // device_blocks
    length = total_blocks * BLOCK_TOKENS
    pairs = steps * BLOCK_TOKENS * WIDE
    accumulator = (length, 2 * HEAD_WIDTH)
    out_rows = steps * BLOCK_TOKENS // targets
    if joined:
        out_shape = [
            pltpu.HBM((targets, 2 * out_rows + 2 * length // targets, HEAD_WIDTH), jnp.bfloat16)
        ]
    else:
        out_shape = [pltpu.HBM((2 * out_rows, HEAD_WIDTH), jnp.bfloat16)] * targets
    scratch = [
        pltpu.VMEM((team_blocks, WIDE), jnp.float32),
        pltpu.VMEM((UNROLL, 2 * BLOCK_TOKENS, WIDE), jnp.bfloat16),
        pltpu.VMEM((targets, 2 * out_rows, HEAD_WIDTH), jnp.bfloat16),
    ]
    if joined:
        scratch = [pltpu.VMEM(accumulator, jnp.float32)] + scratch
    else:
        out_shape.append((pltpu.VMEM if keep_sums else pltpu.HBM)(accumulator, jnp.float32))
    if joined:
        scratch += [
            pltpu.VMEM(out_shape[0].shape, jnp.bfloat16),
            pltpu.SemaphoreType.DMA((targets,)),
        ]
    sums_bytes = 8 * length * HEAD_WIDTH
    limit = VMEM_LIMIT + 2 * (kv.size + source.size) + sums_bytes
    flat = [in_vmem(t.reshape(-1, HEAD_WIDTH)) for t in (kv, qd) if t is not None]
    operands = flat + ([] if start is None else [in_vmem(start)])
    return pl.pallas_call(
        functools.partial(
            attention_kernel,
            total_blocks - 1,
            device_blocks,
            per,
            piece,
            out_rows,
            kv.shape[1],
            source.shape[1],
            qd_begin,
            qd is not None,
            start is not None,
            joined,
            tokens,
            targets,
        ),
        out_shape=out_shape,
        in_specs=[smem, smem, smem, smem, vmem] + [vmem] * len(operands),
        out_specs=[pl.BlockSpec(memory_space=pl.ANY)] if joined else [vmem] * len(out_shape),
        scratch_shapes=scratch,
        compiler_params=pltpu.CompilerParams(vmem_limit_bytes=limit),
        cost_estimate=pl.CostEstimate(
            flops=128 * pairs * HEAD_WIDTH,
            bytes_accessed=2 * (source.size + kv.size) + 8 * length * HEAD_WIDTH,
            transcendentals=pairs,
        ),
    )(ids, starts, first_block, member, in_hbm(drop), *operands)


def per_device(queries, keys, values, grad_out, rand_blocks, global_ids, drop_mask):
    shards = lax.axis_size("seq")
    groups = lax.axis_size("head")
    shard = lax.axis_index("seq")
    heads, shard_blocks, _ = rand_blocks.shape
    tokens = queries.shape[0]
    device_blocks = tokens // BLOCK_TOKENS
    shard_tokens = shard_blocks * BLOCK_TOKENS
    teams = shards // heads
    team, member = lax.div(shard, heads), lax.rem(shard, heads)
    team_blocks = heads * shard_blocks
    total_blocks = shards * shard_blocks
    first_block = team * team_blocks
    whole = teams == 1
    pieces = device_blocks if whole else 1
    per = device_blocks // pieces
    rows = tokens // pieces
    same_team_all = (
        None
        if whole
        else [
            [(t * heads + m) * groups + g for m in range(heads) for g in range(groups)]
            for t in range(teams)
        ]
    )
    same_head = [[t * heads + m for t in range(teams)] for m in range(heads)]

    def to_heads(packed):
        return lax.all_to_all(
            packed,
            ("seq", "head"),
            split_axis=0,
            concat_axis=0,
            tiled=True,
            axis_index_groups=same_team_all,
        )

    def to_shards(results):
        received = list(results)
        for k in reversed(range(1, heads)):
            pairs = [(s, s ^ k) for s in range(shards)]
            received[k] = lax.ppermute(results[k], "seq", pairs)
        return received

    table_rows = -(-(shard_blocks + R) // 16) * 16
    sources = [[(queries, c, rows), (grad_out, c, rows)] for c in range(pieces)]
    qd_begin = 2 * tokens
    table_begin = qd_begin + 2 * rows
    kv = to_heads(
        pack(
            groups,
            heads,
            [(keys, 0, tokens), (values, 0, tokens)] + sources[0],
            (drop_mask, rand_blocks.transpose(2, 0, 1)),
            table_rows,
        )
    )
    later = [to_heads(pack(groups, heads, each)) for each in sources[1:]]
    tables = lax.dynamic_index_in_dim(
        kv.reshape(heads, groups, -1, HEAD_WIDTH)[:, :, table_begin:],
        lax.axis_index("head"),
        axis=1,
        keepdims=False,
    ).astype(jnp.int32)
    drops = tables[:, :shard_blocks, :SLOTS].reshape(team_blocks, SLOTS)
    randoms = tables[:, shard_blocks : shard_blocks + R, :shard_blocks].transpose(0, 2, 1)
    randoms = randoms.reshape(team_blocks, R)
    qd = [None] + later
    if not whole:
        qd[0] = kv[:, qd_begin:table_begin]
        kv = lax.all_gather(kv[:, : 2 * tokens], "seq", axis=0, tiled=True, axis_index_groups=same_head)
    blocks = first_block + jnp.arange(team_blocks, dtype=jnp.int32)
    window = jnp.stack([blocks - 1, blocks, blocks + 1], axis=1)
    listed = jnp.concatenate(
        [window, jnp.broadcast_to(global_ids[None], (team_blocks, G)), randoms], axis=1
    )
    listed = jnp.clip(listed, 0, total_blocks - 1).reshape(-1)
    starts = listed // device_blocks * kv.shape[1] + listed % device_blocks * BLOCK_TOKENS
    pieces_out = []
    held = []
    sums = []
    for c in range(pieces):
        pieces_out.append(
            attend(
                listed,
                starts,
                first_block.reshape(1),
                member.reshape(1),
                drops,
                kv,
                qd[c],
                qd_begin if qd[c] is None else 0,
                sums[0] if sums else None,
                c,
                per,
                whole and c == pieces - 1,
                device_blocks,
                total_blocks,
                tokens,
                heads,
                c + 1 < pieces,
            )
        )
        sums = pieces_out[c][heads:]
        if c + 1 < pieces:
            early = 3 * heads // 4
            qd[c + 1], *results = lax.optimization_barrier((qd[c + 1], *pieces_out[c][1:early]))
            held.append([*results, *pieces_out[c][early:heads]])
    runs = shard_blocks // device_blocks
    begin = shard_tokens // pieces
    near = []
    for c, out in enumerate(pieces_out):
        if len(out) > 1:
            results = out[:heads]
            if c + 1 < pieces:
                results = [results[0], *held[c]]
            near.append(to_shards(results))
    att, dq = None, None
    if whole:
        rest = pieces_out[-1][0]
        if near:
            rest, *near[-1][heads // 2 :] = lax.optimization_barrier(
                (rest, *near[-1][heads // 2 :])
            )
        rest = lax.all_to_all(rest, "seq", split_axis=0, concat_axis=0, tiled=True)
    for c in range(len(near)):
        parts = [(0, rows, runs, pieces, c, att), (begin, rows, runs, pieces, c, dq)]
        att, dq = unpack(member.reshape(1), near[c], parts)
    if whole:
        c = pieces - 1
        parts = [(0, rows, runs, pieces, c, att), (begin, rows, runs, pieces, c, dq)]
        grads = [(2 * begin + n * shard_tokens, shard_tokens, 1, 1, 0, None) for n in range(2)]
        att, dq, dk, dv = unpack_all(rest, parts + grads)
    else:
        grads = lax.psum_scatter(
            sums[0], "seq", scatter_dimension=0, tiled=True, axis_index_groups=same_head
        ).reshape(heads, shard_tokens, 2, HEAD_WIDTH)
        grads = jnp.concatenate(
            [grads[:, :, 0] * HEAD_WIDTH ** (-0.5), grads[:, :, 1]], axis=1
        ).astype(jnp.bfloat16)
        grads = to_shards(
            [lax.dynamic_index_in_dim(grads, member ^ k, 0, keepdims=False) for k in range(heads)]
        )
        dk, dv = unpack(
            member.reshape(1),
            grads,
            [(n * shard_tokens, shard_tokens, 1, 1, 0, None) for n in range(2)],
        )
    return tuple(t.reshape(shard_tokens, heads * HEAD_WIDTH) for t in (att, dq, dk, dv))


def solution(mesh):
    return jax.shard_map(
        per_device,
        mesh=mesh,
        in_specs=(
            P(("seq", "head"), None),
            P(("seq", "head"), None),
            P(("seq", "head"), None),
            P(("seq", "head"), None),
            P("head", "seq", None),
            P(),
            P("head", "seq", None),
        ),
        out_specs=(P("seq", "head"), P("seq", "head"), P("seq", "head"), P("seq", "head")),
        check_vma=False,
    )
```

```python
import functools
import math

import jax
import jax.numpy as jnp
from jax import lax
from jax.experimental import pallas as pl
from jax.experimental.pallas import tpu as pltpu
from jax.sharding import PartitionSpec as P

HEAD_WIDTH = 128
BLOCK_TOKENS = 64
R = 3
G = 2
SLOTS = 3 + G + R
WIDE = SLOTS * BLOCK_TOKENS
UNROLL = 2
STRIP = 16
VMEM_LIMIT = 16 * 1024 * 1024
VMEM_BYTES = 64 * 1024 * 1024

keep_prob = 0.9

vmem = pl.BlockSpec(memory_space=pltpu.VMEM)
smem = pl.BlockSpec(memory_space=pltpu.SMEM)
anywhere = pl.BlockSpec(memory_space=pl.ANY)


def in_vmem(array):
    return pltpu.with_memory_space_constraint(array, pltpu.VMEM)


def in_hbm(array):
    return pltpu.with_memory_space_constraint(array, pltpu.HBM)


def copy_cost(size):
    return pl.CostEstimate(flops=0, bytes_accessed=4 * size, transcendentals=0)


def block_rows(number):
    start = number * BLOCK_TOKENS
    if not isinstance(number, int):
        start = pl.multiple_of(start, BLOCK_TOKENS)
    return pl.ds(start, BLOCK_TOKENS)


def pack_kernel(heads, groups, sources, table_rows, *refs):
    refs = list(refs)
    if table_rows:
        drop_ref, rand_ref, table = refs.pop(0), refs.pop(0), refs.pop()
    count = len(sources)
    arrays, out_ref = refs[:count], refs[count]
    wholes, packed, in_sems, out_sems = refs[count + 1 : -3], refs[-3], refs[-2], refs[-1]
    width = heads * HEAD_WIDTH
    loads = []
    for g in range(groups):
        for n, (at, rows) in enumerate(sources):
            columns = pl.ds(g * width, width)
            loads.append(
                pltpu.make_async_copy(
                    arrays[n].at[pl.ds(at * rows, rows), columns],
                    wholes[n].at[:, columns],
                    in_sems.at[g, n],
                )
            )
    for load in loads:
        load.start()
    begin = sum(rows for _, rows in sources)
    if table_rows:
        blocks = drop_ref.shape[1]
        table[...] = jnp.zeros_like(table)
        for m in range(heads):
            table[pl.ds(0, blocks), pl.ds(0, SLOTS)] = drop_ref[m].astype(jnp.float32)
            for r in range(R):
                table[pl.ds(blocks + r, 1), pl.ds(0, blocks)] = rand_ref[
                    r, pl.ds(m, 1), :
                ].astype(jnp.float32)
            rounded = table[...].astype(jnp.bfloat16)
            for g in range(groups):
                packed[m, g, pl.ds(begin, table_rows), :] = rounded
    stores = []
    for g in range(groups):
        for n in range(count):
            loads[g * count + n].wait()
        for m in range(heads):
            begin = 0
            for n, (_, rows) in enumerate(sources):
                packed[m, g, pl.ds(begin, rows), :] = wholes[n][
                    :, pl.ds((g * heads + m) * HEAD_WIDTH, HEAD_WIDTH)
                ]
                begin += rows
            stores.append(
                pltpu.make_async_copy(packed.at[m, g], out_ref.at[m, g], out_sems.at[g, m])
            )
            stores[-1].start()
    for store in stores:
        store.wait()


def pack(groups, heads, sources, tables=(), table_rows=0):
    total = sum(rows for _, _, rows in sources) + table_rows
    shape = (heads, groups, total, HEAD_WIDTH)
    scratch = [
        pltpu.VMEM((rows, groups * heads * HEAD_WIDTH), jnp.bfloat16) for _, _, rows in sources
    ] + [
        pltpu.VMEM(shape, jnp.bfloat16),
        pltpu.SemaphoreType.DMA((groups, len(sources))),
        pltpu.SemaphoreType.DMA((groups, heads)),
    ]
    if table_rows:
        scratch.append(pltpu.VMEM((table_rows, HEAD_WIDTH), jnp.float32))
    packed = pl.pallas_call(
        functools.partial(
            pack_kernel, heads, groups, tuple((at, rows) for _, at, rows in sources), table_rows
        ),
        out_shape=pltpu.HBM(shape, jnp.bfloat16),
        in_specs=[vmem] * len(tables) + [anywhere] * len(sources),
        out_specs=anywhere,
        scratch_shapes=scratch,
        compiler_params=pltpu.CompilerParams(vmem_limit_bytes=VMEM_LIMIT),
        cost_estimate=copy_cost(math.prod(shape)),
    )(*[in_hbm(t) for t in tables], *[in_hbm(a) for a, _, _ in sources])
    return packed.reshape(heads * groups, total, HEAD_WIDTH)


def unpack_kernel(parts, member_ref, *refs):
    outs = refs[len(refs) - len(parts) :]
    heads = outs[0].shape[-1] // HEAD_WIDTH
    for n in range(heads):
        k = (heads - n) % heads
        column = pl.multiple_of((member_ref[0] ^ k) * HEAD_WIDTH, HEAD_WIDTH)
        for begin, out in zip(parts, outs):
            runs, _, rows, _ = out.shape
            for i in range(runs):
                out[i, 0, :, pl.ds(column, HEAD_WIDTH)] = refs[n][pl.ds(begin + i * rows, rows), :]


def unpack(member, received, parts):
    heads = len(received)
    shapes, specs, olds, aliases, size = [], [], [], {}, 0
    for n, (_, rows, runs, pieces, piece, old) in enumerate(parts):
        shapes.append(
            jax.ShapeDtypeStruct((runs, pieces, rows, heads * HEAD_WIDTH), jnp.bfloat16)
        )
        specs.append(
            pl.BlockSpec(
                (runs, 1, rows, heads * HEAD_WIDTH),
                functools.partial(lambda piece, h: (0, piece, 0, 0), piece),
            )
        )
        size += rows * runs * heads * HEAD_WIDTH
        if old is not None:
            aliases[1 + heads + len(olds)] = n
            olds.append(old)
    return pl.pallas_call(
        functools.partial(unpack_kernel, tuple(part[0] for part in parts)),
        grid=(1,),
        out_shape=shapes,
        in_specs=[smem]
        + [pl.BlockSpec(received[0].shape, lambda h: (0, 0))] * heads
        + [pl.BlockSpec(memory_space=pl.ANY)] * len(olds),
        out_specs=specs,
        input_output_aliases=aliases,
        compiler_params=pltpu.CompilerParams(vmem_limit_bytes=VMEM_LIMIT),
        cost_estimate=copy_cost(size),
    )(member, received[0], *received[:0:-1], *olds)


def unpack_all_kernel(begins, step_heads, piece_ref, *refs):
    outs = refs[len(refs) - len(begins) :]
    for begin, out in zip(begins, outs):
        runs, _, rows, _ = out.shape
        for m in range(step_heads):
            for i in range(runs):
                out[i, 0, :, pl.ds(m * HEAD_WIDTH, HEAD_WIDTH)] = piece_ref[
                    m, pl.ds(begin + i * rows, rows), :
                ]


def unpack_all(received, parts):
    heads, total, _ = received.shape
    step_heads = 2 if heads % 2 == 0 else 1
    width = step_heads * HEAD_WIDTH
    shapes, out_specs, begins, olds, aliases = [], [], [], [], {}
    size = 0
    for n, (begin, rows, runs, pieces, piece, old) in enumerate(parts):
        begins.append(begin)
        shapes.append(
            jax.ShapeDtypeStruct((runs, pieces, rows, heads * HEAD_WIDTH), jnp.bfloat16)
        )
        out_specs.append(
            pl.BlockSpec(
                (runs, 1, rows, width), functools.partial(lambda piece, h: (0, piece, 0, h), piece)
            )
        )
        size += rows * runs * heads * HEAD_WIDTH
        if old is not None:
            aliases[1 + len(olds)] = n
            olds.append(old)
    return pl.pallas_call(
        functools.partial(unpack_all_kernel, begins, step_heads),
        grid=(heads // step_heads,),
        out_shape=shapes,
        in_specs=[pl.BlockSpec((step_heads, total, HEAD_WIDTH), lambda h: (h, 0, 0))]
        + [pl.BlockSpec(memory_space=pl.ANY)] * len(olds),
        out_specs=out_specs,
        input_output_aliases=aliases,
        compiler_params=pltpu.CompilerParams(vmem_limit_bytes=VMEM_LIMIT),
        cost_estimate=copy_cost(size),
    )(in_vmem(received), *olds)


def attention_kernel(
    last_block,
    device_blocks,
    per,
    piece,
    out_rows,
    source_rows,
    qd_rows,
    qd_begin,
    has_qd,
    has_start,
    joined,
    tokens,
    targets,
    ids_ref,
    starts_ref,
    first_ref,
    member_ref,
    drop_ref,
    kv_ref,
    *refs,
):
    refs = list(refs)
    qd_ref = refs.pop(0) if has_qd else kv_ref
    start_ref = refs.pop(0) if has_start else None
    out_refs = [refs.pop(0) for _ in range(1 if joined else targets)]
    acc, retain, waiting, near = refs[:4]
    done, sems = refs[4:6] if joined else (None, None)
    earlier, start_sem = refs[-2:] if has_start else (None, None)
    scale = HEAD_WIDTH ** (-0.5)
    steps = targets * (out_rows // BLOCK_TOKENS)
    slot_of_lane = lax.broadcasted_iota(jnp.int32, (SLOTS, WIDE), 1) // BLOCK_TOKENS
    slot_row = lax.broadcasted_iota(jnp.int32, (SLOTS, WIDE), 0)
    expand = (slot_of_lane == slot_row).astype(jnp.float32)
    retain[...] = jnp.dot(
        drop_ref[...].astype(jnp.float32), expand, preferred_element_type=jnp.float32
    ) * (1.0 / keep_prob)
    acc[...] = jnp.zeros_like(acc)
    if has_start:
        fetch = pltpu.make_async_copy(start_ref, earlier, start_sem)
        fetch.start()
    lane = lax.broadcasted_iota(jnp.int32, (1, WIDE), 1)
    nt = (((1,), (1,)), ((), ()))
    tn = (((0,), (0,)), ((), ()))
    out_steps = steps // targets

    def place(i):
        if per == 1:
            source, sub = i, 0
        else:
            source, sub = lax.div(i, per), lax.rem(i, per)
        return source, sub, source * device_blocks + piece * per + sub

    def load(i):
        source, sub, j = place(i)
        starts = [starts_ref[j * SLOTS + s] for s in range(SLOTS)]
        q, do = [
            qd_ref[
                pl.ds(
                    pl.multiple_of(
                        source * qd_rows + (n * per + sub) * BLOCK_TOKENS + qd_begin, 16
                    ),
                    BLOCK_TOKENS,
                ),
                :,
            ]
            for n in range(2)
        ]
        keys, vals = [
            jnp.concatenate(
                [kv_ref[pl.ds(pl.multiple_of(r + n * tokens, 16), BLOCK_TOKENS), :] for r in starts],
                axis=0,
            )
            for n in range(2)
        ]
        return q, do, keys, vals

    def score(i):
        q, do, keys, vals = load(i)
        logits = lax.dot_general(q, keys, nt, preferred_element_type=jnp.float32)
        raw = lax.dot_general(do, vals, nt, preferred_element_type=jnp.float32)
        return logits, raw

    def factor(i, u, logits, raw):
        j = place(i)[2]
        block_id = first_ref[0] + j
        absent = ((block_id == 0) & (lane < BLOCK_TOKENS)) | (
            (block_id == last_block) & (lane >= 2 * BLOCK_TOKENS) & (lane < 3 * BLOCK_TOKENS)
        )
        keep = retain[pl.ds(j, 1), :]
        for r in range(0, BLOCK_TOKENS, STRIP):
            part = jnp.where(absent, -jnp.inf, logits[r : r + STRIP])
            top = jnp.max(part, axis=-1, keepdims=True)
            expd = jnp.exp2((part - top) * (scale / math.log(2.0)))
            probs = expd * (1.0 / jnp.sum(expd, axis=-1, keepdims=True))
            kept = probs * keep
            weighted = kept * raw[r : r + STRIP]
            delta = jnp.sum(weighted, axis=-1, keepdims=True)
            waiting[u, pl.ds(r, STRIP), :] = (weighted - probs * delta).astype(jnp.bfloat16)
            waiting[u, pl.ds(BLOCK_TOKENS + r, STRIP), :] = kept.astype(jnp.bfloat16)

    def finish(i, u):
        j = place(i)[2]
        q, do, keys, vals = load(i)
        factors = waiting[u]
        dq = jnp.dot(factors[:BLOCK_TOKENS], keys, preferred_element_type=jnp.float32) * scale
        att = jnp.dot(factors[BLOCK_TOKENS:], vals, preferred_element_type=jnp.float32)
        none = jnp.zeros_like(q)
        pair = jnp.concatenate(
            [jnp.concatenate([q, none], axis=1), jnp.concatenate([none, do], axis=1)], axis=0
        )
        terms = lax.dot_general(factors, pair, tn, preferred_element_type=jnp.float32)
        for s in range(SLOTS):
            acc[block_rows(ids_ref[j * SLOTS + s]), :] += terms[
                s * BLOCK_TOKENS : (s + 1) * BLOCK_TOKENS
            ]
        target, pos = lax.div(i, out_steps), lax.rem(i, out_steps)
        near[target, block_rows(pos), :] = att.astype(jnp.bfloat16)
        near[target, block_rows(out_steps + pos), :] = dq.astype(jnp.bfloat16)

    def step(t, carry):
        scores = [score(t * UNROLL + u) for u in range(UNROLL)]
        for u in range(UNROLL):
            finish((t - 1) * UNROLL + u, u)
        for u in range(UNROLL):
            factor(t * UNROLL + u, u, *scores[u])
        return carry

    for u in range(UNROLL):
        factor(u, u, *score(u))
    lax.fori_loop(1, steps // UNROLL, step, 0)
    for u in range(UNROLL):
        finish(steps - UNROLL + u, u)
    if has_start:
        fetch.wait()
    if joined:
        rows = acc.shape[0] // targets
        stores = []
        for target in range(targets):
            part = pl.ds(target * rows, rows)
            sums = acc[part, :]
            if has_start:
                sums += earlier[part, :]
            done[target, pl.ds(0, 2 * out_rows), :] = near[target]
            done[target, pl.ds(2 * out_rows, rows), :] = (sums[:, :HEAD_WIDTH] * scale).astype(
                jnp.bfloat16
            )
            done[target, pl.ds(2 * out_rows + rows, rows), :] = sums[:, HEAD_WIDTH:].astype(
                jnp.bfloat16
            )
            stores.append(
                pltpu.make_async_copy(done.at[target], out_refs[0].at[target], sems.at[target])
            )
            stores[-1].start()
        for store in stores:
            store.wait()
    else:
        for k, out_ref in enumerate(out_refs):
            out_ref[...] = near[member_ref[0] ^ k]


def attend(
    ids, starts, first_block, member, drop, kv, qd, qd_begin, start, piece, per, joined, device_blocks, total_blocks, tokens, targets
):
    team_blocks = drop.shape[0]
    source = kv if qd is None else qd
    steps = team_blocks * per // device_blocks
    length = total_blocks * BLOCK_TOKENS
    pairs = steps * BLOCK_TOKENS * WIDE
    accumulator = (length, 2 * HEAD_WIDTH)
    out_rows = steps * BLOCK_TOKENS // targets
    if joined:
        out_shape = [
            pltpu.HBM((targets, 2 * out_rows + 2 * length // targets, HEAD_WIDTH), jnp.bfloat16)
        ]
    else:
        out_shape = [pltpu.HBM((2 * out_rows, HEAD_WIDTH), jnp.bfloat16)] * targets
    scratch = [
        pltpu.VMEM((team_blocks, WIDE), jnp.float32),
        pltpu.VMEM((UNROLL, 2 * BLOCK_TOKENS, WIDE), jnp.bfloat16),
        pltpu.VMEM((targets, 2 * out_rows, HEAD_WIDTH), jnp.bfloat16),
    ]
    if joined:
        scratch = [pltpu.VMEM(accumulator, jnp.float32)] + scratch
    else:
        out_shape.append(pltpu.HBM(accumulator, jnp.float32))
    if joined:
        scratch += [
            pltpu.VMEM(out_shape[0].shape, jnp.bfloat16),
            pltpu.SemaphoreType.DMA((targets,)),
        ]
    sums_bytes = 8 * length * HEAD_WIDTH
    limit = VMEM_LIMIT + 2 * (kv.size + source.size) + (1 if start is None else 2) * sums_bytes
    keep = in_vmem if 2 * limit < VMEM_BYTES else lambda t: t
    flat = [keep(t.reshape(-1, HEAD_WIDTH)) for t in (kv, qd) if t is not None]
    if start is not None:
        scratch += [pltpu.VMEM(accumulator, jnp.float32), pltpu.SemaphoreType.DMA]
    operands = flat + ([] if start is None else [in_hbm(start)])
    operand_specs = [vmem] * len(flat) + [anywhere] * (start is not None)
    return pl.pallas_call(
        functools.partial(
            attention_kernel,
            total_blocks - 1,
            device_blocks,
            per,
            piece,
            out_rows,
            kv.shape[1],
            source.shape[1],
            qd_begin,
            qd is not None,
            start is not None,
            joined,
            tokens,
            targets,
        ),
        out_shape=out_shape,
        in_specs=[smem, smem, smem, smem, vmem] + operand_specs,
        out_specs=[anywhere] if joined else [vmem] * len(out_shape),
        scratch_shapes=scratch,
        compiler_params=pltpu.CompilerParams(vmem_limit_bytes=limit),
        cost_estimate=pl.CostEstimate(
            flops=128 * pairs * HEAD_WIDTH,
            bytes_accessed=2 * (source.size + kv.size) + 8 * length * HEAD_WIDTH,
            transcendentals=pairs,
        ),
    )(ids, starts, first_block, member, in_hbm(drop), *operands)


def per_device(queries, keys, values, grad_out, rand_blocks, global_ids, drop_mask):
    shards = lax.axis_size("seq")
    groups = lax.axis_size("head")
    shard = lax.axis_index("seq")
    heads, shard_blocks, _ = rand_blocks.shape
    tokens = queries.shape[0]
    device_blocks = tokens // BLOCK_TOKENS
    shard_tokens = shard_blocks * BLOCK_TOKENS
    teams = shards // heads
    team, member = lax.div(shard, heads), lax.rem(shard, heads)
    team_blocks = heads * shard_blocks
    total_blocks = shards * shard_blocks
    first_block = team * team_blocks
    whole = teams == 1
    pieces = device_blocks if whole else 1
    per = device_blocks // pieces
    rows = tokens // pieces
    same_team_all = (
        None
        if whole
        else [
            [(t * heads + m) * groups + g for m in range(heads) for g in range(groups)]
            for t in range(teams)
        ]
    )
    same_head = [[t * heads + m for t in range(teams)] for m in range(heads)]

    def to_heads(packed):
        return lax.all_to_all(
            packed,
            ("seq", "head"),
            split_axis=0,
            concat_axis=0,
            tiled=True,
            axis_index_groups=same_team_all,
        )

    def to_shards(results):
        received = list(results)
        for k in reversed(range(1, heads)):
            pairs = [(s, s ^ k) for s in range(shards)]
            received[k] = lax.ppermute(results[k], "seq", pairs)
        return received

    table_rows = -(-(shard_blocks + R) // 16) * 16
    sources = [[(queries, c, rows), (grad_out, c, rows)] for c in range(pieces)]
    qd_begin = 2 * tokens
    table_begin = qd_begin + 2 * rows
    kv = to_heads(
        pack(
            groups,
            heads,
            [(keys, 0, tokens), (values, 0, tokens)] + sources[0],
            (drop_mask, rand_blocks.transpose(2, 0, 1)),
            table_rows,
        )
    )
    later = [to_heads(pack(groups, heads, each)) for each in sources[1:]]
    tables = lax.dynamic_index_in_dim(
        kv.reshape(heads, groups, -1, HEAD_WIDTH)[:, :, table_begin:],
        lax.axis_index("head"),
        axis=1,
        keepdims=False,
    ).astype(jnp.int32)
    drops = tables[:, :shard_blocks, :SLOTS].reshape(team_blocks, SLOTS)
    randoms = tables[:, shard_blocks : shard_blocks + R, :shard_blocks].transpose(0, 2, 1)
    randoms = randoms.reshape(team_blocks, R)
    qd = [None] + later
    if not whole:
        qd[0] = kv[:, qd_begin:table_begin]
        kv = lax.all_gather(kv[:, : 2 * tokens], "seq", axis=0, tiled=True, axis_index_groups=same_head)
    blocks = first_block + jnp.arange(team_blocks, dtype=jnp.int32)
    window = jnp.stack([blocks - 1, blocks, blocks + 1], axis=1)
    listed = jnp.concatenate(
        [window, jnp.broadcast_to(global_ids[None], (team_blocks, G)), randoms], axis=1
    )
    listed = jnp.clip(listed, 0, total_blocks - 1).reshape(-1)
    starts = listed // device_blocks * kv.shape[1] + listed % device_blocks * BLOCK_TOKENS
    pieces_out = []
    held = []
    sums = []
    for c in range(pieces):
        pieces_out.append(
            attend(
                listed,
                starts,
                first_block.reshape(1),
                member.reshape(1),
                drops,
                kv,
                qd[c],
                qd_begin if qd[c] is None else 0,
                sums[0] if sums else None,
                c,
                per,
                whole and c == pieces - 1,
                device_blocks,
                total_blocks,
                tokens,
                heads,
            )
        )
        sums = pieces_out[c][heads:]
        if c + 1 < pieces:
            late = 3 * heads // 4
            qd[c + 1], *results = lax.optimization_barrier((qd[c + 1], *pieces_out[c][late:heads]))
            held.append([*pieces_out[c][1:late], *results])
    runs = shard_blocks // device_blocks
    begin = shard_tokens // pieces
    near = []
    for c, out in enumerate(pieces_out):
        if len(out) > 1:
            results = out[:heads]
            if c + 1 < pieces:
                results = [results[0], *held[c]]
            near.append(to_shards(results))
    att, dq = None, None
    if whole:
        rest = pieces_out[-1][0]
        if near:
            rest, *near[-1][heads // 2 :] = lax.optimization_barrier(
                (rest, *near[-1][heads // 2 :])
            )
        rest = lax.all_to_all(rest, "seq", split_axis=0, concat_axis=0, tiled=True)
    for c in range(len(near)):
        parts = [(0, rows, runs, pieces, c, att), (begin, rows, runs, pieces, c, dq)]
        att, dq = unpack(member.reshape(1), near[c], parts)
    if whole:
        c = pieces - 1
        parts = [(0, rows, runs, pieces, c, att), (begin, rows, runs, pieces, c, dq)]
        grads = [(2 * begin + n * shard_tokens, shard_tokens, 1, 1, 0, None) for n in range(2)]
        att, dq, dk, dv = unpack_all(rest, parts + grads)
    else:
        grads = lax.psum_scatter(
            sums[0], "seq", scatter_dimension=0, tiled=True, axis_index_groups=same_head
        ).reshape(heads, shard_tokens, 2, HEAD_WIDTH)
        grads = jnp.concatenate(
            [grads[:, :, 0] * HEAD_WIDTH ** (-0.5), grads[:, :, 1]], axis=1
        ).astype(jnp.bfloat16)
        grads = to_shards(
            [lax.dynamic_index_in_dim(grads, member ^ k, 0, keepdims=False) for k in range(heads)]
        )
        dk, dv = unpack(
            member.reshape(1),
            grads,
            [(n * shard_tokens, shard_tokens, 1, 1, 0, None) for n in range(2)],
        )
    return tuple(t.reshape(shard_tokens, heads * HEAD_WIDTH) for t in (att, dq, dk, dv))


def solution(mesh):
    return jax.shard_map(
        per_device,
        mesh=mesh,
        in_specs=(
            P(("seq", "head"), None),
            P(("seq", "head"), None),
            P(("seq", "head"), None),
            P(("seq", "head"), None),
            P("head", "seq", None),
            P(),
            P("head", "seq", None),
        ),
        out_specs=(P("seq", "head"), P("seq", "head"), P("seq", "head"), P("seq", "head")),
        check_vma=False,
    )
```

```python
import functools
import math

import jax
import jax.numpy as jnp
from jax import lax
from jax.experimental import pallas as pl
from jax.experimental.pallas import tpu as pltpu
from jax.sharding import PartitionSpec as P

HEAD_WIDTH = 128
BLOCK_TOKENS = 64
R = 3
G = 2
SLOTS = 3 + G + R
WIDE = SLOTS * BLOCK_TOKENS
UNROLL = 2
STRIP = 16
VMEM_LIMIT = 16 * 1024 * 1024
VMEM_BYTES = 64 * 1024 * 1024

keep_prob = 0.9

vmem = pl.BlockSpec(memory_space=pltpu.VMEM)
smem = pl.BlockSpec(memory_space=pltpu.SMEM)
anywhere = pl.BlockSpec(memory_space=pl.ANY)


def in_vmem(array):
    return pltpu.with_memory_space_constraint(array, pltpu.VMEM)


def in_hbm(array):
    return pltpu.with_memory_space_constraint(array, pltpu.HBM)


def copy_cost(size):
    return pl.CostEstimate(flops=0, bytes_accessed=4 * size, transcendentals=0)


def block_rows(number):
    start = number * BLOCK_TOKENS
    if not isinstance(number, int):
        start = pl.multiple_of(start, BLOCK_TOKENS)
    return pl.ds(start, BLOCK_TOKENS)


def pack_kernel(heads, groups, sources, table_rows, *refs):
    refs = list(refs)
    if table_rows:
        drop_ref, rand_ref, table = refs.pop(0), refs.pop(0), refs.pop()
    count = len(sources)
    arrays, out_ref = refs[:count], refs[count]
    wholes, packed, in_sems, out_sems = refs[count + 1 : -3], refs[-3], refs[-2], refs[-1]
    width = heads * HEAD_WIDTH
    loads = []
    for g in range(groups):
        for n, (at, rows) in enumerate(sources):
            columns = pl.ds(g * width, width)
            loads.append(
                pltpu.make_async_copy(
                    arrays[n].at[pl.ds(at * rows, rows), columns],
                    wholes[n].at[:, columns],
                    in_sems.at[g, n],
                )
            )
    for load in loads:
        load.start()
    begin = sum(rows for _, rows in sources)
    if table_rows:
        blocks = drop_ref.shape[1]
        table[...] = jnp.zeros_like(table)
        for m in range(heads):
            table[pl.ds(0, blocks), pl.ds(0, SLOTS)] = drop_ref[m].astype(jnp.float32)
            for r in range(R):
                table[pl.ds(blocks + r, 1), pl.ds(0, blocks)] = rand_ref[
                    r, pl.ds(m, 1), :
                ].astype(jnp.float32)
            rounded = table[...].astype(jnp.bfloat16)
            for g in range(groups):
                packed[m, g, pl.ds(begin, table_rows), :] = rounded
    stores = []
    for g in range(groups):
        for n in range(count):
            loads[g * count + n].wait()
        for m in range(heads):
            begin = 0
            for n, (_, rows) in enumerate(sources):
                packed[m, g, pl.ds(begin, rows), :] = wholes[n][
                    :, pl.ds((g * heads + m) * HEAD_WIDTH, HEAD_WIDTH)
                ]
                begin += rows
            stores.append(
                pltpu.make_async_copy(packed.at[m, g], out_ref.at[m, g], out_sems.at[g, m])
            )
            stores[-1].start()
    for store in stores:
        store.wait()


def pack(groups, heads, sources, tables=(), table_rows=0):
    total = sum(rows for _, _, rows in sources) + table_rows
    shape = (heads, groups, total, HEAD_WIDTH)
    scratch = [
        pltpu.VMEM((rows, groups * heads * HEAD_WIDTH), jnp.bfloat16) for _, _, rows in sources
    ] + [
        pltpu.VMEM(shape, jnp.bfloat16),
        pltpu.SemaphoreType.DMA((groups, len(sources))),
        pltpu.SemaphoreType.DMA((groups, heads)),
    ]
    if table_rows:
        scratch.append(pltpu.VMEM((table_rows, HEAD_WIDTH), jnp.float32))
    packed = pl.pallas_call(
        functools.partial(
            pack_kernel, heads, groups, tuple((at, rows) for _, at, rows in sources), table_rows
        ),
        out_shape=pltpu.HBM(shape, jnp.bfloat16),
        in_specs=[vmem] * len(tables) + [anywhere] * len(sources),
        out_specs=anywhere,
        scratch_shapes=scratch,
        compiler_params=pltpu.CompilerParams(vmem_limit_bytes=VMEM_LIMIT),
        cost_estimate=copy_cost(math.prod(shape)),
    )(*[in_hbm(t) for t in tables], *[in_hbm(a) for a, _, _ in sources])
    return packed.reshape(heads * groups, total, HEAD_WIDTH)


def unpack_kernel(half, groups, copies, count, member_ref, *refs):
    refs = list(refs)
    inputs = [[refs.pop(0) for _ in range(size)] for _, size, _ in groups]
    sems = refs.pop()
    stages = refs[len(refs) - copies :]
    outs = refs[len(refs) - copies - count : len(refs) - copies]
    local = lax.rem(member_ref[0], half)
    own_half = member_ref[0] - local
    stores = []
    at = 0
    for (far, _, parts), arrays in zip(groups, inputs):
        first = own_half ^ half if far else own_half
        columns = pl.ds(pl.multiple_of(first * HEAD_WIDTH, HEAD_WIDTH), half * HEAD_WIDTH)
        for begin, rows, runs, piece, n in parts:
            for i in range(runs):
                stage = stages[at]
                source = pl.ds(begin + i * rows, rows)
                for j in range(half):
                    if far:
                        column = pl.multiple_of((local ^ j) * HEAD_WIDTH, HEAD_WIDTH)
                        stage[:, pl.ds(column, HEAD_WIDTH)] = arrays[j][source, :]
                    else:
                        stage[:, pl.ds(j * HEAD_WIDTH, HEAD_WIDTH)] = arrays[0][j, source, :]
                stores.append(
                    pltpu.make_async_copy(stage, outs[n].at[i, piece, :, columns], sems.at[at])
                )
                stores[-1].start()
                at += 1
    for store in stores:
        store.wait()


def unpack(member, groups, shapes, olds=()):
    half = groups[0][1][0].shape[0] if not groups[0][0] else len(groups[0][1])
    arrays = [t for _, each, _ in groups for t in each]
    stages = [
        pltpu.VMEM((rows, half * HEAD_WIDTH), jnp.bfloat16)
        for _, _, parts in groups
        for _, rows, runs, _, _ in parts
        for _ in range(runs)
    ]
    size = sum(math.prod(stage.shape) for stage in stages)
    return pl.pallas_call(
        functools.partial(
            unpack_kernel,
            half,
            tuple((far, len(each), tuple(parts)) for far, each, parts in groups),
            len(stages),
            len(shapes),
        ),
        out_shape=[pltpu.HBM(shape, jnp.bfloat16) for shape in shapes],
        in_specs=[smem] + [vmem] * len(arrays) + [anywhere] * len(olds),
        out_specs=[anywhere] * len(shapes),
        input_output_aliases={1 + len(arrays) + n: n for n in range(len(olds))},
        scratch_shapes=stages + [pltpu.SemaphoreType.DMA((len(stages),))],
        compiler_params=pltpu.CompilerParams(vmem_limit_bytes=VMEM_LIMIT),
        cost_estimate=copy_cost(size),
    )(member, *[in_vmem(t) for t in arrays], *olds)


def attention_kernel(
    last_block,
    device_blocks,
    per,
    piece,
    out_rows,
    source_rows,
    qd_rows,
    qd_begin,
    has_qd,
    has_start,
    joined,
    tokens,
    targets,
    ids_ref,
    starts_ref,
    first_ref,
    member_ref,
    drop_ref,
    kv_ref,
    *refs,
):
    refs = list(refs)
    qd_ref = refs.pop(0) if has_qd else kv_ref
    start_ref, near_start = (refs.pop(0), refs.pop(0)) if has_start else (None, None)
    half = targets // 2
    far_refs = [refs.pop(0) for _ in range(half)]
    near_ref = refs.pop(0)
    acc, retain, waiting, near = refs[:4]
    if joined:
        far_done, near_done, sems, earlier, start_sems = refs[4:]
    scale = HEAD_WIDTH ** (-0.5)
    steps = targets * (out_rows // BLOCK_TOKENS)
    slot_of_lane = lax.broadcasted_iota(jnp.int32, (SLOTS, WIDE), 1) // BLOCK_TOKENS
    slot_row = lax.broadcasted_iota(jnp.int32, (SLOTS, WIDE), 0)
    expand = (slot_of_lane == slot_row).astype(jnp.float32)
    retain[...] = jnp.dot(
        drop_ref[...].astype(jnp.float32), expand, preferred_element_type=jnp.float32
    ) * (1.0 / keep_prob)
    acc[...] = jnp.zeros_like(acc)
    if has_start:
        early_rows = near_start.shape[1]
        fetches = [pltpu.make_async_copy(start_ref, earlier, start_sems.at[0])] + [
            pltpu.make_async_copy(
                near_start.at[j], near_done.at[j, pl.ds(0, early_rows), :], start_sems.at[1 + j]
            )
            for j in range(half)
        ]
        for fetch in fetches:
            fetch.start()
    lane = lax.broadcasted_iota(jnp.int32, (1, WIDE), 1)
    nt = (((1,), (1,)), ((), ()))
    tn = (((0,), (0,)), ((), ()))
    out_steps = steps // targets

    def place(i):
        if per == 1:
            source, sub = i, 0
        else:
            source, sub = lax.div(i, per), lax.rem(i, per)
        return source, sub, source * device_blocks + piece * per + sub

    def load(i):
        source, sub, j = place(i)
        starts = [starts_ref[j * SLOTS + s] for s in range(SLOTS)]
        q, do = [
            qd_ref[
                pl.ds(
                    pl.multiple_of(
                        source * qd_rows + (n * per + sub) * BLOCK_TOKENS + qd_begin, 16
                    ),
                    BLOCK_TOKENS,
                ),
                :,
            ]
            for n in range(2)
        ]
        keys, vals = [
            jnp.concatenate(
                [kv_ref[pl.ds(pl.multiple_of(r + n * tokens, 16), BLOCK_TOKENS), :] for r in starts],
                axis=0,
            )
            for n in range(2)
        ]
        return q, do, keys, vals

    def score(i):
        q, do, keys, vals = load(i)
        logits = lax.dot_general(q, keys, nt, preferred_element_type=jnp.float32)
        raw = lax.dot_general(do, vals, nt, preferred_element_type=jnp.float32)
        return logits, raw

    def factor(i, u, logits, raw):
        j = place(i)[2]
        block_id = first_ref[0] + j
        absent = ((block_id == 0) & (lane < BLOCK_TOKENS)) | (
            (block_id == last_block) & (lane >= 2 * BLOCK_TOKENS) & (lane < 3 * BLOCK_TOKENS)
        )
        keep = retain[pl.ds(j, 1), :]
        for r in range(0, BLOCK_TOKENS, STRIP):
            part = jnp.where(absent, -jnp.inf, logits[r : r + STRIP])
            top = jnp.max(part, axis=-1, keepdims=True)
            expd = jnp.exp2((part - top) * (scale / math.log(2.0)))
            probs = expd * (1.0 / jnp.sum(expd, axis=-1, keepdims=True))
            kept = probs * keep
            weighted = kept * raw[r : r + STRIP]
            delta = jnp.sum(weighted, axis=-1, keepdims=True)
            waiting[u, pl.ds(r, STRIP), :] = (weighted - probs * delta).astype(jnp.bfloat16)
            waiting[u, pl.ds(BLOCK_TOKENS + r, STRIP), :] = kept.astype(jnp.bfloat16)

    def finish(i, u):
        j = place(i)[2]
        q, do, keys, vals = load(i)
        factors = waiting[u]
        dq = jnp.dot(factors[:BLOCK_TOKENS], keys, preferred_element_type=jnp.float32) * scale
        att = jnp.dot(factors[BLOCK_TOKENS:], vals, preferred_element_type=jnp.float32)
        none = jnp.zeros_like(q)
        pair = jnp.concatenate(
            [jnp.concatenate([q, none], axis=1), jnp.concatenate([none, do], axis=1)], axis=0
        )
        terms = lax.dot_general(factors, pair, tn, preferred_element_type=jnp.float32)
        for s in range(SLOTS):
            acc[block_rows(ids_ref[j * SLOTS + s]), :] += terms[
                s * BLOCK_TOKENS : (s + 1) * BLOCK_TOKENS
            ]
        target, pos = lax.div(i, out_steps), lax.rem(i, out_steps)
        near[target, block_rows(pos), :] = att.astype(jnp.bfloat16)
        near[target, block_rows(out_steps + pos), :] = dq.astype(jnp.bfloat16)

    def step(t, carry):
        scores = [score(t * UNROLL + u) for u in range(UNROLL)]
        for u in range(UNROLL):
            finish((t - 1) * UNROLL + u, u)
        for u in range(UNROLL):
            factor(t * UNROLL + u, u, *scores[u])
        return carry

    for u in range(UNROLL):
        factor(u, u, *score(u))
    lax.fori_loop(1, steps // UNROLL, step, 0)
    for u in range(UNROLL):
        finish(steps - UNROLL + u, u)
    local = lax.rem(member_ref[0], half)
    own_half = member_ref[0] - local

    def put(target, ref, begin, done):
        ref[pl.ds(begin, 2 * out_rows), :] = near[target]
        if done:
            rows = acc.shape[0] // targets
            part = pl.ds(pl.multiple_of(target * rows, rows), rows)
            sums = acc[part, :] + earlier[part, :]
            begin += 2 * out_rows
            ref[pl.ds(begin, rows), :] = (sums[:, :HEAD_WIDTH] * scale).astype(jnp.bfloat16)
            ref[pl.ds(begin + rows, rows), :] = sums[:, HEAD_WIDTH:].astype(jnp.bfloat16)

    if joined:
        for fetch in fetches:
            fetch.wait()
        stores = []
        for j in range(half):
            put(member_ref[0] ^ (half + j), far_done.at[j], 0, True)
            stores.append(pltpu.make_async_copy(far_done.at[j], far_refs[j], sems.at[j]))
            stores[-1].start()
        for j in range(half):
            put(own_half + j, near_done.at[j], early_rows, True)
            stores.append(
                pltpu.make_async_copy(near_done.at[j], near_ref.at[j], sems.at[half + j])
            )
            stores[-1].start()
        for store in stores:
            store.wait()
    else:
        for j in range(half):
            put(member_ref[0] ^ (half + j), far_refs[j], 0, False)
            put(own_half + j, near_ref.at[j], 0, False)


def attend(
    ids, starts, first_block, member, drop, kv, qd, qd_begin, start, near_start, piece, per, joined, device_blocks, total_blocks, tokens, targets
):
    team_blocks = drop.shape[0]
    source = kv if qd is None else qd
    steps = team_blocks * per // device_blocks
    length = total_blocks * BLOCK_TOKENS
    pairs = steps * BLOCK_TOKENS * WIDE
    accumulator = (length, 2 * HEAD_WIDTH)
    out_rows = steps * BLOCK_TOKENS // targets
    half = targets // 2
    far_rows = 2 * out_rows + (2 * length // targets if joined else 0)
    near_rows = far_rows + (near_start.shape[1] if joined else 0)
    out_shape = [pltpu.HBM((far_rows, HEAD_WIDTH), jnp.bfloat16)] * half + [
        pltpu.HBM((half, near_rows, HEAD_WIDTH), jnp.bfloat16)
    ]
    scratch = [
        pltpu.VMEM((team_blocks, WIDE), jnp.float32),
        pltpu.VMEM((UNROLL, 2 * BLOCK_TOKENS, WIDE), jnp.bfloat16),
        pltpu.VMEM((targets, 2 * out_rows, HEAD_WIDTH), jnp.bfloat16),
    ]
    if joined:
        scratch = [pltpu.VMEM(accumulator, jnp.float32)] + scratch
    else:
        out_shape.append(pltpu.HBM(accumulator, jnp.float32))
    if joined:
        scratch += [
            pltpu.VMEM((half, far_rows, HEAD_WIDTH), jnp.bfloat16),
            pltpu.VMEM((half, near_rows, HEAD_WIDTH), jnp.bfloat16),
            pltpu.SemaphoreType.DMA((targets,)),
            pltpu.VMEM(accumulator, jnp.float32),
            pltpu.SemaphoreType.DMA((1 + half,)),
        ]
    sums_bytes = 8 * length * HEAD_WIDTH
    limit = VMEM_LIMIT + 2 * (kv.size + source.size) + (2 if joined else 1) * sums_bytes
    keep = in_vmem if 2 * limit < VMEM_BYTES else lambda t: t
    flat = [keep(t.reshape(-1, HEAD_WIDTH)) for t in (kv, qd) if t is not None]
    operands = flat + ([in_hbm(start), in_hbm(near_start)] if joined else [])
    operand_specs = [vmem] * len(flat) + [anywhere] * (len(operands) - len(flat))
    return pl.pallas_call(
        functools.partial(
            attention_kernel,
            total_blocks - 1,
            device_blocks,
            per,
            piece,
            out_rows,
            kv.shape[1],
            source.shape[1],
            qd_begin,
            qd is not None,
            start is not None,
            joined,
            tokens,
            targets,
        ),
        out_shape=out_shape,
        in_specs=[smem, smem, smem, smem, vmem] + operand_specs,
        out_specs=[anywhere if joined else vmem] * len(out_shape),
        scratch_shapes=scratch,
        compiler_params=pltpu.CompilerParams(vmem_limit_bytes=limit),
        cost_estimate=pl.CostEstimate(
            flops=128 * pairs * HEAD_WIDTH,
            bytes_accessed=2 * (source.size + kv.size) + 8 * length * HEAD_WIDTH,
            transcendentals=pairs,
        ),
    )(ids, starts, first_block, member, in_hbm(drop), *operands)


def per_device(queries, keys, values, grad_out, rand_blocks, global_ids, drop_mask):
    shards = lax.axis_size("seq")
    groups = lax.axis_size("head")
    shard = lax.axis_index("seq")
    heads, shard_blocks, _ = rand_blocks.shape
    tokens = queries.shape[0]
    device_blocks = tokens // BLOCK_TOKENS
    shard_tokens = shard_blocks * BLOCK_TOKENS
    teams = shards // heads
    team, member = lax.div(shard, heads), lax.rem(shard, heads)
    team_blocks = heads * shard_blocks
    total_blocks = shards * shard_blocks
    first_block = team * team_blocks
    whole = teams == 1
    pieces = 2 if whole and device_blocks == 2 else 1
    half = heads // 2
    per = device_blocks // pieces
    rows = tokens // pieces
    same_team_all = (
        None
        if whole
        else [
            [(t * heads + m) * groups + g for m in range(heads) for g in range(groups)]
            for t in range(teams)
        ]
    )
    same_head = [[t * heads + m for t in range(teams)] for m in range(heads)]

    def to_heads(packed):
        return lax.all_to_all(
            packed,
            ("seq", "head"),
            split_axis=0,
            concat_axis=0,
            tiled=True,
            axis_index_groups=same_team_all,
        )

    def exchange_far(results):
        return [
            lax.ppermute(t, "seq", [(s, s ^ (half + j)) for s in range(shards)])
            for j, t in enumerate(results)
        ]

    def exchange_near(results):
        return lax.all_to_all(
            results,
            "seq",
            split_axis=0,
            concat_axis=0,
            tiled=True,
            axis_index_groups=[list(range(s, s + half)) for s in range(0, shards, half)],
        )

    table_rows = -(-(shard_blocks + R) // 16) * 16
    sources = [[(queries, c, rows), (grad_out, c, rows)] for c in range(pieces)]
    qd_begin = 2 * tokens
    table_begin = qd_begin + 2 * rows
    kv = to_heads(
        pack(
            groups,
            heads,
            [(keys, 0, tokens), (values, 0, tokens)] + sources[0],
            (drop_mask, rand_blocks.transpose(2, 0, 1)),
            table_rows,
        )
    )
    later = [to_heads(pack(groups, heads, each)) for each in sources[1:]]
    tables = lax.dynamic_index_in_dim(
        kv.reshape(heads, groups, -1, HEAD_WIDTH)[:, :, table_begin:],
        lax.axis_index("head"),
        axis=1,
        keepdims=False,
    ).astype(jnp.int32)
    drops = tables[:, :shard_blocks, :SLOTS].reshape(team_blocks, SLOTS)
    randoms = tables[:, shard_blocks : shard_blocks + R, :shard_blocks].transpose(0, 2, 1)
    randoms = randoms.reshape(team_blocks, R)
    qd = [None] + later
    if not whole:
        qd[0] = kv[:, qd_begin:table_begin]
        kv = lax.all_gather(kv[:, : 2 * tokens], "seq", axis=0, tiled=True, axis_index_groups=same_head)
    blocks = first_block + jnp.arange(team_blocks, dtype=jnp.int32)
    window = jnp.stack([blocks - 1, blocks, blocks + 1], axis=1)
    listed = jnp.concatenate(
        [window, jnp.broadcast_to(global_ids[None], (team_blocks, G)), randoms], axis=1
    )
    listed = jnp.clip(listed, 0, total_blocks - 1).reshape(-1)
    starts = listed // device_blocks * kv.shape[1] + listed % device_blocks * BLOCK_TOKENS
    member = member.reshape(1)

    def run(c, start=None, near_start=None):
        out = attend(
            listed,
            starts,
            first_block.reshape(1),
            member,
            drops,
            kv,
            qd[c],
            qd_begin if qd[c] is None else 0,
            start,
            near_start,
            c,
            per,
            start is not None,
            device_blocks,
            total_blocks,
            tokens,
            heads,
        )
        return list(out[:half]), *out[half:]

    runs = shard_blocks // device_blocks
    begin = shard_tokens // pieces
    shapes = [(runs, pieces, rows, heads * HEAD_WIDTH)] * 2 + [
        (1, 1, shard_tokens, heads * HEAD_WIDTH)
    ] * 2

    def results_at(first, c):
        return [(first + n * begin, rows, runs, c, n) for n in range(2)]

    def grads_at(first, n=2):
        return [(first + i * shard_tokens, shard_tokens, 1, 0, n + i) for i in range(2)]

    far, near, sums = run(0)
    if pieces == 2:
        qd[1], *far = lax.optimization_barrier((qd[1], *far))
        first = exchange_far(far)
        far, near = run(1, sums, near)
        for j in range(half):
            far[j], first[j] = lax.optimization_barrier((far[j], first[j]))
        near, *first = lax.optimization_barrier((near, *first))
        last = exchange_far(far)
        near = exchange_near(near)
        everything = results_at(0, 0) + results_at(2 * begin, 1) + grads_at(4 * begin)
        outs = unpack(
            member, [(False, [near], everything), (True, first, results_at(0, 0))], shapes
        )
        outs = unpack(member, [(True, last, results_at(0, 1) + grads_at(2 * begin))], shapes, outs)
    else:
        outs = unpack(
            member,
            [
                (False, [exchange_near(near)], results_at(0, 0)),
                (True, exchange_far(far), results_at(0, 0)),
            ],
            shapes[:2],
        )
        if not whole:
            sums = lax.psum_scatter(
                sums, "seq", scatter_dimension=0, tiled=True, axis_index_groups=same_head
            )
        sums = sums.reshape(heads, shard_tokens, 2, HEAD_WIDTH)
        sums = jnp.concatenate(
            [sums[:, :, 0] * HEAD_WIDTH ** (-0.5), sums[:, :, 1]], axis=1
        ).astype(jnp.bfloat16)
        far = [
            lax.dynamic_index_in_dim(sums, member[0] ^ (half + j), 0, keepdims=False)
            for j in range(half)
        ]
        near = lax.dynamic_slice_in_dim(sums, member[0] - lax.rem(member[0], half), half, axis=0)
        outs += unpack(
            member,
            [
                (False, [exchange_near(near)], grads_at(0, 0)),
                (True, exchange_far(far), grads_at(0, 0)),
            ],
            shapes[2:],
        )
    return tuple(t.reshape(shard_tokens, heads * HEAD_WIDTH) for t in outs)


def solution(mesh):
    return jax.shard_map(
        per_device,
        mesh=mesh,
        in_specs=(
            P(("seq", "head"), None),
            P(("seq", "head"), None),
            P(("seq", "head"), None),
            P(("seq", "head"), None),
            P("head", "seq", None),
            P(),
            P("head", "seq", None),
        ),
        out_specs=(P("seq", "head"), P("seq", "head"), P("seq", "head"), P("seq", "head")),
        check_vma=False,
    )
```

```python
import functools
import math

import jax
import jax.numpy as jnp
from jax import lax
from jax.experimental import pallas as pl
from jax.experimental.pallas import tpu as pltpu
from jax.sharding import PartitionSpec as P

HEAD_WIDTH = 128
BLOCK_TOKENS = 64
R = 3
G = 2
SLOTS = 3 + G + R
WIDE = SLOTS * BLOCK_TOKENS
UNROLL = 2
STRIP = 16
VMEM_LIMIT = 16 * 1024 * 1024
VMEM_BYTES = 64 * 1024 * 1024

keep_prob = 0.9

vmem = pl.BlockSpec(memory_space=pltpu.VMEM)
smem = pl.BlockSpec(memory_space=pltpu.SMEM)
anywhere = pl.BlockSpec(memory_space=pl.ANY)


def in_vmem(array):
    return pltpu.with_memory_space_constraint(array, pltpu.VMEM)


def in_hbm(array):
    return pltpu.with_memory_space_constraint(array, pltpu.HBM)


def copy_cost(size):
    return pl.CostEstimate(flops=0, bytes_accessed=4 * size, transcendentals=0)


def block_rows(number):
    start = number * BLOCK_TOKENS
    if not isinstance(number, int):
        start = pl.multiple_of(start, BLOCK_TOKENS)
    return pl.ds(start, BLOCK_TOKENS)


def pack_kernel(heads, groups, sources, table_rows, *refs):
    refs = list(refs)
    if table_rows:
        drop_ref, rand_ref, table = refs.pop(0), refs.pop(0), refs.pop()
    count = len(sources)
    arrays, out_ref = refs[:count], refs[count]
    wholes, packed, in_sems, out_sems = refs[count + 1 : -3], refs[-3], refs[-2], refs[-1]
    width = heads * HEAD_WIDTH
    loads = []
    for g in range(groups):
        for n, (at, rows) in enumerate(sources):
            columns = pl.ds(g * width, width)
            loads.append(
                pltpu.make_async_copy(
                    arrays[n].at[pl.ds(at * rows, rows), columns],
                    wholes[n].at[:, columns],
                    in_sems.at[g, n],
                )
            )
    for load in loads:
        load.start()
    begin = sum(rows for _, rows in sources)
    if table_rows:
        blocks = drop_ref.shape[1]
        table[...] = jnp.zeros_like(table)
        for m in range(heads):
            table[pl.ds(0, blocks), pl.ds(0, SLOTS)] = drop_ref[m].astype(jnp.float32)
            for r in range(R):
                table[pl.ds(blocks + r, 1), pl.ds(0, blocks)] = rand_ref[
                    r, pl.ds(m, 1), :
                ].astype(jnp.float32)
            rounded = table[...].astype(jnp.bfloat16)
            for g in range(groups):
                packed[m, g, pl.ds(begin, table_rows), :] = rounded
    stores = []
    for g in range(groups):
        for n in range(count):
            loads[g * count + n].wait()
        for m in range(heads):
            begin = 0
            for n, (_, rows) in enumerate(sources):
                packed[m, g, pl.ds(begin, rows), :] = wholes[n][
                    :, pl.ds((g * heads + m) * HEAD_WIDTH, HEAD_WIDTH)
                ]
                begin += rows
            stores.append(
                pltpu.make_async_copy(packed.at[m, g], out_ref.at[m, g], out_sems.at[g, m])
            )
            stores[-1].start()
    for store in stores:
        store.wait()


def pack(groups, heads, sources, tables=(), table_rows=0):
    total = sum(rows for _, _, rows in sources) + table_rows
    shape = (heads, groups, total, HEAD_WIDTH)
    scratch = [
        pltpu.VMEM((rows, groups * heads * HEAD_WIDTH), jnp.bfloat16) for _, _, rows in sources
    ] + [
        pltpu.VMEM(shape, jnp.bfloat16),
        pltpu.SemaphoreType.DMA((groups, len(sources))),
        pltpu.SemaphoreType.DMA((groups, heads)),
    ]
    if table_rows:
        scratch.append(pltpu.VMEM((table_rows, HEAD_WIDTH), jnp.float32))
    packed = pl.pallas_call(
        functools.partial(
            pack_kernel, heads, groups, tuple((at, rows) for _, at, rows in sources), table_rows
        ),
        out_shape=pltpu.HBM(shape, jnp.bfloat16),
        in_specs=[vmem] * len(tables) + [anywhere] * len(sources),
        out_specs=anywhere,
        scratch_shapes=scratch,
        compiler_params=pltpu.CompilerParams(vmem_limit_bytes=VMEM_LIMIT),
        cost_estimate=copy_cost(math.prod(shape)),
    )(*[in_hbm(t) for t in tables], *[in_hbm(a) for a, _, _ in sources])
    return packed.reshape(heads * groups, total, HEAD_WIDTH)


def unpack_kernel(parts, member_ref, *refs):
    outs = refs[len(refs) - len(parts) :]
    heads = outs[0].shape[-1] // HEAD_WIDTH
    for n in range(heads):
        k = (heads - n) % heads
        column = pl.multiple_of((member_ref[0] ^ k) * HEAD_WIDTH, HEAD_WIDTH)
        for begin, out in zip(parts, outs):
            runs, _, rows, _ = out.shape
            for i in range(runs):
                out[i, 0, :, pl.ds(column, HEAD_WIDTH)] = refs[n][pl.ds(begin + i * rows, rows), :]


def unpack(member, received, parts):
    heads = len(received)
    shapes, specs, olds, aliases, size = [], [], [], {}, 0
    for n, (_, rows, runs, pieces, piece, old) in enumerate(parts):
        shapes.append(
            jax.ShapeDtypeStruct((runs, pieces, rows, heads * HEAD_WIDTH), jnp.bfloat16)
        )
        specs.append(
            pl.BlockSpec(
                (runs, 1, rows, heads * HEAD_WIDTH),
                functools.partial(lambda piece, h: (0, piece, 0, 0), piece),
            )
        )
        size += rows * runs * heads * HEAD_WIDTH
        if old is not None:
            aliases[1 + heads + len(olds)] = n
            olds.append(old)
    return pl.pallas_call(
        functools.partial(unpack_kernel, tuple(part[0] for part in parts)),
        grid=(1,),
        out_shape=shapes,
        in_specs=[smem]
        + [pl.BlockSpec(received[0].shape, lambda h: (0, 0))] * heads
        + [pl.BlockSpec(memory_space=pl.ANY)] * len(olds),
        out_specs=specs,
        input_output_aliases=aliases,
        compiler_params=pltpu.CompilerParams(vmem_limit_bytes=VMEM_LIMIT),
        cost_estimate=copy_cost(size),
    )(member, received[0], *received[:0:-1], *olds)


def unpack_all_kernel(begins, step_heads, piece_ref, *refs):
    outs = refs[len(refs) - len(begins) :]
    for begin, out in zip(begins, outs):
        runs, _, rows, _ = out.shape
        for m in range(step_heads):
            for i in range(runs):
                out[i, 0, :, pl.ds(m * HEAD_WIDTH, HEAD_WIDTH)] = piece_ref[
                    m, pl.ds(begin + i * rows, rows), :
                ]


def unpack_all(received, parts):
    heads, total, _ = received.shape
    step_heads = 2 if heads % 2 == 0 else 1
    width = step_heads * HEAD_WIDTH
    shapes, out_specs, begins, olds, aliases = [], [], [], [], {}
    size = 0
    for n, (begin, rows, runs, pieces, piece, old) in enumerate(parts):
        begins.append(begin)
        shapes.append(
            jax.ShapeDtypeStruct((runs, pieces, rows, heads * HEAD_WIDTH), jnp.bfloat16)
        )
        out_specs.append(
            pl.BlockSpec(
                (runs, 1, rows, width), functools.partial(lambda piece, h: (0, piece, 0, h), piece)
            )
        )
        size += rows * runs * heads * HEAD_WIDTH
        if old is not None:
            aliases[1 + len(olds)] = n
            olds.append(old)
    return pl.pallas_call(
        functools.partial(unpack_all_kernel, begins, step_heads),
        grid=(heads // step_heads,),
        out_shape=shapes,
        in_specs=[pl.BlockSpec((step_heads, total, HEAD_WIDTH), lambda h: (h, 0, 0))]
        + [pl.BlockSpec(memory_space=pl.ANY)] * len(olds),
        out_specs=out_specs,
        input_output_aliases=aliases,
        compiler_params=pltpu.CompilerParams(vmem_limit_bytes=VMEM_LIMIT),
        cost_estimate=copy_cost(size),
    )(in_vmem(received), *olds)


def attention_kernel(
    last_block,
    device_blocks,
    per,
    piece,
    out_rows,
    source_rows,
    qd_rows,
    qd_begin,
    has_qd,
    has_start,
    joined,
    tokens,
    targets,
    ids_ref,
    starts_ref,
    first_ref,
    member_ref,
    drop_ref,
    kv_ref,
    *refs,
):
    refs = list(refs)
    qd_ref = refs.pop(0) if has_qd else kv_ref
    start_ref = refs.pop(0) if has_start else None
    out_refs = [refs.pop(0) for _ in range(1 if joined else targets)]
    sums_ref = None if joined else refs.pop(0)
    acc, retain, waiting, near, sems = refs[:5]
    done = refs[5] if joined else None
    earlier, start_sem = refs[-2:] if has_start else (None, None)
    scale = HEAD_WIDTH ** (-0.5)
    steps = targets * (out_rows // BLOCK_TOKENS)
    slot_of_lane = lax.broadcasted_iota(jnp.int32, (SLOTS, WIDE), 1) // BLOCK_TOKENS
    slot_row = lax.broadcasted_iota(jnp.int32, (SLOTS, WIDE), 0)
    expand = (slot_of_lane == slot_row).astype(jnp.float32)
    retain[...] = jnp.dot(
        drop_ref[...].astype(jnp.float32), expand, preferred_element_type=jnp.float32
    ) * (1.0 / keep_prob)
    acc[...] = jnp.zeros_like(acc)
    if has_start:
        fetch = pltpu.make_async_copy(start_ref, earlier, start_sem)
        fetch.start()
    lane = lax.broadcasted_iota(jnp.int32, (1, WIDE), 1)
    nt = (((1,), (1,)), ((), ()))
    tn = (((0,), (0,)), ((), ()))
    out_steps = steps // targets

    def place(i):
        if per == 1:
            source, sub = i, 0
        else:
            source, sub = lax.div(i, per), lax.rem(i, per)
        return source, sub, source * device_blocks + piece * per + sub

    def load(i):
        source, sub, j = place(i)
        starts = [starts_ref[j * SLOTS + s] for s in range(SLOTS)]
        q, do = [
            qd_ref[
                pl.ds(
                    pl.multiple_of(
                        source * qd_rows + (n * per + sub) * BLOCK_TOKENS + qd_begin, 16
                    ),
                    BLOCK_TOKENS,
                ),
                :,
            ]
            for n in range(2)
        ]
        keys, vals = [
            jnp.concatenate(
                [kv_ref[pl.ds(pl.multiple_of(r + n * tokens, 16), BLOCK_TOKENS), :] for r in starts],
                axis=0,
            )
            for n in range(2)
        ]
        return q, do, keys, vals

    def score(i):
        q, do, keys, vals = load(i)
        logits = lax.dot_general(q, keys, nt, preferred_element_type=jnp.float32)
        raw = lax.dot_general(do, vals, nt, preferred_element_type=jnp.float32)
        return logits, raw

    def factor(i, u, logits, raw):
        j = place(i)[2]
        block_id = first_ref[0] + j
        absent = ((block_id == 0) & (lane < BLOCK_TOKENS)) | (
            (block_id == last_block) & (lane >= 2 * BLOCK_TOKENS) & (lane < 3 * BLOCK_TOKENS)
        )
        keep = retain[pl.ds(j, 1), :]
        for r in range(0, BLOCK_TOKENS, STRIP):
            part = jnp.where(absent, -jnp.inf, logits[r : r + STRIP])
            top = jnp.max(part, axis=-1, keepdims=True)
            expd = jnp.exp2((part - top) * (scale / math.log(2.0)))
            probs = expd * (1.0 / jnp.sum(expd, axis=-1, keepdims=True))
            kept = probs * keep
            weighted = kept * raw[r : r + STRIP]
            delta = jnp.sum(weighted, axis=-1, keepdims=True)
            waiting[u, pl.ds(r, STRIP), :] = (weighted - probs * delta).astype(jnp.bfloat16)
            waiting[u, pl.ds(BLOCK_TOKENS + r, STRIP), :] = kept.astype(jnp.bfloat16)

    def finish(i, u):
        j = place(i)[2]
        q, do, keys, vals = load(i)
        factors = waiting[u]
        dq = jnp.dot(factors[:BLOCK_TOKENS], keys, preferred_element_type=jnp.float32) * scale
        att = jnp.dot(factors[BLOCK_TOKENS:], vals, preferred_element_type=jnp.float32)
        none = jnp.zeros_like(q)
        pair = jnp.concatenate(
            [jnp.concatenate([q, none], axis=1), jnp.concatenate([none, do], axis=1)], axis=0
        )
        terms = lax.dot_general(factors, pair, tn, preferred_element_type=jnp.float32)
        for s in range(SLOTS):
            acc[block_rows(ids_ref[j * SLOTS + s]), :] += terms[
                s * BLOCK_TOKENS : (s + 1) * BLOCK_TOKENS
            ]
        target, pos = lax.div(i, out_steps), lax.rem(i, out_steps)
        near[target, block_rows(pos), :] = att.astype(jnp.bfloat16)
        near[target, block_rows(out_steps + pos), :] = dq.astype(jnp.bfloat16)

    def step(t, carry):
        scores = [score(t * UNROLL + u) for u in range(UNROLL)]
        for u in range(UNROLL):
            finish((t - 1) * UNROLL + u, u)
        for u in range(UNROLL):
            factor(t * UNROLL + u, u, *scores[u])
        return carry

    for u in range(UNROLL):
        factor(u, u, *score(u))
    lax.fori_loop(1, steps // UNROLL, step, 0)
    for u in range(UNROLL):
        finish(steps - UNROLL + u, u)
    if has_start:
        fetch.wait()
    if joined:
        rows = acc.shape[0] // targets
        stores = []
        for target in range(targets):
            part = pl.ds(target * rows, rows)
            sums = acc[part, :]
            if has_start:
                sums += earlier[part, :]
            done[target, pl.ds(0, 2 * out_rows), :] = near[target]
            done[target, pl.ds(2 * out_rows, rows), :] = (sums[:, :HEAD_WIDTH] * scale).astype(
                jnp.bfloat16
            )
            done[target, pl.ds(2 * out_rows + rows, rows), :] = sums[:, HEAD_WIDTH:].astype(
                jnp.bfloat16
            )
            stores.append(
                pltpu.make_async_copy(done.at[target], out_refs[0].at[target], sems.at[target])
            )
            stores[-1].start()
        for store in stores:
            store.wait()
    else:
        rows = acc.shape[0] // targets
        stores = [
            pltpu.make_async_copy(
                acc.at[pl.ds(n * rows, rows), :], sums_ref.at[pl.ds(n * rows, rows), :], sems.at[n]
            )
            for n in range(targets)
        ]
        for store in stores:
            store.start()
        for k, out_ref in enumerate(out_refs):
            out_ref[...] = near[member_ref[0] ^ k]
        for store in stores:
            store.wait()


def attend(
    ids, starts, first_block, member, drop, kv, qd, qd_begin, start, piece, per, joined, device_blocks, total_blocks, tokens, targets
):
    team_blocks = drop.shape[0]
    source = kv if qd is None else qd
    steps = team_blocks * per // device_blocks
    length = total_blocks * BLOCK_TOKENS
    pairs = steps * BLOCK_TOKENS * WIDE
    accumulator = (length, 2 * HEAD_WIDTH)
    out_rows = steps * BLOCK_TOKENS // targets
    if joined:
        out_shape = [
            pltpu.HBM((targets, 2 * out_rows + 2 * length // targets, HEAD_WIDTH), jnp.bfloat16)
        ]
    else:
        out_shape = [pltpu.HBM((2 * out_rows, HEAD_WIDTH), jnp.bfloat16)] * targets
    scratch = [
        pltpu.VMEM((team_blocks, WIDE), jnp.float32),
        pltpu.VMEM((UNROLL, 2 * BLOCK_TOKENS, WIDE), jnp.bfloat16),
        pltpu.VMEM((targets, 2 * out_rows, HEAD_WIDTH), jnp.bfloat16),
    ]
    scratch = [pltpu.VMEM(accumulator, jnp.float32)] + scratch + [
        pltpu.SemaphoreType.DMA((targets,))
    ]
    if not joined:
        out_shape.append(pltpu.HBM(accumulator, jnp.float32))
    if joined:
        scratch.append(pltpu.VMEM(out_shape[0].shape, jnp.bfloat16))
    sums_bytes = 8 * length * HEAD_WIDTH
    limit = VMEM_LIMIT + 2 * (kv.size + source.size) + (1 if start is None else 2) * sums_bytes
    keep = in_vmem if 2 * limit < VMEM_BYTES else lambda t: t
    flat = [keep(t.reshape(-1, HEAD_WIDTH)) for t in (kv, qd) if t is not None]
    if start is not None:
        scratch += [pltpu.VMEM(accumulator, jnp.float32), pltpu.SemaphoreType.DMA]
    operands = flat + ([] if start is None else [in_hbm(start)])
    operand_specs = [vmem] * len(flat) + [anywhere] * (start is not None)
    return pl.pallas_call(
        functools.partial(
            attention_kernel,
            total_blocks - 1,
            device_blocks,
            per,
            piece,
            out_rows,
            kv.shape[1],
            source.shape[1],
            qd_begin,
            qd is not None,
            start is not None,
            joined,
            tokens,
            targets,
        ),
        out_shape=out_shape,
        in_specs=[smem, smem, smem, smem, vmem] + operand_specs,
        out_specs=[anywhere] if joined else [vmem] * targets + [anywhere],
        scratch_shapes=scratch,
        compiler_params=pltpu.CompilerParams(vmem_limit_bytes=limit),
        cost_estimate=pl.CostEstimate(
            flops=128 * pairs * HEAD_WIDTH,
            bytes_accessed=2 * (source.size + kv.size) + 8 * length * HEAD_WIDTH,
            transcendentals=pairs,
        ),
    )(ids, starts, first_block, member, in_hbm(drop), *operands)


def per_device(queries, keys, values, grad_out, rand_blocks, global_ids, drop_mask):
    shards = lax.axis_size("seq")
    groups = lax.axis_size("head")
    shard = lax.axis_index("seq")
    heads, shard_blocks, _ = rand_blocks.shape
    tokens = queries.shape[0]
    device_blocks = tokens // BLOCK_TOKENS
    shard_tokens = shard_blocks * BLOCK_TOKENS
    teams = shards // heads
    team, member = lax.div(shard, heads), lax.rem(shard, heads)
    team_blocks = heads * shard_blocks
    total_blocks = shards * shard_blocks
    first_block = team * team_blocks
    whole = teams == 1
    pieces = device_blocks if whole else 1
    per = device_blocks // pieces
    rows = tokens // pieces
    same_team_all = (
        None
        if whole
        else [
            [(t * heads + m) * groups + g for m in range(heads) for g in range(groups)]
            for t in range(teams)
        ]
    )
    same_head = [[t * heads + m for t in range(teams)] for m in range(heads)]

    def to_heads(packed):
        return lax.all_to_all(
            packed,
            ("seq", "head"),
            split_axis=0,
            concat_axis=0,
            tiled=True,
            axis_index_groups=same_team_all,
        )

    def to_shards(results):
        received = list(results)
        for k in reversed(range(1, heads)):
            pairs = [(s, s ^ k) for s in range(shards)]
            received[k] = lax.ppermute(results[k], "seq", pairs)
        return received

    table_rows = -(-(shard_blocks + R) // 16) * 16
    sources = [[(queries, c, rows), (grad_out, c, rows)] for c in range(pieces)]
    qd_begin = 2 * tokens
    table_begin = qd_begin + 2 * rows
    kv = to_heads(
        pack(
            groups,
            heads,
            [(keys, 0, tokens), (values, 0, tokens)] + sources[0],
            (drop_mask, rand_blocks.transpose(2, 0, 1)),
            table_rows,
        )
    )
    later = [to_heads(pack(groups, heads, each)) for each in sources[1:]]
    tables = lax.dynamic_index_in_dim(
        kv.reshape(heads, groups, -1, HEAD_WIDTH)[:, :, table_begin:],
        lax.axis_index("head"),
        axis=1,
        keepdims=False,
    ).astype(jnp.int32)
    drops = tables[:, :shard_blocks, :SLOTS].reshape(team_blocks, SLOTS)
    randoms = tables[:, shard_blocks : shard_blocks + R, :shard_blocks].transpose(0, 2, 1)
    randoms = randoms.reshape(team_blocks, R)
    qd = [None] + later
    if not whole:
        qd[0] = kv[:, qd_begin:table_begin]
        kv = lax.all_gather(kv[:, : 2 * tokens], "seq", axis=0, tiled=True, axis_index_groups=same_head)
    blocks = first_block + jnp.arange(team_blocks, dtype=jnp.int32)
    window = jnp.stack([blocks - 1, blocks, blocks + 1], axis=1)
    listed = jnp.concatenate(
        [window, jnp.broadcast_to(global_ids[None], (team_blocks, G)), randoms], axis=1
    )
    listed = jnp.clip(listed, 0, total_blocks - 1).reshape(-1)
    starts = listed // device_blocks * kv.shape[1] + listed % device_blocks * BLOCK_TOKENS
    pieces_out = []
    held = []
    sums = []
    for c in range(pieces):
        pieces_out.append(
            attend(
                listed,
                starts,
                first_block.reshape(1),
                member.reshape(1),
                drops,
                kv,
                qd[c],
                qd_begin if qd[c] is None else 0,
                sums[0] if sums else None,
                c,
                per,
                whole and c == pieces - 1,
                device_blocks,
                total_blocks,
                tokens,
                heads,
            )
        )
        sums = pieces_out[c][heads:]
        if c + 1 < pieces:
            held.append(pieces_out[c][1:heads])
    runs = shard_blocks // device_blocks
    begin = shard_tokens // pieces
    near = []
    for c, out in enumerate(pieces_out):
        if len(out) > 1:
            results = out[:heads]
            if c + 1 < pieces:
                results = [results[0], *held[c]]
            near.append(to_shards(results))
    att, dq = None, None
    if whole:
        rest = pieces_out[-1][0]
        if near:
            rest, *near[-1][heads // 2 :] = lax.optimization_barrier(
                (rest, *near[-1][heads // 2 :])
            )
        rest = lax.all_to_all(rest, "seq", split_axis=0, concat_axis=0, tiled=True)
    for c in range(len(near)):
        parts = [(0, rows, runs, pieces, c, att), (begin, rows, runs, pieces, c, dq)]
        att, dq = unpack(member.reshape(1), near[c], parts)
    if whole:
        c = pieces - 1
        parts = [(0, rows, runs, pieces, c, att), (begin, rows, runs, pieces, c, dq)]
        grads = [(2 * begin + n * shard_tokens, shard_tokens, 1, 1, 0, None) for n in range(2)]
        att, dq, dk, dv = unpack_all(rest, parts + grads)
    else:
        grads = lax.psum_scatter(
            sums[0], "seq", scatter_dimension=0, tiled=True, axis_index_groups=same_head
        ).reshape(heads, shard_tokens, 2, HEAD_WIDTH)
        grads = jnp.concatenate(
            [grads[:, :, 0] * HEAD_WIDTH ** (-0.5), grads[:, :, 1]], axis=1
        ).astype(jnp.bfloat16)
        grads = to_shards(
            [lax.dynamic_index_in_dim(grads, member ^ k, 0, keepdims=False) for k in range(heads)]
        )
        dk, dv = unpack(
            member.reshape(1),
            grads,
            [(n * shard_tokens, shard_tokens, 1, 1, 0, None) for n in range(2)],
        )
    return tuple(t.reshape(shard_tokens, heads * HEAD_WIDTH) for t in (att, dq, dk, dv))


def solution(mesh):
    return jax.shard_map(
        per_device,
        mesh=mesh,
        in_specs=(
            P(("seq", "head"), None),
            P(("seq", "head"), None),
            P(("seq", "head"), None),
            P(("seq", "head"), None),
            P("head", "seq", None),
            P(),
            P("head", "seq", None),
        ),
        out_specs=(P("seq", "head"), P("seq", "head"), P("seq", "head"), P("seq", "head")),
        check_vma=False,
    )
```

```python
import functools
import math

import jax
import jax.numpy as jnp
from jax import lax
from jax.experimental import pallas as pl
from jax.experimental.pallas import tpu as pltpu
from jax.sharding import PartitionSpec as P

HEAD_WIDTH = 128
BLOCK_TOKENS = 64
R = 3
G = 2
SLOTS = 3 + G + R
WIDE = SLOTS * BLOCK_TOKENS
UNROLL = 2
STRIP = 16
VMEM_LIMIT = 16 * 1024 * 1024
VMEM_BYTES = 64 * 1024 * 1024

keep_prob = 0.9

vmem = pl.BlockSpec(memory_space=pltpu.VMEM)
smem = pl.BlockSpec(memory_space=pltpu.SMEM)
anywhere = pl.BlockSpec(memory_space=pl.ANY)


def in_vmem(array):
    return pltpu.with_memory_space_constraint(array, pltpu.VMEM)


def in_hbm(array):
    return pltpu.with_memory_space_constraint(array, pltpu.HBM)


def copy_cost(size):
    return pl.CostEstimate(flops=0, bytes_accessed=4 * size, transcendentals=0)


def block_rows(number):
    start = number * BLOCK_TOKENS
    if not isinstance(number, int):
        start = pl.multiple_of(start, BLOCK_TOKENS)
    return pl.ds(start, BLOCK_TOKENS)


def pack_kernel(heads, groups, sources, table_rows, *refs):
    refs = list(refs)
    if table_rows:
        drop_ref, rand_ref, table = refs.pop(0), refs.pop(0), refs.pop()
    count = len(sources)
    arrays, out_ref = refs[:count], refs[count]
    wholes, packed, in_sems, out_sems = refs[count + 1 : -3], refs[-3], refs[-2], refs[-1]
    width = heads * HEAD_WIDTH
    loads = []
    for g in range(groups):
        for n, (at, rows) in enumerate(sources):
            columns = pl.ds(g * width, width)
            loads.append(
                pltpu.make_async_copy(
                    arrays[n].at[pl.ds(at * rows, rows), columns],
                    wholes[n].at[:, columns],
                    in_sems.at[g, n],
                )
            )
    for load in loads:
        load.start()
    begin = sum(rows for _, rows in sources)
    if table_rows:
        blocks = drop_ref.shape[1]
        table[...] = jnp.zeros_like(table)
        for m in range(heads):
            table[pl.ds(0, blocks), pl.ds(0, SLOTS)] = drop_ref[m].astype(jnp.float32)
            for r in range(R):
                table[pl.ds(blocks + r, 1), pl.ds(0, blocks)] = rand_ref[
                    r, pl.ds(m, 1), :
                ].astype(jnp.float32)
            rounded = table[...].astype(jnp.bfloat16)
            for g in range(groups):
                packed[m, g, pl.ds(begin, table_rows), :] = rounded
    stores = []
    for g in range(groups):
        for n in range(count):
            loads[g * count + n].wait()
        for m in range(heads):
            begin = 0
            for n, (_, rows) in enumerate(sources):
                packed[m, g, pl.ds(begin, rows), :] = wholes[n][
                    :, pl.ds((g * heads + m) * HEAD_WIDTH, HEAD_WIDTH)
                ]
                begin += rows
            stores.append(
                pltpu.make_async_copy(packed.at[m, g], out_ref.at[m, g], out_sems.at[g, m])
            )
            stores[-1].start()
    for store in stores:
        store.wait()


def pack(groups, heads, sources, tables=(), table_rows=0):
    total = sum(rows for _, _, rows in sources) + table_rows
    shape = (heads, groups, total, HEAD_WIDTH)
    scratch = [
        pltpu.VMEM((rows, groups * heads * HEAD_WIDTH), jnp.bfloat16) for _, _, rows in sources
    ] + [
        pltpu.VMEM(shape, jnp.bfloat16),
        pltpu.SemaphoreType.DMA((groups, len(sources))),
        pltpu.SemaphoreType.DMA((groups, heads)),
    ]
    if table_rows:
        scratch.append(pltpu.VMEM((table_rows, HEAD_WIDTH), jnp.float32))
    packed = pl.pallas_call(
        functools.partial(
            pack_kernel, heads, groups, tuple((at, rows) for _, at, rows in sources), table_rows
        ),
        out_shape=pltpu.HBM(shape, jnp.bfloat16),
        in_specs=[vmem] * len(tables) + [anywhere] * len(sources),
        out_specs=anywhere,
        scratch_shapes=scratch,
        compiler_params=pltpu.CompilerParams(vmem_limit_bytes=VMEM_LIMIT),
        cost_estimate=copy_cost(math.prod(shape)),
    )(*[in_hbm(t) for t in tables], *[in_hbm(a) for a, _, _ in sources])
    return packed.reshape(heads * groups, total, HEAD_WIDTH)


def unpack_kernel(parts, member_ref, *refs):
    outs = refs[len(refs) - len(parts) :]
    heads = outs[0].shape[-1] // HEAD_WIDTH
    for n in range(heads):
        k = (heads - n) % heads
        column = pl.multiple_of((member_ref[0] ^ k) * HEAD_WIDTH, HEAD_WIDTH)
        for begin, out in zip(parts, outs):
            runs, _, rows, _ = out.shape
            for i in range(runs):
                out[i, 0, :, pl.ds(column, HEAD_WIDTH)] = refs[n][pl.ds(begin + i * rows, rows), :]


def unpack(member, received, parts):
    heads = len(received)
    shapes, specs, olds, aliases, size = [], [], [], {}, 0
    for n, (_, rows, runs, pieces, piece, old) in enumerate(parts):
        shapes.append(
            jax.ShapeDtypeStruct((runs, pieces, rows, heads * HEAD_WIDTH), jnp.bfloat16)
        )
        specs.append(
            pl.BlockSpec(
                (runs, 1, rows, heads * HEAD_WIDTH),
                functools.partial(lambda piece, h: (0, piece, 0, 0), piece),
            )
        )
        size += rows * runs * heads * HEAD_WIDTH
        if old is not None:
            aliases[1 + heads + len(olds)] = n
            olds.append(old)
    return pl.pallas_call(
        functools.partial(unpack_kernel, tuple(part[0] for part in parts)),
        grid=(1,),
        out_shape=shapes,
        in_specs=[smem]
        + [pl.BlockSpec(received[0].shape, lambda h: (0, 0))] * heads
        + [pl.BlockSpec(memory_space=pl.ANY)] * len(olds),
        out_specs=specs,
        input_output_aliases=aliases,
        compiler_params=pltpu.CompilerParams(vmem_limit_bytes=VMEM_LIMIT),
        cost_estimate=copy_cost(size),
    )(member, received[0], *received[:0:-1], *olds)


def unpack_all_kernel(begins, step_heads, piece_ref, *refs):
    outs = refs[len(refs) - len(begins) :]
    for begin, out in zip(begins, outs):
        runs, _, rows, _ = out.shape
        for m in range(step_heads):
            for i in range(runs):
                out[i, 0, :, pl.ds(m * HEAD_WIDTH, HEAD_WIDTH)] = piece_ref[
                    m, pl.ds(begin + i * rows, rows), :
                ]


def unpack_all(received, parts):
    heads, total, _ = received.shape
    step_heads = 2 if heads % 2 == 0 else 1
    width = step_heads * HEAD_WIDTH
    shapes, out_specs, begins, olds, aliases = [], [], [], [], {}
    size = 0
    for n, (begin, rows, runs, pieces, piece, old) in enumerate(parts):
        begins.append(begin)
        shapes.append(
            jax.ShapeDtypeStruct((runs, pieces, rows, heads * HEAD_WIDTH), jnp.bfloat16)
        )
        out_specs.append(
            pl.BlockSpec(
                (runs, 1, rows, width), functools.partial(lambda piece, h: (0, piece, 0, h), piece)
            )
        )
        size += rows * runs * heads * HEAD_WIDTH
        if old is not None:
            aliases[1 + len(olds)] = n
            olds.append(old)
    return pl.pallas_call(
        functools.partial(unpack_all_kernel, begins, step_heads),
        grid=(heads // step_heads,),
        out_shape=shapes,
        in_specs=[pl.BlockSpec((step_heads, total, HEAD_WIDTH), lambda h: (h, 0, 0))]
        + [pl.BlockSpec(memory_space=pl.ANY)] * len(olds),
        out_specs=out_specs,
        input_output_aliases=aliases,
        compiler_params=pltpu.CompilerParams(vmem_limit_bytes=VMEM_LIMIT),
        cost_estimate=copy_cost(size),
    )(in_vmem(received), *olds)


def attention_kernel(
    last_block,
    device_blocks,
    per,
    piece,
    out_rows,
    source_rows,
    qd_rows,
    qd_begin,
    has_qd,
    has_start,
    joined,
    tokens,
    targets,
    ids_ref,
    starts_ref,
    first_ref,
    member_ref,
    drop_ref,
    kv_ref,
    *refs,
):
    refs = list(refs)
    qd_ref = refs.pop(0) if has_qd else kv_ref
    start_ref = refs.pop(0) if has_start else None
    out_refs = [refs.pop(0) for _ in range(1 if joined else targets)]
    sums_ref = None if joined else refs.pop(0)
    acc, retain, waiting, near, sems = refs[:5]
    done = refs[5] if joined else None
    earlier, start_sem = refs[-2:] if has_start else (None, None)
    scale = HEAD_WIDTH ** (-0.5)
    steps = targets * (out_rows // BLOCK_TOKENS)
    slot_of_lane = lax.broadcasted_iota(jnp.int32, (SLOTS, WIDE), 1) // BLOCK_TOKENS
    slot_row = lax.broadcasted_iota(jnp.int32, (SLOTS, WIDE), 0)
    expand = (slot_of_lane == slot_row).astype(jnp.float32)
    retain[...] = jnp.dot(
        drop_ref[...].astype(jnp.float32), expand, preferred_element_type=jnp.float32
    ) * (1.0 / keep_prob)
    acc[...] = jnp.zeros_like(acc)
    if has_start:
        fetch = pltpu.make_async_copy(start_ref, earlier, start_sem)
        fetch.start()
    lane = lax.broadcasted_iota(jnp.int32, (1, WIDE), 1)
    nt = (((1,), (1,)), ((), ()))
    tn = (((0,), (0,)), ((), ()))
    out_steps = steps // targets

    def place(i):
        if per == 1:
            source, sub = i, 0
        else:
            source, sub = lax.div(i, per), lax.rem(i, per)
        return source, sub, source * device_blocks + piece * per + sub

    def load(i):
        source, sub, j = place(i)
        starts = [starts_ref[j * SLOTS + s] for s in range(SLOTS)]
        q, do = [
            qd_ref[
                pl.ds(
                    pl.multiple_of(
                        source * qd_rows + (n * per + sub) * BLOCK_TOKENS + qd_begin, 16
                    ),
                    BLOCK_TOKENS,
                ),
                :,
            ]
            for n in range(2)
        ]
        keys, vals = [
            jnp.concatenate(
                [kv_ref[pl.ds(pl.multiple_of(r + n * tokens, 16), BLOCK_TOKENS), :] for r in starts],
                axis=0,
            )
            for n in range(2)
        ]
        return q, do, keys, vals

    def score(i):
        q, do, keys, vals = load(i)
        logits = lax.dot_general(q, keys, nt, preferred_element_type=jnp.float32)
        raw = lax.dot_general(do, vals, nt, preferred_element_type=jnp.float32)
        return logits, raw

    def factor(i, u, logits, raw):
        j = place(i)[2]
        block_id = first_ref[0] + j
        absent = ((block_id == 0) & (lane < BLOCK_TOKENS)) | (
            (block_id == last_block) & (lane >= 2 * BLOCK_TOKENS) & (lane < 3 * BLOCK_TOKENS)
        )
        keep = retain[pl.ds(j, 1), :]
        for r in range(0, BLOCK_TOKENS, STRIP):
            part = jnp.where(absent, -jnp.inf, logits[r : r + STRIP])
            top = jnp.max(part, axis=-1, keepdims=True)
            expd = jnp.exp2((part - top) * (scale / math.log(2.0)))
            probs = expd * (1.0 / jnp.sum(expd, axis=-1, keepdims=True))
            kept = probs * keep
            weighted = kept * raw[r : r + STRIP]
            delta = jnp.sum(weighted, axis=-1, keepdims=True)
            waiting[u, pl.ds(r, STRIP), :] = (weighted - probs * delta).astype(jnp.bfloat16)
            waiting[u, pl.ds(BLOCK_TOKENS + r, STRIP), :] = kept.astype(jnp.bfloat16)

    def finish(i, u):
        j = place(i)[2]
        q, do, keys, vals = load(i)
        factors = waiting[u]
        dq = jnp.dot(factors[:BLOCK_TOKENS], keys, preferred_element_type=jnp.float32) * scale
        att = jnp.dot(factors[BLOCK_TOKENS:], vals, preferred_element_type=jnp.float32)
        none = jnp.zeros_like(q)
        pair = jnp.concatenate(
            [jnp.concatenate([q, none], axis=1), jnp.concatenate([none, do], axis=1)], axis=0
        )
        terms = lax.dot_general(factors, pair, tn, preferred_element_type=jnp.float32)
        for s in range(SLOTS):
            acc[block_rows(ids_ref[j * SLOTS + s]), :] += terms[
                s * BLOCK_TOKENS : (s + 1) * BLOCK_TOKENS
            ]
        target, pos = lax.div(i, out_steps), lax.rem(i, out_steps)
        near[target, block_rows(pos), :] = att.astype(jnp.bfloat16)
        near[target, block_rows(out_steps + pos), :] = dq.astype(jnp.bfloat16)

    def step(t, carry):
        scores = [score(t * UNROLL + u) for u in range(UNROLL)]
        for u in range(UNROLL):
            finish((t - 1) * UNROLL + u, u)
        for u in range(UNROLL):
            factor(t * UNROLL + u, u, *scores[u])
        return carry

    for u in range(UNROLL):
        factor(u, u, *score(u))
    lax.fori_loop(1, steps // UNROLL, step, 0)
    for u in range(UNROLL):
        finish(steps - UNROLL + u, u)
    if has_start:
        fetch.wait()
    if joined:
        rows = acc.shape[0] // targets
        stores = []
        for target in range(targets):
            part = pl.ds(target * rows, rows)
            sums = acc[part, :]
            if has_start:
                sums += earlier[part, :]
            done[target, pl.ds(0, 2 * out_rows), :] = near[target]
            done[target, pl.ds(2 * out_rows, rows), :] = (sums[:, :HEAD_WIDTH] * scale).astype(
                jnp.bfloat16
            )
            done[target, pl.ds(2 * out_rows + rows, rows), :] = sums[:, HEAD_WIDTH:].astype(
                jnp.bfloat16
            )
            stores.append(
                pltpu.make_async_copy(done.at[target], out_refs[0].at[target], sems.at[target])
            )
            stores[-1].start()
        for store in stores:
            store.wait()
    else:
        rows = acc.shape[0] // targets
        stores = [
            pltpu.make_async_copy(
                acc.at[pl.ds(n * rows, rows), :], sums_ref.at[pl.ds(n * rows, rows), :], sems.at[n]
            )
            for n in range(targets)
        ]
        for store in stores:
            store.start()
        for k, out_ref in enumerate(out_refs):
            out_ref[...] = near[member_ref[0] ^ k]
        for store in stores:
            store.wait()


def attend(
    ids, starts, first_block, member, drop, kv, qd, qd_begin, start, piece, per, joined, device_blocks, total_blocks, tokens, targets
):
    team_blocks = drop.shape[0]
    source = kv if qd is None else qd
    steps = team_blocks * per // device_blocks
    length = total_blocks * BLOCK_TOKENS
    pairs = steps * BLOCK_TOKENS * WIDE
    accumulator = (length, 2 * HEAD_WIDTH)
    out_rows = steps * BLOCK_TOKENS // targets
    if joined:
        out_shape = [
            pltpu.HBM((targets, 2 * out_rows + 2 * length // targets, HEAD_WIDTH), jnp.bfloat16)
        ]
    else:
        out_shape = [pltpu.HBM((2 * out_rows, HEAD_WIDTH), jnp.bfloat16)] * targets
    scratch = [
        pltpu.VMEM((team_blocks, WIDE), jnp.float32),
        pltpu.VMEM((UNROLL, 2 * BLOCK_TOKENS, WIDE), jnp.bfloat16),
        pltpu.VMEM((targets, 2 * out_rows, HEAD_WIDTH), jnp.bfloat16),
    ]
    scratch = [pltpu.VMEM(accumulator, jnp.float32)] + scratch + [
        pltpu.SemaphoreType.DMA((targets,))
    ]
    if not joined:
        out_shape.append(pltpu.HBM(accumulator, jnp.float32))
    if joined:
        scratch.append(pltpu.VMEM(out_shape[0].shape, jnp.bfloat16))
    sums_bytes = 8 * length * HEAD_WIDTH
    limit = VMEM_LIMIT + 2 * (kv.size + source.size) + (1 if start is None else 2) * sums_bytes
    keep = in_vmem if 2 * limit < VMEM_BYTES else lambda t: t
    flat = [keep(t.reshape(-1, HEAD_WIDTH)) for t in (kv, qd) if t is not None]
    if start is not None:
        scratch += [pltpu.VMEM(accumulator, jnp.float32), pltpu.SemaphoreType.DMA]
    operands = flat + ([] if start is None else [in_hbm(start)])
    operand_specs = [vmem] * len(flat) + [anywhere] * (start is not None)
    return pl.pallas_call(
        functools.partial(
            attention_kernel,
            total_blocks - 1,
            device_blocks,
            per,
            piece,
            out_rows,
            kv.shape[1],
            source.shape[1],
            qd_begin,
            qd is not None,
            start is not None,
            joined,
            tokens,
            targets,
        ),
        out_shape=out_shape,
        in_specs=[smem, smem, smem, smem, vmem] + operand_specs,
        out_specs=[anywhere] if joined else [vmem] * targets + [anywhere],
        scratch_shapes=scratch,
        compiler_params=pltpu.CompilerParams(vmem_limit_bytes=limit),
        cost_estimate=pl.CostEstimate(
            flops=128 * pairs * HEAD_WIDTH,
            bytes_accessed=2 * (source.size + kv.size) + 8 * length * HEAD_WIDTH,
            transcendentals=pairs,
        ),
    )(ids, starts, first_block, member, in_hbm(drop), *operands)


def per_device(queries, keys, values, grad_out, rand_blocks, global_ids, drop_mask):
    shards = lax.axis_size("seq")
    groups = lax.axis_size("head")
    shard = lax.axis_index("seq")
    heads, shard_blocks, _ = rand_blocks.shape
    tokens = queries.shape[0]
    device_blocks = tokens // BLOCK_TOKENS
    shard_tokens = shard_blocks * BLOCK_TOKENS
    teams = shards // heads
    team, member = lax.div(shard, heads), lax.rem(shard, heads)
    team_blocks = heads * shard_blocks
    total_blocks = shards * shard_blocks
    first_block = team * team_blocks
    whole = teams == 1
    half = heads // 2
    pieces = device_blocks if whole else 1
    per = device_blocks // pieces
    rows = tokens // pieces
    same_team_all = (
        None
        if whole
        else [
            [(t * heads + m) * groups + g for m in range(heads) for g in range(groups)]
            for t in range(teams)
        ]
    )
    same_head = [[t * heads + m for t in range(teams)] for m in range(heads)]

    def to_heads(packed):
        return lax.all_to_all(
            packed,
            ("seq", "head"),
            split_axis=0,
            concat_axis=0,
            tiled=True,
            axis_index_groups=same_team_all,
        )

    def to_shards(results, partners):
        received = list(results)
        for k in reversed(partners):
            pairs = [(s, s ^ k) for s in range(shards)]
            received[k] = lax.ppermute(results[k], "seq", pairs)
        return received

    table_rows = -(-(shard_blocks + R) // 16) * 16
    sources = [[(queries, c, rows), (grad_out, c, rows)] for c in range(pieces)]
    qd_begin = 2 * tokens
    table_begin = qd_begin + 2 * rows
    kv = to_heads(
        pack(
            groups,
            heads,
            [(keys, 0, tokens), (values, 0, tokens)] + sources[0],
            (drop_mask, rand_blocks.transpose(2, 0, 1)),
            table_rows,
        )
    )
    later = [to_heads(pack(groups, heads, each)) for each in sources[1:]]
    tables = lax.dynamic_index_in_dim(
        kv.reshape(heads, groups, -1, HEAD_WIDTH)[:, :, table_begin:],
        lax.axis_index("head"),
        axis=1,
        keepdims=False,
    ).astype(jnp.int32)
    drops = tables[:, :shard_blocks, :SLOTS].reshape(team_blocks, SLOTS)
    randoms = tables[:, shard_blocks : shard_blocks + R, :shard_blocks].transpose(0, 2, 1)
    randoms = randoms.reshape(team_blocks, R)
    qd = [None] + later
    if not whole:
        qd[0] = kv[:, qd_begin:table_begin]
        kv = lax.all_gather(kv[:, : 2 * tokens], "seq", axis=0, tiled=True, axis_index_groups=same_head)
    blocks = first_block + jnp.arange(team_blocks, dtype=jnp.int32)
    window = jnp.stack([blocks - 1, blocks, blocks + 1], axis=1)
    listed = jnp.concatenate(
        [window, jnp.broadcast_to(global_ids[None], (team_blocks, G)), randoms], axis=1
    )
    listed = jnp.clip(listed, 0, total_blocks - 1).reshape(-1)
    starts = listed // device_blocks * kv.shape[1] + listed % device_blocks * BLOCK_TOKENS
    pieces_out = []
    near = []
    sums = []
    for c in range(pieces):
        pieces_out.append(
            attend(
                listed,
                starts,
                first_block.reshape(1),
                member.reshape(1),
                drops,
                kv,
                qd[c],
                qd_begin if qd[c] is None else 0,
                sums[0] if sums else None,
                c,
                per,
                whole and c == pieces - 1,
                device_blocks,
                total_blocks,
                tokens,
                heads,
            )
        )
        sums = pieces_out[c][heads:]
        if c + 1 < pieces:
            late = 3 * heads // 4
            ready = list(pieces_out[c][:heads])
            ready = to_shards(ready, range(late, heads))
            qd[c + 1], *ready[late:] = lax.optimization_barrier((qd[c + 1], *ready[late:]))
            qd[c + 1], *ready[half:late] = lax.optimization_barrier((qd[c + 1], *ready[half:late]))
            near.append(to_shards(ready, range(half, late)))
    runs = shard_blocks // device_blocks
    begin = shard_tokens // pieces
    if not whole:
        near.append(to_shards(pieces_out[-1][:heads], range(1, heads)))
    att, dq = None, None
    if whole:
        rest = pieces_out[-1][0]
        if near:
            rest, *near[-1] = lax.optimization_barrier((rest, *near[-1]))
            near[-1] = to_shards(near[-1], range(1, half))
        rest = lax.all_to_all(rest, "seq", split_axis=0, concat_axis=0, tiled=True)
    for c in range(len(near)):
        parts = [(0, rows, runs, pieces, c, att), (begin, rows, runs, pieces, c, dq)]
        att, dq = unpack(member.reshape(1), near[c], parts)
    if whole:
        c = pieces - 1
        parts = [(0, rows, runs, pieces, c, att), (begin, rows, runs, pieces, c, dq)]
        grads = [(2 * begin + n * shard_tokens, shard_tokens, 1, 1, 0, None) for n in range(2)]
        att, dq, dk, dv = unpack_all(rest, parts + grads)
    else:
        grads = lax.psum_scatter(
            sums[0], "seq", scatter_dimension=0, tiled=True, axis_index_groups=same_head
        ).reshape(heads, shard_tokens, 2, HEAD_WIDTH)
        grads = jnp.concatenate(
            [grads[:, :, 0] * HEAD_WIDTH ** (-0.5), grads[:, :, 1]], axis=1
        ).astype(jnp.bfloat16)
        grads = to_shards(
            [lax.dynamic_index_in_dim(grads, member ^ k, 0, keepdims=False) for k in range(heads)],
            range(1, heads),
        )
        dk, dv = unpack(
            member.reshape(1),
            grads,
            [(n * shard_tokens, shard_tokens, 1, 1, 0, None) for n in range(2)],
        )
    return tuple(t.reshape(shard_tokens, heads * HEAD_WIDTH) for t in (att, dq, dk, dv))


def solution(mesh):
    return jax.shard_map(
        per_device,
        mesh=mesh,
        in_specs=(
            P(("seq", "head"), None),
            P(("seq", "head"), None),
            P(("seq", "head"), None),
            P(("seq", "head"), None),
            P("head", "seq", None),
            P(),
            P("head", "seq", None),
        ),
        out_specs=(P("seq", "head"), P("seq", "head"), P("seq", "head"), P("seq", "head")),
        check_vma=False,
    )
```

```python
import functools
import math

import jax
import jax.numpy as jnp
from jax import lax
from jax.experimental import pallas as pl
from jax.experimental.pallas import tpu as pltpu
from jax.sharding import PartitionSpec as P

HEAD_WIDTH = 128
BLOCK_TOKENS = 64
R = 3
G = 2
SLOTS = 3 + G + R
WIDE = SLOTS * BLOCK_TOKENS
UNROLL = 4
STRIP = 16
VMEM_LIMIT = 16 * 1024 * 1024
VMEM_BYTES = 64 * 1024 * 1024

keep_prob = 0.9

vmem = pl.BlockSpec(memory_space=pltpu.VMEM)
smem = pl.BlockSpec(memory_space=pltpu.SMEM)
anywhere = pl.BlockSpec(memory_space=pl.ANY)


def in_vmem(array):
    return pltpu.with_memory_space_constraint(array, pltpu.VMEM)


def in_hbm(array):
    return pltpu.with_memory_space_constraint(array, pltpu.HBM)


def copy_cost(size):
    return pl.CostEstimate(flops=0, bytes_accessed=4 * size, transcendentals=0)


def block_rows(number):
    start = number * BLOCK_TOKENS
    if not isinstance(number, int):
        start = pl.multiple_of(start, BLOCK_TOKENS)
    return pl.ds(start, BLOCK_TOKENS)


def pack_kernel(heads, groups, sources, table_rows, *refs):
    refs = list(refs)
    if table_rows:
        drop_ref, rand_ref, table = refs.pop(0), refs.pop(0), refs.pop()
    count = len(sources)
    arrays, out_ref = refs[:count], refs[count]
    wholes, packed, in_sems, out_sems = refs[count + 1 : -3], refs[-3], refs[-2], refs[-1]
    width = groups * heads * HEAD_WIDTH // 2
    loads = []
    for h in range(2):
        for n, (at, rows) in enumerate(sources):
            columns = pl.ds(h * width, width)
            loads.append(
                pltpu.make_async_copy(
                    arrays[n].at[pl.ds(at * rows, rows), columns],
                    wholes[n].at[:, columns],
                    in_sems.at[h, n],
                )
            )
    for load in loads:
        load.start()
    begin = sum(rows for _, rows in sources)
    if table_rows:
        blocks = drop_ref.shape[1]
        table[...] = jnp.zeros_like(table)
        for m in range(heads):
            table[pl.ds(0, blocks), pl.ds(0, SLOTS)] = drop_ref[m].astype(jnp.float32)
            for r in range(R):
                table[pl.ds(blocks + r, 1), pl.ds(0, blocks)] = rand_ref[
                    r, pl.ds(m, 1), :
                ].astype(jnp.float32)
            rounded = table[...].astype(jnp.bfloat16)
            for g in range(groups):
                packed[m, g, pl.ds(begin, table_rows), :] = rounded
    stores = []
    for g in range(groups):
        if g % (groups // 2) == 0:
            for n in range(count):
                loads[g // (groups // 2) * count + n].wait()
        for m in range(heads):
            begin = 0
            for n, (_, rows) in enumerate(sources):
                packed[m, g, pl.ds(begin, rows), :] = wholes[n][
                    :, pl.ds((g * heads + m) * HEAD_WIDTH, HEAD_WIDTH)
                ]
                begin += rows
        stores.append(
            pltpu.make_async_copy(packed.at[:, g], out_ref.at[:, g], out_sems.at[g])
        )
        stores[-1].start()
    for store in stores:
        store.wait()


def pack(groups, heads, sources, tables=(), table_rows=0):
    total = sum(rows for _, _, rows in sources) + table_rows
    shape = (heads, groups, total, HEAD_WIDTH)
    scratch = [
        pltpu.VMEM((rows, groups * heads * HEAD_WIDTH), jnp.bfloat16) for _, _, rows in sources
    ] + [
        pltpu.VMEM(shape, jnp.bfloat16),
        pltpu.SemaphoreType.DMA((2, len(sources))),
        pltpu.SemaphoreType.DMA((groups,)),
    ]
    if table_rows:
        scratch.append(pltpu.VMEM((table_rows, HEAD_WIDTH), jnp.float32))
    packed = pl.pallas_call(
        functools.partial(
            pack_kernel, heads, groups, tuple((at, rows) for _, at, rows in sources), table_rows
        ),
        out_shape=pltpu.HBM(shape, jnp.bfloat16),
        in_specs=[vmem] * len(tables) + [anywhere] * len(sources),
        out_specs=anywhere,
        scratch_shapes=scratch,
        compiler_params=pltpu.CompilerParams(vmem_limit_bytes=VMEM_LIMIT),
        cost_estimate=copy_cost(math.prod(shape)),
    )(*[in_hbm(t) for t in tables], *[in_hbm(a) for a, _, _ in sources])
    return packed.reshape(heads * groups, total, HEAD_WIDTH)


def unpack_kernel(parts, member_ref, *refs):
    outs = refs[len(refs) - len(parts) :]
    heads = outs[0].shape[-1] // HEAD_WIDTH
    for n in range(heads):
        k = (heads - n) % heads
        column = pl.multiple_of((member_ref[0] ^ k) * HEAD_WIDTH, HEAD_WIDTH)
        for begin, out in zip(parts, outs):
            runs, _, rows, _ = out.shape
            for i in range(runs):
                out[i, 0, :, pl.ds(column, HEAD_WIDTH)] = refs[n][pl.ds(begin + i * rows, rows), :]


def unpack(member, received, parts):
    heads = len(received)
    shapes, specs, olds, aliases, size = [], [], [], {}, 0
    for n, (_, rows, runs, pieces, piece, old) in enumerate(parts):
        shapes.append(
            jax.ShapeDtypeStruct((runs, pieces, rows, heads * HEAD_WIDTH), jnp.bfloat16)
        )
        specs.append(
            pl.BlockSpec(
                (runs, 1, rows, heads * HEAD_WIDTH),
                functools.partial(lambda piece, h: (0, piece, 0, 0), piece),
            )
        )
        size += rows * runs * heads * HEAD_WIDTH
        if old is not None:
            aliases[1 + heads + len(olds)] = n
            olds.append(old)
    return pl.pallas_call(
        functools.partial(unpack_kernel, tuple(part[0] for part in parts)),
        grid=(1,),
        out_shape=shapes,
        in_specs=[smem]
        + [pl.BlockSpec(received[0].shape, lambda h: (0, 0))] * heads
        + [pl.BlockSpec(memory_space=pl.ANY)] * len(olds),
        out_specs=specs,
        input_output_aliases=aliases,
        compiler_params=pltpu.CompilerParams(vmem_limit_bytes=VMEM_LIMIT),
        cost_estimate=copy_cost(size),
    )(member, received[0], *received[:0:-1], *olds)


def unpack_all_kernel(begins, step_heads, piece_ref, *refs):
    outs = refs[len(refs) - len(begins) :]
    for begin, out in zip(begins, outs):
        runs, _, rows, _ = out.shape
        for m in range(step_heads):
            for i in range(runs):
                out[i, 0, :, pl.ds(m * HEAD_WIDTH, HEAD_WIDTH)] = piece_ref[
                    m, pl.ds(begin + i * rows, rows), :
                ]


def unpack_all(received, parts):
    heads, total, _ = received.shape
    step_heads = 2 if heads % 2 == 0 else 1
    width = step_heads * HEAD_WIDTH
    shapes, out_specs, begins, olds, aliases = [], [], [], [], {}
    size = 0
    for n, (begin, rows, runs, pieces, piece, old) in enumerate(parts):
        begins.append(begin)
        shapes.append(
            jax.ShapeDtypeStruct((runs, pieces, rows, heads * HEAD_WIDTH), jnp.bfloat16)
        )
        out_specs.append(
            pl.BlockSpec(
                (runs, 1, rows, width), functools.partial(lambda piece, h: (0, piece, 0, h), piece)
            )
        )
        size += rows * runs * heads * HEAD_WIDTH
        if old is not None:
            aliases[1 + len(olds)] = n
            olds.append(old)
    return pl.pallas_call(
        functools.partial(unpack_all_kernel, begins, step_heads),
        grid=(heads // step_heads,),
        out_shape=shapes,
        in_specs=[pl.BlockSpec((step_heads, total, HEAD_WIDTH), lambda h: (h, 0, 0))]
        + [pl.BlockSpec(memory_space=pl.ANY)] * len(olds),
        out_specs=out_specs,
        input_output_aliases=aliases,
        compiler_params=pltpu.CompilerParams(vmem_limit_bytes=VMEM_LIMIT),
        cost_estimate=copy_cost(size),
    )(in_vmem(received), *olds)


def attention_kernel(
    last_block,
    device_blocks,
    per,
    piece,
    out_rows,
    source_rows,
    qd_rows,
    qd_begin,
    has_qd,
    has_start,
    joined,
    tokens,
    targets,
    ids_ref,
    starts_ref,
    first_ref,
    member_ref,
    drop_ref,
    kv_ref,
    *refs,
):
    refs = list(refs)
    qd_ref = refs.pop(0) if has_qd else kv_ref
    start_ref = refs.pop(0) if has_start else None
    out_refs = [refs.pop(0) for _ in range(1 if joined else targets)]
    sums_ref = None if joined else refs.pop(0)
    acc, retain, waiting, near, sems = refs[:5]
    done = refs[5] if joined else None
    earlier, start_sem = refs[-2:] if has_start else (None, None)
    scale = HEAD_WIDTH ** (-0.5)
    steps = targets * (out_rows // BLOCK_TOKENS)
    slot_of_lane = lax.broadcasted_iota(jnp.int32, (SLOTS, WIDE), 1) // BLOCK_TOKENS
    slot_row = lax.broadcasted_iota(jnp.int32, (SLOTS, WIDE), 0)
    expand = (slot_of_lane == slot_row).astype(jnp.float32)
    retain[...] = jnp.dot(
        drop_ref[...].astype(jnp.float32), expand, preferred_element_type=jnp.float32
    ) * (1.0 / keep_prob)
    acc[...] = jnp.zeros_like(acc)
    if has_start:
        fetch = pltpu.make_async_copy(start_ref, earlier, start_sem)
        fetch.start()
    lane = lax.broadcasted_iota(jnp.int32, (1, WIDE), 1)
    nt = (((1,), (1,)), ((), ()))
    tn = (((0,), (0,)), ((), ()))
    out_steps = steps // targets

    def place(i):
        if per == 1:
            source, sub = i, 0
        else:
            source, sub = lax.div(i, per), lax.rem(i, per)
        return source, sub, source * device_blocks + piece * per + sub

    def load(i):
        source, sub, j = place(i)
        starts = [starts_ref[j * SLOTS + s] for s in range(SLOTS)]
        q, do = [
            qd_ref[
                pl.ds(
                    pl.multiple_of(
                        source * qd_rows + (n * per + sub) * BLOCK_TOKENS + qd_begin, 16
                    ),
                    BLOCK_TOKENS,
                ),
                :,
            ]
            for n in range(2)
        ]
        keys, vals = [
            jnp.concatenate(
                [kv_ref[pl.ds(pl.multiple_of(r + n * tokens, 16), BLOCK_TOKENS), :] for r in starts],
                axis=0,
            )
            for n in range(2)
        ]
        return q, do, keys, vals

    def score(i):
        q, do, keys, vals = load(i)
        logits = lax.dot_general(q, keys, nt, preferred_element_type=jnp.float32)
        raw = lax.dot_general(do, vals, nt, preferred_element_type=jnp.float32)
        return logits, raw

    def factor(i, u, logits, raw):
        j = place(i)[2]
        block_id = first_ref[0] + j
        absent = ((block_id == 0) & (lane < BLOCK_TOKENS)) | (
            (block_id == last_block) & (lane >= 2 * BLOCK_TOKENS) & (lane < 3 * BLOCK_TOKENS)
        )
        keep = retain[pl.ds(j, 1), :]
        for r in range(0, BLOCK_TOKENS, STRIP):
            part = jnp.where(absent, -jnp.inf, logits[r : r + STRIP])
            top = jnp.max(part, axis=-1, keepdims=True)
            expd = jnp.exp2((part - top) * (scale / math.log(2.0)))
            probs = expd * (1.0 / jnp.sum(expd, axis=-1, keepdims=True))
            kept = probs * keep
            weighted = kept * raw[r : r + STRIP]
            delta = jnp.sum(weighted, axis=-1, keepdims=True)
            waiting[u, pl.ds(r, STRIP), :] = (weighted - probs * delta).astype(jnp.bfloat16)
            waiting[u, pl.ds(BLOCK_TOKENS + r, STRIP), :] = kept.astype(jnp.bfloat16)

    def finish(i, u):
        j = place(i)[2]
        q, do, keys, vals = load(i)
        factors = waiting[u]
        dq = jnp.dot(factors[:BLOCK_TOKENS], keys, preferred_element_type=jnp.float32) * scale
        att = jnp.dot(factors[BLOCK_TOKENS:], vals, preferred_element_type=jnp.float32)
        none = jnp.zeros_like(q)
        pair = jnp.concatenate(
            [jnp.concatenate([q, none], axis=1), jnp.concatenate([none, do], axis=1)], axis=0
        )
        terms = lax.dot_general(factors, pair, tn, preferred_element_type=jnp.float32)
        for s in range(SLOTS):
            acc[block_rows(ids_ref[j * SLOTS + s]), :] += terms[
                s * BLOCK_TOKENS : (s + 1) * BLOCK_TOKENS
            ]
        target, pos = lax.div(i, out_steps), lax.rem(i, out_steps)
        near[target, block_rows(pos), :] = att.astype(jnp.bfloat16)
        near[target, block_rows(out_steps + pos), :] = dq.astype(jnp.bfloat16)

    def step(t, carry):
        scores = [score(t * UNROLL + u) for u in range(UNROLL)]
        for u in range(UNROLL):
            finish((t - 1) * UNROLL + u, u)
        for u in range(UNROLL):
            factor(t * UNROLL + u, u, *scores[u])
        return carry

    for u in range(UNROLL):
        factor(u, u, *score(u))
    lax.fori_loop(1, steps // UNROLL, step, 0)
    for u in range(UNROLL):
        finish(steps - UNROLL + u, u)
    if has_start:
        fetch.wait()
    if joined:
        rows = acc.shape[0] // targets
        stores = []
        for target in range(targets):
            part = pl.ds(target * rows, rows)
            sums = acc[part, :]
            if has_start:
                sums += earlier[part, :]
            done[target, pl.ds(0, 2 * out_rows), :] = near[target]
            done[target, pl.ds(2 * out_rows, rows), :] = (sums[:, :HEAD_WIDTH] * scale).astype(
                jnp.bfloat16
            )
            done[target, pl.ds(2 * out_rows + rows, rows), :] = sums[:, HEAD_WIDTH:].astype(
                jnp.bfloat16
            )
            stores.append(
                pltpu.make_async_copy(done.at[target], out_refs[0].at[target], sems.at[target])
            )
            stores[-1].start()
        for store in stores:
            store.wait()
    else:
        rows = acc.shape[0] // targets
        stores = [
            pltpu.make_async_copy(
                acc.at[pl.ds(n * rows, rows), :], sums_ref.at[pl.ds(n * rows, rows), :], sems.at[n]
            )
            for n in range(targets)
        ]
        for store in stores:
            store.start()
        for k, out_ref in enumerate(out_refs):
            out_ref[...] = near[member_ref[0] ^ k]
        for store in stores:
            store.wait()


def attend(
    ids, starts, first_block, member, drop, kv, qd, qd_begin, start, piece, per, joined, device_blocks, total_blocks, tokens, targets
):
    team_blocks = drop.shape[0]
    source = kv if qd is None else qd
    steps = team_blocks * per // device_blocks
    length = total_blocks * BLOCK_TOKENS
    pairs = steps * BLOCK_TOKENS * WIDE
    accumulator = (length, 2 * HEAD_WIDTH)
    out_rows = steps * BLOCK_TOKENS // targets
    if joined:
        out_shape = [
            pltpu.HBM((targets, 2 * out_rows + 2 * length // targets, HEAD_WIDTH), jnp.bfloat16)
        ]
    else:
        out_shape = [pltpu.HBM((2 * out_rows, HEAD_WIDTH), jnp.bfloat16)] * targets
    scratch = [
        pltpu.VMEM((team_blocks, WIDE), jnp.float32),
        pltpu.VMEM((UNROLL, 2 * BLOCK_TOKENS, WIDE), jnp.bfloat16),
        pltpu.VMEM((targets, 2 * out_rows, HEAD_WIDTH), jnp.bfloat16),
    ]
    scratch = [pltpu.VMEM(accumulator, jnp.float32)] + scratch + [
        pltpu.SemaphoreType.DMA((targets,))
    ]
    if not joined:
        out_shape.append(pltpu.HBM(accumulator, jnp.float32))
    if joined:
        scratch.append(pltpu.VMEM(out_shape[0].shape, jnp.bfloat16))
    sums_bytes = 8 * length * HEAD_WIDTH
    limit = VMEM_LIMIT + 2 * (kv.size + source.size) + (1 if start is None else 2) * sums_bytes
    keep = in_vmem if 2 * limit < VMEM_BYTES else lambda t: t
    flat = [keep(t.reshape(-1, HEAD_WIDTH)) for t in (kv, qd) if t is not None]
    if start is not None:
        scratch += [pltpu.VMEM(accumulator, jnp.float32), pltpu.SemaphoreType.DMA]
    operands = flat + ([] if start is None else [in_hbm(start)])
    operand_specs = [vmem] * len(flat) + [anywhere] * (start is not None)
    return pl.pallas_call(
        functools.partial(
            attention_kernel,
            total_blocks - 1,
            device_blocks,
            per,
            piece,
            out_rows,
            kv.shape[1],
            source.shape[1],
            qd_begin,
            qd is not None,
            start is not None,
            joined,
            tokens,
            targets,
        ),
        out_shape=out_shape,
        in_specs=[smem, smem, smem, smem, vmem] + operand_specs,
        out_specs=[anywhere] if joined else [vmem] * targets + [anywhere],
        scratch_shapes=scratch,
        compiler_params=pltpu.CompilerParams(vmem_limit_bytes=limit),
        cost_estimate=pl.CostEstimate(
            flops=128 * pairs * HEAD_WIDTH,
            bytes_accessed=2 * (source.size + kv.size) + 8 * length * HEAD_WIDTH,
            transcendentals=pairs,
        ),
    )(ids, starts, first_block, member, in_hbm(drop), *operands)


def per_device(queries, keys, values, grad_out, rand_blocks, global_ids, drop_mask):
    shards = lax.axis_size("seq")
    groups = lax.axis_size("head")
    shard = lax.axis_index("seq")
    heads, shard_blocks, _ = rand_blocks.shape
    tokens = queries.shape[0]
    device_blocks = tokens // BLOCK_TOKENS
    shard_tokens = shard_blocks * BLOCK_TOKENS
    teams = shards // heads
    team, member = lax.div(shard, heads), lax.rem(shard, heads)
    team_blocks = heads * shard_blocks
    total_blocks = shards * shard_blocks
    first_block = team * team_blocks
    whole = teams == 1
    pieces = device_blocks if whole else 1
    per = device_blocks // pieces
    rows = tokens // pieces
    same_team_all = (
        None
        if whole
        else [
            [(t * heads + m) * groups + g for m in range(heads) for g in range(groups)]
            for t in range(teams)
        ]
    )
    same_head = [[t * heads + m for t in range(teams)] for m in range(heads)]

    def to_heads(packed):
        return lax.all_to_all(
            packed,
            ("seq", "head"),
            split_axis=0,
            concat_axis=0,
            tiled=True,
            axis_index_groups=same_team_all,
        )

    def to_shards(results):
        received = list(results)
        for k in reversed(range(1, heads)):
            pairs = [(s, s ^ k) for s in range(shards)]
            received[k] = lax.ppermute(results[k], "seq", pairs)
        return received

    table_rows = -(-(shard_blocks + R) // 16) * 16
    sources = [[(queries, c, rows), (grad_out, c, rows)] for c in range(pieces)]
    qd_begin = 2 * tokens
    table_begin = qd_begin + 2 * rows
    kv = to_heads(
        pack(
            groups,
            heads,
            [(keys, 0, tokens), (values, 0, tokens)] + sources[0],
            (drop_mask, rand_blocks.transpose(2, 0, 1)),
            table_rows,
        )
    )
    later = [to_heads(pack(groups, heads, each)) for each in sources[1:]]
    tables = lax.dynamic_index_in_dim(
        kv.reshape(heads, groups, -1, HEAD_WIDTH)[:, :, table_begin:],
        lax.axis_index("head"),
        axis=1,
        keepdims=False,
    ).astype(jnp.int32)
    drops = tables[:, :shard_blocks, :SLOTS].reshape(team_blocks, SLOTS)
    randoms = tables[:, shard_blocks : shard_blocks + R, :shard_blocks].transpose(0, 2, 1)
    randoms = randoms.reshape(team_blocks, R)
    qd = [None] + later
    if not whole:
        qd[0] = kv[:, qd_begin:table_begin]
        kv = lax.all_gather(kv[:, : 2 * tokens], "seq", axis=0, tiled=True, axis_index_groups=same_head)
    blocks = first_block + jnp.arange(team_blocks, dtype=jnp.int32)
    window = jnp.stack([blocks - 1, blocks, blocks + 1], axis=1)
    listed = jnp.concatenate(
        [window, jnp.broadcast_to(global_ids[None], (team_blocks, G)), randoms], axis=1
    )
    listed = jnp.clip(listed, 0, total_blocks - 1).reshape(-1)
    starts = listed // device_blocks * kv.shape[1] + listed % device_blocks * BLOCK_TOKENS
    pieces_out = []
    held = []
    sums = []
    for c in range(pieces):
        pieces_out.append(
            attend(
                listed,
                starts,
                first_block.reshape(1),
                member.reshape(1),
                drops,
                kv,
                qd[c],
                qd_begin if qd[c] is None else 0,
                sums[0] if sums else None,
                c,
                per,
                whole and c == pieces - 1,
                device_blocks,
                total_blocks,
                tokens,
                heads,
            )
        )
        sums = pieces_out[c][heads:]
        if c + 1 < pieces:
            held.append(pieces_out[c][1:heads])
    runs = shard_blocks // device_blocks
    begin = shard_tokens // pieces
    near = []
    for c, out in enumerate(pieces_out):
        if len(out) > 1:
            results = out[:heads]
            if c + 1 < pieces:
                results = [results[0], *held[c]]
            near.append(to_shards(results))
    att, dq = None, None
    if whole:
        rest = pieces_out[-1][0]
        if near:
            rest, *near[-1][heads // 2 :] = lax.optimization_barrier(
                (rest, *near[-1][heads // 2 :])
            )
        rest = lax.all_to_all(rest, "seq", split_axis=0, concat_axis=0, tiled=True)
    for c in range(len(near)):
        parts = [(0, rows, runs, pieces, c, att), (begin, rows, runs, pieces, c, dq)]
        att, dq = unpack(member.reshape(1), near[c], parts)
    if whole:
        c = pieces - 1
        parts = [(0, rows, runs, pieces, c, att), (begin, rows, runs, pieces, c, dq)]
        grads = [(2 * begin + n * shard_tokens, shard_tokens, 1, 1, 0, None) for n in range(2)]
        att, dq, dk, dv = unpack_all(rest, parts + grads)
    else:
        grads = lax.psum_scatter(
            sums[0], "seq", scatter_dimension=0, tiled=True, axis_index_groups=same_head
        ).reshape(heads, shard_tokens, 2, HEAD_WIDTH)
        grads = jnp.concatenate(
            [grads[:, :, 0] * HEAD_WIDTH ** (-0.5), grads[:, :, 1]], axis=1
        ).astype(jnp.bfloat16)
        grads = to_shards(
            [lax.dynamic_index_in_dim(grads, member ^ k, 0, keepdims=False) for k in range(heads)]
        )
        dk, dv = unpack(
            member.reshape(1),
            grads,
            [(n * shard_tokens, shard_tokens, 1, 1, 0, None) for n in range(2)],
        )
    return tuple(t.reshape(shard_tokens, heads * HEAD_WIDTH) for t in (att, dq, dk, dv))


def solution(mesh):
    return jax.shard_map(
        per_device,
        mesh=mesh,
        in_specs=(
            P(("seq", "head"), None),
            P(("seq", "head"), None),
            P(("seq", "head"), None),
            P(("seq", "head"), None),
            P("head", "seq", None),
            P(),
            P("head", "seq", None),
        ),
        out_specs=(P("seq", "head"), P("seq", "head"), P("seq", "head"), P("seq", "head")),
        check_vma=False,
    )
```

```python
import functools
import math

import jax
import jax.numpy as jnp
from jax import lax
from jax.experimental import pallas as pl
from jax.experimental.pallas import tpu as pltpu
from jax.sharding import PartitionSpec as P

HEAD_WIDTH = 128
BLOCK_TOKENS = 64
R = 3
G = 2
SLOTS = 3 + G + R
WIDE = SLOTS * BLOCK_TOKENS
UNROLL = 4
STRIP = 16
VMEM_LIMIT = 16 * 1024 * 1024
VMEM_BYTES = 64 * 1024 * 1024

keep_prob = 0.9

vmem = pl.BlockSpec(memory_space=pltpu.VMEM)
smem = pl.BlockSpec(memory_space=pltpu.SMEM)
anywhere = pl.BlockSpec(memory_space=pl.ANY)


def in_vmem(array):
    return pltpu.with_memory_space_constraint(array, pltpu.VMEM)


def in_hbm(array):
    return pltpu.with_memory_space_constraint(array, pltpu.HBM)


def copy_cost(size):
    return pl.CostEstimate(flops=0, bytes_accessed=4 * size, transcendentals=0)


def block_rows(number):
    start = number * BLOCK_TOKENS
    if not isinstance(number, int):
        start = pl.multiple_of(start, BLOCK_TOKENS)
    return pl.ds(start, BLOCK_TOKENS)


def pack_kernel(heads, groups, sources, table_rows, *refs):
    refs = list(refs)
    if table_rows:
        drop_hbm, rand_hbm = refs.pop(0), refs.pop(0)
        table, drop_ref, rand_ref, table_sems = refs[-4:]
        refs = refs[:-4]
    count = len(sources)
    arrays, out_ref = refs[:count], refs[count]
    wholes, packed, in_sems, out_sems = refs[count + 1 : -3], refs[-3], refs[-2], refs[-1]
    width = groups * heads * HEAD_WIDTH // 2
    loads = []
    for h in range(2):
        for n, (at, rows) in enumerate(sources):
            columns = pl.ds(h * width, width)
            loads.append(
                pltpu.make_async_copy(
                    arrays[n].at[pl.ds(at * rows, rows), columns],
                    wholes[n].at[:, columns],
                    in_sems.at[h, n],
                )
            )
    for load in loads:
        load.start()
    begin = sum(rows for _, rows in sources)
    if table_rows:
        fetches = [
            pltpu.make_async_copy(drop_hbm, drop_ref, table_sems.at[0]),
            pltpu.make_async_copy(rand_hbm, rand_ref, table_sems.at[1]),
        ]
        for fetch in fetches:
            fetch.start()
        for fetch in fetches:
            fetch.wait()
        blocks = drop_ref.shape[1]
        table[...] = jnp.zeros_like(table)
        for m in range(heads):
            table[pl.ds(0, blocks), pl.ds(0, SLOTS)] = drop_ref[m].astype(jnp.float32)
            for r in range(R):
                table[pl.ds(blocks + r, 1), pl.ds(0, blocks)] = rand_ref[
                    r, pl.ds(m, 1), :
                ].astype(jnp.float32)
            rounded = table[...].astype(jnp.bfloat16)
            for g in range(groups):
                packed[m, g, pl.ds(begin, table_rows), :] = rounded
    stores = []
    for g in range(groups):
        if g % (groups // 2) == 0:
            for n in range(count):
                loads[g // (groups // 2) * count + n].wait()
        for m in range(heads):
            begin = 0
            for n, (_, rows) in enumerate(sources):
                packed[m, g, pl.ds(begin, rows), :] = wholes[n][
                    :, pl.ds((g * heads + m) * HEAD_WIDTH, HEAD_WIDTH)
                ]
                begin += rows
        stores.append(
            pltpu.make_async_copy(packed.at[:, g], out_ref.at[:, g], out_sems.at[g])
        )
        stores[-1].start()
    for store in stores:
        store.wait()


def pack(groups, heads, sources, tables=(), table_rows=0):
    total = sum(rows for _, _, rows in sources) + table_rows
    shape = (heads, groups, total, HEAD_WIDTH)
    scratch = [
        pltpu.VMEM((rows, groups * heads * HEAD_WIDTH), jnp.bfloat16) for _, _, rows in sources
    ] + [
        pltpu.VMEM(shape, jnp.bfloat16),
        pltpu.SemaphoreType.DMA((2, len(sources))),
        pltpu.SemaphoreType.DMA((groups,)),
    ]
    if table_rows:
        scratch.append(pltpu.VMEM((table_rows, HEAD_WIDTH), jnp.float32))
        scratch += [pltpu.VMEM(t.shape, t.dtype) for t in tables]
        scratch.append(pltpu.SemaphoreType.DMA((len(tables),)))
    packed = pl.pallas_call(
        functools.partial(
            pack_kernel, heads, groups, tuple((at, rows) for _, at, rows in sources), table_rows
        ),
        out_shape=pltpu.HBM(shape, jnp.bfloat16),
        in_specs=[anywhere] * (len(tables) + len(sources)),
        out_specs=anywhere,
        scratch_shapes=scratch,
        compiler_params=pltpu.CompilerParams(vmem_limit_bytes=VMEM_LIMIT),
        cost_estimate=copy_cost(math.prod(shape)),
    )(*[in_hbm(t) for t in tables], *[in_hbm(a) for a, _, _ in sources])
    return packed.reshape(heads * groups, total, HEAD_WIDTH)


def unpack_kernel(parts, member_ref, *refs):
    outs = refs[len(refs) - len(parts) :]
    heads = outs[0].shape[-1] // HEAD_WIDTH
    for n in range(heads):
        k = (heads - n) % heads
        column = pl.multiple_of((member_ref[0] ^ k) * HEAD_WIDTH, HEAD_WIDTH)
        for begin, out in zip(parts, outs):
            runs, _, rows, _ = out.shape
            for i in range(runs):
                out[i, 0, :, pl.ds(column, HEAD_WIDTH)] = refs[n][pl.ds(begin + i * rows, rows), :]


def unpack(member, received, parts):
    heads = len(received)
    shapes, specs, olds, aliases, size = [], [], [], {}, 0
    for n, (_, rows, runs, pieces, piece, old) in enumerate(parts):
        shapes.append(
            jax.ShapeDtypeStruct((runs, pieces, rows, heads * HEAD_WIDTH), jnp.bfloat16)
        )
        specs.append(
            pl.BlockSpec(
                (runs, 1, rows, heads * HEAD_WIDTH),
                functools.partial(lambda piece, h: (0, piece, 0, 0), piece),
            )
        )
        size += rows * runs * heads * HEAD_WIDTH
        if old is not None:
            aliases[1 + heads + len(olds)] = n
            olds.append(old)
    return pl.pallas_call(
        functools.partial(unpack_kernel, tuple(part[0] for part in parts)),
        grid=(1,),
        out_shape=shapes,
        in_specs=[smem]
        + [pl.BlockSpec(received[0].shape, lambda h: (0, 0))] * heads
        + [pl.BlockSpec(memory_space=pl.ANY)] * len(olds),
        out_specs=specs,
        input_output_aliases=aliases,
        compiler_params=pltpu.CompilerParams(vmem_limit_bytes=VMEM_LIMIT),
        cost_estimate=copy_cost(size),
    )(member, received[0], *received[:0:-1], *olds)


def unpack_all_kernel(parts, piece_ref, *refs):
    sems = refs[-1]
    stages = refs[-1 - len(parts) : -1]
    outs = refs[-1 - 2 * len(parts) : -1 - len(parts)]
    stores = []
    for (begin, rows, runs, _, piece), stage, out in zip(parts, stages, outs):
        for i in range(runs):
            for m in range(piece_ref.shape[0]):
                stage[i, :, pl.ds(m * HEAD_WIDTH, HEAD_WIDTH)] = piece_ref[
                    m, pl.ds(begin + i * rows, rows), :
                ]
            stores.append(
                pltpu.make_async_copy(stage.at[i], out.at[i, piece], sems.at[len(stores)])
            )
            stores[-1].start()
    for store in stores:
        store.wait()


def unpack_all(received, parts):
    heads = received.shape[0]
    shapes, stages, olds, aliases, count = [], [], [], {}, 0
    for n, (_, rows, runs, pieces, _, old) in enumerate(parts):
        shapes.append(pltpu.HBM((runs, pieces, rows, heads * HEAD_WIDTH), jnp.bfloat16))
        stages.append(pltpu.VMEM((runs, rows, heads * HEAD_WIDTH), jnp.bfloat16))
        count += runs
        if old is not None:
            aliases[1 + len(olds)] = n
            olds.append(old)
    return pl.pallas_call(
        functools.partial(unpack_all_kernel, tuple(part[:-1] for part in parts)),
        out_shape=shapes,
        in_specs=[vmem] + [anywhere] * len(olds),
        out_specs=[anywhere] * len(shapes),
        input_output_aliases=aliases,
        scratch_shapes=stages + [pltpu.SemaphoreType.DMA((count,))],
        compiler_params=pltpu.CompilerParams(vmem_limit_bytes=VMEM_LIMIT),
        cost_estimate=copy_cost(received.size),
    )(in_vmem(received), *olds)


def attention_kernel(
    last_block,
    device_blocks,
    per,
    piece,
    out_rows,
    source_rows,
    qd_rows,
    qd_begin,
    has_qd,
    has_start,
    joined,
    tokens,
    targets,
    ids_ref,
    starts_ref,
    first_ref,
    member_ref,
    drop_ref,
    kv_ref,
    *refs,
):
    refs = list(refs)
    qd_ref = refs.pop(0) if has_qd else kv_ref
    start_ref = refs.pop(0) if has_start else None
    out_refs = [refs.pop(0) for _ in range(1 if joined else targets)]
    sums_ref = None if joined else refs.pop(0)
    acc, retain, waiting, near, sems = refs[:5]
    done = refs[5] if joined else None
    earlier, start_sem = refs[-2:] if has_start else (None, None)
    scale = HEAD_WIDTH ** (-0.5)
    steps = targets * (out_rows // BLOCK_TOKENS)
    slot_of_lane = lax.broadcasted_iota(jnp.int32, (SLOTS, WIDE), 1) // BLOCK_TOKENS
    slot_row = lax.broadcasted_iota(jnp.int32, (SLOTS, WIDE), 0)
    expand = (slot_of_lane == slot_row).astype(jnp.float32)
    retain[...] = jnp.dot(
        drop_ref[...].astype(jnp.float32), expand, preferred_element_type=jnp.float32
    ) * (1.0 / keep_prob)
    acc[...] = jnp.zeros_like(acc)
    if has_start:
        fetch = pltpu.make_async_copy(start_ref, earlier, start_sem)
        fetch.start()
    lane = lax.broadcasted_iota(jnp.int32, (1, WIDE), 1)
    nt = (((1,), (1,)), ((), ()))
    tn = (((0,), (0,)), ((), ()))
    out_steps = steps // targets

    def place(i):
        if per == 1:
            source, sub = i, 0
        else:
            source, sub = lax.div(i, per), lax.rem(i, per)
        return source, sub, source * device_blocks + piece * per + sub

    def load(i):
        source, sub, j = place(i)
        starts = [starts_ref[j * SLOTS + s] for s in range(SLOTS)]
        q, do = [
            qd_ref[
                pl.ds(
                    pl.multiple_of(
                        source * qd_rows + (n * per + sub) * BLOCK_TOKENS + qd_begin, 16
                    ),
                    BLOCK_TOKENS,
                ),
                :,
            ]
            for n in range(2)
        ]
        keys, vals = [
            jnp.concatenate(
                [kv_ref[pl.ds(pl.multiple_of(r + n * tokens, 16), BLOCK_TOKENS), :] for r in starts],
                axis=0,
            )
            for n in range(2)
        ]
        return q, do, keys, vals

    def score(i):
        q, do, keys, vals = load(i)
        logits = lax.dot_general(q, keys, nt, preferred_element_type=jnp.float32)
        raw = lax.dot_general(do, vals, nt, preferred_element_type=jnp.float32)
        return logits, raw

    def factor(i, u, logits, raw):
        j = place(i)[2]
        block_id = first_ref[0] + j
        absent = ((block_id == 0) & (lane < BLOCK_TOKENS)) | (
            (block_id == last_block) & (lane >= 2 * BLOCK_TOKENS) & (lane < 3 * BLOCK_TOKENS)
        )
        keep = retain[pl.ds(j, 1), :]
        for r in range(0, BLOCK_TOKENS, STRIP):
            part = jnp.where(absent, -jnp.inf, logits[r : r + STRIP])
            top = jnp.max(part, axis=-1, keepdims=True)
            expd = jnp.exp2((part - top) * (scale / math.log(2.0)))
            probs = expd * (1.0 / jnp.sum(expd, axis=-1, keepdims=True))
            kept = probs * keep
            weighted = kept * raw[r : r + STRIP]
            delta = jnp.sum(weighted, axis=-1, keepdims=True)
            waiting[u, pl.ds(r, STRIP), :] = (weighted - probs * delta).astype(jnp.bfloat16)
            waiting[u, pl.ds(BLOCK_TOKENS + r, STRIP), :] = kept.astype(jnp.bfloat16)

    def finish(i, u):
        j = place(i)[2]
        q, do, keys, vals = load(i)
        factors = waiting[u]
        dq = jnp.dot(factors[:BLOCK_TOKENS], keys, preferred_element_type=jnp.float32) * scale
        att = jnp.dot(factors[BLOCK_TOKENS:], vals, preferred_element_type=jnp.float32)
        none = jnp.zeros_like(q)
        pair = jnp.concatenate(
            [jnp.concatenate([q, none], axis=1), jnp.concatenate([none, do], axis=1)], axis=0
        )
        terms = lax.dot_general(factors, pair, tn, preferred_element_type=jnp.float32)
        for s in range(SLOTS):
            acc[block_rows(ids_ref[j * SLOTS + s]), :] += terms[
                s * BLOCK_TOKENS : (s + 1) * BLOCK_TOKENS
            ]
        target, pos = lax.div(i, out_steps), lax.rem(i, out_steps)
        near[target, block_rows(pos), :] = att.astype(jnp.bfloat16)
        near[target, block_rows(out_steps + pos), :] = dq.astype(jnp.bfloat16)

    def step(t, carry):
        scores = [score(t * UNROLL + u) for u in range(UNROLL)]
        for u in range(UNROLL):
            finish((t - 1) * UNROLL + u, u)
        for u in range(UNROLL):
            factor(t * UNROLL + u, u, *scores[u])
        return carry

    for u in range(UNROLL):
        factor(u, u, *score(u))
    lax.fori_loop(1, steps // UNROLL, step, 0)
    for u in range(UNROLL):
        finish(steps - UNROLL + u, u)
    if has_start:
        fetch.wait()
    if joined:
        rows = acc.shape[0] // targets
        stores = []
        for target in range(targets):
            part = pl.ds(target * rows, rows)
            sums = acc[part, :]
            if has_start:
                sums += earlier[part, :]
            done[target, pl.ds(0, 2 * out_rows), :] = near[target]
            done[target, pl.ds(2 * out_rows, rows), :] = (sums[:, :HEAD_WIDTH] * scale).astype(
                jnp.bfloat16
            )
            done[target, pl.ds(2 * out_rows + rows, rows), :] = sums[:, HEAD_WIDTH:].astype(
                jnp.bfloat16
            )
            stores.append(
                pltpu.make_async_copy(done.at[target], out_refs[0].at[target], sems.at[target])
            )
            stores[-1].start()
        for store in stores:
            store.wait()
    else:
        rows = acc.shape[0] // targets
        stores = [
            pltpu.make_async_copy(
                acc.at[pl.ds(n * rows, rows), :], sums_ref.at[pl.ds(n * rows, rows), :], sems.at[n]
            )
            for n in range(targets)
        ]
        for store in stores:
            store.start()
        for k, out_ref in enumerate(out_refs):
            out_ref[...] = near[member_ref[0] ^ k]
        for store in stores:
            store.wait()


def attend(
    ids, starts, first_block, member, drop, kv, qd, qd_begin, start, piece, per, joined, device_blocks, total_blocks, tokens, targets
):
    team_blocks = drop.shape[0]
    source = kv if qd is None else qd
    steps = team_blocks * per // device_blocks
    length = total_blocks * BLOCK_TOKENS
    pairs = steps * BLOCK_TOKENS * WIDE
    accumulator = (length, 2 * HEAD_WIDTH)
    out_rows = steps * BLOCK_TOKENS // targets
    if joined:
        out_shape = [
            pltpu.HBM((targets, 2 * out_rows + 2 * length // targets, HEAD_WIDTH), jnp.bfloat16)
        ]
    else:
        out_shape = [pltpu.HBM((2 * out_rows, HEAD_WIDTH), jnp.bfloat16)] * targets
    scratch = [
        pltpu.VMEM((team_blocks, WIDE), jnp.float32),
        pltpu.VMEM((UNROLL, 2 * BLOCK_TOKENS, WIDE), jnp.bfloat16),
        pltpu.VMEM((targets, 2 * out_rows, HEAD_WIDTH), jnp.bfloat16),
    ]
    scratch = [pltpu.VMEM(accumulator, jnp.float32)] + scratch + [
        pltpu.SemaphoreType.DMA((targets,))
    ]
    if not joined:
        out_shape.append(pltpu.HBM(accumulator, jnp.float32))
    if joined:
        scratch.append(pltpu.VMEM(out_shape[0].shape, jnp.bfloat16))
    sums_bytes = 8 * length * HEAD_WIDTH
    limit = VMEM_LIMIT + 2 * (kv.size + source.size) + (1 if start is None else 2) * sums_bytes
    keep = in_vmem if 2 * limit < VMEM_BYTES else lambda t: t
    flat = [keep(t.reshape(-1, HEAD_WIDTH)) for t in (kv, qd) if t is not None]
    if start is not None:
        scratch += [pltpu.VMEM(accumulator, jnp.float32), pltpu.SemaphoreType.DMA]
    operands = flat + ([] if start is None else [in_hbm(start)])
    operand_specs = [vmem] * len(flat) + [anywhere] * (start is not None)
    return pl.pallas_call(
        functools.partial(
            attention_kernel,
            total_blocks - 1,
            device_blocks,
            per,
            piece,
            out_rows,
            kv.shape[1],
            source.shape[1],
            qd_begin,
            qd is not None,
            start is not None,
            joined,
            tokens,
            targets,
        ),
        out_shape=out_shape,
        in_specs=[smem, smem, smem, smem, vmem] + operand_specs,
        out_specs=[anywhere] if joined else [vmem] * targets + [anywhere],
        scratch_shapes=scratch,
        compiler_params=pltpu.CompilerParams(vmem_limit_bytes=limit),
        cost_estimate=pl.CostEstimate(
            flops=128 * pairs * HEAD_WIDTH,
            bytes_accessed=2 * (source.size + kv.size) + 8 * length * HEAD_WIDTH,
            transcendentals=pairs,
        ),
    )(ids, starts, first_block, member, in_hbm(drop), *operands)


def per_device(queries, keys, values, grad_out, rand_blocks, global_ids, drop_mask):
    shards = lax.axis_size("seq")
    groups = lax.axis_size("head")
    shard = lax.axis_index("seq")
    heads, shard_blocks, _ = rand_blocks.shape
    tokens = queries.shape[0]
    device_blocks = tokens // BLOCK_TOKENS
    shard_tokens = shard_blocks * BLOCK_TOKENS
    teams = shards // heads
    team, member = lax.div(shard, heads), lax.rem(shard, heads)
    team_blocks = heads * shard_blocks
    total_blocks = shards * shard_blocks
    first_block = team * team_blocks
    whole = teams == 1
    pieces = device_blocks if whole else 1
    per = device_blocks // pieces
    rows = tokens // pieces
    same_team_all = (
        None
        if whole
        else [
            [(t * heads + m) * groups + g for m in range(heads) for g in range(groups)]
            for t in range(teams)
        ]
    )
    same_head = [[t * heads + m for t in range(teams)] for m in range(heads)]

    def to_heads(packed):
        return lax.all_to_all(
            packed,
            ("seq", "head"),
            split_axis=0,
            concat_axis=0,
            tiled=True,
            axis_index_groups=same_team_all,
        )

    def to_shards(results):
        received = list(results)
        for k in reversed(range(1, heads)):
            pairs = [(s, s ^ k) for s in range(shards)]
            received[k] = lax.ppermute(results[k], "seq", pairs)
        return received

    table_rows = -(-(shard_blocks + R) // 16) * 16
    sources = [[(queries, c, rows), (grad_out, c, rows)] for c in range(pieces)]
    qd_begin = 2 * tokens
    table_begin = qd_begin + 2 * rows
    kv = to_heads(
        pack(
            groups,
            heads,
            [(keys, 0, tokens), (values, 0, tokens)] + sources[0],
            (drop_mask, rand_blocks.transpose(2, 0, 1)),
            table_rows,
        )
    )
    later = [to_heads(pack(groups, heads, each)) for each in sources[1:]]
    tables = lax.dynamic_index_in_dim(
        kv.reshape(heads, groups, -1, HEAD_WIDTH)[:, :, table_begin:],
        lax.axis_index("head"),
        axis=1,
        keepdims=False,
    ).astype(jnp.int32)
    drops = tables[:, :shard_blocks, :SLOTS].reshape(team_blocks, SLOTS)
    randoms = tables[:, shard_blocks : shard_blocks + R, :shard_blocks].transpose(0, 2, 1)
    randoms = randoms.reshape(team_blocks, R)
    qd = [None] + later
    if not whole:
        qd[0] = kv[:, qd_begin:table_begin]
        kv = lax.all_gather(kv[:, : 2 * tokens], "seq", axis=0, tiled=True, axis_index_groups=same_head)
    blocks = first_block + jnp.arange(team_blocks, dtype=jnp.int32)
    window = jnp.stack([blocks - 1, blocks, blocks + 1], axis=1)
    listed = jnp.concatenate(
        [window, jnp.broadcast_to(global_ids[None], (team_blocks, G)), randoms], axis=1
    )
    listed = jnp.clip(listed, 0, total_blocks - 1).reshape(-1)
    starts = listed // device_blocks * kv.shape[1] + listed % device_blocks * BLOCK_TOKENS
    pieces_out = []
    held = []
    sums = []
    for c in range(pieces):
        pieces_out.append(
            attend(
                listed,
                starts,
                first_block.reshape(1),
                member.reshape(1),
                drops,
                kv,
                qd[c],
                qd_begin if qd[c] is None else 0,
                sums[0] if sums else None,
                c,
                per,
                whole and c == pieces - 1,
                device_blocks,
                total_blocks,
                tokens,
                heads,
            )
        )
        sums = pieces_out[c][heads:]
        if c + 1 < pieces:
            held.append(pieces_out[c][1:heads])
    runs = shard_blocks // device_blocks
    begin = shard_tokens // pieces
    near = []
    for c, out in enumerate(pieces_out):
        if len(out) > 1:
            results = out[:heads]
            if c + 1 < pieces:
                results = [results[0], *held[c]]
            near.append(to_shards(results))
    att, dq = None, None
    if whole:
        rest = pieces_out[-1][0]
        if near:
            rest, *near[-1][heads // 2 :] = lax.optimization_barrier(
                (rest, *near[-1][heads // 2 :])
            )
        rest = lax.all_to_all(rest, "seq", split_axis=0, concat_axis=0, tiled=True)
    for c in range(len(near)):
        parts = [(0, rows, runs, pieces, c, att), (begin, rows, runs, pieces, c, dq)]
        att, dq = unpack(member.reshape(1), near[c], parts)
    if whole:
        c = pieces - 1
        parts = [(0, rows, runs, pieces, c, att), (begin, rows, runs, pieces, c, dq)]
        grads = [
            (2 * begin + n * shard_tokens, shard_tokens // runs, runs, 1, 0, None) for n in range(2)
        ]
        att, dq, dk, dv = unpack_all(rest, parts + grads)
    else:
        grads = lax.psum_scatter(
            sums[0], "seq", scatter_dimension=0, tiled=True, axis_index_groups=same_head
        ).reshape(heads, shard_tokens, 2, HEAD_WIDTH)
        grads = jnp.concatenate(
            [grads[:, :, 0] * HEAD_WIDTH ** (-0.5), grads[:, :, 1]], axis=1
        ).astype(jnp.bfloat16)
        grads = to_shards(
            [lax.dynamic_index_in_dim(grads, member ^ k, 0, keepdims=False) for k in range(heads)]
        )
        dk, dv = unpack(
            member.reshape(1),
            grads,
            [(n * shard_tokens, shard_tokens, 1, 1, 0, None) for n in range(2)],
        )
    return tuple(t.reshape(shard_tokens, heads * HEAD_WIDTH) for t in (att, dq, dk, dv))


def solution(mesh):
    return jax.shard_map(
        per_device,
        mesh=mesh,
        in_specs=(
            P(("seq", "head"), None),
            P(("seq", "head"), None),
            P(("seq", "head"), None),
            P(("seq", "head"), None),
            P("head", "seq", None),
            P(),
            P("head", "seq", None),
        ),
        out_specs=(P("seq", "head"), P("seq", "head"), P("seq", "head"), P("seq", "head")),
        check_vma=False,
    )
```

```python
import functools
import math

import jax
import jax.numpy as jnp
from jax import lax
from jax.experimental import pallas as pl
from jax.experimental.pallas import tpu as pltpu
from jax.sharding import PartitionSpec as P

HEAD_WIDTH = 128
BLOCK_TOKENS = 64
R = 3
G = 2
SLOTS = 3 + G + R
WIDE = SLOTS * BLOCK_TOKENS
UNROLL = 8
STRIP = 16
VMEM_LIMIT = 16 * 1024 * 1024
VMEM_BYTES = 64 * 1024 * 1024

keep_prob = 0.9

vmem = pl.BlockSpec(memory_space=pltpu.VMEM)
smem = pl.BlockSpec(memory_space=pltpu.SMEM)
anywhere = pl.BlockSpec(memory_space=pl.ANY)


def in_vmem(array):
    return pltpu.with_memory_space_constraint(array, pltpu.VMEM)


def in_hbm(array):
    return pltpu.with_memory_space_constraint(array, pltpu.HBM)


def copy_cost(size):
    return pl.CostEstimate(flops=0, bytes_accessed=4 * size, transcendentals=0)


def block_rows(number):
    start = number * BLOCK_TOKENS
    if not isinstance(number, int):
        start = pl.multiple_of(start, BLOCK_TOKENS)
    return pl.ds(start, BLOCK_TOKENS)


def pack_kernel(heads, groups, sources, table_rows, *refs):
    refs = list(refs)
    if table_rows:
        drop_hbm, rand_hbm = refs.pop(0), refs.pop(0)
        table, drop_ref, rand_ref, table_sems = refs[-4:]
        refs = refs[:-4]
    count = len(sources)
    arrays, out_ref = refs[:count], refs[count]
    wholes, packed, in_sems, out_sems = refs[count + 1 : -3], refs[-3], refs[-2], refs[-1]
    width = heads * HEAD_WIDTH
    loads = []
    for h in range(groups):
        for n, (at, rows) in enumerate(sources):
            columns = pl.ds(h * width, width)
            loads.append(
                pltpu.make_async_copy(
                    arrays[n].at[pl.ds(at * rows, rows), columns],
                    wholes[n].at[:, columns],
                    in_sems.at[h, n],
                )
            )
    for load in loads:
        load.start()
    begin = sum(rows for _, rows in sources)
    if table_rows:
        fetches = [
            pltpu.make_async_copy(drop_hbm, drop_ref, table_sems.at[0]),
            pltpu.make_async_copy(rand_hbm, rand_ref, table_sems.at[1]),
        ]
        for fetch in fetches:
            fetch.start()
        for fetch in fetches:
            fetch.wait()
        blocks = drop_ref.shape[1]
        table[...] = jnp.zeros_like(table)
        for m in range(heads):
            table[pl.ds(0, blocks), pl.ds(0, SLOTS)] = drop_ref[m].astype(jnp.float32)
            for r in range(R):
                table[pl.ds(blocks + r, 1), pl.ds(0, blocks)] = rand_ref[
                    r, pl.ds(m, 1), :
                ].astype(jnp.float32)
            rounded = table[...].astype(jnp.bfloat16)
            for g in range(groups):
                packed[m, g, pl.ds(begin, table_rows), :] = rounded
    stores = []
    for g in range(groups):
        for n in range(count):
            loads[g * count + n].wait()
        for m in range(heads):
            begin = 0
            for n, (_, rows) in enumerate(sources):
                packed[m, g, pl.ds(begin, rows), :] = wholes[n][
                    :, pl.ds((g * heads + m) * HEAD_WIDTH, HEAD_WIDTH)
                ]
                begin += rows
        stores.append(
            pltpu.make_async_copy(packed.at[:, g], out_ref.at[:, g], out_sems.at[g])
        )
        stores[-1].start()
    for store in stores:
        store.wait()


def pack(groups, heads, sources, tables=(), table_rows=0):
    total = sum(rows for _, _, rows in sources) + table_rows
    shape = (heads, groups, total, HEAD_WIDTH)
    scratch = [
        pltpu.VMEM((rows, groups * heads * HEAD_WIDTH), jnp.bfloat16) for _, _, rows in sources
    ] + [
        pltpu.VMEM(shape, jnp.bfloat16),
        pltpu.SemaphoreType.DMA((groups, len(sources))),
        pltpu.SemaphoreType.DMA((groups,)),
    ]
    if table_rows:
        scratch.append(pltpu.VMEM((table_rows, HEAD_WIDTH), jnp.float32))
        scratch += [pltpu.VMEM(t.shape, t.dtype) for t in tables]
        scratch.append(pltpu.SemaphoreType.DMA((len(tables),)))
    packed = pl.pallas_call(
        functools.partial(
            pack_kernel, heads, groups, tuple((at, rows) for _, at, rows in sources), table_rows
        ),
        out_shape=pltpu.HBM(shape, jnp.bfloat16),
        in_specs=[anywhere] * (len(tables) + len(sources)),
        out_specs=anywhere,
        scratch_shapes=scratch,
        compiler_params=pltpu.CompilerParams(vmem_limit_bytes=VMEM_LIMIT),
        cost_estimate=copy_cost(math.prod(shape)),
    )(*[in_hbm(t) for t in tables], *[in_hbm(a) for a, _, _ in sources])
    return packed.reshape(heads * groups, total, HEAD_WIDTH)


def unpack_kernel(parts, member_ref, *refs):
    outs = refs[len(refs) - len(parts) :]
    heads = outs[0].shape[-1] // HEAD_WIDTH
    for n in range(heads):
        k = (heads - n) % heads
        column = pl.multiple_of((member_ref[0] ^ k) * HEAD_WIDTH, HEAD_WIDTH)
        for begin, out in zip(parts, outs):
            runs, _, rows, _ = out.shape
            for i in range(runs):
                out[i, 0, :, pl.ds(column, HEAD_WIDTH)] = refs[n][pl.ds(begin + i * rows, rows), :]


def unpack(member, received, parts):
    heads = len(received)
    shapes, specs, olds, aliases, size = [], [], [], {}, 0
    for n, (_, rows, runs, pieces, piece, old) in enumerate(parts):
        shapes.append(
            jax.ShapeDtypeStruct((runs, pieces, rows, heads * HEAD_WIDTH), jnp.bfloat16)
        )
        specs.append(
            pl.BlockSpec(
                (runs, 1, rows, heads * HEAD_WIDTH),
                functools.partial(lambda piece, h: (0, piece, 0, 0), piece),
            )
        )
        size += rows * runs * heads * HEAD_WIDTH
        if old is not None:
            aliases[1 + heads + len(olds)] = n
            olds.append(old)
    return pl.pallas_call(
        functools.partial(unpack_kernel, tuple(part[0] for part in parts)),
        grid=(1,),
        out_shape=shapes,
        in_specs=[smem]
        + [pl.BlockSpec(received[0].shape, lambda h: (0, 0))] * heads
        + [pl.BlockSpec(memory_space=pl.ANY)] * len(olds),
        out_specs=specs,
        input_output_aliases=aliases,
        compiler_params=pltpu.CompilerParams(vmem_limit_bytes=VMEM_LIMIT),
        cost_estimate=copy_cost(size),
    )(member, received[0], *received[:0:-1], *olds)


def unpack_all_kernel(parts, piece_ref, *refs):
    sems = refs[-1]
    stages = refs[-1 - len(parts) : -1]
    outs = refs[-1 - 2 * len(parts) : -1 - len(parts)]
    stores = []
    for (begin, rows, runs, _, piece), stage, out in zip(parts, stages, outs):
        for i in range(runs):
            for m in range(piece_ref.shape[0]):
                stage[i, :, pl.ds(m * HEAD_WIDTH, HEAD_WIDTH)] = piece_ref[
                    m, pl.ds(begin + i * rows, rows), :
                ]
            stores.append(
                pltpu.make_async_copy(stage.at[i], out.at[i, piece], sems.at[len(stores)])
            )
            stores[-1].start()
    for store in stores:
        store.wait()


def unpack_all(received, parts):
    heads = received.shape[0]
    shapes, stages, olds, aliases, count = [], [], [], {}, 0
    for n, (_, rows, runs, pieces, _, old) in enumerate(parts):
        shapes.append(pltpu.HBM((runs, pieces, rows, heads * HEAD_WIDTH), jnp.bfloat16))
        stages.append(pltpu.VMEM((runs, rows, heads * HEAD_WIDTH), jnp.bfloat16))
        count += runs
        if old is not None:
            aliases[1 + len(olds)] = n
            olds.append(old)
    return pl.pallas_call(
        functools.partial(unpack_all_kernel, tuple(part[:-1] for part in parts)),
        out_shape=shapes,
        in_specs=[vmem] + [anywhere] * len(olds),
        out_specs=[anywhere] * len(shapes),
        input_output_aliases=aliases,
        scratch_shapes=stages + [pltpu.SemaphoreType.DMA((count,))],
        compiler_params=pltpu.CompilerParams(vmem_limit_bytes=VMEM_LIMIT),
        cost_estimate=copy_cost(received.size),
    )(in_vmem(received), *olds)


def attention_kernel(
    last_block,
    device_blocks,
    per,
    piece,
    out_rows,
    source_rows,
    qd_rows,
    qd_begin,
    has_qd,
    has_start,
    joined,
    tokens,
    targets,
    ids_ref,
    starts_ref,
    first_ref,
    member_ref,
    drop_ref,
    kv_ref,
    *refs,
):
    refs = list(refs)
    qd_ref = refs.pop(0) if has_qd else kv_ref
    start_ref = refs.pop(0) if has_start else None
    out_refs = [refs.pop(0) for _ in range(1 if joined else targets)]
    sums_ref = None if joined else refs.pop(0)
    acc, retain, waiting, near, sems = refs[:5]
    done = refs[5] if joined else None
    earlier, start_sem = refs[-2:] if has_start else (None, None)
    scale = HEAD_WIDTH ** (-0.5)
    steps = targets * (out_rows // BLOCK_TOKENS)
    slot_of_lane = lax.broadcasted_iota(jnp.int32, (SLOTS, WIDE), 1) // BLOCK_TOKENS
    slot_row = lax.broadcasted_iota(jnp.int32, (SLOTS, WIDE), 0)
    expand = (slot_of_lane == slot_row).astype(jnp.float32)
    retain[...] = jnp.dot(
        drop_ref[...].astype(jnp.float32), expand, preferred_element_type=jnp.float32
    ) * (1.0 / keep_prob)
    acc[...] = jnp.zeros_like(acc)
    if has_start:
        fetch = pltpu.make_async_copy(start_ref, earlier, start_sem)
        fetch.start()
    lane = lax.broadcasted_iota(jnp.int32, (1, WIDE), 1)
    nt = (((1,), (1,)), ((), ()))
    tn = (((0,), (0,)), ((), ()))
    out_steps = steps // targets

    def place(i):
        if per == 1:
            source, sub = i, 0
        else:
            source, sub = lax.div(i, per), lax.rem(i, per)
        return source, sub, source * device_blocks + piece * per + sub

    def load(i):
        source, sub, j = place(i)
        starts = [starts_ref[j * SLOTS + s] for s in range(SLOTS)]
        q, do = [
            qd_ref[
                pl.ds(
                    pl.multiple_of(
                        source * qd_rows + (n * per + sub) * BLOCK_TOKENS + qd_begin, 16
                    ),
                    BLOCK_TOKENS,
                ),
                :,
            ]
            for n in range(2)
        ]
        keys, vals = [
            jnp.concatenate(
                [kv_ref[pl.ds(pl.multiple_of(r + n * tokens, 16), BLOCK_TOKENS), :] for r in starts],
                axis=0,
            )
            for n in range(2)
        ]
        return q, do, keys, vals

    def score(i):
        q, do, keys, vals = load(i)
        logits = lax.dot_general(q, keys, nt, preferred_element_type=jnp.float32)
        raw = lax.dot_general(do, vals, nt, preferred_element_type=jnp.float32)
        return logits, raw

    def factor(i, u, logits, raw):
        j = place(i)[2]
        block_id = first_ref[0] + j
        absent = ((block_id == 0) & (lane < BLOCK_TOKENS)) | (
            (block_id == last_block) & (lane >= 2 * BLOCK_TOKENS) & (lane < 3 * BLOCK_TOKENS)
        )
        keep = retain[pl.ds(j, 1), :]
        for r in range(0, BLOCK_TOKENS, STRIP):
            part = jnp.where(absent, -jnp.inf, logits[r : r + STRIP])
            top = jnp.max(part, axis=-1, keepdims=True)
            expd = jnp.exp2((part - top) * (scale / math.log(2.0)))
            probs = expd * (1.0 / jnp.sum(expd, axis=-1, keepdims=True))
            kept = probs * keep
            weighted = kept * raw[r : r + STRIP]
            delta = jnp.sum(weighted, axis=-1, keepdims=True)
            waiting[u, pl.ds(r, STRIP), :] = (weighted - probs * delta).astype(jnp.bfloat16)
            waiting[u, pl.ds(BLOCK_TOKENS + r, STRIP), :] = kept.astype(jnp.bfloat16)

    def finish(i, u):
        j = place(i)[2]
        q, do, keys, vals = load(i)
        factors = waiting[u]
        dq = jnp.dot(factors[:BLOCK_TOKENS], keys, preferred_element_type=jnp.float32) * scale
        att = jnp.dot(factors[BLOCK_TOKENS:], vals, preferred_element_type=jnp.float32)
        none = jnp.zeros_like(q)
        pair = jnp.concatenate(
            [jnp.concatenate([q, none], axis=1), jnp.concatenate([none, do], axis=1)], axis=0
        )
        terms = lax.dot_general(factors, pair, tn, preferred_element_type=jnp.float32)
        for s in range(SLOTS):
            acc[block_rows(ids_ref[j * SLOTS + s]), :] += terms[
                s * BLOCK_TOKENS : (s + 1) * BLOCK_TOKENS
            ]
        target, pos = lax.div(i, out_steps), lax.rem(i, out_steps)
        near[target, block_rows(pos), :] = att.astype(jnp.bfloat16)
        near[target, block_rows(out_steps + pos), :] = dq.astype(jnp.bfloat16)

    def step(t, carry):
        scores = [score(t * UNROLL + u) for u in range(UNROLL)]
        for u in range(UNROLL):
            finish((t - 1) * UNROLL + u, u)
        for u in range(UNROLL):
            factor(t * UNROLL + u, u, *scores[u])
        return carry

    for u in range(UNROLL):
        factor(u, u, *score(u))
    lax.fori_loop(1, steps // UNROLL, step, 0)
    for u in range(UNROLL):
        finish(steps - UNROLL + u, u)
    if has_start:
        fetch.wait()
    if joined:
        rows = acc.shape[0] // targets
        stores = []
        for target in range(targets):
            part = pl.ds(target * rows, rows)
            sums = acc[part, :]
            if has_start:
                sums += earlier[part, :]
            done[target, pl.ds(0, 2 * out_rows), :] = near[target]
            done[target, pl.ds(2 * out_rows, rows), :] = (sums[:, :HEAD_WIDTH] * scale).astype(
                jnp.bfloat16
            )
            done[target, pl.ds(2 * out_rows + rows, rows), :] = sums[:, HEAD_WIDTH:].astype(
                jnp.bfloat16
            )
            stores.append(
                pltpu.make_async_copy(done.at[target], out_refs[0].at[target], sems.at[target])
            )
            stores[-1].start()
        for store in stores:
            store.wait()
    else:
        rows = acc.shape[0] // targets
        stores = [
            pltpu.make_async_copy(
                acc.at[pl.ds(n * rows, rows), :], sums_ref.at[pl.ds(n * rows, rows), :], sems.at[n]
            )
            for n in range(targets)
        ]
        for store in stores:
            store.start()
        for k, out_ref in enumerate(out_refs):
            out_ref[...] = near[member_ref[0] ^ k]
        for store in stores:
            store.wait()


def attend(
    ids, starts, first_block, member, drop, kv, qd, qd_begin, start, piece, per, joined, device_blocks, total_blocks, tokens, targets
):
    team_blocks = drop.shape[0]
    source = kv if qd is None else qd
    steps = team_blocks * per // device_blocks
    length = total_blocks * BLOCK_TOKENS
    pairs = steps * BLOCK_TOKENS * WIDE
    accumulator = (length, 2 * HEAD_WIDTH)
    out_rows = steps * BLOCK_TOKENS // targets
    if joined:
        out_shape = [
            pltpu.HBM((targets, 2 * out_rows + 2 * length // targets, HEAD_WIDTH), jnp.bfloat16)
        ]
    else:
        out_shape = [pltpu.HBM((2 * out_rows, HEAD_WIDTH), jnp.bfloat16)] * targets
    scratch = [
        pltpu.VMEM((team_blocks, WIDE), jnp.float32),
        pltpu.VMEM((UNROLL, 2 * BLOCK_TOKENS, WIDE), jnp.bfloat16),
        pltpu.VMEM((targets, 2 * out_rows, HEAD_WIDTH), jnp.bfloat16),
    ]
    scratch = [pltpu.VMEM(accumulator, jnp.float32)] + scratch + [
        pltpu.SemaphoreType.DMA((targets,))
    ]
    if not joined:
        out_shape.append(pltpu.HBM(accumulator, jnp.float32))
    if joined:
        scratch.append(pltpu.VMEM(out_shape[0].shape, jnp.bfloat16))
    sums_bytes = 8 * length * HEAD_WIDTH
    limit = VMEM_LIMIT + 2 * (kv.size + source.size) + (1 if start is None else 2) * sums_bytes
    keep = in_vmem if 2 * limit < VMEM_BYTES else lambda t: t
    flat = [keep(t.reshape(-1, HEAD_WIDTH)) for t in (kv, qd) if t is not None]
    if start is not None:
        scratch += [pltpu.VMEM(accumulator, jnp.float32), pltpu.SemaphoreType.DMA]
    operands = flat + ([] if start is None else [in_hbm(start)])
    operand_specs = [vmem] * len(flat) + [anywhere] * (start is not None)
    return pl.pallas_call(
        functools.partial(
            attention_kernel,
            total_blocks - 1,
            device_blocks,
            per,
            piece,
            out_rows,
            kv.shape[1],
            source.shape[1],
            qd_begin,
            qd is not None,
            start is not None,
            joined,
            tokens,
            targets,
        ),
        out_shape=out_shape,
        in_specs=[smem, smem, smem, smem, vmem] + operand_specs,
        out_specs=[anywhere] if joined else [vmem] * targets + [anywhere],
        scratch_shapes=scratch,
        compiler_params=pltpu.CompilerParams(vmem_limit_bytes=limit),
        cost_estimate=pl.CostEstimate(
            flops=128 * pairs * HEAD_WIDTH,
            bytes_accessed=2 * (source.size + kv.size) + 8 * length * HEAD_WIDTH,
            transcendentals=pairs,
        ),
    )(ids, starts, first_block, member, in_hbm(drop), *operands)


def per_device(queries, keys, values, grad_out, rand_blocks, global_ids, drop_mask):
    shards = lax.axis_size("seq")
    groups = lax.axis_size("head")
    shard = lax.axis_index("seq")
    heads, shard_blocks, _ = rand_blocks.shape
    tokens = queries.shape[0]
    device_blocks = tokens // BLOCK_TOKENS
    shard_tokens = shard_blocks * BLOCK_TOKENS
    teams = shards // heads
    team, member = lax.div(shard, heads), lax.rem(shard, heads)
    team_blocks = heads * shard_blocks
    total_blocks = shards * shard_blocks
    first_block = team * team_blocks
    whole = teams == 1
    pieces = device_blocks if whole else 1
    per = device_blocks // pieces
    rows = tokens // pieces
    same_team_all = (
        None
        if whole
        else [
            [(t * heads + m) * groups + g for m in range(heads) for g in range(groups)]
            for t in range(teams)
        ]
    )
    same_head = [[t * heads + m for t in range(teams)] for m in range(heads)]

    def to_heads(packed):
        return lax.all_to_all(
            packed,
            ("seq", "head"),
            split_axis=0,
            concat_axis=0,
            tiled=True,
            axis_index_groups=same_team_all,
        )

    def to_shards(results):
        received = list(results)
        for k in reversed(range(1, heads)):
            pairs = [(s, s ^ k) for s in range(shards)]
            received[k] = lax.ppermute(results[k], "seq", pairs)
        return received

    table_rows = -(-(shard_blocks + R) // 16) * 16
    sources = [[(queries, c, rows), (grad_out, c, rows)] for c in range(pieces)]
    qd_begin = 2 * tokens
    table_begin = qd_begin + 2 * rows
    kv = to_heads(
        pack(
            groups,
            heads,
            [(keys, 0, tokens), (values, 0, tokens)] + sources[0],
            (drop_mask, rand_blocks.transpose(2, 0, 1)),
            table_rows,
        )
    )
    later = [to_heads(pack(groups, heads, each)) for each in sources[1:]]
    tables = lax.dynamic_index_in_dim(
        kv.reshape(heads, groups, -1, HEAD_WIDTH)[:, :, table_begin:],
        lax.axis_index("head"),
        axis=1,
        keepdims=False,
    ).astype(jnp.int32)
    drops = tables[:, :shard_blocks, :SLOTS].reshape(team_blocks, SLOTS)
    randoms = tables[:, shard_blocks : shard_blocks + R, :shard_blocks].transpose(0, 2, 1)
    randoms = randoms.reshape(team_blocks, R)
    qd = [None] + later
    if not whole:
        qd[0] = kv[:, qd_begin:table_begin]
        kv = lax.all_gather(kv[:, : 2 * tokens], "seq", axis=0, tiled=True, axis_index_groups=same_head)
    blocks = first_block + jnp.arange(team_blocks, dtype=jnp.int32)
    window = jnp.stack([blocks - 1, blocks, blocks + 1], axis=1)
    listed = jnp.concatenate(
        [window, jnp.broadcast_to(global_ids[None], (team_blocks, G)), randoms], axis=1
    )
    listed = jnp.clip(listed, 0, total_blocks - 1).reshape(-1)
    starts = listed // device_blocks * kv.shape[1] + listed % device_blocks * BLOCK_TOKENS
    pieces_out = []
    held = []
    sums = []
    for c in range(pieces):
        pieces_out.append(
            attend(
                listed,
                starts,
                first_block.reshape(1),
                member.reshape(1),
                drops,
                kv,
                qd[c],
                qd_begin if qd[c] is None else 0,
                sums[0] if sums else None,
                c,
                per,
                whole and c == pieces - 1,
                device_blocks,
                total_blocks,
                tokens,
                heads,
            )
        )
        sums = pieces_out[c][heads:]
        if c + 1 < pieces:
            held.append(pieces_out[c][1:heads])
    runs = shard_blocks // device_blocks
    begin = shard_tokens // pieces
    near = []
    for c, out in enumerate(pieces_out):
        if len(out) > 1:
            results = out[:heads]
            if c + 1 < pieces:
                results = [results[0], *held[c]]
            near.append(to_shards(results))
    att, dq = None, None
    if whole:
        rest = pieces_out[-1][0]
        if near:
            rest, *near[-1][heads // 2 :] = lax.optimization_barrier(
                (rest, *near[-1][heads // 2 :])
            )
        rest = lax.all_to_all(rest, "seq", split_axis=0, concat_axis=0, tiled=True)
    for c in range(len(near)):
        parts = [(0, rows, runs, pieces, c, att), (begin, rows, runs, pieces, c, dq)]
        att, dq = unpack(member.reshape(1), near[c], parts)
    if whole:
        c = pieces - 1
        parts = [(0, rows, runs, pieces, c, att), (begin, rows, runs, pieces, c, dq)]
        grads = [
            (2 * begin + n * shard_tokens, shard_tokens // runs, runs, 1, 0, None) for n in range(2)
        ]
        att, dq, dk, dv = unpack_all(rest, parts + grads)
    else:
        grads = lax.psum_scatter(
            sums[0], "seq", scatter_dimension=0, tiled=True, axis_index_groups=same_head
        ).reshape(heads, shard_tokens, 2, HEAD_WIDTH)
        grads = jnp.concatenate(
            [grads[:, :, 0] * HEAD_WIDTH ** (-0.5), grads[:, :, 1]], axis=1
        ).astype(jnp.bfloat16)
        grads = to_shards(
            [lax.dynamic_index_in_dim(grads, member ^ k, 0, keepdims=False) for k in range(heads)]
        )
        dk, dv = unpack(
            member.reshape(1),
            grads,
            [(n * shard_tokens, shard_tokens, 1, 1, 0, None) for n in range(2)],
        )
    return tuple(t.reshape(shard_tokens, heads * HEAD_WIDTH) for t in (att, dq, dk, dv))


def solution(mesh):
    return jax.shard_map(
        per_device,
        mesh=mesh,
        in_specs=(
            P(("seq", "head"), None),
            P(("seq", "head"), None),
            P(("seq", "head"), None),
            P(("seq", "head"), None),
            P("head", "seq", None),
            P(),
            P("head", "seq", None),
        ),
        out_specs=(P("seq", "head"), P("seq", "head"), P("seq", "head"), P("seq", "head")),
        check_vma=False,
    )
```

```python
import functools
import math

import jax
import jax.numpy as jnp
from jax import lax
from jax.experimental import pallas as pl
from jax.experimental.pallas import tpu as pltpu
from jax.sharding import PartitionSpec as P

HEAD_WIDTH = 128
BLOCK_TOKENS = 64
R = 3
G = 2
SLOTS = 3 + G + R
WIDE = SLOTS * BLOCK_TOKENS
UNROLL = 8
STRIP = 16
VMEM_LIMIT = 16 * 1024 * 1024
VMEM_BYTES = 64 * 1024 * 1024

keep_prob = 0.9

vmem = pl.BlockSpec(memory_space=pltpu.VMEM)
smem = pl.BlockSpec(memory_space=pltpu.SMEM)
anywhere = pl.BlockSpec(memory_space=pl.ANY)


def in_vmem(array):
    return pltpu.with_memory_space_constraint(array, pltpu.VMEM)


def in_hbm(array):
    return pltpu.with_memory_space_constraint(array, pltpu.HBM)


def copy_cost(size):
    return pl.CostEstimate(flops=0, bytes_accessed=4 * size, transcendentals=0)


def block_rows(number):
    start = number * BLOCK_TOKENS
    if not isinstance(number, int):
        start = pl.multiple_of(start, BLOCK_TOKENS)
    return pl.ds(start, BLOCK_TOKENS)


def pack_kernel(heads, groups, sources, table_rows, *refs):
    refs = list(refs)
    if table_rows:
        drop_hbm, rand_hbm = refs.pop(0), refs.pop(0)
        table, drop_ref, rand_ref, table_sems = refs[-4:]
        refs = refs[:-4]
    count = len(sources)
    arrays, out_ref = refs[:count], refs[count]
    wholes, packed, in_sems, out_sems = refs[count + 1 : -3], refs[-3], refs[-2], refs[-1]
    width = heads * HEAD_WIDTH
    loads = []
    for h in range(groups):
        for n, (at, rows) in enumerate(sources):
            columns = pl.ds(h * width, width)
            loads.append(
                pltpu.make_async_copy(
                    arrays[n].at[pl.ds(at * rows, rows), columns],
                    wholes[n].at[:, columns],
                    in_sems.at[h, n],
                )
            )
    for load in loads:
        load.start()
    begin = sum(rows for _, rows in sources)
    if table_rows:
        fetches = [
            pltpu.make_async_copy(drop_hbm, drop_ref, table_sems.at[0]),
            pltpu.make_async_copy(rand_hbm, rand_ref, table_sems.at[1]),
        ]
        for fetch in fetches:
            fetch.start()
        for fetch in fetches:
            fetch.wait()
        blocks = drop_ref.shape[1]
        table[...] = jnp.zeros_like(table)
        for m in range(heads):
            table[pl.ds(0, blocks), pl.ds(0, SLOTS)] = drop_ref[m].astype(jnp.float32)
            for r in range(R):
                table[pl.ds(blocks + r, 1), pl.ds(0, blocks)] = rand_ref[
                    r, pl.ds(m, 1), :
                ].astype(jnp.float32)
            rounded = table[...].astype(jnp.bfloat16)
            for g in range(groups):
                packed[m, g, pl.ds(begin, table_rows), :] = rounded
    stores = []
    for g in range(groups):
        for n in range(count):
            loads[g * count + n].wait()
        for m in range(heads):
            begin = 0
            for n, (_, rows) in enumerate(sources):
                packed[m, g, pl.ds(begin, rows), :] = wholes[n][
                    :, pl.ds((g * heads + m) * HEAD_WIDTH, HEAD_WIDTH)
                ]
                begin += rows
        stores.append(
            pltpu.make_async_copy(packed.at[:, g], out_ref.at[:, g], out_sems.at[g])
        )
        stores[-1].start()
    for store in stores:
        store.wait()


def pack(groups, heads, sources, tables=(), table_rows=0):
    total = sum(rows for _, _, rows in sources) + table_rows
    shape = (heads, groups, total, HEAD_WIDTH)
    scratch = [
        pltpu.VMEM((rows, groups * heads * HEAD_WIDTH), jnp.bfloat16) for _, _, rows in sources
    ] + [
        pltpu.VMEM(shape, jnp.bfloat16),
        pltpu.SemaphoreType.DMA((groups, len(sources))),
        pltpu.SemaphoreType.DMA((groups,)),
    ]
    if table_rows:
        scratch.append(pltpu.VMEM((table_rows, HEAD_WIDTH), jnp.float32))
        scratch += [pltpu.VMEM(t.shape, t.dtype) for t in tables]
        scratch.append(pltpu.SemaphoreType.DMA((len(tables),)))
    packed = pl.pallas_call(
        functools.partial(
            pack_kernel, heads, groups, tuple((at, rows) for _, at, rows in sources), table_rows
        ),
        out_shape=pltpu.HBM(shape, jnp.bfloat16),
        in_specs=[anywhere] * (len(tables) + len(sources)),
        out_specs=anywhere,
        scratch_shapes=scratch,
        compiler_params=pltpu.CompilerParams(vmem_limit_bytes=VMEM_LIMIT),
        cost_estimate=copy_cost(math.prod(shape)),
    )(*[in_hbm(t) for t in tables], *[in_hbm(a) for a, _, _ in sources])
    return packed.reshape(heads * groups, total, HEAD_WIDTH)


def unpack_kernel(parts, member_ref, *refs):
    outs = refs[len(refs) - len(parts) :]
    heads = outs[0].shape[-1] // HEAD_WIDTH
    for n in range(heads):
        k = (heads - n) % heads
        column = pl.multiple_of((member_ref[0] ^ k) * HEAD_WIDTH, HEAD_WIDTH)
        for begin, out in zip(parts, outs):
            runs, _, rows, _ = out.shape
            for i in range(runs):
                out[i, 0, :, pl.ds(column, HEAD_WIDTH)] = refs[n][pl.ds(begin + i * rows, rows), :]


def unpack(member, received, parts):
    heads = len(received)
    shapes, specs, olds, aliases, size = [], [], [], {}, 0
    for n, (_, rows, runs, pieces, piece, old) in enumerate(parts):
        shapes.append(
            jax.ShapeDtypeStruct((runs, pieces, rows, heads * HEAD_WIDTH), jnp.bfloat16)
        )
        specs.append(
            pl.BlockSpec(
                (runs, 1, rows, heads * HEAD_WIDTH),
                functools.partial(lambda piece, h: (0, piece, 0, 0), piece),
            )
        )
        size += rows * runs * heads * HEAD_WIDTH
        if old is not None:
            aliases[1 + heads + len(olds)] = n
            olds.append(old)
    return pl.pallas_call(
        functools.partial(unpack_kernel, tuple(part[0] for part in parts)),
        grid=(1,),
        out_shape=shapes,
        in_specs=[smem]
        + [pl.BlockSpec(received[0].shape, lambda h: (0, 0))] * heads
        + [pl.BlockSpec(memory_space=pl.ANY)] * len(olds),
        out_specs=specs,
        input_output_aliases=aliases,
        compiler_params=pltpu.CompilerParams(vmem_limit_bytes=VMEM_LIMIT),
        cost_estimate=copy_cost(size),
    )(member, received[0], *received[:0:-1], *olds)


def unpack_all_kernel(parts, piece_ref, *refs):
    sems = refs[-1]
    stages = refs[-1 - len(parts) : -1]
    outs = refs[-1 - 2 * len(parts) : -1 - len(parts)]
    stores = []
    for (begin, rows, runs, _, piece), stage, out in zip(parts, stages, outs):
        for i in range(runs):
            for m in range(piece_ref.shape[0]):
                stage[i, :, pl.ds(m * HEAD_WIDTH, HEAD_WIDTH)] = piece_ref[
                    m, pl.ds(begin + i * rows, rows), :
                ]
            stores.append(
                pltpu.make_async_copy(stage.at[i], out.at[i, piece], sems.at[len(stores)])
            )
            stores[-1].start()
    for store in stores:
        store.wait()


def unpack_all(received, parts):
    heads = received.shape[0]
    shapes, stages, olds, aliases, count = [], [], [], {}, 0
    for n, (_, rows, runs, pieces, _, old) in enumerate(parts):
        shapes.append(pltpu.HBM((runs, pieces, rows, heads * HEAD_WIDTH), jnp.bfloat16))
        stages.append(pltpu.VMEM((runs, rows, heads * HEAD_WIDTH), jnp.bfloat16))
        count += runs
        if old is not None:
            aliases[1 + len(olds)] = n
            olds.append(old)
    return pl.pallas_call(
        functools.partial(unpack_all_kernel, tuple(part[:-1] for part in parts)),
        out_shape=shapes,
        in_specs=[vmem] + [anywhere] * len(olds),
        out_specs=[anywhere] * len(shapes),
        input_output_aliases=aliases,
        scratch_shapes=stages + [pltpu.SemaphoreType.DMA((count,))],
        compiler_params=pltpu.CompilerParams(vmem_limit_bytes=VMEM_LIMIT),
        cost_estimate=copy_cost(received.size),
    )(in_vmem(received), *olds)


def attention_kernel(
    last_block,
    device_blocks,
    per,
    piece,
    out_rows,
    source_rows,
    qd_rows,
    qd_begin,
    has_qd,
    has_start,
    joined,
    tokens,
    targets,
    ids_ref,
    starts_ref,
    first_ref,
    member_ref,
    drop_ref,
    kv_ref,
    *refs,
):
    refs = list(refs)
    qd_ref = refs.pop(0) if has_qd else kv_ref
    start_ref = refs.pop(0) if has_start else None
    out_refs = [refs.pop(0) for _ in range(1 if joined else targets)]
    sums_ref = None if joined else refs.pop(0)
    acc, retain, waiting, near, sems = refs[:5]
    done = refs[5] if joined else None
    start_sems = refs[-1] if has_start else None
    scale = HEAD_WIDTH ** (-0.5)
    steps = targets * (out_rows // BLOCK_TOKENS)
    slot_of_lane = lax.broadcasted_iota(jnp.int32, (SLOTS, WIDE), 1) // BLOCK_TOKENS
    slot_row = lax.broadcasted_iota(jnp.int32, (SLOTS, WIDE), 0)
    expand = (slot_of_lane == slot_row).astype(jnp.float32)
    retain[...] = jnp.dot(
        drop_ref[...].astype(jnp.float32), expand, preferred_element_type=jnp.float32
    ) * (1.0 / keep_prob)
    shares = [pl.ds(n * (acc.shape[0] // targets), acc.shape[0] // targets) for n in range(targets)]
    fetches = []
    if has_start:
        for n, share in enumerate(shares):
            fetches.append(
                pltpu.make_async_copy(start_ref.at[share, :], acc.at[share, :], start_sems.at[n])
            )
            fetches[-1].start()
    else:
        acc[...] = jnp.zeros_like(acc)
    lane = lax.broadcasted_iota(jnp.int32, (1, WIDE), 1)
    nt = (((1,), (1,)), ((), ()))
    tn = (((0,), (0,)), ((), ()))
    out_steps = steps // targets

    def place(i):
        if per == 1:
            source, sub = i, 0
        else:
            source, sub = lax.div(i, per), lax.rem(i, per)
        return source, sub, source * device_blocks + piece * per + sub

    def load(i):
        source, sub, j = place(i)
        starts = [starts_ref[j * SLOTS + s] for s in range(SLOTS)]
        q, do = [
            qd_ref[
                pl.ds(
                    pl.multiple_of(
                        source * qd_rows + (n * per + sub) * BLOCK_TOKENS + qd_begin, 16
                    ),
                    BLOCK_TOKENS,
                ),
                :,
            ]
            for n in range(2)
        ]
        keys, vals = [
            jnp.concatenate(
                [kv_ref[pl.ds(pl.multiple_of(r + n * tokens, 16), BLOCK_TOKENS), :] for r in starts],
                axis=0,
            )
            for n in range(2)
        ]
        return q, do, keys, vals

    def score(i):
        q, do, keys, vals = load(i)
        logits = lax.dot_general(q, keys, nt, preferred_element_type=jnp.float32)
        raw = lax.dot_general(do, vals, nt, preferred_element_type=jnp.float32)
        return logits, raw

    def factor(i, u, logits, raw):
        j = place(i)[2]
        block_id = first_ref[0] + j
        absent = ((block_id == 0) & (lane < BLOCK_TOKENS)) | (
            (block_id == last_block) & (lane >= 2 * BLOCK_TOKENS) & (lane < 3 * BLOCK_TOKENS)
        )
        keep = retain[pl.ds(j, 1), :]
        for r in range(0, BLOCK_TOKENS, STRIP):
            part = jnp.where(absent, -jnp.inf, logits[r : r + STRIP])
            top = jnp.max(part, axis=-1, keepdims=True)
            expd = jnp.exp2((part - top) * (scale / math.log(2.0)))
            probs = expd * (1.0 / jnp.sum(expd, axis=-1, keepdims=True))
            kept = probs * keep
            weighted = kept * raw[r : r + STRIP]
            delta = jnp.sum(weighted, axis=-1, keepdims=True)
            waiting[u, pl.ds(r, STRIP), :] = (weighted - probs * delta).astype(jnp.bfloat16)
            waiting[u, pl.ds(BLOCK_TOKENS + r, STRIP), :] = kept.astype(jnp.bfloat16)

    def finish(i, u):
        j = place(i)[2]
        q, do, keys, vals = load(i)
        factors = waiting[u]
        dq = jnp.dot(factors[:BLOCK_TOKENS], keys, preferred_element_type=jnp.float32) * scale
        att = jnp.dot(factors[BLOCK_TOKENS:], vals, preferred_element_type=jnp.float32)
        none = jnp.zeros_like(q)
        pair = jnp.concatenate(
            [jnp.concatenate([q, none], axis=1), jnp.concatenate([none, do], axis=1)], axis=0
        )
        terms = lax.dot_general(factors, pair, tn, preferred_element_type=jnp.float32)
        for s in range(SLOTS):
            acc[block_rows(ids_ref[j * SLOTS + s]), :] += terms[
                s * BLOCK_TOKENS : (s + 1) * BLOCK_TOKENS
            ]
        target, pos = lax.div(i, out_steps), lax.rem(i, out_steps)
        near[target, block_rows(pos), :] = att.astype(jnp.bfloat16)
        near[target, block_rows(out_steps + pos), :] = dq.astype(jnp.bfloat16)

    def step(t, carry):
        scores = [score(t * UNROLL + u) for u in range(UNROLL)]
        for u in range(UNROLL):
            finish((t - 1) * UNROLL + u, u)
        for u in range(UNROLL):
            factor(t * UNROLL + u, u, *scores[u])
        return carry

    for u in range(UNROLL):
        factor(u, u, *score(u))
    for fetch in fetches:
        fetch.wait()
    lax.fori_loop(1, steps // UNROLL, step, 0)
    for u in range(UNROLL):
        finish(steps - UNROLL + u, u)
    if joined:
        rows = acc.shape[0] // targets
        stores = []
        for target, share in enumerate(shares):
            sums = acc[share, :]
            done[target, pl.ds(0, 2 * out_rows), :] = near[target]
            done[target, pl.ds(2 * out_rows, rows), :] = (sums[:, :HEAD_WIDTH] * scale).astype(
                jnp.bfloat16
            )
            done[target, pl.ds(2 * out_rows + rows, rows), :] = sums[:, HEAD_WIDTH:].astype(
                jnp.bfloat16
            )
            stores.append(
                pltpu.make_async_copy(done.at[target], out_refs[0].at[target], sems.at[target])
            )
            stores[-1].start()
        for store in stores:
            store.wait()
    else:
        stores = [
            pltpu.make_async_copy(acc.at[share, :], sums_ref.at[share, :], sems.at[n])
            for n, share in enumerate(shares)
        ]
        for store in stores:
            store.start()
        for k, out_ref in enumerate(out_refs):
            out_ref[...] = near[member_ref[0] ^ k]
        for store in stores:
            store.wait()


def attend(
    ids, starts, first_block, member, drop, kv, qd, qd_begin, start, piece, per, joined, device_blocks, total_blocks, tokens, targets
):
    team_blocks = drop.shape[0]
    source = kv if qd is None else qd
    steps = team_blocks * per // device_blocks
    length = total_blocks * BLOCK_TOKENS
    pairs = steps * BLOCK_TOKENS * WIDE
    accumulator = (length, 2 * HEAD_WIDTH)
    out_rows = steps * BLOCK_TOKENS // targets
    if joined:
        out_shape = [
            pltpu.HBM((targets, 2 * out_rows + 2 * length // targets, HEAD_WIDTH), jnp.bfloat16)
        ]
    else:
        out_shape = [pltpu.HBM((2 * out_rows, HEAD_WIDTH), jnp.bfloat16)] * targets
    scratch = [
        pltpu.VMEM((team_blocks, WIDE), jnp.float32),
        pltpu.VMEM((UNROLL, 2 * BLOCK_TOKENS, WIDE), jnp.bfloat16),
        pltpu.VMEM((targets, 2 * out_rows, HEAD_WIDTH), jnp.bfloat16),
    ]
    scratch = [pltpu.VMEM(accumulator, jnp.float32)] + scratch + [
        pltpu.SemaphoreType.DMA((targets,))
    ]
    if not joined:
        out_shape.append(pltpu.HBM(accumulator, jnp.float32))
    if joined:
        scratch.append(pltpu.VMEM(out_shape[0].shape, jnp.bfloat16))
    sums_bytes = 8 * length * HEAD_WIDTH
    limit = VMEM_LIMIT + 2 * (kv.size + source.size) + sums_bytes
    keep = in_vmem if 2 * limit < VMEM_BYTES else lambda t: t
    flat = [keep(t.reshape(-1, HEAD_WIDTH)) for t in (kv, qd) if t is not None]
    if start is not None:
        scratch.append(pltpu.SemaphoreType.DMA((targets,)))
    operands = flat + ([] if start is None else [in_hbm(start)])
    operand_specs = [vmem] * len(flat) + [anywhere] * (start is not None)
    return pl.pallas_call(
        functools.partial(
            attention_kernel,
            total_blocks - 1,
            device_blocks,
            per,
            piece,
            out_rows,
            kv.shape[1],
            source.shape[1],
            qd_begin,
            qd is not None,
            start is not None,
            joined,
            tokens,
            targets,
        ),
        out_shape=out_shape,
        in_specs=[smem, smem, smem, smem, vmem] + operand_specs,
        out_specs=[anywhere] if joined else [vmem] * targets + [anywhere],
        scratch_shapes=scratch,
        compiler_params=pltpu.CompilerParams(vmem_limit_bytes=limit),
        cost_estimate=pl.CostEstimate(
            flops=128 * pairs * HEAD_WIDTH,
            bytes_accessed=2 * (source.size + kv.size) + 8 * length * HEAD_WIDTH,
            transcendentals=pairs,
        ),
    )(ids, starts, first_block, member, in_hbm(drop), *operands)


def per_device(queries, keys, values, grad_out, rand_blocks, global_ids, drop_mask):
    shards = lax.axis_size("seq")
    groups = lax.axis_size("head")
    shard = lax.axis_index("seq")
    heads, shard_blocks, _ = rand_blocks.shape
    tokens = queries.shape[0]
    device_blocks = tokens // BLOCK_TOKENS
    shard_tokens = shard_blocks * BLOCK_TOKENS
    teams = shards // heads
    team, member = lax.div(shard, heads), lax.rem(shard, heads)
    team_blocks = heads * shard_blocks
    total_blocks = shards * shard_blocks
    first_block = team * team_blocks
    whole = teams == 1
    pieces = device_blocks if whole else 1
    per = device_blocks // pieces
    rows = tokens // pieces
    same_team_all = (
        None
        if whole
        else [
            [(t * heads + m) * groups + g for m in range(heads) for g in range(groups)]
            for t in range(teams)
        ]
    )
    same_head = [[t * heads + m for t in range(teams)] for m in range(heads)]

    def to_heads(packed):
        return lax.all_to_all(
            packed,
            ("seq", "head"),
            split_axis=0,
            concat_axis=0,
            tiled=True,
            axis_index_groups=same_team_all,
        )

    def to_shards(results):
        received = list(results)
        for k in reversed(range(1, heads)):
            pairs = [(s, s ^ k) for s in range(shards)]
            received[k] = lax.ppermute(results[k], "seq", pairs)
        return received

    table_rows = -(-(shard_blocks + R) // 16) * 16
    sources = [[(queries, c, rows), (grad_out, c, rows)] for c in range(pieces)]
    qd_begin = 2 * tokens
    table_begin = qd_begin + 2 * rows
    kv = to_heads(
        pack(
            groups,
            heads,
            [(keys, 0, tokens), (values, 0, tokens)] + sources[0],
            (drop_mask, rand_blocks.transpose(2, 0, 1)),
            table_rows,
        )
    )
    later = [to_heads(pack(groups, heads, each)) for each in sources[1:]]
    tables = lax.dynamic_index_in_dim(
        kv.reshape(heads, groups, -1, HEAD_WIDTH)[:, :, table_begin:],
        lax.axis_index("head"),
        axis=1,
        keepdims=False,
    ).astype(jnp.int32)
    drops = tables[:, :shard_blocks, :SLOTS].reshape(team_blocks, SLOTS)
    randoms = tables[:, shard_blocks : shard_blocks + R, :shard_blocks].transpose(0, 2, 1)
    randoms = randoms.reshape(team_blocks, R)
    qd = [None] + later
    if not whole:
        qd[0] = kv[:, qd_begin:table_begin]
        kv = lax.all_gather(kv[:, : 2 * tokens], "seq", axis=0, tiled=True, axis_index_groups=same_head)
    blocks = first_block + jnp.arange(team_blocks, dtype=jnp.int32)
    window = jnp.stack([blocks - 1, blocks, blocks + 1], axis=1)
    listed = jnp.concatenate(
        [window, jnp.broadcast_to(global_ids[None], (team_blocks, G)), randoms], axis=1
    )
    listed = jnp.clip(listed, 0, total_blocks - 1).reshape(-1)
    starts = listed // device_blocks * kv.shape[1] + listed % device_blocks * BLOCK_TOKENS
    pieces_out = []
    held = []
    sums = []
    for c in range(pieces):
        pieces_out.append(
            attend(
                listed,
                starts,
                first_block.reshape(1),
                member.reshape(1),
                drops,
                kv,
                qd[c],
                qd_begin if qd[c] is None else 0,
                sums[0] if sums else None,
                c,
                per,
                whole and c == pieces - 1,
                device_blocks,
                total_blocks,
                tokens,
                heads,
            )
        )
        sums = pieces_out[c][heads:]
        if c + 1 < pieces:
            held.append(pieces_out[c][1:heads])
    runs = shard_blocks // device_blocks
    begin = shard_tokens // pieces
    near = []
    for c, out in enumerate(pieces_out):
        if len(out) > 1:
            results = out[:heads]
            if c + 1 < pieces:
                results = [results[0], *held[c]]
            near.append(to_shards(results))
    att, dq = None, None
    if whole:
        rest = pieces_out[-1][0]
        if near:
            rest, *near[-1][heads // 2 :] = lax.optimization_barrier(
                (rest, *near[-1][heads // 2 :])
            )
        rest = lax.all_to_all(rest, "seq", split_axis=0, concat_axis=0, tiled=True)
    for c in range(len(near)):
        parts = [(0, rows, runs, pieces, c, att), (begin, rows, runs, pieces, c, dq)]
        att, dq = unpack(member.reshape(1), near[c], parts)
    if whole:
        c = pieces - 1
        parts = [(0, rows, runs, pieces, c, att), (begin, rows, runs, pieces, c, dq)]
        grads = [
            (2 * begin + n * shard_tokens, shard_tokens // runs, runs, 1, 0, None) for n in range(2)
        ]
        att, dq, dk, dv = unpack_all(rest, parts + grads)
    else:
        grads = lax.psum_scatter(
            sums[0], "seq", scatter_dimension=0, tiled=True, axis_index_groups=same_head
        ).reshape(heads, shard_tokens, 2, HEAD_WIDTH)
        grads = jnp.concatenate(
            [grads[:, :, 0] * HEAD_WIDTH ** (-0.5), grads[:, :, 1]], axis=1
        ).astype(jnp.bfloat16)
        grads = to_shards(
            [lax.dynamic_index_in_dim(grads, member ^ k, 0, keepdims=False) for k in range(heads)]
        )
        dk, dv = unpack(
            member.reshape(1),
            grads,
            [(n * shard_tokens, shard_tokens, 1, 1, 0, None) for n in range(2)],
        )
    return tuple(t.reshape(shard_tokens, heads * HEAD_WIDTH) for t in (att, dq, dk, dv))


def solution(mesh):
    return jax.shard_map(
        per_device,
        mesh=mesh,
        in_specs=(
            P(("seq", "head"), None),
            P(("seq", "head"), None),
            P(("seq", "head"), None),
            P(("seq", "head"), None),
            P("head", "seq", None),
            P(),
            P("head", "seq", None),
        ),
        out_specs=(P("seq", "head"), P("seq", "head"), P("seq", "head"), P("seq", "head")),
        check_vma=False,
    )
```

```python
import functools
import math

import jax
import jax.numpy as jnp
from jax import lax
from jax.experimental import pallas as pl
from jax.experimental.pallas import tpu as pltpu
from jax.sharding import PartitionSpec as P

HEAD_WIDTH = 128
BLOCK_TOKENS = 64
R = 3
G = 2
SLOTS = 3 + G + R
OWN = 3 + R
WIDE = SLOTS * BLOCK_TOKENS
UNROLL = 8
STRIP = 16
VMEM_LIMIT = 16 * 1024 * 1024
VMEM_BYTES = 64 * 1024 * 1024

keep_prob = 0.9

vmem = pl.BlockSpec(memory_space=pltpu.VMEM)
smem = pl.BlockSpec(memory_space=pltpu.SMEM)
anywhere = pl.BlockSpec(memory_space=pl.ANY)


def in_vmem(array):
    return pltpu.with_memory_space_constraint(array, pltpu.VMEM)


def in_hbm(array):
    return pltpu.with_memory_space_constraint(array, pltpu.HBM)


def copy_cost(size):
    return pl.CostEstimate(flops=0, bytes_accessed=4 * size, transcendentals=0)


def block_rows(number):
    start = number * BLOCK_TOKENS
    if not isinstance(number, int):
        start = pl.multiple_of(start, BLOCK_TOKENS)
    return pl.ds(start, BLOCK_TOKENS)


def pack_kernel(heads, groups, sources, table_rows, *refs):
    refs = list(refs)
    if table_rows:
        drop_hbm, rand_hbm = refs.pop(0), refs.pop(0)
        table, drop_ref, rand_ref, table_sems = refs[-4:]
        refs = refs[:-4]
    count = len(sources)
    arrays, out_ref = refs[:count], refs[count]
    wholes, packed, in_sems, out_sems = refs[count + 1 : -3], refs[-3], refs[-2], refs[-1]
    width = heads * HEAD_WIDTH
    loads = []
    for h in range(groups):
        for n, (at, rows) in enumerate(sources):
            columns = pl.ds(h * width, width)
            loads.append(
                pltpu.make_async_copy(
                    arrays[n].at[pl.ds(at * rows, rows), columns],
                    wholes[n].at[:, columns],
                    in_sems.at[h, n],
                )
            )
    for load in loads:
        load.start()
    begin = sum(rows for _, rows in sources)
    if table_rows:
        fetches = [
            pltpu.make_async_copy(drop_hbm, drop_ref, table_sems.at[0]),
            pltpu.make_async_copy(rand_hbm, rand_ref, table_sems.at[1]),
        ]
        for fetch in fetches:
            fetch.start()
        for fetch in fetches:
            fetch.wait()
        blocks = drop_ref.shape[1]
        table[...] = jnp.zeros_like(table)
        for m in range(heads):
            table[pl.ds(0, blocks), pl.ds(0, SLOTS)] = drop_ref[m].astype(jnp.float32)
            for r in range(R):
                table[pl.ds(blocks + r, 1), pl.ds(0, blocks)] = rand_ref[
                    r, pl.ds(m, 1), :
                ].astype(jnp.float32)
            rounded = table[...].astype(jnp.bfloat16)
            for g in range(groups):
                packed[m, g, pl.ds(begin, table_rows), :] = rounded
    stores = []
    for g in range(groups):
        for n in range(count):
            loads[g * count + n].wait()
        for m in range(heads):
            begin = 0
            for n, (_, rows) in enumerate(sources):
                packed[m, g, pl.ds(begin, rows), :] = wholes[n][
                    :, pl.ds((g * heads + m) * HEAD_WIDTH, HEAD_WIDTH)
                ]
                begin += rows
        stores.append(
            pltpu.make_async_copy(packed.at[:, g], out_ref.at[:, g], out_sems.at[g])
        )
        stores[-1].start()
    for store in stores:
        store.wait()


def pack(groups, heads, sources, tables=(), table_rows=0):
    total = sum(rows for _, _, rows in sources) + table_rows
    shape = (heads, groups, total, HEAD_WIDTH)
    scratch = [
        pltpu.VMEM((rows, groups * heads * HEAD_WIDTH), jnp.bfloat16) for _, _, rows in sources
    ] + [
        pltpu.VMEM(shape, jnp.bfloat16),
        pltpu.SemaphoreType.DMA((groups, len(sources))),
        pltpu.SemaphoreType.DMA((groups,)),
    ]
    if table_rows:
        scratch.append(pltpu.VMEM((table_rows, HEAD_WIDTH), jnp.float32))
        scratch += [pltpu.VMEM(t.shape, t.dtype) for t in tables]
        scratch.append(pltpu.SemaphoreType.DMA((len(tables),)))
    packed = pl.pallas_call(
        functools.partial(
            pack_kernel, heads, groups, tuple((at, rows) for _, at, rows in sources), table_rows
        ),
        out_shape=pltpu.HBM(shape, jnp.bfloat16),
        in_specs=[anywhere] * (len(tables) + len(sources)),
        out_specs=anywhere,
        scratch_shapes=scratch,
        compiler_params=pltpu.CompilerParams(vmem_limit_bytes=VMEM_LIMIT),
        cost_estimate=copy_cost(math.prod(shape)),
    )(*[in_hbm(t) for t in tables], *[in_hbm(a) for a, _, _ in sources])
    return packed.reshape(heads * groups, total, HEAD_WIDTH)


def unpack_kernel(parts, member_ref, *refs):
    outs = refs[len(refs) - len(parts) :]
    heads = outs[0].shape[-1] // HEAD_WIDTH
    for n in range(heads):
        k = (heads - n) % heads
        column = pl.multiple_of((member_ref[0] ^ k) * HEAD_WIDTH, HEAD_WIDTH)
        for begin, out in zip(parts, outs):
            runs, _, rows, _ = out.shape
            for i in range(runs):
                out[i, 0, :, pl.ds(column, HEAD_WIDTH)] = refs[n][pl.ds(begin + i * rows, rows), :]


def unpack(member, received, parts):
    heads = len(received)
    shapes, specs, olds, aliases, size = [], [], [], {}, 0
    for n, (_, rows, runs, pieces, piece, old) in enumerate(parts):
        shapes.append(
            jax.ShapeDtypeStruct((runs, pieces, rows, heads * HEAD_WIDTH), jnp.bfloat16)
        )
        specs.append(
            pl.BlockSpec(
                (runs, 1, rows, heads * HEAD_WIDTH),
                functools.partial(lambda piece, h: (0, piece, 0, 0), piece),
            )
        )
        size += rows * runs * heads * HEAD_WIDTH
        if old is not None:
            aliases[1 + heads + len(olds)] = n
            olds.append(old)
    return pl.pallas_call(
        functools.partial(unpack_kernel, tuple(part[0] for part in parts)),
        grid=(1,),
        out_shape=shapes,
        in_specs=[smem]
        + [pl.BlockSpec(received[0].shape, lambda h: (0, 0))] * heads
        + [pl.BlockSpec(memory_space=pl.ANY)] * len(olds),
        out_specs=specs,
        input_output_aliases=aliases,
        compiler_params=pltpu.CompilerParams(vmem_limit_bytes=VMEM_LIMIT),
        cost_estimate=copy_cost(size),
    )(member, received[0], *received[:0:-1], *olds)


def unpack_all_kernel(parts, piece_ref, *refs):
    sems = refs[-1]
    stages = refs[-1 - len(parts) : -1]
    outs = refs[-1 - 2 * len(parts) : -1 - len(parts)]
    stores = []
    for (begin, rows, runs, _, piece), stage, out in zip(parts, stages, outs):
        for i in range(runs):
            for m in range(piece_ref.shape[0]):
                stage[i, :, pl.ds(m * HEAD_WIDTH, HEAD_WIDTH)] = piece_ref[
                    m, pl.ds(begin + i * rows, rows), :
                ]
            stores.append(
                pltpu.make_async_copy(stage.at[i], out.at[i, piece], sems.at[len(stores)])
            )
            stores[-1].start()
    for store in stores:
        store.wait()


def unpack_all(received, parts):
    heads = received.shape[0]
    shapes, stages, olds, aliases, count = [], [], [], {}, 0
    for n, (_, rows, runs, pieces, _, old) in enumerate(parts):
        shapes.append(pltpu.HBM((runs, pieces, rows, heads * HEAD_WIDTH), jnp.bfloat16))
        stages.append(pltpu.VMEM((runs, rows, heads * HEAD_WIDTH), jnp.bfloat16))
        count += runs
        if old is not None:
            aliases[1 + len(olds)] = n
            olds.append(old)
    return pl.pallas_call(
        functools.partial(unpack_all_kernel, tuple(part[:-1] for part in parts)),
        out_shape=shapes,
        in_specs=[vmem] + [anywhere] * len(olds),
        out_specs=[anywhere] * len(shapes),
        input_output_aliases=aliases,
        scratch_shapes=stages + [pltpu.SemaphoreType.DMA((count,))],
        compiler_params=pltpu.CompilerParams(vmem_limit_bytes=VMEM_LIMIT),
        cost_estimate=copy_cost(received.size),
    )(in_vmem(received), *olds)


def attention_kernel(
    last_block,
    device_blocks,
    per,
    piece,
    out_rows,
    source_rows,
    qd_rows,
    qd_begin,
    has_qd,
    has_start,
    joined,
    tokens,
    targets,
    ids_ref,
    starts_ref,
    first_ref,
    member_ref,
    drop_ref,
    kv_ref,
    *refs,
):
    refs = list(refs)
    qd_ref = refs.pop(0) if has_qd else kv_ref
    start_ref = refs.pop(0) if has_start else None
    out_refs = [refs.pop(0) for _ in range(1 if joined else targets)]
    sums_ref = None if joined else refs.pop(0)
    acc, retain, waiting, near, sems = refs[:5]
    done = refs[5] if joined else None
    earlier, start_sem = refs[-2:] if has_start else (None, None)
    scale = HEAD_WIDTH ** (-0.5)
    steps = targets * (out_rows // BLOCK_TOKENS)
    slot_of_lane = lax.broadcasted_iota(jnp.int32, (SLOTS, WIDE), 1) // BLOCK_TOKENS
    slot_row = lax.broadcasted_iota(jnp.int32, (SLOTS, WIDE), 0)
    expand = (slot_of_lane == slot_row).astype(jnp.float32)
    retain[...] = jnp.dot(
        drop_ref[...].astype(jnp.float32), expand, preferred_element_type=jnp.float32
    ) * (1.0 / keep_prob)
    acc[...] = jnp.zeros_like(acc)
    if has_start:
        fetch = pltpu.make_async_copy(start_ref, earlier, start_sem)
        fetch.start()
    lane = lax.broadcasted_iota(jnp.int32, (1, WIDE), 1)
    nt = (((1,), (1,)), ((), ()))
    tn = (((0,), (0,)), ((), ()))
    out_steps = steps // targets

    def place(i):
        if per == 1:
            source, sub = i, 0
        else:
            source, sub = lax.div(i, per), lax.rem(i, per)
        return source, sub, source * device_blocks + piece * per + sub

    def load(i):
        source, sub, j = place(i)
        starts = [starts_ref[j * SLOTS + s] for s in range(SLOTS)]
        q, do = [
            qd_ref[
                pl.ds(
                    pl.multiple_of(
                        source * qd_rows + (n * per + sub) * BLOCK_TOKENS + qd_begin, 16
                    ),
                    BLOCK_TOKENS,
                ),
                :,
            ]
            for n in range(2)
        ]
        keys, vals = [
            jnp.concatenate(
                [kv_ref[pl.ds(pl.multiple_of(r + n * tokens, 16), BLOCK_TOKENS), :] for r in starts],
                axis=0,
            )
            for n in range(2)
        ]
        return q, do, keys, vals

    def score(i):
        q, do, keys, vals = load(i)
        logits = lax.dot_general(q, keys, nt, preferred_element_type=jnp.float32)
        raw = lax.dot_general(do, vals, nt, preferred_element_type=jnp.float32)
        return logits, raw

    def factor(i, u, logits, raw):
        j = place(i)[2]
        block_id = first_ref[0] + j
        absent = ((block_id == 0) & (lane < BLOCK_TOKENS)) | (
            (block_id == last_block) & (lane >= 2 * BLOCK_TOKENS) & (lane < 3 * BLOCK_TOKENS)
        )
        keep = retain[pl.ds(j, 1), :]
        for r in range(0, BLOCK_TOKENS, STRIP):
            part = jnp.where(absent, -jnp.inf, logits[r : r + STRIP])
            top = jnp.max(part, axis=-1, keepdims=True)
            expd = jnp.exp2((part - top) * (scale / math.log(2.0)))
            probs = expd * (1.0 / jnp.sum(expd, axis=-1, keepdims=True))
            kept = probs * keep
            weighted = kept * raw[r : r + STRIP]
            delta = jnp.sum(weighted, axis=-1, keepdims=True)
            waiting[u, pl.ds(r, STRIP), :] = (weighted - probs * delta).astype(jnp.bfloat16)
            waiting[u, pl.ds(BLOCK_TOKENS + r, STRIP), :] = kept.astype(jnp.bfloat16)

    def finish(i, u):
        j = place(i)[2]
        q, do, keys, vals = load(i)
        factors = waiting[u]
        dq = jnp.dot(factors[:BLOCK_TOKENS], keys, preferred_element_type=jnp.float32) * scale
        att = jnp.dot(factors[BLOCK_TOKENS:], vals, preferred_element_type=jnp.float32)
        none = jnp.zeros_like(q)
        pair = jnp.concatenate(
            [jnp.concatenate([q, none], axis=1), jnp.concatenate([none, do], axis=1)], axis=0
        )
        terms = lax.dot_general(
            factors[:, : OWN * BLOCK_TOKENS], pair, tn, preferred_element_type=jnp.float32
        )
        for s in range(OWN):
            acc[block_rows(ids_ref[j * SLOTS + s]), :] += terms[
                s * BLOCK_TOKENS : (s + 1) * BLOCK_TOKENS
            ]
        target, pos = lax.div(i, out_steps), lax.rem(i, out_steps)
        near[target, block_rows(pos), :] = att.astype(jnp.bfloat16)
        near[target, block_rows(out_steps + pos), :] = dq.astype(jnp.bfloat16)
        return factors[:, OWN * BLOCK_TOKENS :], pair

    def finish_all(first):
        done_blocks = [finish(first + u, u) for u in range(UNROLL)]
        factors, pairs = [jnp.concatenate(each, axis=0) for each in zip(*done_blocks)]
        terms = lax.dot_general(factors, pairs, tn, preferred_element_type=jnp.float32)
        for n in range(G):
            acc[block_rows(ids_ref[OWN + n]), :] += terms[
                n * BLOCK_TOKENS : (n + 1) * BLOCK_TOKENS
            ]

    def step(t, carry):
        scores = [score(t * UNROLL + u) for u in range(UNROLL)]
        finish_all((t - 1) * UNROLL)
        for u in range(UNROLL):
            factor(t * UNROLL + u, u, *scores[u])
        return carry

    for u in range(UNROLL):
        factor(u, u, *score(u))
    lax.fori_loop(1, steps // UNROLL, step, 0)
    finish_all(steps - UNROLL)
    if has_start:
        fetch.wait()
    if joined:
        rows = acc.shape[0] // targets
        stores = []
        for target in range(targets):
            part = pl.ds(target * rows, rows)
            sums = acc[part, :]
            if has_start:
                sums += earlier[part, :]
            done[target, pl.ds(0, 2 * out_rows), :] = near[target]
            done[target, pl.ds(2 * out_rows, rows), :] = (sums[:, :HEAD_WIDTH] * scale).astype(
                jnp.bfloat16
            )
            done[target, pl.ds(2 * out_rows + rows, rows), :] = sums[:, HEAD_WIDTH:].astype(
                jnp.bfloat16
            )
            stores.append(
                pltpu.make_async_copy(done.at[target], out_refs[0].at[target], sems.at[target])
            )
            stores[-1].start()
        for store in stores:
            store.wait()
    else:
        rows = acc.shape[0] // targets
        stores = [
            pltpu.make_async_copy(
                acc.at[pl.ds(n * rows, rows), :], sums_ref.at[pl.ds(n * rows, rows), :], sems.at[n]
            )
            for n in range(targets)
        ]
        for store in stores:
            store.start()
        for k, out_ref in enumerate(out_refs):
            out_ref[...] = near[member_ref[0] ^ k]
        for store in stores:
            store.wait()


def attend(
    ids, starts, first_block, member, drop, kv, qd, qd_begin, start, piece, per, joined, device_blocks, total_blocks, tokens, targets
):
    team_blocks = drop.shape[0]
    source = kv if qd is None else qd
    steps = team_blocks * per // device_blocks
    length = total_blocks * BLOCK_TOKENS
    pairs = steps * BLOCK_TOKENS * WIDE
    accumulator = (length, 2 * HEAD_WIDTH)
    out_rows = steps * BLOCK_TOKENS // targets
    if joined:
        out_shape = [
            pltpu.HBM((targets, 2 * out_rows + 2 * length // targets, HEAD_WIDTH), jnp.bfloat16)
        ]
    else:
        out_shape = [pltpu.HBM((2 * out_rows, HEAD_WIDTH), jnp.bfloat16)] * targets
    scratch = [
        pltpu.VMEM((team_blocks, WIDE), jnp.float32),
        pltpu.VMEM((UNROLL, 2 * BLOCK_TOKENS, WIDE), jnp.bfloat16),
        pltpu.VMEM((targets, 2 * out_rows, HEAD_WIDTH), jnp.bfloat16),
    ]
    scratch = [pltpu.VMEM(accumulator, jnp.float32)] + scratch + [
        pltpu.SemaphoreType.DMA((targets,))
    ]
    if not joined:
        out_shape.append(pltpu.HBM(accumulator, jnp.float32))
    if joined:
        scratch.append(pltpu.VMEM(out_shape[0].shape, jnp.bfloat16))
    sums_bytes = 8 * length * HEAD_WIDTH
    limit = VMEM_LIMIT + 2 * (kv.size + source.size) + (1 if start is None else 2) * sums_bytes
    keep = in_vmem if 2 * limit < VMEM_BYTES else lambda t: t
    flat = [keep(t.reshape(-1, HEAD_WIDTH)) for t in (kv, qd) if t is not None]
    if start is not None:
        scratch += [pltpu.VMEM(accumulator, jnp.float32), pltpu.SemaphoreType.DMA]
    operands = flat + ([] if start is None else [in_hbm(start)])
    operand_specs = [vmem] * len(flat) + [anywhere] * (start is not None)
    return pl.pallas_call(
        functools.partial(
            attention_kernel,
            total_blocks - 1,
            device_blocks,
            per,
            piece,
            out_rows,
            kv.shape[1],
            source.shape[1],
            qd_begin,
            qd is not None,
            start is not None,
            joined,
            tokens,
            targets,
        ),
        out_shape=out_shape,
        in_specs=[smem, smem, smem, smem, vmem] + operand_specs,
        out_specs=[anywhere] if joined else [vmem] * targets + [anywhere],
        scratch_shapes=scratch,
        compiler_params=pltpu.CompilerParams(vmem_limit_bytes=limit),
        cost_estimate=pl.CostEstimate(
            flops=128 * pairs * HEAD_WIDTH,
            bytes_accessed=2 * (source.size + kv.size) + 8 * length * HEAD_WIDTH,
            transcendentals=pairs,
        ),
    )(ids, starts, first_block, member, in_hbm(drop), *operands)


def per_device(queries, keys, values, grad_out, rand_blocks, global_ids, drop_mask):
    shards = lax.axis_size("seq")
    groups = lax.axis_size("head")
    shard = lax.axis_index("seq")
    heads, shard_blocks, _ = rand_blocks.shape
    tokens = queries.shape[0]
    device_blocks = tokens // BLOCK_TOKENS
    shard_tokens = shard_blocks * BLOCK_TOKENS
    teams = shards // heads
    team, member = lax.div(shard, heads), lax.rem(shard, heads)
    team_blocks = heads * shard_blocks
    total_blocks = shards * shard_blocks
    first_block = team * team_blocks
    whole = teams == 1
    pieces = device_blocks if whole else 1
    per = device_blocks // pieces
    rows = tokens // pieces
    same_team_all = (
        None
        if whole
        else [
            [(t * heads + m) * groups + g for m in range(heads) for g in range(groups)]
            for t in range(teams)
        ]
    )
    same_head = [[t * heads + m for t in range(teams)] for m in range(heads)]

    def to_heads(packed):
        return lax.all_to_all(
            packed,
            ("seq", "head"),
            split_axis=0,
            concat_axis=0,
            tiled=True,
            axis_index_groups=same_team_all,
        )

    def to_shards(results):
        received = list(results)
        for k in reversed(range(1, heads)):
            pairs = [(s, s ^ k) for s in range(shards)]
            received[k] = lax.ppermute(results[k], "seq", pairs)
        return received

    table_rows = -(-(shard_blocks + R) // 16) * 16
    sources = [[(queries, c, rows), (grad_out, c, rows)] for c in range(pieces)]
    qd_begin = 2 * tokens
    table_begin = qd_begin + 2 * rows
    kv = to_heads(
        pack(
            groups,
            heads,
            [(keys, 0, tokens), (values, 0, tokens)] + sources[0],
            (drop_mask, rand_blocks.transpose(2, 0, 1)),
            table_rows,
        )
    )
    later = [to_heads(pack(groups, heads, each)) for each in sources[1:]]
    tables = lax.dynamic_index_in_dim(
        kv.reshape(heads, groups, -1, HEAD_WIDTH)[:, :, table_begin:],
        lax.axis_index("head"),
        axis=1,
        keepdims=False,
    ).astype(jnp.int32)
    drops = tables[:, :shard_blocks, :SLOTS].reshape(team_blocks, SLOTS)
    drops = jnp.concatenate([drops[:, :3], drops[:, 3 + G :], drops[:, 3 : 3 + G]], axis=1)
    randoms = tables[:, shard_blocks : shard_blocks + R, :shard_blocks].transpose(0, 2, 1)
    randoms = randoms.reshape(team_blocks, R)
    qd = [None] + later
    if not whole:
        qd[0] = kv[:, qd_begin:table_begin]
        kv = lax.all_gather(kv[:, : 2 * tokens], "seq", axis=0, tiled=True, axis_index_groups=same_head)
    blocks = first_block + jnp.arange(team_blocks, dtype=jnp.int32)
    window = jnp.stack([blocks - 1, blocks, blocks + 1], axis=1)
    listed = jnp.concatenate(
        [window, randoms, jnp.broadcast_to(global_ids[None], (team_blocks, G))], axis=1
    )
    listed = jnp.clip(listed, 0, total_blocks - 1).reshape(-1)
    starts = listed // device_blocks * kv.shape[1] + listed % device_blocks * BLOCK_TOKENS
    pieces_out = []
    held = []
    sums = []
    for c in range(pieces):
        pieces_out.append(
            attend(
                listed,
                starts,
                first_block.reshape(1),
                member.reshape(1),
                drops,
                kv,
                qd[c],
                qd_begin if qd[c] is None else 0,
                sums[0] if sums else None,
                c,
                per,
                whole and c == pieces - 1,
                device_blocks,
                total_blocks,
                tokens,
                heads,
            )
        )
        sums = pieces_out[c][heads:]
        if c + 1 < pieces:
            held.append(pieces_out[c][1:heads])
    runs = shard_blocks // device_blocks
    begin = shard_tokens // pieces
    near = []
    for c, out in enumerate(pieces_out):
        if len(out) > 1:
            results = out[:heads]
            if c + 1 < pieces:
                results = [results[0], *held[c]]
            near.append(to_shards(results))
    att, dq = None, None
    if whole:
        rest = pieces_out[-1][0]
        if near:
            rest, *near[-1][heads // 2 :] = lax.optimization_barrier(
                (rest, *near[-1][heads // 2 :])
            )
        rest = lax.all_to_all(rest, "seq", split_axis=0, concat_axis=0, tiled=True)
    for c in range(len(near)):
        parts = [(0, rows, runs, pieces, c, att), (begin, rows, runs, pieces, c, dq)]
        att, dq = unpack(member.reshape(1), near[c], parts)
    if whole:
        c = pieces - 1
        parts = [(0, rows, runs, pieces, c, att), (begin, rows, runs, pieces, c, dq)]
        grads = [
            (2 * begin + n * shard_tokens, shard_tokens // runs, runs, 1, 0, None) for n in range(2)
        ]
        att, dq, dk, dv = unpack_all(rest, parts + grads)
    else:
        grads = lax.psum_scatter(
            sums[0], "seq", scatter_dimension=0, tiled=True, axis_index_groups=same_head
        ).reshape(heads, shard_tokens, 2, HEAD_WIDTH)
        grads = jnp.concatenate(
            [grads[:, :, 0] * HEAD_WIDTH ** (-0.5), grads[:, :, 1]], axis=1
        ).astype(jnp.bfloat16)
        grads = to_shards(
            [lax.dynamic_index_in_dim(grads, member ^ k, 0, keepdims=False) for k in range(heads)]
        )
        dk, dv = unpack(
            member.reshape(1),
            grads,
            [(n * shard_tokens, shard_tokens, 1, 1, 0, None) for n in range(2)],
        )
    return tuple(t.reshape(shard_tokens, heads * HEAD_WIDTH) for t in (att, dq, dk, dv))


def solution(mesh):
    return jax.shard_map(
        per_device,
        mesh=mesh,
        in_specs=(
            P(("seq", "head"), None),
            P(("seq", "head"), None),
            P(("seq", "head"), None),
            P(("seq", "head"), None),
            P("head", "seq", None),
            P(),
            P("head", "seq", None),
        ),
        out_specs=(P("seq", "head"), P("seq", "head"), P("seq", "head"), P("seq", "head")),
        check_vma=False,
    )
```

```python
import functools
import math

import jax
import jax.numpy as jnp
from jax import lax
from jax.experimental import pallas as pl
from jax.experimental.pallas import tpu as pltpu
from jax.sharding import PartitionSpec as P

HEAD_WIDTH = 128
BLOCK_TOKENS = 64
R = 3
G = 2
SLOTS = 3 + G + R
OWN = 3 + R
WIDE = SLOTS * BLOCK_TOKENS
NEAR = 4 * BLOCK_TOKENS
UNROLL = 8
STRIP = 16
VMEM_LIMIT = 16 * 1024 * 1024
VMEM_BYTES = 64 * 1024 * 1024

keep_prob = 0.9

vmem = pl.BlockSpec(memory_space=pltpu.VMEM)
smem = pl.BlockSpec(memory_space=pltpu.SMEM)
anywhere = pl.BlockSpec(memory_space=pl.ANY)


def in_vmem(array):
    return pltpu.with_memory_space_constraint(array, pltpu.VMEM)


def in_hbm(array):
    return pltpu.with_memory_space_constraint(array, pltpu.HBM)


def copy_cost(size):
    return pl.CostEstimate(flops=0, bytes_accessed=4 * size, transcendentals=0)


def block_rows(number):
    start = number * BLOCK_TOKENS
    if not isinstance(number, int):
        start = pl.multiple_of(start, BLOCK_TOKENS)
    return pl.ds(start, BLOCK_TOKENS)


def pack_kernel(heads, groups, sources, table_rows, *refs):
    refs = list(refs)
    if table_rows:
        drop_hbm, rand_hbm = refs.pop(0), refs.pop(0)
        table, drop_ref, rand_ref, table_sems = refs[-4:]
        refs = refs[:-4]
    count = len(sources)
    arrays, out_ref = refs[:count], refs[count]
    wholes, packed, in_sems, out_sems = refs[count + 1 : -3], refs[-3], refs[-2], refs[-1]
    width = heads * HEAD_WIDTH
    loads = []
    for h in range(groups):
        for n, (at, rows) in enumerate(sources):
            columns = pl.ds(h * width, width)
            loads.append(
                pltpu.make_async_copy(
                    arrays[n].at[pl.ds(at * rows, rows), columns],
                    wholes[n].at[:, columns],
                    in_sems.at[h, n],
                )
            )
    for load in loads:
        load.start()
    begin = sum(rows for _, rows in sources)
    if table_rows:
        fetches = [
            pltpu.make_async_copy(drop_hbm, drop_ref, table_sems.at[0]),
            pltpu.make_async_copy(rand_hbm, rand_ref, table_sems.at[1]),
        ]
        for fetch in fetches:
            fetch.start()
        for fetch in fetches:
            fetch.wait()
        blocks = drop_ref.shape[1]
        table[...] = jnp.zeros_like(table)
        for m in range(heads):
            table[pl.ds(0, blocks), pl.ds(0, SLOTS)] = drop_ref[m].astype(jnp.float32)
            for r in range(R):
                table[pl.ds(blocks + r, 1), pl.ds(0, blocks)] = rand_ref[
                    r, pl.ds(m, 1), :
                ].astype(jnp.float32)
            rounded = table[...].astype(jnp.bfloat16)
            for g in range(groups):
                packed[m, g, pl.ds(begin, table_rows), :] = rounded
    stores = []
    for g in range(groups):
        for n in range(count):
            loads[g * count + n].wait()
        for m in range(heads):
            begin = 0
            for n, (_, rows) in enumerate(sources):
                packed[m, g, pl.ds(begin, rows), :] = wholes[n][
                    :, pl.ds((g * heads + m) * HEAD_WIDTH, HEAD_WIDTH)
                ]
                begin += rows
        stores.append(
            pltpu.make_async_copy(packed.at[:, g], out_ref.at[:, g], out_sems.at[g])
        )
        stores[-1].start()
    for store in stores:
        store.wait()


def pack(groups, heads, sources, tables=(), table_rows=0):
    total = sum(rows for _, _, rows in sources) + table_rows
    shape = (heads, groups, total, HEAD_WIDTH)
    scratch = [
        pltpu.VMEM((rows, groups * heads * HEAD_WIDTH), jnp.bfloat16) for _, _, rows in sources
    ] + [
        pltpu.VMEM(shape, jnp.bfloat16),
        pltpu.SemaphoreType.DMA((groups, len(sources))),
        pltpu.SemaphoreType.DMA((groups,)),
    ]
    if table_rows:
        scratch.append(pltpu.VMEM((table_rows, HEAD_WIDTH), jnp.float32))
        scratch += [pltpu.VMEM(t.shape, t.dtype) for t in tables]
        scratch.append(pltpu.SemaphoreType.DMA((len(tables),)))
    packed = pl.pallas_call(
        functools.partial(
            pack_kernel, heads, groups, tuple((at, rows) for _, at, rows in sources), table_rows
        ),
        out_shape=pltpu.HBM(shape, jnp.bfloat16),
        in_specs=[anywhere] * (len(tables) + len(sources)),
        out_specs=anywhere,
        scratch_shapes=scratch,
        compiler_params=pltpu.CompilerParams(vmem_limit_bytes=VMEM_LIMIT),
        cost_estimate=copy_cost(math.prod(shape)),
    )(*[in_hbm(t) for t in tables], *[in_hbm(a) for a, _, _ in sources])
    return packed.reshape(heads * groups, total, HEAD_WIDTH)


def unpack_kernel(parts, member_ref, *refs):
    outs = refs[len(refs) - len(parts) :]
    heads = outs[0].shape[-1] // HEAD_WIDTH
    for n in range(heads):
        k = (heads - n) % heads
        column = pl.multiple_of((member_ref[0] ^ k) * HEAD_WIDTH, HEAD_WIDTH)
        for begin, out in zip(parts, outs):
            runs, _, rows, _ = out.shape
            for i in range(runs):
                out[i, 0, :, pl.ds(column, HEAD_WIDTH)] = refs[n][pl.ds(begin + i * rows, rows), :]


def unpack(member, received, parts):
    heads = len(received)
    shapes, specs, olds, aliases, size = [], [], [], {}, 0
    for n, (_, rows, runs, pieces, piece, old) in enumerate(parts):
        shapes.append(
            jax.ShapeDtypeStruct((runs, pieces, rows, heads * HEAD_WIDTH), jnp.bfloat16)
        )
        specs.append(
            pl.BlockSpec(
                (runs, 1, rows, heads * HEAD_WIDTH),
                functools.partial(lambda piece, h: (0, piece, 0, 0), piece),
            )
        )
        size += rows * runs * heads * HEAD_WIDTH
        if old is not None:
            aliases[1 + heads + len(olds)] = n
            olds.append(old)
    return pl.pallas_call(
        functools.partial(unpack_kernel, tuple(part[0] for part in parts)),
        grid=(1,),
        out_shape=shapes,
        in_specs=[smem]
        + [pl.BlockSpec(received[0].shape, lambda h: (0, 0))] * heads
        + [pl.BlockSpec(memory_space=pl.ANY)] * len(olds),
        out_specs=specs,
        input_output_aliases=aliases,
        compiler_params=pltpu.CompilerParams(vmem_limit_bytes=VMEM_LIMIT),
        cost_estimate=copy_cost(size),
    )(member, received[0], *received[:0:-1], *olds)


def unpack_all_kernel(parts, piece_ref, *refs):
    sems = refs[-1]
    stages = refs[-1 - len(parts) : -1]
    outs = refs[-1 - 2 * len(parts) : -1 - len(parts)]
    stores = []
    for (begin, rows, runs, _, piece), stage, out in zip(parts, stages, outs):
        for i in range(runs):
            for m in range(piece_ref.shape[0]):
                stage[i, :, pl.ds(m * HEAD_WIDTH, HEAD_WIDTH)] = piece_ref[
                    m, pl.ds(begin + i * rows, rows), :
                ]
            stores.append(
                pltpu.make_async_copy(stage.at[i], out.at[i, piece], sems.at[len(stores)])
            )
            stores[-1].start()
    for store in stores:
        store.wait()


def unpack_all(received, parts):
    heads = received.shape[0]
    shapes, stages, olds, aliases, count = [], [], [], {}, 0
    for n, (_, rows, runs, pieces, _, old) in enumerate(parts):
        shapes.append(pltpu.HBM((runs, pieces, rows, heads * HEAD_WIDTH), jnp.bfloat16))
        stages.append(pltpu.VMEM((runs, rows, heads * HEAD_WIDTH), jnp.bfloat16))
        count += runs
        if old is not None:
            aliases[1 + len(olds)] = n
            olds.append(old)
    return pl.pallas_call(
        functools.partial(unpack_all_kernel, tuple(part[:-1] for part in parts)),
        out_shape=shapes,
        in_specs=[vmem] + [anywhere] * len(olds),
        out_specs=[anywhere] * len(shapes),
        input_output_aliases=aliases,
        scratch_shapes=stages + [pltpu.SemaphoreType.DMA((count,))],
        compiler_params=pltpu.CompilerParams(vmem_limit_bytes=VMEM_LIMIT),
        cost_estimate=copy_cost(received.size),
    )(in_vmem(received), *olds)


def attention_kernel(
    last_block,
    device_blocks,
    per,
    piece,
    out_rows,
    source_rows,
    qd_rows,
    qd_begin,
    has_qd,
    has_start,
    joined,
    tokens,
    targets,
    ids_ref,
    starts_ref,
    first_ref,
    member_ref,
    drop_ref,
    kv_ref,
    *refs,
):
    refs = list(refs)
    qd_ref = refs.pop(0) if has_qd else kv_ref
    start_ref = refs.pop(0) if has_start else None
    out_refs = [refs.pop(0) for _ in range(1 if joined else targets)]
    sums_ref = None if joined else refs.pop(0)
    acc, retain, waiting, near, sems = refs[:5]
    done = refs[5] if joined else None
    earlier, start_sem = refs[-2:] if has_start else (None, None)
    scale = HEAD_WIDTH ** (-0.5)
    steps = targets * (out_rows // BLOCK_TOKENS)
    slot_of_lane = lax.broadcasted_iota(jnp.int32, (SLOTS, WIDE), 1) // BLOCK_TOKENS
    slot_row = lax.broadcasted_iota(jnp.int32, (SLOTS, WIDE), 0)
    expand = (slot_of_lane == slot_row).astype(jnp.float32)
    retain[...] = jnp.dot(
        drop_ref[...].astype(jnp.float32), expand, preferred_element_type=jnp.float32
    ) * (1.0 / keep_prob)
    acc[...] = jnp.zeros_like(acc)
    if has_start:
        fetch = pltpu.make_async_copy(start_ref, earlier, start_sem)
        fetch.start()
    lane = lax.broadcasted_iota(jnp.int32, (1, NEAR), 1)
    nt = (((1,), (1,)), ((), ()))
    tn = (((0,), (0,)), ((), ()))
    out_steps = steps // targets

    def place(i):
        if per == 1:
            source, sub = i, 0
        else:
            source, sub = lax.div(i, per), lax.rem(i, per)
        return source, sub, source * device_blocks + piece * per + sub

    def load(i):
        source, sub, j = place(i)
        starts = [starts_ref[j * SLOTS + s] for s in range(SLOTS)]
        q, do = [
            qd_ref[
                pl.ds(
                    pl.multiple_of(
                        source * qd_rows + (n * per + sub) * BLOCK_TOKENS + qd_begin, 16
                    ),
                    BLOCK_TOKENS,
                ),
                :,
            ]
            for n in range(2)
        ]
        keys, vals = [
            jnp.concatenate(
                [kv_ref[pl.ds(pl.multiple_of(r + n * tokens, 16), BLOCK_TOKENS), :] for r in starts],
                axis=0,
            )
            for n in range(2)
        ]
        return q, do, keys, vals

    def score(i):
        q, do, keys, vals = load(i)
        logits = lax.dot_general(q, keys, nt, preferred_element_type=jnp.float32)
        raw = lax.dot_general(do, vals, nt, preferred_element_type=jnp.float32)
        return logits, raw

    def factor(i, u, logits, raw):
        j = place(i)[2]
        block_id = first_ref[0] + j
        absent = ((block_id == 0) & (lane < BLOCK_TOKENS)) | (
            (block_id == last_block) & (lane >= 2 * BLOCK_TOKENS) & (lane < 3 * BLOCK_TOKENS)
        )
        keep = retain[pl.ds(j, 1), :]
        for r in range(0, BLOCK_TOKENS, STRIP):
            part = logits[r : r + STRIP]
            part = jnp.concatenate(
                [jnp.where(absent, -jnp.inf, part[:, :NEAR]), part[:, NEAR:]], axis=1
            )
            top = jnp.max(part, axis=-1, keepdims=True)
            expd = jnp.exp2((part - top) * (scale / math.log(2.0)))
            probs = expd * (1.0 / jnp.sum(expd, axis=-1, keepdims=True))
            kept = probs * keep
            weighted = kept * raw[r : r + STRIP]
            delta = jnp.sum(weighted, axis=-1, keepdims=True)
            waiting[u, pl.ds(r, STRIP), :] = (weighted - probs * delta).astype(jnp.bfloat16)
            waiting[u, pl.ds(BLOCK_TOKENS + r, STRIP), :] = kept.astype(jnp.bfloat16)

    def finish(i, u):
        j = place(i)[2]
        q, do, keys, vals = load(i)
        factors = waiting[u]
        dq = jnp.dot(factors[:BLOCK_TOKENS], keys, preferred_element_type=jnp.float32) * scale
        att = jnp.dot(factors[BLOCK_TOKENS:], vals, preferred_element_type=jnp.float32)
        none = jnp.zeros_like(q)
        pair = jnp.concatenate(
            [jnp.concatenate([q, none], axis=1), jnp.concatenate([none, do], axis=1)], axis=0
        )
        terms = lax.dot_general(
            factors[:, : OWN * BLOCK_TOKENS], pair, tn, preferred_element_type=jnp.float32
        )
        for s in range(OWN):
            acc[block_rows(ids_ref[j * SLOTS + s]), :] += terms[
                s * BLOCK_TOKENS : (s + 1) * BLOCK_TOKENS
            ]
        target, pos = lax.div(i, out_steps), lax.rem(i, out_steps)
        near[target, block_rows(pos), :] = att.astype(jnp.bfloat16)
        near[target, block_rows(out_steps + pos), :] = dq.astype(jnp.bfloat16)
        return factors[:, OWN * BLOCK_TOKENS :], pair

    def finish_all(first):
        done_blocks = [finish(first + u, u) for u in range(UNROLL)]
        factors, pairs = [jnp.concatenate(each, axis=0) for each in zip(*done_blocks)]
        terms = lax.dot_general(factors, pairs, tn, preferred_element_type=jnp.float32)
        for n in range(G):
            acc[block_rows(ids_ref[OWN + n]), :] += terms[
                n * BLOCK_TOKENS : (n + 1) * BLOCK_TOKENS
            ]

    def step(t, carry):
        scores = [score(t * UNROLL + u) for u in range(UNROLL)]
        finish_all((t - 1) * UNROLL)
        for u in range(UNROLL):
            factor(t * UNROLL + u, u, *scores[u])
        return carry

    for u in range(UNROLL):
        factor(u, u, *score(u))
    lax.fori_loop(1, steps // UNROLL, step, 0)
    finish_all(steps - UNROLL)
    if has_start:
        fetch.wait()
    if joined:
        rows = acc.shape[0] // targets
        stores = []
        for target in range(targets):
            part = pl.ds(target * rows, rows)
            sums = acc[part, :]
            if has_start:
                sums += earlier[part, :]
            done[target, pl.ds(0, 2 * out_rows), :] = near[target]
            done[target, pl.ds(2 * out_rows, rows), :] = (sums[:, :HEAD_WIDTH] * scale).astype(
                jnp.bfloat16
            )
            done[target, pl.ds(2 * out_rows + rows, rows), :] = sums[:, HEAD_WIDTH:].astype(
                jnp.bfloat16
            )
            stores.append(
                pltpu.make_async_copy(done.at[target], out_refs[0].at[target], sems.at[target])
            )
            stores[-1].start()
        for store in stores:
            store.wait()
    else:
        rows = acc.shape[0] // targets
        stores = [
            pltpu.make_async_copy(
                acc.at[pl.ds(n * rows, rows), :], sums_ref.at[pl.ds(n * rows, rows), :], sems.at[n]
            )
            for n in range(targets)
        ]
        for store in stores:
            store.start()
        for k, out_ref in enumerate(out_refs):
            out_ref[...] = near[member_ref[0] ^ k]
        for store in stores:
            store.wait()


def attend(
    ids, starts, first_block, member, drop, kv, qd, qd_begin, start, piece, per, joined, device_blocks, total_blocks, tokens, targets
):
    team_blocks = drop.shape[0]
    source = kv if qd is None else qd
    steps = team_blocks * per // device_blocks
    length = total_blocks * BLOCK_TOKENS
    pairs = steps * BLOCK_TOKENS * WIDE
    accumulator = (length, 2 * HEAD_WIDTH)
    out_rows = steps * BLOCK_TOKENS // targets
    if joined:
        out_shape = [
            pltpu.HBM((targets, 2 * out_rows + 2 * length // targets, HEAD_WIDTH), jnp.bfloat16)
        ]
    else:
        out_shape = [pltpu.HBM((2 * out_rows, HEAD_WIDTH), jnp.bfloat16)] * targets
    scratch = [
        pltpu.VMEM((team_blocks, WIDE), jnp.float32),
        pltpu.VMEM((UNROLL, 2 * BLOCK_TOKENS, WIDE), jnp.bfloat16),
        pltpu.VMEM((targets, 2 * out_rows, HEAD_WIDTH), jnp.bfloat16),
    ]
    scratch = [pltpu.VMEM(accumulator, jnp.float32)] + scratch + [
        pltpu.SemaphoreType.DMA((targets,))
    ]
    if not joined:
        out_shape.append(pltpu.HBM(accumulator, jnp.float32))
    if joined:
        scratch.append(pltpu.VMEM(out_shape[0].shape, jnp.bfloat16))
    sums_bytes = 8 * length * HEAD_WIDTH
    limit = VMEM_LIMIT + 2 * (kv.size + source.size) + (1 if start is None else 2) * sums_bytes
    keep = in_vmem if 2 * limit < VMEM_BYTES else lambda t: t
    flat = [keep(t.reshape(-1, HEAD_WIDTH)) for t in (kv, qd) if t is not None]
    if start is not None:
        scratch += [pltpu.VMEM(accumulator, jnp.float32), pltpu.SemaphoreType.DMA]
    operands = flat + ([] if start is None else [in_hbm(start)])
    operand_specs = [vmem] * len(flat) + [anywhere] * (start is not None)
    return pl.pallas_call(
        functools.partial(
            attention_kernel,
            total_blocks - 1,
            device_blocks,
            per,
            piece,
            out_rows,
            kv.shape[1],
            source.shape[1],
            qd_begin,
            qd is not None,
            start is not None,
            joined,
            tokens,
            targets,
        ),
        out_shape=out_shape,
        in_specs=[smem, smem, smem, smem, vmem] + operand_specs,
        out_specs=[anywhere] if joined else [vmem] * targets + [anywhere],
        scratch_shapes=scratch,
        compiler_params=pltpu.CompilerParams(vmem_limit_bytes=limit),
        cost_estimate=pl.CostEstimate(
            flops=128 * pairs * HEAD_WIDTH,
            bytes_accessed=2 * (source.size + kv.size) + 8 * length * HEAD_WIDTH,
            transcendentals=pairs,
        ),
    )(ids, starts, first_block, member, in_hbm(drop), *operands)


def per_device(queries, keys, values, grad_out, rand_blocks, global_ids, drop_mask):
    shards = lax.axis_size("seq")
    groups = lax.axis_size("head")
    shard = lax.axis_index("seq")
    heads, shard_blocks, _ = rand_blocks.shape
    tokens = queries.shape[0]
    device_blocks = tokens // BLOCK_TOKENS
    shard_tokens = shard_blocks * BLOCK_TOKENS
    teams = shards // heads
    team, member = lax.div(shard, heads), lax.rem(shard, heads)
    team_blocks = heads * shard_blocks
    total_blocks = shards * shard_blocks
    first_block = team * team_blocks
    whole = teams == 1
    pieces = device_blocks if whole else 1
    per = device_blocks // pieces
    rows = tokens // pieces
    same_team_all = (
        None
        if whole
        else [
            [(t * heads + m) * groups + g for m in range(heads) for g in range(groups)]
            for t in range(teams)
        ]
    )
    same_head = [[t * heads + m for t in range(teams)] for m in range(heads)]

    def to_heads(packed):
        return lax.all_to_all(
            packed,
            ("seq", "head"),
            split_axis=0,
            concat_axis=0,
            tiled=True,
            axis_index_groups=same_team_all,
        )

    def to_shards(results):
        received = list(results)
        for k in reversed(range(1, heads)):
            pairs = [(s, s ^ k) for s in range(shards)]
            received[k] = lax.ppermute(results[k], "seq", pairs)
        return received

    table_rows = -(-(shard_blocks + R) // 16) * 16
    sources = [[(queries, c, rows), (grad_out, c, rows)] for c in range(pieces)]
    qd_begin = 2 * tokens
    table_begin = qd_begin + 2 * rows
    kv = to_heads(
        pack(
            groups,
            heads,
            [(keys, 0, tokens), (values, 0, tokens)] + sources[0],
            (drop_mask, rand_blocks.transpose(2, 0, 1)),
            table_rows,
        )
    )
    later = [to_heads(pack(groups, heads, each)) for each in sources[1:]]
    tables = lax.dynamic_index_in_dim(
        kv.reshape(heads, groups, -1, HEAD_WIDTH)[:, :, table_begin:],
        lax.axis_index("head"),
        axis=1,
        keepdims=False,
    ).astype(jnp.int32)
    drops = tables[:, :shard_blocks, :SLOTS].reshape(team_blocks, SLOTS)
    drops = jnp.concatenate([drops[:, :3], drops[:, 3 + G :], drops[:, 3 : 3 + G]], axis=1)
    randoms = tables[:, shard_blocks : shard_blocks + R, :shard_blocks].transpose(0, 2, 1)
    randoms = randoms.reshape(team_blocks, R)
    qd = [None] + later
    if not whole:
        qd[0] = kv[:, qd_begin:table_begin]
        kv = lax.all_gather(kv[:, : 2 * tokens], "seq", axis=0, tiled=True, axis_index_groups=same_head)
    blocks = first_block + jnp.arange(team_blocks, dtype=jnp.int32)
    window = jnp.stack([blocks - 1, blocks, blocks + 1], axis=1)
    listed = jnp.concatenate(
        [window, randoms, jnp.broadcast_to(global_ids[None], (team_blocks, G))], axis=1
    )
    listed = jnp.clip(listed, 0, total_blocks - 1).reshape(-1)
    starts = listed // device_blocks * kv.shape[1] + listed % device_blocks * BLOCK_TOKENS
    pieces_out = []
    held = []
    sums = []
    for c in range(pieces):
        pieces_out.append(
            attend(
                listed,
                starts,
                first_block.reshape(1),
                member.reshape(1),
                drops,
                kv,
                qd[c],
                qd_begin if qd[c] is None else 0,
                sums[0] if sums else None,
                c,
                per,
                whole and c == pieces - 1,
                device_blocks,
                total_blocks,
                tokens,
                heads,
            )
        )
        sums = pieces_out[c][heads:]
        if c + 1 < pieces:
            held.append(pieces_out[c][1:heads])
    runs = shard_blocks // device_blocks
    begin = shard_tokens // pieces
    near = []
    for c, out in enumerate(pieces_out):
        if len(out) > 1:
            results = out[:heads]
            if c + 1 < pieces:
                results = [results[0], *held[c]]
            near.append(to_shards(results))
    att, dq = None, None
    if whole:
        rest = pieces_out[-1][0]
        if near:
            rest, *near[-1][heads // 2 :] = lax.optimization_barrier(
                (rest, *near[-1][heads // 2 :])
            )
        rest = lax.all_to_all(rest, "seq", split_axis=0, concat_axis=0, tiled=True)
    for c in range(len(near)):
        parts = [(0, rows, runs, pieces, c, att), (begin, rows, runs, pieces, c, dq)]
        att, dq = unpack(member.reshape(1), near[c], parts)
    if whole:
        c = pieces - 1
        parts = [(0, rows, runs, pieces, c, att), (begin, rows, runs, pieces, c, dq)]
        grads = [
            (2 * begin + n * shard_tokens, shard_tokens // runs, runs, 1, 0, None) for n in range(2)
        ]
        att, dq, dk, dv = unpack_all(rest, parts + grads)
    else:
        grads = lax.psum_scatter(
            sums[0], "seq", scatter_dimension=0, tiled=True, axis_index_groups=same_head
        ).reshape(heads, shard_tokens, 2, HEAD_WIDTH)
        grads = jnp.concatenate(
            [grads[:, :, 0] * HEAD_WIDTH ** (-0.5), grads[:, :, 1]], axis=1
        ).astype(jnp.bfloat16)
        grads = to_shards(
            [lax.dynamic_index_in_dim(grads, member ^ k, 0, keepdims=False) for k in range(heads)]
        )
        dk, dv = unpack(
            member.reshape(1),
            grads,
            [(n * shard_tokens, shard_tokens, 1, 1, 0, None) for n in range(2)],
        )
    return tuple(t.reshape(shard_tokens, heads * HEAD_WIDTH) for t in (att, dq, dk, dv))


def solution(mesh):
    return jax.shard_map(
        per_device,
        mesh=mesh,
        in_specs=(
            P(("seq", "head"), None),
            P(("seq", "head"), None),
            P(("seq", "head"), None),
            P(("seq", "head"), None),
            P("head", "seq", None),
            P(),
            P("head", "seq", None),
        ),
        out_specs=(P("seq", "head"), P("seq", "head"), P("seq", "head"), P("seq", "head")),
        check_vma=False,
    )
```
